32 devices in a mesh: grp: 2 (over x), rep: 16 (over z, y, core).
Axes of the slice: x: 2, y: 2, z: 4, core: 2. Of those that a mesh axis runs over, the one named last changes fastest.
Arguments:
- tokens: bfloat16 [2, 4096, 2048], P(None, ('grp', 'rep')), may hold values from -6 to 6
- attn_gain: bfloat16 [2048], P('grp'), may hold values from 0.5 to 1.5
- w_query: bfloat16 [2048, 2048], P('grp'), may hold values from -0.25 to 0.25
- w_key: bfloat16 [2048, 2048], P('grp'), may hold values from -0.125 to 0.125
- w_value: bfloat16 [2048, 2048], P('grp'), may hold values from -0.125 to 0.125
- w_output: bfloat16 [2048, 2048], P('grp'), may hold values from -0.5 to 0.5
- mlp_gain: bfloat16 [2048], P('grp'), may hold values from 0.5 to 1.5
- w_gate: bfloat16 [2048, 4096], P('grp'), may hold values from -0.125 to 0.125
- w_up: bfloat16 [2048, 4096], P('grp'), may hold values from -0.125 to 0.125
- w_down: bfloat16 [4096, 2048], P('grp'), may hold values from -0.1875 to 0.1875
- out_grad: bfloat16 [2, 4096, 2048], P(None, ('grp', 'rep')), may hold values from -6 to 6
- lengths: int32 [2, 4], replicated, may hold values from 1 to 64, 128 in all within a row
Outputs:
- block_out: bfloat16 [2, 4096, 2048], P(None, ('grp', 'rep'))
- token_grad: bfloat16 [2, 4096, 2048], P(None, ('grp', 'rep'))
- attn_gain_grad: float32 [2048], P(('grp', 'rep'))
- query_grad: float32 [2048, 2048], P(('grp', 'rep'))
- key_grad: float32 [2048, 2048], P(('grp', 'rep'))
- value_grad: float32 [2048, 2048], P(('grp', 'rep'))
- output_grad: float32 [2048, 2048], P(('grp', 'rep'))
- mlp_gain_grad: float32 [2048], P(('grp', 'rep'))
- gate_grad: float32 [2048, 4096], P(('grp', 'rep'))
- up_grad: float32 [2048, 4096], P(('grp', 'rep'))
- down_grad: float32 [4096, 2048], P(('grp', 'rep'))
The draws below stay inside these ranges and needn't reach their ends.
Inputs may be any that keep to these rules, and one draw needn't show every extreme that they name: `lengths`: each row sums to 128 and its largest entry is 64.
All inputs are finite; a program needn't handle non-finite values.
Results may differ from the reference program's by a relative error of at most 0.018.
Values may be sent and summed in bfloat16 or wider, within the bound.
A program may use at most 448 MiB of HBM per device.

```python
import math
import jax
import jax.numpy as jnp
import numpy as np
from jax import lax

D = 2048
H = 32
HD = 64
FF = 4096
WINDOW = 2048
UNITS = 64
MB = 2
ROWS = 128
SEQ_MAX = 2048
SEQS = 4
TOKENS = 4096
N_GRP = 2
N_REP = 16


def steps_of(key, shape, split, least, high):
    level, own = 1.0, jax.random.fold_in(key, 6)
    for axis_at, blocks in split:
        draws = jnp.exp(jax.random.uniform(jax.random.fold_in(own, axis_at), (blocks,), jnp.float32, least / len(split), high / len(split)))
        level = level * jnp.repeat(draws, shape[axis_at] // blocks).reshape([-1 if axis == axis_at else 1 for axis in range(len(shape))])
    return level


def length_profile(amount, total, most, skew):
    weights = [(1 << 20) // math.isqrt(standing ** skew) + 1 for standing in range(2, amount + 1)]
    spare, given = total - most - (amount - 1), [1] * (amount - 1)
    while spare > 0:
        movable = [i for i in range(amount - 1) if given[i] < most]
        pool, budget = sum([weights[i] for i in movable]), spare
        for i in movable:
            addition = min(most - given[i], max(1, budget * weights[i] // pool), spare)
            given[i] = given[i] + addition
            spare = spare - addition
    return np.array([most] + given)


def uneven(key, amount, total, reach, slope):
    if amount == 2:
        one = jax.random.randint(key, (), max(1, total - reach), min(reach, total - 1) + 1)
        return jnp.stack([one, total - one])
    sizes = jnp.asarray(length_profile(amount, total, reach, slope), jnp.int32)
    couples = (amount - 1) // 2
    source_of, taker = sizes[1:1 + 2 * couples:2], sizes[2:2 + 2 * couples:2]
    margin = jnp.minimum(source_of - 1, reach - taker)
    shifted = jax.random.randint(jax.random.fold_in(key, 1), (couples,), 0, 1 << 20) % (margin + 1)
    sizes = sizes.at[1:1 + 2 * couples:2].set(source_of - shifted).at[2:2 + 2 * couples:2].set(taker + shifted)
    return sizes[jax.random.permutation(jax.random.fold_in(key, 2), amount)]


def gaussian(key, shape, width, bound, cuts=(), kind=jnp.bfloat16):
    factor_of = steps_of(key, shape, cuts, -0.22, 0.18) if cuts else 1.0
    entries = jax.random.normal(key, shape, jnp.float32) * width * factor_of
    return jnp.minimum(jnp.maximum(entries, -bound), bound).astype(kind)


def setup_inputs(seed: int = 0) -> dict:
    seeds = jax.random.split(jax.random.key(seed), 13)
    return {
        "tokens": gaussian(seeds[0], (MB, TOKENS, D), 1.0, 6.0, ((1, 32),)),
        "attn_gain": jnp.clip(1.0 + 0.1 * jax.random.normal(seeds[1], (D,), jnp.float32), 0.5, 1.5).astype(jnp.bfloat16),
        "w_query": gaussian(seeds[2], (D, D), (D // 4) ** -0.5, 0.25, ((0, 2),)),
        "w_key": gaussian(seeds[3], (D, D), D ** -0.5, 0.125, ((0, 2),)),
        "w_value": gaussian(seeds[4], (D, D), D ** -0.5, 0.125, ((0, 2),)),
        "w_output": gaussian(seeds[5], (D, D), (D // 16) ** -0.5, 0.5, ((0, 2),)),
        "mlp_gain": jnp.clip(1.0 + 0.1 * jax.random.normal(seeds[6], (D,), jnp.float32), 0.5, 1.5).astype(jnp.bfloat16),
        "w_gate": gaussian(seeds[7], (D, FF), D ** -0.5, 0.125, ((0, 2),)),
        "w_up": gaussian(seeds[8], (D, FF), D ** -0.5, 0.125, ((0, 2),)),
        "w_down": gaussian(seeds[9], (FF, D), (FF // 4) ** -0.5, 0.1875, ((0, 2),)),
        "out_grad": gaussian(seeds[10], (MB, TOKENS, D), 1.0, 6.0, ((1, 32),)),
        "lengths": jax.vmap(lambda own: uneven(own, SEQS, ROWS, UNITS, 1))(jax.random.split(seeds[11], MB)).reshape((MB, SEQS)).astype(jnp.int32),
    }


@jax.custom_vjp
def low(v):
    return lax.optimization_barrier(v.astype(jnp.bfloat16)).astype(jnp.float32)

@jax.custom_vjp
def low_back(v):
    return v

def low_keep(v):
    return (low(v), None)

def low_pass(kept, grad):
    return (grad,)

def back_keep(v):
    return (v, None)

def back_low(kept, grad):
    return (low(grad),)
low.defvjp(low_keep, low_pass)
low_back.defvjp(back_keep, back_low)
epsilon = 1e-05
rope_base = 10000.0
masked_score = -1e+30

def matmul(left_side, right_side):
    return jnp.dot(left_side, right_side, precision=lax.Precision.HIGHEST, preferred_element_type=jnp.float32)

def rms_norm(values, gain_full):
    inverse = lax.rsqrt(lax.optimization_barrier(jnp.mean(values * values, axis=-1, keepdims=True)) + epsilon)
    return values * inverse * gain_full

def rotary(values, positions):
    half_width = HD // 2
    frequency = jnp.power(rope_base, -2.0 * jnp.arange(half_width, dtype=jnp.float32) / HD)
    angles = positions.astype(jnp.float32)[:, None] * frequency[None, :]
    cosine = jnp.cos(angles)[:, None, :]
    sine_table = jnp.sin(angles)[:, None, :]
    first_half = values[..., :half_width]
    second_half = values[..., half_width:]
    return jnp.concatenate([first_half * cosine - second_half * sine_table, second_half * cosine + first_half * sine_table], axis=-1)

def attend_sequence(pieces):
    queries, keys_in, values_in = pieces
    head_shape = (SEQ_MAX, H, HD)
    positions = jnp.arange(SEQ_MAX, dtype=jnp.int32)
    rot_q = low(rotary(queries.reshape(head_shape), positions))
    rot_k = low(rotary(keys_in.reshape(head_shape), positions))
    front_pad = jnp.zeros((WINDOW, H, HD), jnp.float32)
    key_pad = jnp.concatenate([front_pad, rot_k], axis=0)
    value_pad = jnp.concatenate([front_pad, values_in.reshape(head_shape)], axis=0)
    block_rows = math.gcd(SEQ_MAX, 512)
    score_scale = 1.0 / math.sqrt(HD)

    def one_block(query_start):
        query_block = lax.dynamic_slice_in_dim(rot_q, query_start, block_rows, 0)
        key_block = lax.dynamic_slice_in_dim(key_pad, query_start, block_rows + WINDOW, 0)
        value_block = lax.dynamic_slice_in_dim(value_pad, query_start, block_rows + WINDOW, 0)
        query_pos = query_start + jnp.arange(block_rows, dtype=jnp.int32)
        key_pos = query_start - WINDOW + jnp.arange(block_rows + WINDOW, dtype=jnp.int32)
        scores = low_back(jnp.einsum('qhd,khd->hqk', query_block, key_block, precision=lax.Precision.HIGHEST) * score_scale)
        allowed = (key_pos[None, :] >= 0) & (key_pos[None, :] <= query_pos[:, None]) & (query_pos[:, None] - key_pos[None, :] < WINDOW)
        scores = jnp.where(allowed[None], scores, masked_score)
        row_max = lax.optimization_barrier(jnp.max(scores, axis=-1, keepdims=True))
        weights_exp = jnp.exp(scores - row_max)
        soft_probs = weights_exp / lax.optimization_barrier(jnp.sum(weights_exp, axis=-1, keepdims=True))
        return jnp.einsum('hqk,khd->qhd', low(soft_probs), value_block, precision=lax.Precision.HIGHEST)
    block_starts = jnp.arange(SEQ_MAX // block_rows, dtype=jnp.int32) * block_rows
    attended = lax.map(jax.checkpoint(one_block), block_starts)
    return attended.reshape(SEQ_MAX, D)

def reference(tokens, attn_gain, w_query, w_key, w_value, w_output, mlp_gain, w_gate, w_up, w_down, out_grad, lengths):
    devices = N_GRP * N_REP
    seq_ends = jnp.cumsum(lengths, axis=1).astype(jnp.int32)
    starts = (seq_ends - lengths).astype(jnp.int32)
    slot_len = lengths.astype(jnp.int32)
    slot_start = starts
    places = jnp.arange(SEQ_MAX, dtype=jnp.int32)
    micro_ids = jnp.arange(MB, dtype=jnp.int32)
    dealt_valid = places[None, None, :] < (slot_len * devices)[:, :, None]
    source_row = micro_ids[:, None, None] * TOKENS + (places % devices)[None, None, :] * ROWS + slot_start[:, :, None] + (places // devices)[None, None, :]
    source_row = jnp.where(dealt_valid, source_row, 0).astype(jnp.int32).reshape(-1)
    valid_float = dealt_valid.astype(jnp.float32).reshape(MB * SEQS, SEQ_MAX, 1)
    whole_rows = jnp.arange(TOKENS, dtype=jnp.int32)
    device_of = whole_rows // ROWS
    unit_of = whole_rows % ROWS
    seq_of = lax.optimization_barrier(jnp.sum((seq_ends[:, None, :] <= unit_of[None, :, None]).astype(jnp.int32), axis=2)).astype(jnp.int32)
    position = (unit_of[None, :] - jnp.take_along_axis(starts, seq_of, axis=1)) * devices + device_of[None, :]
    slot_of = seq_of
    return_row = ((micro_ids[:, None] * SEQS + slot_of) * SEQ_MAX + position).astype(jnp.int32).reshape(-1)

    def deal_rows(values):
        flat_rows = values.reshape(MB * TOKENS, D)
        return jnp.take(flat_rows, source_row, axis=0).reshape(MB * SEQS, SEQ_MAX, D) * valid_float

    def forward(inputs, gain_one, query_w, key_w, value_w, output_w, gain_two, gate_w, up_w, down_w):
        normed_in = low(rms_norm(inputs, gain_one))
        queries = low_back(low(matmul(normed_in, query_w)))
        keys_in = low_back(low(matmul(normed_in, key_w)))
        values_in = low_back(low(matmul(normed_in, value_w)))
        attended = lax.map(attend_sequence, (deal_rows(queries), deal_rows(keys_in), deal_rows(values_in)))
        attended = jnp.take(attended.reshape(MB * SEQS * SEQ_MAX, D), return_row, axis=0).reshape(MB, TOKENS, D)
        attended = low_back(low(attended))
        mixed = inputs + low_back(matmul(attended, output_w))
        normed_mid = low(rms_norm(mixed, gain_two))
        gate_pre = low_back(matmul(normed_mid, gate_w))
        up_pre = low_back(matmul(normed_mid, up_w))
        hidden = low(jax.nn.silu(gate_pre) * up_pre)
        return mixed + low_back(matmul(hidden, down_w))
    primal = (tokens.astype(jnp.float32), attn_gain.astype(jnp.float32), w_query.astype(jnp.float32), w_key.astype(jnp.float32), w_value.astype(jnp.float32), w_output.astype(jnp.float32), mlp_gain.astype(jnp.float32), w_gate.astype(jnp.float32), w_up.astype(jnp.float32), w_down.astype(jnp.float32))
    result, pullback = jax.vjp(forward, *primal)
    gradients = pullback(out_grad.astype(jnp.float32))
    return (result.astype(jnp.bfloat16), gradients[0].astype(jnp.bfloat16), gradients[1], gradients[2], gradients[3], gradients[4], gradients[5], gradients[6], gradients[7], gradients[8], gradients[9])
```

```python
import functools
import math

import jax
import jax.numpy as jnp
from jax import lax
from jax.experimental import pallas as pl
from jax.experimental.pallas import tpu as pltpu
from jax.sharding import PartitionSpec as P

HD = 64
WINDOW = 2048


epsilon = 1e-05
rope_base = 10000.0
masked_score = -1e30
BOTH = ("grp", "rep")
LANES = 128
UNIT_BLOCK = 8
UNIT_PAIR = 16
KERNEL_VMEM = 56 * 1024 * 1024


def from_behind(value, axis, steps):
    count = lax.axis_size(axis)
    first, last = (max(0, -steps), min(count, count - steps))
    return lax.ppermute(value, axis, [(source, source + steps) for source in range(first, last)])


def rms_scale(values):
    return lax.rsqrt(jnp.mean(values * values, axis=-1, keepdims=True) + epsilon)


def norm_backward(values, gain_full, grad_normed):
    inverse = rms_scale(values)
    normed = values * inverse
    gain_grad = jnp.sum(grad_normed * normed, axis=0)
    weighted = grad_normed * gain_full
    return (
        inverse * (weighted - normed * jnp.mean(weighted * normed, axis=-1, keepdims=True)),
        gain_grad,
    )


def rotary(values, cosine, sine_table):
    half_width = values.shape[-1] // 2
    first_half = values[..., :half_width]
    second_half = values[..., half_width:]
    return jnp.concatenate(
        [
            first_half * cosine - second_half * sine_table,
            second_half * cosine + first_half * sine_table,
        ],
        axis=-1,
    )


def pick_rows(rows_block, row_ids):
    return jnp.take(rows_block, row_ids, axis=0)


def take_rows(values, row_ids):
    return jax.vmap(pick_rows)(values, row_ids)


def gather_attn(attn_gain, w_query, w_key, w_value, w_output):
    return (
        lax.all_gather(attn_gain, "grp", axis=0, tiled=True),
        lax.all_gather(w_query, "grp", axis=0, tiled=True),
        lax.all_gather(w_key, "grp", axis=0, tiled=True),
        lax.all_gather(w_value, "grp", axis=0, tiled=True),
        lax.all_gather(w_output, "grp", axis=0, tiled=True),
    )


def gather_mlp(mlp_gain, w_gate, w_up, w_down):
    return (
        lax.all_gather(mlp_gain, "grp", axis=0, tiled=True),
        lax.all_gather(w_gate, "grp", axis=0, tiled=True),
        lax.all_gather(w_up, "grp", axis=0, tiled=True),
        lax.all_gather(w_down, "grp", axis=0, tiled=True),
    )


def reduce_attn(gain_grad, query_grad, key_grad, value_grad, output_grad):
    return (
        lax.psum_scatter(gain_grad, ("grp", "rep"), scatter_dimension=0, tiled=True),
        lax.psum_scatter(query_grad, ("grp", "rep"), scatter_dimension=0, tiled=True),
        lax.psum_scatter(key_grad, ("grp", "rep"), scatter_dimension=0, tiled=True),
        lax.psum_scatter(value_grad, ("grp", "rep"), scatter_dimension=0, tiled=True),
        lax.psum_scatter(output_grad, ("grp", "rep"), scatter_dimension=0, tiled=True),
    )


def reduce_mlp(gain_grad, gate_grad, up_grad, down_grad):
    return (
        lax.psum_scatter(gain_grad, ("grp", "rep"), scatter_dimension=0, tiled=True),
        lax.psum_scatter(gate_grad, ("grp", "rep"), scatter_dimension=0, tiled=True),
        lax.psum_scatter(up_grad, ("grp", "rep"), scatter_dimension=0, tiled=True),
        lax.psum_scatter(down_grad, ("grp", "rep"), scatter_dimension=0, tiled=True),
    )


def pass_on(carried, unused):
    arrived = from_behind(carried, ("grp", "rep"), 1)
    return (arrived, arrived)


def pass_back(running, portion):
    arrived = from_behind(running.astype(jnp.bfloat16), ("grp", "rep"), -1).astype(running.dtype)
    return (arrived + portion, None)


def ring_body(
    tokens,
    attn_gain,
    w_query,
    w_key,
    w_value,
    w_output,
    mlp_gain,
    w_gate,
    w_up,
    w_down,
    out_grad,
    lengths,
):
    devices = lax.axis_size(("grp", "rep"))
    rank_here = lax.axis_index(("grp", "rep"))
    micro_count, row_count, model_width = tokens.shape
    per_dev = row_count // devices
    head_count = model_width // HD
    reach_count = (WINDOW + row_count - 2) // row_count
    head_group = math.gcd(head_count, 4)
    group_count = head_count // head_group
    score_scale = 1.0 / math.sqrt(HD)
    unit_ids = jnp.arange(row_count, dtype=jnp.int32)
    seq_ends = jnp.cumsum(lengths, axis=1)
    starts = seq_ends - lengths
    seq_order = jnp.arange(lengths.shape[1], dtype=jnp.int32)
    earlier = seq_order[None, :] < seq_order[:, None]
    dealt_start = jnp.sum(jnp.where(earlier[None], lengths[:, None, :], 0), axis=2)
    seq_of = jnp.sum((seq_ends[:, None, :] <= unit_ids[None, :, None]).astype(jnp.int32), axis=2)
    seq_dealt = jnp.take_along_axis(dealt_start, seq_of, axis=1)
    unit_of = seq_dealt + unit_ids[None, :] - jnp.take_along_axis(starts, seq_of, axis=1)
    micro_ids = jnp.arange(micro_count, dtype=jnp.int32)[:, None]
    source_unit = (
        jnp.zeros((micro_count, row_count), jnp.int32)
        .at[micro_ids, unit_of]
        .set(jnp.broadcast_to(unit_ids[None, :], unit_of.shape))
    )
    unit_begin = (
        jnp.zeros((micro_count, row_count), jnp.int32).at[micro_ids, unit_of].set(seq_dealt)
    )
    local_ids = jnp.arange(row_count, dtype=jnp.int32)
    local_step = local_ids % per_dev
    local_source = local_ids // per_dev
    distance = jnp.arange(reach_count + 1, dtype=jnp.int32)
    owner_dev = rank_here - distance
    owner_ok = owner_dev >= 0
    owner_unit = jnp.maximum(owner_dev, 0)[:, None] * per_dev + local_step[None, :]
    key_begin = unit_begin[:, owner_unit]
    key_pos = (owner_unit[None] - key_begin) * devices + local_source[None, None, :]
    query_begin = key_begin[:, 0]
    query_pos = key_pos[:, 0]
    allowed = (
        owner_ok[None, None, :, None]
        & (query_begin[:, :, None, None] == key_begin[:, None, :, :])
        & (key_pos[:, None, :, :] <= query_pos[:, :, None, None])
        & (query_pos[:, :, None, None] - key_pos[:, None, :, :] < WINDOW)
    )
    mask_full = allowed[:, None]
    half_width = HD // 2
    frequency = jnp.power(rope_base, -2.0 * jnp.arange(half_width, dtype=jnp.float32) / HD)
    angles = query_pos.astype(jnp.float32)[:, :, None] * frequency[None, None, :]
    cosine = jnp.cos(angles)[:, :, None, :]
    sine_table = jnp.sin(angles)[:, :, None, :]
    head_shape = (micro_count, row_count, head_count, HD)
    block_shape = (micro_count, row_count, model_width)
    gathered = gather_attn(attn_gain, w_query, w_key, w_value, w_output)
    gain_one = gathered[0].astype(jnp.float32)
    inputs = tokens.astype(jnp.float32).reshape(micro_count * row_count, model_width)
    normed_in = (inputs * rms_scale(inputs) * gain_one).astype(jnp.bfloat16)
    queries = jnp.dot(normed_in, gathered[1], preferred_element_type=jnp.float32).astype(
        jnp.bfloat16
    )
    keys_in = jnp.dot(normed_in, gathered[2], preferred_element_type=jnp.float32).astype(
        jnp.bfloat16
    )
    values_in = jnp.dot(normed_in, gathered[3], preferred_element_type=jnp.float32).astype(
        jnp.bfloat16
    )
    dealt = (
        lax.all_to_all(
            take_rows(queries.reshape(block_shape), source_unit),
            ("grp", "rep"),
            split_axis=1,
            concat_axis=1,
            tiled=True,
        ),
        lax.all_to_all(
            take_rows(keys_in.reshape(block_shape), source_unit),
            ("grp", "rep"),
            split_axis=1,
            concat_axis=1,
            tiled=True,
        ),
        lax.all_to_all(
            take_rows(values_in.reshape(block_shape), source_unit),
            ("grp", "rep"),
            split_axis=1,
            concat_axis=1,
            tiled=True,
        ),
    )
    rot_q = rotary(dealt[0].reshape(head_shape).astype(jnp.float32), cosine, sine_table).astype(
        jnp.bfloat16
    )
    rot_k = rotary(dealt[1].reshape(head_shape).astype(jnp.float32), cosine, sine_table).astype(
        jnp.bfloat16
    )
    own_pair = jnp.stack([rot_k.reshape(block_shape), dealt[2]], axis=0)
    last_pair, farther = lax.scan(pass_on, own_pair, None, length=reach_count)
    context = jnp.concatenate([own_pair[None], farther], axis=0).reshape(
        reach_count + 1, 2, micro_count, row_count, head_count, HD
    )

    def group_scores(query_part, pair_part):
        scores = (
            jnp.einsum(
                "mqge,dmkge->mgqdk", query_part, pair_part[:, 0], preferred_element_type=jnp.float32
            )
            * score_scale
        )
        return jnp.where(mask_full, scores, masked_score)

    def forward_group(group_index, carried):
        attended_all, log_all = carried
        head_start = group_index * head_group
        query_part = lax.dynamic_slice_in_dim(rot_q, head_start, head_group, axis=2)
        pair_part = lax.dynamic_slice_in_dim(context, head_start, head_group, axis=4)
        scores = group_scores(query_part, pair_part)
        row_max = jnp.max(scores, axis=(3, 4), keepdims=True)
        weights_exp = jnp.exp(scores - row_max)
        row_sum = jnp.sum(weights_exp, axis=(3, 4), keepdims=True)
        soft_probs = (weights_exp / row_sum).astype(jnp.bfloat16)
        attended = jnp.einsum(
            "mgqdk,dmkge->mqge", soft_probs, pair_part[:, 1], preferred_element_type=jnp.float32
        ).astype(jnp.bfloat16)
        attended_all = lax.dynamic_update_slice_in_dim(attended_all, attended, head_start, axis=2)
        log_all = lax.dynamic_update_slice_in_dim(
            log_all, row_max + jnp.log(row_sum), head_start, axis=1
        )
        return (attended_all, log_all)

    attended_heads, log_sum = lax.fori_loop(
        0,
        group_count,
        forward_group,
        (
            jnp.zeros(head_shape, jnp.bfloat16),
            jnp.zeros((micro_count, head_count, row_count, 1, 1), jnp.float32),
        ),
    )
    returned = lax.all_to_all(
        attended_heads.reshape(block_shape), ("grp", "rep"), split_axis=1, concat_axis=1, tiled=True
    )
    attn_rows = take_rows(returned, unit_of).reshape(micro_count * row_count, model_width)
    mixed = inputs + jnp.dot(attn_rows, gathered[4], preferred_element_type=jnp.float32)
    mlp_set = gather_mlp(mlp_gain, w_gate, w_up, w_down)
    gain_two = mlp_set[0].astype(jnp.float32)
    normed_mid = (mixed * rms_scale(mixed) * gain_two).astype(jnp.bfloat16)
    gate_pre = jnp.dot(normed_mid, mlp_set[1], preferred_element_type=jnp.float32)
    up_pre = jnp.dot(normed_mid, mlp_set[2], preferred_element_type=jnp.float32)
    gate_sig = jax.nn.sigmoid(gate_pre)
    gate_silu = gate_pre * gate_sig
    hidden = (gate_silu * up_pre).astype(jnp.bfloat16)
    block_out = (mixed + jnp.dot(hidden, mlp_set[3], preferred_element_type=jnp.float32)).astype(
        jnp.bfloat16
    )
    mlp_set = gather_mlp(mlp_gain, w_gate, w_up, w_down)
    out_rows = out_grad.reshape(micro_count * row_count, model_width)
    down_grad = jnp.einsum("tf,td->fd", hidden, out_rows, preferred_element_type=jnp.float32)
    grad_hidden = jnp.einsum("td,fd->tf", out_rows, mlp_set[3], preferred_element_type=jnp.float32)
    grad_gate = (grad_hidden * up_pre * gate_sig * (1.0 + gate_pre * (1.0 - gate_sig))).astype(
        jnp.bfloat16
    )
    grad_up = (grad_hidden * gate_silu).astype(jnp.bfloat16)
    gate_grad = jnp.einsum("td,tf->df", normed_mid, grad_gate, preferred_element_type=jnp.float32)
    up_grad = jnp.einsum("td,tf->df", normed_mid, grad_up, preferred_element_type=jnp.float32)
    grad_mid = jnp.einsum(
        "tf,df->td", grad_gate, mlp_set[1], preferred_element_type=jnp.float32
    ) + jnp.einsum("tf,df->td", grad_up, mlp_set[2], preferred_element_type=jnp.float32)
    grad_norm_mid, mlp_gain_grad = norm_backward(mixed, gain_two, grad_mid)
    grad_mixed = out_rows.astype(jnp.float32) + grad_norm_mid
    mlp_sums = reduce_mlp(mlp_gain_grad, gate_grad, up_grad, down_grad)
    gathered = gather_attn(attn_gain, w_query, w_key, w_value, w_output)
    grad_branch = grad_mixed.astype(jnp.bfloat16)
    output_grad = jnp.einsum(
        "td,te->de", attn_rows, grad_branch, preferred_element_type=jnp.float32
    )
    grad_att = jnp.einsum(
        "te,de->td", grad_branch, gathered[4], preferred_element_type=jnp.float32
    ).astype(jnp.bfloat16)
    grad_dealt = lax.all_to_all(
        take_rows(grad_att.reshape(block_shape), source_unit),
        ("grp", "rep"),
        split_axis=1,
        concat_axis=1,
        tiled=True,
    )
    grad_heads = grad_dealt.reshape(head_shape)

    def backward_group(group_index, carried):
        query_total, pair_total = carried
        head_start = group_index * head_group
        query_part = lax.dynamic_slice_in_dim(rot_q, head_start, head_group, axis=2)
        grad_part = lax.dynamic_slice_in_dim(grad_heads, head_start, head_group, axis=2)
        pair_part = lax.dynamic_slice_in_dim(context, head_start, head_group, axis=4)
        log_part = lax.dynamic_slice_in_dim(log_sum, head_start, head_group, axis=1)
        scores = group_scores(query_part, pair_part)
        soft_probs = jnp.exp(scores - log_part)
        grad_probs = jnp.einsum(
            "mqge,dmkge->mgqdk", grad_part, pair_part[:, 1], preferred_element_type=jnp.float32
        )
        inner_sum = jnp.sum(soft_probs * grad_probs, axis=(3, 4), keepdims=True)
        grad_scores = (soft_probs * (grad_probs - inner_sum)).astype(jnp.bfloat16)
        query_piece = (
            jnp.einsum(
                "mgqdk,dmkge->mqge",
                grad_scores,
                pair_part[:, 0],
                preferred_element_type=jnp.float32,
            )
            * score_scale
        )
        key_part = (
            jnp.einsum(
                "mgqdk,mqge->dmkge", grad_scores, query_part, preferred_element_type=jnp.float32
            )
            * score_scale
        )
        value_part = jnp.einsum(
            "mgqdk,mqge->dmkge",
            soft_probs.astype(jnp.bfloat16),
            grad_part,
            preferred_element_type=jnp.float32,
        )
        query_total = lax.dynamic_update_slice_in_dim(query_total, query_piece, head_start, axis=2)
        pair_total = lax.dynamic_update_slice_in_dim(
            pair_total, jnp.stack([key_part, value_part], axis=1), head_start, axis=4
        )
        return (query_total, pair_total)

    query_total, pair_total = lax.fori_loop(
        0,
        group_count,
        backward_group,
        (
            jnp.zeros(head_shape, jnp.float32),
            jnp.zeros((reach_count + 1, 2) + head_shape, jnp.float32),
        ),
    )
    partials = pair_total.reshape(reach_count + 1, 2, micro_count, row_count, model_width)
    own_total, unused_out = lax.scan(
        pass_back, partials[reach_count], partials[:reach_count], reverse=True
    )
    query_back = rotary(query_total, cosine, -sine_table).astype(jnp.bfloat16)
    key_back = rotary(own_total[0].reshape(head_shape), cosine, -sine_table).astype(jnp.bfloat16)
    value_back = own_total[1].astype(jnp.bfloat16)
    grad_back = (
        lax.all_to_all(
            query_back.reshape(block_shape), ("grp", "rep"), split_axis=1, concat_axis=1, tiled=True
        ),
        lax.all_to_all(
            key_back.reshape(block_shape), ("grp", "rep"), split_axis=1, concat_axis=1, tiled=True
        ),
        lax.all_to_all(value_back, ("grp", "rep"), split_axis=1, concat_axis=1, tiled=True),
    )
    query_rows = take_rows(grad_back[0], unit_of).reshape(micro_count * row_count, model_width)
    key_rows = take_rows(grad_back[1], unit_of).reshape(micro_count * row_count, model_width)
    value_rows = take_rows(grad_back[2], unit_of).reshape(micro_count * row_count, model_width)
    query_grad = jnp.einsum("td,te->de", normed_in, query_rows, preferred_element_type=jnp.float32)
    key_grad = jnp.einsum("td,te->de", normed_in, key_rows, preferred_element_type=jnp.float32)
    value_grad = jnp.einsum("td,te->de", normed_in, value_rows, preferred_element_type=jnp.float32)
    grad_in = jnp.einsum("te,de->td", query_rows, gathered[1], preferred_element_type=jnp.float32)
    grad_in = grad_in + jnp.einsum(
        "te,de->td", key_rows, gathered[2], preferred_element_type=jnp.float32
    )
    grad_in = grad_in + jnp.einsum(
        "te,de->td", value_rows, gathered[3], preferred_element_type=jnp.float32
    )
    grad_norm_in, attn_gain_grad = norm_backward(inputs, gain_one, grad_in)
    token_grad = (grad_mixed + grad_norm_in).astype(jnp.bfloat16)
    attn_sums = reduce_attn(attn_gain_grad, query_grad, key_grad, value_grad, output_grad)
    return (
        block_out.reshape(block_shape),
        token_grad.reshape(block_shape),
        attn_sums[0],
        attn_sums[1],
        attn_sums[2],
        attn_sums[3],
        attn_sums[4],
        mlp_sums[0],
        mlp_sums[1],
        mlp_sums[2],
        mlp_sums[3],
    )


def contract(left_side, right_side, left_dim, right_dim, kind=jnp.float32):
    return lax.dot_general(
        left_side,
        right_side,
        (((left_dim,), (right_dim,)), ((), ())),
        preferred_element_type=jnp.float32,
    ).astype(kind)


def swap_halves(values):
    lane = lax.broadcasted_iota(jnp.int32, values.shape, 1)
    ahead = pltpu.roll(values, LANES - HD // 2, 1)
    behind = pltpu.roll(values, HD // 2, 1)
    return jnp.where(lane % HD < HD // 2, -ahead, behind)


def pair_angles(unit_at, cos_unit, sin_unit, cos_part, sin_part):
    unit_cos = cos_unit[pl.ds(unit_at, UNIT_PAIR), :][None]
    unit_sin = sin_unit[pl.ds(unit_at, UNIT_PAIR), :][None]
    part_cos = cos_part[...][:, None, :]
    part_sin = sin_part[...][:, None, :]
    cosine = unit_cos * part_cos - unit_sin * part_sin
    sine = unit_sin * part_cos + unit_cos * part_sin
    return cosine, sine


def key_offsets(block):
    row = lax.broadcasted_iota(jnp.int32, (block, block), 0)
    return (row % UNIT_BLOCK) * (block // UNIT_BLOCK) + row // UNIT_BLOCK


def query_offsets(block):
    column = lax.broadcasted_iota(jnp.int32, (block, block), 1)
    return (column % UNIT_BLOCK) * (block // UNIT_BLOCK) + column // UNIT_BLOCK


def attend_kernel(
    slot_ref,
    first_ref,
    plain_ref,
    cos_unit,
    sin_unit,
    cos_part,
    sin_part,
    low_ref,
    qkv_ref,
    att_ref,
    out_ref,
    log_ref,
    query_ref,
    key_ref,
    value_ref,
    query_t,
    value_t,
    key_at,
    causal_at,
):
    parts, units, _ = qkv_ref.shape
    block = parts * UNIT_BLOCK
    pairs = units // UNIT_PAIR
    key_at[...] = key_offsets(block)
    causal_at[...] = jnp.where(key_offsets(block) <= query_offsets(block), 0.0, masked_score)
    extra = value_t.shape[2] - HD

    def lay_out(pair, unused):
        unit_at = pl.multiple_of(pair * UNIT_PAIR, UNIT_PAIR)
        rows = jnp.stack(
            [qkv_ref[slot_ref[part], pl.ds(unit_at, UNIT_PAIR), :] for part in range(parts)]
        )
        cosine, sine = pair_angles(unit_at, cos_unit, sin_unit, cos_part, sin_part)
        flat = (parts * UNIT_PAIR, LANES)
        cosine = cosine.reshape(flat)
        sine = sine.reshape(flat)

        def rotated(values):
            values = values.astype(jnp.float32).reshape(flat)
            turned = values * cosine + swap_halves(values) * sine
            return turned.reshape(parts, UNIT_PAIR, LANES)

        query = rotated(rows[:, :, :LANES]) * (1.0 / math.sqrt(HD))
        key = rotated(rows[:, :, LANES : 2 * LANES])
        value = rows[:, :, 2 * LANES :].astype(jnp.float32)
        for half in range(UNIT_PAIR // UNIT_BLOCK):
            at = pair * (UNIT_PAIR // UNIT_BLOCK) + half
            cut = slice(half * UNIT_BLOCK, (half + 1) * UNIT_BLOCK)
            query_rows = query[:, cut].reshape(block, LANES)
            value_rows = value[:, cut].reshape(block, LANES)
            query_ref[at] = query_rows.astype(jnp.bfloat16)
            key_ref[at] = key[:, cut].reshape(block, LANES).astype(jnp.bfloat16)
            value_ref[at] = value_rows.astype(jnp.bfloat16)
            turned = jnp.transpose(query_rows)
            row = lax.broadcasted_iota(jnp.int32, turned.shape, 0)
            query_t[0, at] = jnp.where(row < HD, turned, 0.0).astype(jnp.bfloat16)
            query_t[1, at] = jnp.where(row < HD, 0.0, turned).astype(jnp.bfloat16)
            turned = jnp.transpose(value_rows).astype(jnp.bfloat16)
            for head in range(2):
                value_t[head, at, pl.ds(0, HD), :] = turned[head * HD : (head + 1) * HD]
                value_t[head, at, pl.ds(HD, extra), :] = jnp.ones((extra, block), jnp.bfloat16)
        return unused

    lax.fori_loop(0, pairs, lay_out, 0)

    def query_block(at):
        low = low_ref[at, 0:1, :]

        def step(key_block, carried, causal, bounded):
            new = []
            for head in range(2):
                top, total = carried[2 * head : 2 * head + 2]
                scores = jnp.dot(
                    key_ref[key_block], query_t[head, at], preferred_element_type=jnp.float32
                )
                if causal:
                    scores = scores + causal_at[...]
                if bounded:
                    scores = jnp.where(
                        key_at[...] >= low - key_block * block, scores, masked_score
                    )
                high = jnp.maximum(top, jnp.max(scores, axis=0, keepdims=True))
                weights = jnp.exp(scores - high).astype(jnp.bfloat16)
                total = total * jnp.exp(top - high) + jnp.dot(
                    value_t[head, key_block], weights, preferred_element_type=jnp.float32
                )
                new += [high, total]
            return tuple(new)

        empty = (
            jnp.full((1, block), masked_score, jnp.float32),
            jnp.zeros((HD + extra, block), jnp.float32),
        )
        carried = step(at, empty * 2, True, True)
        carried = lax.fori_loop(
            first_ref[at],
            plain_ref[at],
            lambda key_block, held: step(key_block, held, False, True),
            carried,
        )
        carried = lax.fori_loop(
            plain_ref[at],
            at,
            lambda key_block, held: step(key_block, held, False, False),
            carried,
        )
        heads = []
        for head in range(2):
            top, total = carried[2 * head : 2 * head + 2]
            heads.append(total[:HD] / total[HD : HD + 1])
            log_ref[at, head : head + 1, :] = top + jnp.log(total[HD : HD + 1])
        both = jnp.concatenate(heads, axis=0)
        out_ref[at] = both
        return jnp.transpose(both).reshape(parts, UNIT_BLOCK, LANES)

    def query_pair(pair, unused):
        halves = UNIT_PAIR // UNIT_BLOCK
        done = [query_block(pair * halves + half) for half in range(halves)]
        unit_at = pl.multiple_of(pair * UNIT_PAIR, UNIT_PAIR)
        att_ref[:, pl.ds(unit_at, UNIT_PAIR), :] = jnp.concatenate(done, axis=1).astype(
            jnp.bfloat16
        )
        return unused

    lax.fori_loop(0, pairs, query_pair, 0)


def attend_back_kernel(
    slot_ref,
    first_ref,
    plain_ref,
    cos_unit,
    sin_unit,
    cos_part,
    sin_part,
    low_ref,
    query_ref,
    key_ref,
    value_ref,
    out_ref,
    log_ref,
    grad_ref,
    back_ref,
    key_t,
    key_total,
    value_total,
    key_at,
    causal_at,
):
    parts, units, _ = grad_ref.shape
    block = parts * UNIT_BLOCK
    pairs = units // UNIT_PAIR
    halves = UNIT_PAIR // UNIT_BLOCK
    key_at[...] = key_offsets(block)
    causal_at[...] = jnp.where(key_offsets(block) <= query_offsets(block), 0.0, masked_score)

    def lay_out(at, unused):
        key_t[at] = jnp.transpose(key_ref[at].astype(jnp.float32)).astype(jnp.bfloat16)
        key_total[at] = jnp.zeros((block, LANES), jnp.float32)
        value_total[at] = jnp.zeros((block, LANES), jnp.float32)
        return unused

    lax.fori_loop(0, pairs * halves, lay_out, 0)

    def split_heads(values, axis):
        place = lax.broadcasted_iota(jnp.int32, values.shape, axis)
        zero = jnp.zeros_like(values)
        return [
            jnp.where(place < HD, values, zero).astype(jnp.bfloat16),
            jnp.where(place < HD, zero, values).astype(jnp.bfloat16),
        ]

    def query_block(at, grad_rows):
        low = low_ref[at, 0:1, :]
        query_rows = query_ref[at].astype(jnp.float32)
        query_heads = jnp.concatenate(split_heads(query_rows, 1), axis=0)
        grad_heads = jnp.concatenate(split_heads(grad_rows, 1), axis=0)
        query_t = split_heads(jnp.transpose(query_rows), 0)
        grad_turned = jnp.transpose(grad_rows)
        grad_t = split_heads(grad_turned, 0)
        product = grad_turned * out_ref[at]
        inner = [
            jnp.sum(product[head * HD : (head + 1) * HD], axis=0, keepdims=True)
            for head in range(2)
        ]
        logs = [log_ref[at, head : head + 1, :] for head in range(2)]

        def step(key_block, carried, causal, bounded):
            probs, slopes, new = [], [], []
            for head in range(2):
                scores = jnp.dot(
                    key_ref[key_block], query_t[head], preferred_element_type=jnp.float32
                )
                if causal:
                    scores = scores + causal_at[...]
                if bounded:
                    scores = jnp.where(
                        key_at[...] >= low - key_block * block, scores, masked_score
                    )
                soft = jnp.exp(scores - logs[head])
                grad_probs = jnp.dot(
                    value_ref[key_block], grad_t[head], preferred_element_type=jnp.float32
                )
                slope = (soft * (grad_probs - inner[head])).astype(jnp.bfloat16)
                probs.append(soft.astype(jnp.bfloat16))
                slopes.append(slope)
                new.append(
                    carried[head]
                    + jnp.dot(
                        key_t[key_block, pl.ds(head * HD, HD), :],
                        slope,
                        preferred_element_type=jnp.float32,
                    )
                )
            value_total[key_block] += jnp.dot(
                jnp.concatenate(probs, axis=1), grad_heads, preferred_element_type=jnp.float32
            )
            key_total[key_block] += jnp.dot(
                jnp.concatenate(slopes, axis=1), query_heads, preferred_element_type=jnp.float32
            )
            return tuple(new)

        carried = step(at, (jnp.zeros((HD, block), jnp.float32),) * 2, True, True)
        carried = lax.fori_loop(
            first_ref[at],
            plain_ref[at],
            lambda key_block, held: step(key_block, held, False, True),
            carried,
        )
        carried = lax.fori_loop(
            plain_ref[at],
            at,
            lambda key_block, held: step(key_block, held, False, False),
            carried,
        )
        return jnp.transpose(jnp.concatenate(carried, axis=0)) * (1.0 / math.sqrt(HD))

    def turn_back(rows, cosine, sine):
        flat = (parts * UNIT_PAIR, LANES)
        rows = jnp.concatenate(
            [one.reshape(parts, UNIT_BLOCK, LANES) for one in rows], axis=1
        ).reshape(flat)
        turned = rows * cosine.reshape(flat) - swap_halves(rows) * sine.reshape(flat)
        return turned.reshape(parts, UNIT_PAIR, LANES).astype(jnp.bfloat16)

    def put(values, unit_at, lane_at):
        for part in range(parts):
            back_ref[slot_ref[part], pl.ds(unit_at, UNIT_PAIR), pl.ds(lane_at, LANES)] = values[part]

    def query_pair(pair, unused):
        unit_at = pl.multiple_of(pair * UNIT_PAIR, UNIT_PAIR)
        grads = grad_ref[:, pl.ds(unit_at, UNIT_PAIR), :].astype(jnp.float32)
        done = [
            query_block(
                pair * halves + half,
                grads[:, half * UNIT_BLOCK : (half + 1) * UNIT_BLOCK].reshape(block, LANES),
            )
            for half in range(halves)
        ]
        cosine, sine = pair_angles(unit_at, cos_unit, sin_unit, cos_part, sin_part)
        put(turn_back(done, cosine, sine), unit_at, 0)
        return unused

    lax.fori_loop(0, pairs, query_pair, 0)

    def key_pair(pair, unused):
        unit_at = pl.multiple_of(pair * UNIT_PAIR, UNIT_PAIR)
        cosine, sine = pair_angles(unit_at, cos_unit, sin_unit, cos_part, sin_part)
        ids = [pair * halves + half for half in range(halves)]
        put(turn_back([key_total[at] for at in ids], cosine, sine), unit_at, LANES)
        values = jnp.concatenate(
            [value_total[at].reshape(parts, UNIT_BLOCK, LANES) for at in ids], axis=1
        ).astype(jnp.bfloat16)
        put(values, unit_at, 2 * LANES)
        return unused

    lax.fori_loop(0, pairs, key_pair, 0)


def attend(tables, qkv):
    parts, units, _ = qkv.shape
    block = parts * UNIT_BLOCK
    blocks = units // UNIT_BLOCK
    smem = pl.BlockSpec(memory_space=pltpu.SMEM)
    vmem = pl.BlockSpec(memory_space=pltpu.VMEM)
    rows = jax.ShapeDtypeStruct((blocks, block, LANES), jnp.bfloat16)
    extra = UNIT_PAIR
    return pl.pallas_call(
        attend_kernel,
        out_shape=(
            jax.ShapeDtypeStruct((parts, units, LANES), jnp.bfloat16),
            jax.ShapeDtypeStruct((blocks, LANES, block), jnp.float32),
            jax.ShapeDtypeStruct((blocks, 8, block), jnp.float32),
            rows,
            rows,
            rows,
        ),
        in_specs=[smem] * 3 + [vmem] * 6,
        out_specs=(vmem,) * 6,
        scratch_shapes=[
            pltpu.VMEM((2, blocks, LANES, block), jnp.bfloat16),
            pltpu.VMEM((2, blocks, HD + extra, block), jnp.bfloat16),
            pltpu.VMEM((block, block), jnp.int32),
            pltpu.VMEM((block, block), jnp.float32),
        ],
        compiler_params=pltpu.CompilerParams(vmem_limit_bytes=KERNEL_VMEM),
        cost_estimate=pl.CostEstimate(
            flops=20 * 10**9, bytes_accessed=16 << 20, transcendentals=20 * 10**6
        ),
        name="attend",
    )(*tables, qkv)


def attend_back(tables, query, key, value, out, log, grad):
    parts, units, _ = grad.shape
    block = parts * UNIT_BLOCK
    blocks = units // UNIT_BLOCK
    smem = pl.BlockSpec(memory_space=pltpu.SMEM)
    vmem = pl.BlockSpec(memory_space=pltpu.VMEM)
    return pl.pallas_call(
        attend_back_kernel,
        out_shape=jax.ShapeDtypeStruct((parts, units, 3 * LANES), jnp.bfloat16),
        in_specs=[smem] * 3 + [vmem] * 11,
        out_specs=vmem,
        scratch_shapes=[
            pltpu.VMEM((blocks, LANES, block), jnp.bfloat16),
            pltpu.VMEM((blocks, block, LANES), jnp.float32),
            pltpu.VMEM((blocks, block, LANES), jnp.float32),
            pltpu.VMEM((block, block), jnp.int32),
            pltpu.VMEM((block, block), jnp.float32),
        ],
        compiler_params=pltpu.CompilerParams(vmem_limit_bytes=KERNEL_VMEM),
        cost_estimate=pl.CostEstimate(
            flops=50 * 10**9, bytes_accessed=16 << 20, transcendentals=20 * 10**6
        ),
        name="attend_back",
    )(*tables, query, key, value, out, log, grad)


def attention_tables(lengths, grp_here, rep_here, units):
    reps = lax.axis_size("rep")
    parts = lax.axis_size("grp") * reps
    block = parts * UNIT_BLOCK
    blocks = units // UNIT_BLOCK
    own = lax.dynamic_index_in_dim(lengths, grp_here, 0, keepdims=False)
    ends = jnp.cumsum(own)
    unit_ids = jnp.arange(units, dtype=jnp.int32)
    begin = jnp.max(
        jnp.where(ends[None, :] <= unit_ids[:, None], ends[None, :], 0), axis=1
    ).astype(jnp.int32)
    part_ids = jnp.arange(parts, dtype=jnp.int32)
    offset = part_ids % reps ^ rep_here
    slot = offset * lax.axis_size("grp") + (part_ids // reps ^ grp_here)
    frequency = jnp.power(
        rope_base, -2.0 * (jnp.arange(LANES) % (HD // 2)).astype(jnp.float32) / HD
    )
    unit_angle = ((unit_ids - begin) * parts).astype(jnp.float32)[:, None] * frequency[None, :]
    part_angle = part_ids.astype(jnp.float32)[:, None] * frequency[None, :]
    low = jnp.maximum(
        (begin * parts)[:, None], unit_ids[:, None] * parts + part_ids[None, :] - (WINDOW - 1)
    )
    low = low.reshape(blocks, UNIT_BLOCK, parts)
    least = jnp.min(low, axis=(1, 2))
    most = jnp.max(low, axis=(1, 2))
    block_ids = jnp.arange(blocks, dtype=jnp.int32)
    first = jnp.maximum(least, 0) // block
    plain = jnp.clip((most + block - 1) // block, first, block_ids)
    low_rows = jnp.broadcast_to(
        low.transpose(0, 2, 1).reshape(blocks, 1, block), (blocks, 8, block)
    )
    return (
        slot,
        first,
        plain,
        jnp.cos(unit_angle),
        jnp.sin(unit_angle),
        jnp.cos(part_angle),
        jnp.sin(part_angle),
        low_rows,
    )


def swap(value, grp_step, rep_step):
    groups, reps = lax.axis_size("grp"), lax.axis_size("rep")
    pairs = [
        (grp * reps + rep, (grp ^ grp_step) * reps + (rep ^ rep_step))
        for grp in range(groups)
        for rep in range(reps)
    ]
    return lax.ppermute(value, BOTH, pairs)


def ordered(flag, own, other, axis=0):
    return jnp.where(
        flag == 0,
        jnp.concatenate([own, other], axis=axis),
        jnp.concatenate([other, own], axis=axis),
    )


def pick(value, index, axis):
    return lax.dynamic_index_in_dim(value, index, axis, keepdims=False)


def halve(value, axis, bit, grp_step, rep_step):
    kept = pick(value, bit, axis)
    sent = pick(value, 1 - bit, axis).astype(jnp.bfloat16)
    arrived = swap(sent, grp_step, rep_step)
    return kept.astype(jnp.float32) + arrived.astype(jnp.float32)


def narrow(value):
    return value.astype(jnp.bfloat16)


def heads_body(
    tokens,
    attn_gain,
    w_query,
    w_key,
    w_value,
    w_output,
    mlp_gain,
    w_gate,
    w_up,
    w_down,
    out_grad,
    lengths,
):
    groups, reps = lax.axis_size("grp"), lax.axis_size("rep")
    here, there = lax.axis_index("grp"), lax.axis_index("rep")
    core = there % 2
    micro_count, row_count, width = tokens.shape
    rows = micro_count * row_count
    hidden_width = w_gate.shape[1]
    half_width = width // groups
    own_width = hidden_width // (2 * groups)
    stripes = reps // 2

    gain_one = ordered(here, attn_gain, swap(attn_gain, 1, 0)).astype(jnp.float32)
    gain_two = ordered(here, mlp_gain, swap(mlp_gain, 1, 0)).astype(jnp.float32)
    inputs = tokens.astype(jnp.float32)
    normed_in = (inputs * rms_scale(inputs) * gain_one).astype(jnp.bfloat16)
    base = jnp.stack(
        [pick(normed_in, here, 0), swap(pick(normed_in, 1 - here, 0), 1, 0)], axis=0
    ).reshape(groups * row_count, width)

    def own_columns(weight):
        return lax.dynamic_slice_in_dim(weight, there * LANES, LANES, axis=1)

    w_heads = jnp.concatenate(
        [own_columns(w_query), own_columns(w_key), own_columns(w_value)], axis=1
    )
    w_heads = ordered(here, w_heads, swap(w_heads, 1, 0))

    chunks = {0: base}
    for step in range(reps - 4, 0, -4):
        chunks[step] = swap(base, 0, step)
    for step in [0] + list(range(reps - 4, 0, -4)):
        chunks[step + 2] = swap(chunks[step], 0, 2)
    for step in [0] + list(range(reps - 4, 0, -4)):
        for part in (0, 2):
            chunks[step + part + 1] = swap(chunks[step + part], 0, 1)
    qkv = jnp.concatenate(
        [jnp.dot(chunks[step], w_heads, preferred_element_type=jnp.float32).astype(jnp.bfloat16) for step in range(reps)],
        axis=0,
    ).reshape(reps * groups, row_count, 3 * LANES)

    output_other = swap(
        lax.dynamic_slice_in_dim(w_output, core * (half_width // 2), half_width // 2, axis=0), 1, 0
    )
    output_other = ordered(core, output_other, swap(output_other, 0, 1))
    w_output_full = ordered(here, w_output, output_other)

    def striped(weight):
        return weight.reshape(half_width, groups, stripes, 2, LANES)

    def own_stripes(weight, grp):
        cut = pick(pick(striped(weight), grp, 1), core, 2)
        return cut.reshape(half_width, own_width)

    w_in = jnp.concatenate([own_stripes(w_gate, here), own_stripes(w_up, here)], axis=1)
    w_in_other = swap(
        jnp.concatenate([own_stripes(w_gate, 1 - here), own_stripes(w_up, 1 - here)], axis=1), 1, 0
    )
    w_in = ordered(here, w_in, w_in_other)
    w_out = pick(w_down.reshape(stripes, 2, LANES, width), core, 1).reshape(own_width, width)

    def gather_quad(value):
        across = swap(value, 1, 0)
        return jnp.concatenate([value, swap(value, 0, 1), across, swap(across, 0, 1)], axis=0)

    out_rows = out_grad.reshape(rows, width)
    out_quad = gather_quad(out_rows)
    grad_hidden = contract(out_quad, w_out, 1, 1)

    tables = attention_tables(lengths, here, there, row_count)
    attended, out_heads, log_sum, query, key, value = attend(tables, qkv)
    returned = lax.all_to_all(attended, BOTH, split_axis=0, concat_axis=0, tiled=True)
    attn_rows = (
        returned.reshape(groups, reps, row_count, LANES).transpose(0, 2, 1, 3).reshape(rows, width)
    )
    mixed = inputs.reshape(rows, width) + jnp.dot(
        attn_rows, w_output_full, preferred_element_type=jnp.float32
    )
    normed_mid = (mixed * rms_scale(mixed) * gain_two).astype(jnp.bfloat16)
    mid_quad = gather_quad(normed_mid)
    gate_up = jnp.dot(mid_quad, w_in, preferred_element_type=jnp.float32)
    gate_pre, up_pre = gate_up[:, :own_width], gate_up[:, own_width:]
    gate_sig = jax.nn.sigmoid(gate_pre)
    gate_silu = gate_pre * gate_sig
    hidden = (gate_silu * up_pre).astype(jnp.bfloat16)
    grad_gate = (grad_hidden * up_pre * gate_sig * (1.0 + gate_pre * (1.0 - gate_sig))).astype(
        jnp.bfloat16
    )
    grad_up = (grad_hidden * gate_silu).astype(jnp.bfloat16)
    grad_in_mlp = jnp.concatenate([grad_gate, grad_up], axis=1)

    def scatter_quad(parts):
        parts = parts.reshape(2, 2, rows, width)
        both = parts[:, 0].astype(jnp.float32) + swap(narrow(parts[:, 1]), 0, 1).astype(jnp.float32)
        return both[0] + swap(narrow(both[1]), 1, 0).astype(jnp.float32)

    grad_mid = scatter_quad(contract(grad_in_mlp, w_in, 1, 1, jnp.bfloat16))
    grad_norm_mid, unused_gain = norm_backward(mixed, gain_two, grad_mid)
    grad_mixed = out_rows.astype(jnp.float32) + grad_norm_mid
    grad_branch = grad_mixed.astype(jnp.bfloat16)
    grad_att = contract(grad_branch, w_output_full, 1, 1, jnp.bfloat16)
    grad_heads = lax.all_to_all(
        grad_att.reshape(groups, row_count, reps, LANES)
        .transpose(0, 2, 1, 3)
        .reshape(groups * reps, row_count, LANES),
        BOTH,
        split_axis=0,
        concat_axis=0,
        tiled=True,
    )

    block_out = (
        mixed + scatter_quad(jnp.dot(hidden, w_out, preferred_element_type=jnp.float32).astype(jnp.bfloat16))
    ).astype(jnp.bfloat16)

    bits = [(there // step) % 2 for step in (1, 2)]
    far = [1 << place for place in range(2, reps.bit_length() - 1)]

    def scatter_stripes(parts):
        lead, rest = parts.shape[0], parts.shape[2:]
        parts = halve(parts.reshape((lead, stripes // 2, 2) + rest), 2, bits[1], 0, 2)
        for step in far:
            count = parts.shape[1]
            parts = halve(
                narrow(parts).reshape((lead, count // 2, 2) + rest), 2, (there // step) % 2, 0, step
            )
        return parts[:, 0]

    mlp_in_grad = contract(mid_quad, grad_in_mlp, 0, 0, jnp.bfloat16)
    own_rows = width // (groups * reps)
    mlp_in_part = narrow(
        scatter_stripes(
            mlp_in_grad.reshape(groups, stripes, 2, own_rows, 2 * own_width)
        )
    )
    down_grad = scatter_stripes(
        contract(hidden, out_quad, 0, 0, jnp.bfloat16).reshape(1, stripes, LANES, width)
    )[0]

    kept = pick(mlp_in_part, here, 0)
    crossed = swap(pick(mlp_in_part, 1 - here, 0), 1, 0)
    columns = []
    for part in (kept, crossed):
        columns.append(pick(part, core, 0))
        columns.append(swap(pick(part, 1 - core, 0), 0, 1))
    by_grp = [
        jnp.where(
            core == 0,
            jnp.stack([columns[2 * at], columns[2 * at + 1]], axis=1),
            jnp.stack([columns[2 * at + 1], columns[2 * at]], axis=1),
        )
        for at in range(2)
    ]
    pieces = jnp.where(
        here == 0,
        jnp.stack([by_grp[0], by_grp[1]], axis=1),
        jnp.stack([by_grp[1], by_grp[0]], axis=1),
    )
    pieces = pieces.reshape(own_rows, groups, 2, 2, stripes, LANES).transpose(3, 0, 1, 4, 2, 5)
    pieces = pieces.reshape(2, own_rows, hidden_width).astype(jnp.float32)
    gate_grad, up_grad = pieces[0], pieces[1]

    output_part = contract(attn_rows, grad_branch, 0, 0, jnp.bfloat16)
    output_part = output_part.reshape(groups, stripes, 2, own_rows, width)
    output_part = halve(output_part, 2, core, 0, 1)
    output_part = halve(narrow(output_part), 0, here, 1, 0)
    output_grad = scatter_stripes(narrow(output_part)[None])[0]

    back = attend_back(tables, query, key, value, out_heads, log_sum, grad_heads)
    back = back.reshape(reps, groups * row_count, 3 * LANES)

    grad_in = None
    for step in list(range(reps - 4, 0, -4)) + [0]:
        summed = None
        for part in (2, 0):
            away = swap(contract(back[step + part + 1], w_heads, 1, 1, jnp.bfloat16), 0, 1)
            total = contract(back[step + part], w_heads, 1, 1) + away.astype(jnp.float32)
            if part == 2:
                summed = swap(narrow(total), 0, 2).astype(jnp.float32)
            else:
                summed = summed + total
        if step:
            summed = swap(narrow(summed), 0, step).astype(jnp.float32)
        grad_in = summed if grad_in is None else grad_in + summed
    grad_in = grad_in.reshape(groups, row_count, width)
    grad_in = ordered(here, grad_in[:1], swap(narrow(grad_in[1:]), 1, 0).astype(jnp.float32))
    grad_norm_in, unused_gain = norm_backward(
        inputs.reshape(rows, width), gain_one, grad_in.reshape(rows, width)
    )
    token_grad = (grad_mixed + grad_norm_in).astype(jnp.bfloat16)

    gathered_rows = jnp.concatenate([chunks[step] for step in range(reps)], axis=0)
    heads_grad = contract(gathered_rows, back.reshape(reps * groups * row_count, 3 * LANES), 0, 0)
    heads_grad = halve(heads_grad.reshape(groups, half_width, 3 * LANES), 0, here, 1, 0)
    heads_grad = lax.all_to_all(
        narrow(heads_grad).reshape(reps, own_rows, 3 * LANES),
        "rep",
        split_axis=0,
        concat_axis=0,
        tiled=True,
    )
    heads_grad = (
        heads_grad.reshape(reps, own_rows, 3, LANES)
        .transpose(2, 1, 0, 3)
        .reshape(3, own_rows, width)
        .astype(jnp.float32)
    )

    def own_part(value):
        return lax.dynamic_slice_in_dim(value, there * own_rows, own_rows, axis=0).astype(
            jnp.float32
        )

    attn_gain_grad = (
        jnp.sum(own_part(w_query) * heads_grad[0], axis=1)
        + jnp.sum(own_part(w_key) * heads_grad[1], axis=1)
        + jnp.sum(own_part(w_value) * heads_grad[2], axis=1)
    ) / own_part(attn_gain)
    mlp_gain_grad = (
        jnp.sum(own_part(w_gate) * gate_grad, axis=1) + jnp.sum(own_part(w_up) * up_grad, axis=1)
    ) / own_part(mlp_gain)
    block_shape = tokens.shape
    return (
        block_out.reshape(block_shape),
        token_grad.reshape(block_shape),
        attn_gain_grad,
        heads_grad[0],
        heads_grad[1],
        heads_grad[2],
        output_grad,
        mlp_gain_grad,
        gate_grad,
        up_grad,
        down_grad,
    )


def pick_body(*arrays):
    tokens = arrays[0]
    groups, reps = lax.axis_size("grp"), lax.axis_size("rep")
    fits = (
        groups == 2
        and tokens.shape[0] == groups
        and tokens.shape[2] == reps * LANES
        and reps % 4 == 0
        and reps & (reps - 1) == 0
        and tokens.shape[1] % UNIT_PAIR == 0
        and arrays[7].shape[1] % (2 * groups * LANES) == 0
    )
    return heads_body(*arrays) if fits else ring_body(*arrays)


def solution(mesh):
    in_specs = (
        P(None, ("grp", "rep"), None),
        P("grp"),
        P("grp", None),
        P("grp", None),
        P("grp", None),
        P("grp", None),
        P("grp"),
        P("grp", None),
        P("grp", None),
        P("grp", None),
        P(None, ("grp", "rep"), None),
        P(),
    )
    out_specs = (
        P(None, ("grp", "rep"), None),
        P(None, ("grp", "rep"), None),
        P(("grp", "rep")),
        P(("grp", "rep"), None),
        P(("grp", "rep"), None),
        P(("grp", "rep"), None),
        P(("grp", "rep"), None),
        P(("grp", "rep")),
        P(("grp", "rep"), None),
        P(("grp", "rep"), None),
        P(("grp", "rep"), None),
    )
    return jax.shard_map(pick_body, mesh=mesh, in_specs=in_specs, out_specs=out_specs, check_vma=False)
```

```python
import functools
import math

import jax
import jax.numpy as jnp
from jax import lax
from jax.experimental import pallas as pl
from jax.experimental.pallas import tpu as pltpu
from jax.sharding import PartitionSpec as P

HD = 64
WINDOW = 2048


epsilon = 1e-05
rope_base = 10000.0
masked_score = -1e30
BOTH = ("grp", "rep")
LANES = 128
UNIT_BLOCK = 8
UNIT_PAIR = 16
KERNEL_VMEM = 56 * 1024 * 1024


def from_behind(value, axis, steps):
    count = lax.axis_size(axis)
    first, last = (max(0, -steps), min(count, count - steps))
    return lax.ppermute(value, axis, [(source, source + steps) for source in range(first, last)])


def rms_scale(values):
    return lax.rsqrt(jnp.mean(values * values, axis=-1, keepdims=True) + epsilon)


def norm_backward(values, gain_full, grad_normed):
    inverse = rms_scale(values)
    normed = values * inverse
    gain_grad = jnp.sum(grad_normed * normed, axis=0)
    weighted = grad_normed * gain_full
    return (
        inverse * (weighted - normed * jnp.mean(weighted * normed, axis=-1, keepdims=True)),
        gain_grad,
    )


def rotary(values, cosine, sine_table):
    half_width = values.shape[-1] // 2
    first_half = values[..., :half_width]
    second_half = values[..., half_width:]
    return jnp.concatenate(
        [
            first_half * cosine - second_half * sine_table,
            second_half * cosine + first_half * sine_table,
        ],
        axis=-1,
    )


def pick_rows(rows_block, row_ids):
    return jnp.take(rows_block, row_ids, axis=0)


def take_rows(values, row_ids):
    return jax.vmap(pick_rows)(values, row_ids)


def gather_attn(attn_gain, w_query, w_key, w_value, w_output):
    return (
        lax.all_gather(attn_gain, "grp", axis=0, tiled=True),
        lax.all_gather(w_query, "grp", axis=0, tiled=True),
        lax.all_gather(w_key, "grp", axis=0, tiled=True),
        lax.all_gather(w_value, "grp", axis=0, tiled=True),
        lax.all_gather(w_output, "grp", axis=0, tiled=True),
    )


def gather_mlp(mlp_gain, w_gate, w_up, w_down):
    return (
        lax.all_gather(mlp_gain, "grp", axis=0, tiled=True),
        lax.all_gather(w_gate, "grp", axis=0, tiled=True),
        lax.all_gather(w_up, "grp", axis=0, tiled=True),
        lax.all_gather(w_down, "grp", axis=0, tiled=True),
    )


def reduce_attn(gain_grad, query_grad, key_grad, value_grad, output_grad):
    return (
        lax.psum_scatter(gain_grad, ("grp", "rep"), scatter_dimension=0, tiled=True),
        lax.psum_scatter(query_grad, ("grp", "rep"), scatter_dimension=0, tiled=True),
        lax.psum_scatter(key_grad, ("grp", "rep"), scatter_dimension=0, tiled=True),
        lax.psum_scatter(value_grad, ("grp", "rep"), scatter_dimension=0, tiled=True),
        lax.psum_scatter(output_grad, ("grp", "rep"), scatter_dimension=0, tiled=True),
    )


def reduce_mlp(gain_grad, gate_grad, up_grad, down_grad):
    return (
        lax.psum_scatter(gain_grad, ("grp", "rep"), scatter_dimension=0, tiled=True),
        lax.psum_scatter(gate_grad, ("grp", "rep"), scatter_dimension=0, tiled=True),
        lax.psum_scatter(up_grad, ("grp", "rep"), scatter_dimension=0, tiled=True),
        lax.psum_scatter(down_grad, ("grp", "rep"), scatter_dimension=0, tiled=True),
    )


def pass_on(carried, unused):
    arrived = from_behind(carried, ("grp", "rep"), 1)
    return (arrived, arrived)


def pass_back(running, portion):
    arrived = from_behind(running.astype(jnp.bfloat16), ("grp", "rep"), -1).astype(running.dtype)
    return (arrived + portion, None)


def ring_body(
    tokens,
    attn_gain,
    w_query,
    w_key,
    w_value,
    w_output,
    mlp_gain,
    w_gate,
    w_up,
    w_down,
    out_grad,
    lengths,
):
    devices = lax.axis_size(("grp", "rep"))
    rank_here = lax.axis_index(("grp", "rep"))
    micro_count, row_count, model_width = tokens.shape
    per_dev = row_count // devices
    head_count = model_width // HD
    reach_count = (WINDOW + row_count - 2) // row_count
    head_group = math.gcd(head_count, 4)
    group_count = head_count // head_group
    score_scale = 1.0 / math.sqrt(HD)
    unit_ids = jnp.arange(row_count, dtype=jnp.int32)
    seq_ends = jnp.cumsum(lengths, axis=1)
    starts = seq_ends - lengths
    seq_order = jnp.arange(lengths.shape[1], dtype=jnp.int32)
    earlier = seq_order[None, :] < seq_order[:, None]
    dealt_start = jnp.sum(jnp.where(earlier[None], lengths[:, None, :], 0), axis=2)
    seq_of = jnp.sum((seq_ends[:, None, :] <= unit_ids[None, :, None]).astype(jnp.int32), axis=2)
    seq_dealt = jnp.take_along_axis(dealt_start, seq_of, axis=1)
    unit_of = seq_dealt + unit_ids[None, :] - jnp.take_along_axis(starts, seq_of, axis=1)
    micro_ids = jnp.arange(micro_count, dtype=jnp.int32)[:, None]
    source_unit = (
        jnp.zeros((micro_count, row_count), jnp.int32)
        .at[micro_ids, unit_of]
        .set(jnp.broadcast_to(unit_ids[None, :], unit_of.shape))
    )
    unit_begin = (
        jnp.zeros((micro_count, row_count), jnp.int32).at[micro_ids, unit_of].set(seq_dealt)
    )
    local_ids = jnp.arange(row_count, dtype=jnp.int32)
    local_step = local_ids % per_dev
    local_source = local_ids // per_dev
    distance = jnp.arange(reach_count + 1, dtype=jnp.int32)
    owner_dev = rank_here - distance
    owner_ok = owner_dev >= 0
    owner_unit = jnp.maximum(owner_dev, 0)[:, None] * per_dev + local_step[None, :]
    key_begin = unit_begin[:, owner_unit]
    key_pos = (owner_unit[None] - key_begin) * devices + local_source[None, None, :]
    query_begin = key_begin[:, 0]
    query_pos = key_pos[:, 0]
    allowed = (
        owner_ok[None, None, :, None]
        & (query_begin[:, :, None, None] == key_begin[:, None, :, :])
        & (key_pos[:, None, :, :] <= query_pos[:, :, None, None])
        & (query_pos[:, :, None, None] - key_pos[:, None, :, :] < WINDOW)
    )
    mask_full = allowed[:, None]
    half_width = HD // 2
    frequency = jnp.power(rope_base, -2.0 * jnp.arange(half_width, dtype=jnp.float32) / HD)
    angles = query_pos.astype(jnp.float32)[:, :, None] * frequency[None, None, :]
    cosine = jnp.cos(angles)[:, :, None, :]
    sine_table = jnp.sin(angles)[:, :, None, :]
    head_shape = (micro_count, row_count, head_count, HD)
    block_shape = (micro_count, row_count, model_width)
    gathered = gather_attn(attn_gain, w_query, w_key, w_value, w_output)
    gain_one = gathered[0].astype(jnp.float32)
    inputs = tokens.astype(jnp.float32).reshape(micro_count * row_count, model_width)
    normed_in = (inputs * rms_scale(inputs) * gain_one).astype(jnp.bfloat16)
    queries = jnp.dot(normed_in, gathered[1], preferred_element_type=jnp.float32).astype(
        jnp.bfloat16
    )
    keys_in = jnp.dot(normed_in, gathered[2], preferred_element_type=jnp.float32).astype(
        jnp.bfloat16
    )
    values_in = jnp.dot(normed_in, gathered[3], preferred_element_type=jnp.float32).astype(
        jnp.bfloat16
    )
    dealt = (
        lax.all_to_all(
            take_rows(queries.reshape(block_shape), source_unit),
            ("grp", "rep"),
            split_axis=1,
            concat_axis=1,
            tiled=True,
        ),
        lax.all_to_all(
            take_rows(keys_in.reshape(block_shape), source_unit),
            ("grp", "rep"),
            split_axis=1,
            concat_axis=1,
            tiled=True,
        ),
        lax.all_to_all(
            take_rows(values_in.reshape(block_shape), source_unit),
            ("grp", "rep"),
            split_axis=1,
            concat_axis=1,
            tiled=True,
        ),
    )
    rot_q = rotary(dealt[0].reshape(head_shape).astype(jnp.float32), cosine, sine_table).astype(
        jnp.bfloat16
    )
    rot_k = rotary(dealt[1].reshape(head_shape).astype(jnp.float32), cosine, sine_table).astype(
        jnp.bfloat16
    )
    own_pair = jnp.stack([rot_k.reshape(block_shape), dealt[2]], axis=0)
    last_pair, farther = lax.scan(pass_on, own_pair, None, length=reach_count)
    context = jnp.concatenate([own_pair[None], farther], axis=0).reshape(
        reach_count + 1, 2, micro_count, row_count, head_count, HD
    )

    def group_scores(query_part, pair_part):
        scores = (
            jnp.einsum(
                "mqge,dmkge->mgqdk", query_part, pair_part[:, 0], preferred_element_type=jnp.float32
            )
            * score_scale
        )
        return jnp.where(mask_full, scores, masked_score)

    def forward_group(group_index, carried):
        attended_all, log_all = carried
        head_start = group_index * head_group
        query_part = lax.dynamic_slice_in_dim(rot_q, head_start, head_group, axis=2)
        pair_part = lax.dynamic_slice_in_dim(context, head_start, head_group, axis=4)
        scores = group_scores(query_part, pair_part)
        row_max = jnp.max(scores, axis=(3, 4), keepdims=True)
        weights_exp = jnp.exp(scores - row_max)
        row_sum = jnp.sum(weights_exp, axis=(3, 4), keepdims=True)
        soft_probs = (weights_exp / row_sum).astype(jnp.bfloat16)
        attended = jnp.einsum(
            "mgqdk,dmkge->mqge", soft_probs, pair_part[:, 1], preferred_element_type=jnp.float32
        ).astype(jnp.bfloat16)
        attended_all = lax.dynamic_update_slice_in_dim(attended_all, attended, head_start, axis=2)
        log_all = lax.dynamic_update_slice_in_dim(
            log_all, row_max + jnp.log(row_sum), head_start, axis=1
        )
        return (attended_all, log_all)

    attended_heads, log_sum = lax.fori_loop(
        0,
        group_count,
        forward_group,
        (
            jnp.zeros(head_shape, jnp.bfloat16),
            jnp.zeros((micro_count, head_count, row_count, 1, 1), jnp.float32),
        ),
    )
    returned = lax.all_to_all(
        attended_heads.reshape(block_shape), ("grp", "rep"), split_axis=1, concat_axis=1, tiled=True
    )
    attn_rows = take_rows(returned, unit_of).reshape(micro_count * row_count, model_width)
    mixed = inputs + jnp.dot(attn_rows, gathered[4], preferred_element_type=jnp.float32)
    mlp_set = gather_mlp(mlp_gain, w_gate, w_up, w_down)
    gain_two = mlp_set[0].astype(jnp.float32)
    normed_mid = (mixed * rms_scale(mixed) * gain_two).astype(jnp.bfloat16)
    gate_pre = jnp.dot(normed_mid, mlp_set[1], preferred_element_type=jnp.float32)
    up_pre = jnp.dot(normed_mid, mlp_set[2], preferred_element_type=jnp.float32)
    gate_sig = jax.nn.sigmoid(gate_pre)
    gate_silu = gate_pre * gate_sig
    hidden = (gate_silu * up_pre).astype(jnp.bfloat16)
    block_out = (mixed + jnp.dot(hidden, mlp_set[3], preferred_element_type=jnp.float32)).astype(
        jnp.bfloat16
    )
    mlp_set = gather_mlp(mlp_gain, w_gate, w_up, w_down)
    out_rows = out_grad.reshape(micro_count * row_count, model_width)
    down_grad = jnp.einsum("tf,td->fd", hidden, out_rows, preferred_element_type=jnp.float32)
    grad_hidden = jnp.einsum("td,fd->tf", out_rows, mlp_set[3], preferred_element_type=jnp.float32)
    grad_gate = (grad_hidden * up_pre * gate_sig * (1.0 + gate_pre * (1.0 - gate_sig))).astype(
        jnp.bfloat16
    )
    grad_up = (grad_hidden * gate_silu).astype(jnp.bfloat16)
    gate_grad = jnp.einsum("td,tf->df", normed_mid, grad_gate, preferred_element_type=jnp.float32)
    up_grad = jnp.einsum("td,tf->df", normed_mid, grad_up, preferred_element_type=jnp.float32)
    grad_mid = jnp.einsum(
        "tf,df->td", grad_gate, mlp_set[1], preferred_element_type=jnp.float32
    ) + jnp.einsum("tf,df->td", grad_up, mlp_set[2], preferred_element_type=jnp.float32)
    grad_norm_mid, mlp_gain_grad = norm_backward(mixed, gain_two, grad_mid)
    grad_mixed = out_rows.astype(jnp.float32) + grad_norm_mid
    mlp_sums = reduce_mlp(mlp_gain_grad, gate_grad, up_grad, down_grad)
    gathered = gather_attn(attn_gain, w_query, w_key, w_value, w_output)
    grad_branch = grad_mixed.astype(jnp.bfloat16)
    output_grad = jnp.einsum(
        "td,te->de", attn_rows, grad_branch, preferred_element_type=jnp.float32
    )
    grad_att = jnp.einsum(
        "te,de->td", grad_branch, gathered[4], preferred_element_type=jnp.float32
    ).astype(jnp.bfloat16)
    grad_dealt = lax.all_to_all(
        take_rows(grad_att.reshape(block_shape), source_unit),
        ("grp", "rep"),
        split_axis=1,
        concat_axis=1,
        tiled=True,
    )
    grad_heads = grad_dealt.reshape(head_shape)

    def backward_group(group_index, carried):
        query_total, pair_total = carried
        head_start = group_index * head_group
        query_part = lax.dynamic_slice_in_dim(rot_q, head_start, head_group, axis=2)
        grad_part = lax.dynamic_slice_in_dim(grad_heads, head_start, head_group, axis=2)
        pair_part = lax.dynamic_slice_in_dim(context, head_start, head_group, axis=4)
        log_part = lax.dynamic_slice_in_dim(log_sum, head_start, head_group, axis=1)
        scores = group_scores(query_part, pair_part)
        soft_probs = jnp.exp(scores - log_part)
        grad_probs = jnp.einsum(
            "mqge,dmkge->mgqdk", grad_part, pair_part[:, 1], preferred_element_type=jnp.float32
        )
        inner_sum = jnp.sum(soft_probs * grad_probs, axis=(3, 4), keepdims=True)
        grad_scores = (soft_probs * (grad_probs - inner_sum)).astype(jnp.bfloat16)
        query_piece = (
            jnp.einsum(
                "mgqdk,dmkge->mqge",
                grad_scores,
                pair_part[:, 0],
                preferred_element_type=jnp.float32,
            )
            * score_scale
        )
        key_part = (
            jnp.einsum(
                "mgqdk,mqge->dmkge", grad_scores, query_part, preferred_element_type=jnp.float32
            )
            * score_scale
        )
        value_part = jnp.einsum(
            "mgqdk,mqge->dmkge",
            soft_probs.astype(jnp.bfloat16),
            grad_part,
            preferred_element_type=jnp.float32,
        )
        query_total = lax.dynamic_update_slice_in_dim(query_total, query_piece, head_start, axis=2)
        pair_total = lax.dynamic_update_slice_in_dim(
            pair_total, jnp.stack([key_part, value_part], axis=1), head_start, axis=4
        )
        return (query_total, pair_total)

    query_total, pair_total = lax.fori_loop(
        0,
        group_count,
        backward_group,
        (
            jnp.zeros(head_shape, jnp.float32),
            jnp.zeros((reach_count + 1, 2) + head_shape, jnp.float32),
        ),
    )
    partials = pair_total.reshape(reach_count + 1, 2, micro_count, row_count, model_width)
    own_total, unused_out = lax.scan(
        pass_back, partials[reach_count], partials[:reach_count], reverse=True
    )
    query_back = rotary(query_total, cosine, -sine_table).astype(jnp.bfloat16)
    key_back = rotary(own_total[0].reshape(head_shape), cosine, -sine_table).astype(jnp.bfloat16)
    value_back = own_total[1].astype(jnp.bfloat16)
    grad_back = (
        lax.all_to_all(
            query_back.reshape(block_shape), ("grp", "rep"), split_axis=1, concat_axis=1, tiled=True
        ),
        lax.all_to_all(
            key_back.reshape(block_shape), ("grp", "rep"), split_axis=1, concat_axis=1, tiled=True
        ),
        lax.all_to_all(value_back, ("grp", "rep"), split_axis=1, concat_axis=1, tiled=True),
    )
    query_rows = take_rows(grad_back[0], unit_of).reshape(micro_count * row_count, model_width)
    key_rows = take_rows(grad_back[1], unit_of).reshape(micro_count * row_count, model_width)
    value_rows = take_rows(grad_back[2], unit_of).reshape(micro_count * row_count, model_width)
    query_grad = jnp.einsum("td,te->de", normed_in, query_rows, preferred_element_type=jnp.float32)
    key_grad = jnp.einsum("td,te->de", normed_in, key_rows, preferred_element_type=jnp.float32)
    value_grad = jnp.einsum("td,te->de", normed_in, value_rows, preferred_element_type=jnp.float32)
    grad_in = jnp.einsum("te,de->td", query_rows, gathered[1], preferred_element_type=jnp.float32)
    grad_in = grad_in + jnp.einsum(
        "te,de->td", key_rows, gathered[2], preferred_element_type=jnp.float32
    )
    grad_in = grad_in + jnp.einsum(
        "te,de->td", value_rows, gathered[3], preferred_element_type=jnp.float32
    )
    grad_norm_in, attn_gain_grad = norm_backward(inputs, gain_one, grad_in)
    token_grad = (grad_mixed + grad_norm_in).astype(jnp.bfloat16)
    attn_sums = reduce_attn(attn_gain_grad, query_grad, key_grad, value_grad, output_grad)
    return (
        block_out.reshape(block_shape),
        token_grad.reshape(block_shape),
        attn_sums[0],
        attn_sums[1],
        attn_sums[2],
        attn_sums[3],
        attn_sums[4],
        mlp_sums[0],
        mlp_sums[1],
        mlp_sums[2],
        mlp_sums[3],
    )


def contract(left_side, right_side, left_dim, right_dim, kind=jnp.float32):
    return lax.dot_general(
        left_side,
        right_side,
        (((left_dim,), (right_dim,)), ((), ())),
        preferred_element_type=jnp.float32,
    ).astype(kind)


def swap_halves(values):
    lane = lax.broadcasted_iota(jnp.int32, values.shape, 1)
    ahead = pltpu.roll(values, LANES - HD // 2, 1)
    behind = pltpu.roll(values, HD // 2, 1)
    return jnp.where(lane % HD < HD // 2, -ahead, behind)


def pair_angles(unit_at, cos_unit, sin_unit, cos_part, sin_part):
    unit_cos = cos_unit[pl.ds(unit_at, UNIT_PAIR), :][None]
    unit_sin = sin_unit[pl.ds(unit_at, UNIT_PAIR), :][None]
    part_cos = cos_part[...][:, None, :]
    part_sin = sin_part[...][:, None, :]
    cosine = unit_cos * part_cos - unit_sin * part_sin
    sine = unit_sin * part_cos + unit_cos * part_sin
    return cosine, sine


def key_offsets(block):
    row = lax.broadcasted_iota(jnp.int32, (block, block), 0)
    return (row % UNIT_BLOCK) * (block // UNIT_BLOCK) + row // UNIT_BLOCK


def query_offsets(block):
    column = lax.broadcasted_iota(jnp.int32, (block, block), 1)
    return (column % UNIT_BLOCK) * (block // UNIT_BLOCK) + column // UNIT_BLOCK


def attend_kernel(
    slot_ref,
    first_ref,
    plain_ref,
    cos_unit,
    sin_unit,
    cos_part,
    sin_part,
    low_ref,
    qkv_ref,
    att_ref,
    out_ref,
    log_ref,
    query_ref,
    key_ref,
    value_ref,
    query_t,
    value_t,
    key_at,
    causal_at,
):
    parts, units, _ = qkv_ref.shape
    block = parts * UNIT_BLOCK
    pairs = units // UNIT_PAIR
    key_at[...] = key_offsets(block)
    causal_at[...] = jnp.where(key_offsets(block) <= query_offsets(block), 0.0, masked_score)
    extra = value_t.shape[2] - HD

    def lay_out(pair, unused):
        unit_at = pl.multiple_of(pair * UNIT_PAIR, UNIT_PAIR)
        rows = jnp.stack(
            [qkv_ref[slot_ref[part], pl.ds(unit_at, UNIT_PAIR), :] for part in range(parts)]
        )
        cosine, sine = pair_angles(unit_at, cos_unit, sin_unit, cos_part, sin_part)
        flat = (parts * UNIT_PAIR, LANES)
        cosine = cosine.reshape(flat)
        sine = sine.reshape(flat)

        def rotated(values):
            values = values.astype(jnp.float32).reshape(flat)
            turned = values * cosine + swap_halves(values) * sine
            return turned.reshape(parts, UNIT_PAIR, LANES)

        query = rotated(rows[:, :, :LANES]) * (1.0 / math.sqrt(HD))
        key = rotated(rows[:, :, LANES : 2 * LANES])
        value = rows[:, :, 2 * LANES :].astype(jnp.float32)
        for half in range(UNIT_PAIR // UNIT_BLOCK):
            at = pair * (UNIT_PAIR // UNIT_BLOCK) + half
            cut = slice(half * UNIT_BLOCK, (half + 1) * UNIT_BLOCK)
            query_rows = query[:, cut].reshape(block, LANES)
            value_rows = value[:, cut].reshape(block, LANES)
            query_ref[at] = query_rows.astype(jnp.bfloat16)
            key_ref[at] = key[:, cut].reshape(block, LANES).astype(jnp.bfloat16)
            value_ref[at] = value_rows.astype(jnp.bfloat16)
            turned = jnp.transpose(query_rows)
            row = lax.broadcasted_iota(jnp.int32, turned.shape, 0)
            query_t[0, at] = jnp.where(row < HD, turned, 0.0).astype(jnp.bfloat16)
            query_t[1, at] = jnp.where(row < HD, 0.0, turned).astype(jnp.bfloat16)
            turned = jnp.transpose(value_rows).astype(jnp.bfloat16)
            for head in range(2):
                value_t[head, at, pl.ds(0, HD), :] = turned[head * HD : (head + 1) * HD]
                value_t[head, at, pl.ds(HD, extra), :] = jnp.ones((extra, block), jnp.bfloat16)
        return unused

    lax.fori_loop(0, pairs, lay_out, 0)

    def query_block(at):
        low = low_ref[at, 0:1, :]

        def step(key_block, carried, causal, bounded):
            new = []
            for head in range(2):
                top, total = carried[2 * head : 2 * head + 2]
                scores = jnp.dot(
                    key_ref[key_block], query_t[head, at], preferred_element_type=jnp.float32
                )
                if causal:
                    scores = scores + causal_at[...]
                if bounded:
                    scores = jnp.where(
                        key_at[...] >= low - key_block * block, scores, masked_score
                    )
                high = jnp.maximum(top, jnp.max(scores, axis=0, keepdims=True))
                weights = jnp.exp(scores - high).astype(jnp.bfloat16)
                total = total * jnp.exp(top - high) + jnp.dot(
                    value_t[head, key_block], weights, preferred_element_type=jnp.float32
                )
                new += [high, total]
            return tuple(new)

        empty = (
            jnp.full((1, block), masked_score, jnp.float32),
            jnp.zeros((HD + extra, block), jnp.float32),
        )
        carried = step(at, empty * 2, True, True)
        carried = lax.fori_loop(
            first_ref[at],
            plain_ref[at],
            lambda key_block, held: step(key_block, held, False, True),
            carried,
        )
        carried = lax.fori_loop(
            plain_ref[at],
            at,
            lambda key_block, held: step(key_block, held, False, False),
            carried,
        )
        heads = []
        for head in range(2):
            top, total = carried[2 * head : 2 * head + 2]
            heads.append(total[:HD] / total[HD : HD + 1])
            log_ref[at, head : head + 1, :] = top + jnp.log(total[HD : HD + 1])
        both = jnp.concatenate(heads, axis=0)
        out_ref[at] = both
        return jnp.transpose(both).reshape(parts, UNIT_BLOCK, LANES)

    def query_pair(pair, unused):
        halves = UNIT_PAIR // UNIT_BLOCK
        done = [query_block(pair * halves + half) for half in range(halves)]
        unit_at = pl.multiple_of(pair * UNIT_PAIR, UNIT_PAIR)
        att_ref[:, pl.ds(unit_at, UNIT_PAIR), :] = jnp.concatenate(done, axis=1).astype(
            jnp.bfloat16
        )
        return unused

    lax.fori_loop(0, pairs, query_pair, 0)


def attend_back_kernel(
    slot_ref,
    first_ref,
    plain_ref,
    cos_unit,
    sin_unit,
    cos_part,
    sin_part,
    low_ref,
    query_ref,
    key_ref,
    value_ref,
    out_ref,
    log_ref,
    grad_ref,
    back_ref,
    key_t,
    key_total,
    value_total,
    key_at,
    causal_at,
):
    parts, units, _ = grad_ref.shape
    block = parts * UNIT_BLOCK
    pairs = units // UNIT_PAIR
    halves = UNIT_PAIR // UNIT_BLOCK
    key_at[...] = key_offsets(block)
    causal_at[...] = jnp.where(key_offsets(block) <= query_offsets(block), 0.0, masked_score)

    def lay_out(at, unused):
        key_t[at] = jnp.transpose(key_ref[at].astype(jnp.float32)).astype(jnp.bfloat16)
        key_total[at] = jnp.zeros((block, LANES), jnp.float32)
        value_total[at] = jnp.zeros((block, LANES), jnp.float32)
        return unused

    lax.fori_loop(0, pairs * halves, lay_out, 0)

    def split_heads(values, axis):
        place = lax.broadcasted_iota(jnp.int32, values.shape, axis)
        zero = jnp.zeros_like(values)
        return [
            jnp.where(place < HD, values, zero).astype(jnp.bfloat16),
            jnp.where(place < HD, zero, values).astype(jnp.bfloat16),
        ]

    def query_block(at, grad_rows):
        low = low_ref[at, 0:1, :]
        query_rows = query_ref[at].astype(jnp.float32)
        query_heads = jnp.concatenate(split_heads(query_rows, 1), axis=0)
        grad_heads = jnp.concatenate(split_heads(grad_rows, 1), axis=0)
        query_t = split_heads(jnp.transpose(query_rows), 0)
        grad_turned = jnp.transpose(grad_rows)
        grad_t = split_heads(grad_turned, 0)
        product = grad_turned * out_ref[at]
        inner = [
            jnp.sum(product[head * HD : (head + 1) * HD], axis=0, keepdims=True)
            for head in range(2)
        ]
        logs = [log_ref[at, head : head + 1, :] for head in range(2)]

        def step(key_block, carried, causal, bounded):
            probs, slopes, new = [], [], []
            for head in range(2):
                scores = jnp.dot(
                    key_ref[key_block], query_t[head], preferred_element_type=jnp.float32
                )
                if causal:
                    scores = scores + causal_at[...]
                if bounded:
                    scores = jnp.where(
                        key_at[...] >= low - key_block * block, scores, masked_score
                    )
                soft = jnp.exp(scores - logs[head])
                grad_probs = jnp.dot(
                    value_ref[key_block], grad_t[head], preferred_element_type=jnp.float32
                )
                slope = (soft * (grad_probs - inner[head])).astype(jnp.bfloat16)
                probs.append(soft.astype(jnp.bfloat16))
                slopes.append(slope)
                new.append(
                    carried[head]
                    + jnp.dot(
                        key_t[key_block, pl.ds(head * HD, HD), :],
                        slope,
                        preferred_element_type=jnp.float32,
                    )
                )
            value_total[key_block] += jnp.dot(
                jnp.concatenate(probs, axis=1), grad_heads, preferred_element_type=jnp.float32
            )
            key_total[key_block] += jnp.dot(
                jnp.concatenate(slopes, axis=1), query_heads, preferred_element_type=jnp.float32
            )
            return tuple(new)

        carried = step(at, (jnp.zeros((HD, block), jnp.float32),) * 2, True, True)
        carried = lax.fori_loop(
            first_ref[at],
            plain_ref[at],
            lambda key_block, held: step(key_block, held, False, True),
            carried,
        )
        carried = lax.fori_loop(
            plain_ref[at],
            at,
            lambda key_block, held: step(key_block, held, False, False),
            carried,
        )
        return jnp.transpose(jnp.concatenate(carried, axis=0)) * (1.0 / math.sqrt(HD))

    def turn_back(rows, cosine, sine):
        flat = (parts * UNIT_PAIR, LANES)
        rows = jnp.concatenate(
            [one.reshape(parts, UNIT_BLOCK, LANES) for one in rows], axis=1
        ).reshape(flat)
        turned = rows * cosine.reshape(flat) - swap_halves(rows) * sine.reshape(flat)
        return turned.reshape(parts, UNIT_PAIR, LANES).astype(jnp.bfloat16)

    def put(values, unit_at, lane_at):
        for part in range(parts):
            back_ref[slot_ref[part], pl.ds(unit_at, UNIT_PAIR), pl.ds(lane_at, LANES)] = values[part]

    def query_pair(pair, unused):
        unit_at = pl.multiple_of(pair * UNIT_PAIR, UNIT_PAIR)
        grads = grad_ref[:, pl.ds(unit_at, UNIT_PAIR), :].astype(jnp.float32)
        done = [
            query_block(
                pair * halves + half,
                grads[:, half * UNIT_BLOCK : (half + 1) * UNIT_BLOCK].reshape(block, LANES),
            )
            for half in range(halves)
        ]
        cosine, sine = pair_angles(unit_at, cos_unit, sin_unit, cos_part, sin_part)
        put(turn_back(done, cosine, sine), unit_at, 0)
        return unused

    lax.fori_loop(0, pairs, query_pair, 0)

    def key_pair(pair, unused):
        unit_at = pl.multiple_of(pair * UNIT_PAIR, UNIT_PAIR)
        cosine, sine = pair_angles(unit_at, cos_unit, sin_unit, cos_part, sin_part)
        ids = [pair * halves + half for half in range(halves)]
        put(turn_back([key_total[at] for at in ids], cosine, sine), unit_at, LANES)
        values = jnp.concatenate(
            [value_total[at].reshape(parts, UNIT_BLOCK, LANES) for at in ids], axis=1
        ).astype(jnp.bfloat16)
        put(values, unit_at, 2 * LANES)
        return unused

    lax.fori_loop(0, pairs, key_pair, 0)


def attend(tables, qkv):
    parts, units, _ = qkv.shape
    block = parts * UNIT_BLOCK
    blocks = units // UNIT_BLOCK
    smem = pl.BlockSpec(memory_space=pltpu.SMEM)
    vmem = pl.BlockSpec(memory_space=pltpu.VMEM)
    rows = jax.ShapeDtypeStruct((blocks, block, LANES), jnp.bfloat16)
    extra = UNIT_PAIR
    return pl.pallas_call(
        attend_kernel,
        out_shape=(
            jax.ShapeDtypeStruct((parts, units, LANES), jnp.bfloat16),
            jax.ShapeDtypeStruct((blocks, LANES, block), jnp.float32),
            jax.ShapeDtypeStruct((blocks, 8, block), jnp.float32),
            rows,
            rows,
            rows,
        ),
        in_specs=[smem] * 3 + [vmem] * 6,
        out_specs=(vmem,) * 6,
        scratch_shapes=[
            pltpu.VMEM((2, blocks, LANES, block), jnp.bfloat16),
            pltpu.VMEM((2, blocks, HD + extra, block), jnp.bfloat16),
            pltpu.VMEM((block, block), jnp.int32),
            pltpu.VMEM((block, block), jnp.float32),
        ],
        compiler_params=pltpu.CompilerParams(vmem_limit_bytes=KERNEL_VMEM),
        cost_estimate=pl.CostEstimate(
            flops=20 * 10**9, bytes_accessed=16 << 20, transcendentals=20 * 10**6
        ),
        name="attend",
    )(*tables, qkv)


def attend_back(tables, query, key, value, out, log, grad):
    parts, units, _ = grad.shape
    block = parts * UNIT_BLOCK
    blocks = units // UNIT_BLOCK
    smem = pl.BlockSpec(memory_space=pltpu.SMEM)
    vmem = pl.BlockSpec(memory_space=pltpu.VMEM)
    return pl.pallas_call(
        attend_back_kernel,
        out_shape=jax.ShapeDtypeStruct((parts, units, 3 * LANES), jnp.bfloat16),
        in_specs=[smem] * 3 + [vmem] * 11,
        out_specs=vmem,
        scratch_shapes=[
            pltpu.VMEM((blocks, LANES, block), jnp.bfloat16),
            pltpu.VMEM((blocks, block, LANES), jnp.float32),
            pltpu.VMEM((blocks, block, LANES), jnp.float32),
            pltpu.VMEM((block, block), jnp.int32),
            pltpu.VMEM((block, block), jnp.float32),
        ],
        compiler_params=pltpu.CompilerParams(vmem_limit_bytes=KERNEL_VMEM),
        cost_estimate=pl.CostEstimate(
            flops=50 * 10**9, bytes_accessed=16 << 20, transcendentals=20 * 10**6
        ),
        name="attend_back",
    )(*tables, query, key, value, out, log, grad)


def attention_tables(lengths, grp_here, rep_here, units):
    reps = lax.axis_size("rep")
    parts = lax.axis_size("grp") * reps
    block = parts * UNIT_BLOCK
    blocks = units // UNIT_BLOCK
    own = lax.dynamic_index_in_dim(lengths, grp_here, 0, keepdims=False)
    ends = jnp.cumsum(own)
    unit_ids = jnp.arange(units, dtype=jnp.int32)
    begin = jnp.max(
        jnp.where(ends[None, :] <= unit_ids[:, None], ends[None, :], 0), axis=1
    ).astype(jnp.int32)
    part_ids = jnp.arange(parts, dtype=jnp.int32)
    offset = part_ids % reps ^ rep_here
    slot = offset * lax.axis_size("grp") + (part_ids // reps ^ grp_here)
    frequency = jnp.power(
        rope_base, -2.0 * (jnp.arange(LANES) % (HD // 2)).astype(jnp.float32) / HD
    )
    unit_angle = ((unit_ids - begin) * parts).astype(jnp.float32)[:, None] * frequency[None, :]
    part_angle = part_ids.astype(jnp.float32)[:, None] * frequency[None, :]
    low = jnp.maximum(
        (begin * parts)[:, None], unit_ids[:, None] * parts + part_ids[None, :] - (WINDOW - 1)
    )
    low = low.reshape(blocks, UNIT_BLOCK, parts)
    least = jnp.min(low, axis=(1, 2))
    most = jnp.max(low, axis=(1, 2))
    block_ids = jnp.arange(blocks, dtype=jnp.int32)
    first = jnp.maximum(least, 0) // block
    plain = jnp.clip((most + block - 1) // block, first, block_ids)
    low_rows = jnp.broadcast_to(
        low.transpose(0, 2, 1).reshape(blocks, 1, block), (blocks, 8, block)
    )
    return (
        slot,
        first,
        plain,
        jnp.cos(unit_angle),
        jnp.sin(unit_angle),
        jnp.cos(part_angle),
        jnp.sin(part_angle),
        low_rows,
    )


def swap(value, grp_step, rep_step):
    groups, reps = lax.axis_size("grp"), lax.axis_size("rep")
    pairs = [
        (grp * reps + rep, (grp ^ grp_step) * reps + (rep ^ rep_step))
        for grp in range(groups)
        for rep in range(reps)
    ]
    return lax.ppermute(value, BOTH, pairs)


def ordered(flag, own, other, axis=0):
    return jnp.where(
        flag == 0,
        jnp.concatenate([own, other], axis=axis),
        jnp.concatenate([other, own], axis=axis),
    )


def pick(value, index, axis):
    return lax.dynamic_index_in_dim(value, index, axis, keepdims=False)


def halve(value, axis, bit, grp_step, rep_step):
    kept = pick(value, bit, axis)
    sent = pick(value, 1 - bit, axis).astype(jnp.bfloat16)
    arrived = swap(sent, grp_step, rep_step)
    return kept.astype(jnp.float32) + arrived.astype(jnp.float32)


def narrow(value):
    return value.astype(jnp.bfloat16)


MESH_IDS = pl.DeviceIdType.MESH


def flipped(index, step):
    return index + step - 2 * step * ((index // step) % 2)


def lowest(offset):
    return offset & -offset


def arrivals(reps):
    far = [step for step in range(4, reps, 4)]
    far.sort(key=lambda step: (bin(step).count("1"), step))
    order = [(2, 0), (0, 1)]
    for at, step in enumerate(far):
        if bin(step).count("1") == 1:
            order.append((step, 0))
    order.append((2, 1))
    for step in far:
        if bin(step).count("1") == 1:
            order.append((step, 1))
    single = [step for step in far if bin(step).count("1") == 1]
    double = [step for step in far if bin(step).count("1") > 1]
    rest = []
    for step in single[:1]:
        rest.append((step + 2, 0))
    for step in double:
        rest.append((step, 0))
    for step in single[:1]:
        rest.append((step + 2, 1))
    for step in double:
        rest.append((step, 1))
    for step in single[1:] + double:
        rest += [(step + 2, 0), (step + 2, 1)]
    return order + rest


def link_of(offset, part, reps):
    if reps > 8 and offset == reps - 2 and part == 1:
        return 4
    return lowest(offset)


def gather_kernel(
    tokens_ref,
    gain_ref,
    w_query,
    w_key,
    w_value,
    normed_out,
    qkv_ref,
    weight_ref,
    raw,
    normed,
    gains,
    weight_sem,
    out_sem,
    send_sem,
    recv_sem,
    side_send,
    side_recv,
):
    here, there = lax.axis_index("grp"), lax.axis_index("rep")
    reps = raw.shape[0]
    slots = normed.shape[0]
    row_count, width = raw.shape[2:]
    steps = [1 << place for place in range(reps.bit_length() - 1)]
    across = (1 - here, there)

    def neighbour(step):
        return (here, flipped(there, step))

    barrier = pltpu.get_barrier_semaphore()
    for target in [across] + [neighbour(step) for step in steps]:
        pl.semaphore_signal(barrier, inc=1, device_id=target, device_id_type=MESH_IDS)
    local = []
    for at, weight in enumerate((w_query, w_key, w_value)):
        local.append(
            pltpu.make_async_copy(
                weight.at[:, pl.ds(pl.multiple_of(there * LANES, LANES), LANES)],
                weight_ref.at[here, :, pl.ds(at * LANES, LANES)],
                weight_sem.at[at],
            )
        )
        local[-1].start()
    raw[0, 0] = tokens_ref[here]
    gains[here] = gain_ref[...]
    pl.semaphore_wait(barrier, len(steps) + 1)

    def side(at, source, target_ref):
        return pltpu.make_async_remote_copy(
            src_ref=source,
            dst_ref=target_ref,
            send_sem=side_send.at[at],
            recv_sem=side_recv.at[at],
            device_id=across,
            device_id_type=MESH_IDS,
        )

    def rows_copy(offset, part):
        if offset == 0:
            return pltpu.make_async_remote_copy(
                src_ref=tokens_ref.at[1 - here],
                dst_ref=raw.at[0, 1],
                send_sem=send_sem.at[1],
                recv_sem=recv_sem.at[1],
                device_id=across,
                device_id_type=MESH_IDS,
            )
        step = link_of(offset, part, reps)
        return pltpu.make_async_remote_copy(
            src_ref=raw.at[offset - step, part],
            dst_ref=raw.at[offset, part],
            send_sem=send_sem.at[2 * offset + part],
            recv_sem=recv_sem.at[2 * offset + part],
            device_id=neighbour(step),
            device_id_type=MESH_IDS,
        )

    order = arrivals(reps)
    copies = {
        (offset, part): rows_copy(offset, part)
        for offset in range(reps)
        for part in (0, 1)
        if offset or part
    }

    def pass_on(offset, part):
        for later, part_of in order:
            if later and part_of == part and later - link_of(later, part, reps) == offset:
                copies[later, part].start()
        copies[offset + 1, part].start()

    gain_copy = side(0, gains.at[here], gains.at[here])
    gain_copy.start()
    copies[0, 1].start()
    pass_on(0, 0)
    for one in local:
        one.wait()
    weight_copy = side(1, weight_ref.at[here], weight_ref.at[here])
    weight_copy.start()

    written = {}
    used = [None] * slots
    tile = 32

    def project(count, offset):
        slot = count % slots
        if used[slot] is not None:
            written[used[slot]].wait()
        used[slot] = offset
        gain = jnp.concatenate([gains[0, 0:1], gains[1, 0:1]], axis=1).astype(jnp.float32)
        for part in range(2):

            def norm_rows(at, unused):
                cut = pl.ds(pl.multiple_of(at * tile, tile), tile)
                values = raw[offset, part, cut, :].astype(jnp.float32)
                scaled = values * rms_scale(values) * gain
                normed[slot, pl.ds(pl.multiple_of(part * row_count + at * tile, tile), tile), :] = (
                    scaled.astype(jnp.bfloat16)
                )
                return unused

            lax.fori_loop(0, row_count // tile, norm_rows, 0)
        written[offset] = pltpu.make_async_copy(
            normed.at[slot], normed_out.at[offset], out_sem.at[offset]
        )
        written[offset].start()
        half = width // 2
        product = jnp.dot(
            normed[slot, :, :half], weight_ref[0], preferred_element_type=jnp.float32
        ) + jnp.dot(normed[slot, :, half:], weight_ref[1], preferred_element_type=jnp.float32)
        qkv_ref[pl.ds(2 * offset, 2)] = product.astype(jnp.bfloat16).reshape(
            2, row_count, 3 * LANES
        )

    ready = []
    arrived = {(0, 0)}
    started = False
    count = 0
    for offset, part in order:
        copies[offset, part].wait_recv()
        pass_on(offset, part)
        arrived.add((offset, part))
        if (offset, 1 - part) in arrived:
            ready.append(offset)
        if not started and len(ready) >= 1:
            gain_copy.wait_recv()
            weight_copy.wait_recv()
            started = True
        if started and len(ready) >= 2:
            base = ready.pop(0)
            project(count, base)
            copies[base + 1, 0].wait_recv()
            copies[base + 1, 1].wait_recv()
            project(count + 1, base + 1)
            count += 2
    for base in ready:
        project(count, base)
        copies[base + 1, 0].wait_recv()
        copies[base + 1, 1].wait_recv()
        project(count + 1, base + 1)
        count += 2
    for offset in used:
        written[offset].wait()
    for one in copies.values():
        one.wait_send()
    gain_copy.wait_send()
    weight_copy.wait_send()


def gather_heads(tokens, gain, w_query, w_key, w_value):
    reps = lax.axis_size("rep")
    _, row_count, width = tokens.shape
    half = width // 2
    gain_rows = jnp.broadcast_to(gain[None], (16, half))
    vmem = pl.BlockSpec(memory_space=pltpu.VMEM)
    anywhere = pl.BlockSpec(memory_space=pl.ANY)
    return pl.pallas_call(
        gather_kernel,
        out_shape=(
            jax.ShapeDtypeStruct((reps, 2 * row_count, width), jnp.bfloat16),
            jax.ShapeDtypeStruct((2 * reps, row_count, 3 * LANES), jnp.bfloat16),
            jax.ShapeDtypeStruct((2, half, 3 * LANES), jnp.bfloat16),
        ),
        in_specs=[vmem, vmem, anywhere, anywhere, anywhere],
        out_specs=(anywhere, vmem, vmem),
        scratch_shapes=[
            pltpu.VMEM((reps, 2, row_count, width), jnp.bfloat16),
            pltpu.VMEM((4, 2 * row_count, width), jnp.bfloat16),
            pltpu.VMEM((2, 16, half), jnp.bfloat16),
            pltpu.SemaphoreType.DMA((3,)),
            pltpu.SemaphoreType.DMA((reps,)),
            pltpu.SemaphoreType.DMA((2 * reps,)),
            pltpu.SemaphoreType.DMA((2 * reps,)),
            pltpu.SemaphoreType.DMA((2,)),
            pltpu.SemaphoreType.DMA((2,)),
        ],
        compiler_params=pltpu.CompilerParams(
            vmem_limit_bytes=KERNEL_VMEM, collective_id=0, has_side_effects=True
        ),
        cost_estimate=pl.CostEstimate(
            flops=8 * 10**9, bytes_accessed=250 << 20, transcendentals=0
        ),
        name="gather_heads",
    )(tokens, gain_rows, w_query, w_key, w_value)


def scatter_kernel(
    back_ref,
    weight_ref,
    normed_ref,
    grad_ref,
    pieces_ref,
    away,
    landed,
    normed,
    back_t,
    weight_t,
    weights_total,
    half_out,
    half_in,
    piece_out,
    normed_sem,
    send_sem,
    recv_sem,
    side_send,
    side_recv,
    piece_send,
    piece_recv,
):
    here, there = lax.axis_index("grp"), lax.axis_index("rep")
    reps, rows, columns = back_ref.shape
    row_count = rows // 2
    width = grad_ref.shape[2]
    half = width // 2
    own_rows = half // reps
    steps = [1 << place for place in range(reps.bit_length() - 1)]
    across = (1 - here, there)

    def other(offset):
        index = there
        for step in steps:
            if offset & step:
                index = flipped(index, step)
        return (here, index)

    barrier = pltpu.get_barrier_semaphore()
    for target in [across] + [other(offset) for offset in range(1, reps)]:
        pl.semaphore_signal(barrier, inc=1, device_id=target, device_id_type=MESH_IDS)

    slots = normed.shape[0]
    fetch = [
        pltpu.make_async_copy(normed_ref.at[offset], normed.at[offset % slots], normed_sem.at[offset])
        for offset in range(reps)
    ]
    for offset in range(slots):
        fetch[offset].start()

    for at in range(2):
        turned = jnp.transpose(weight_ref[at].astype(jnp.float32)).astype(jnp.bfloat16)
        weight_t[:, pl.ds(at * half, half)] = turned
    pl.semaphore_wait(barrier, reps)

    def rows_copy(offset, part):
        if offset == 0:
            return pltpu.make_async_remote_copy(
                src_ref=away.at[0, 1],
                dst_ref=landed.at[0, 1],
                send_sem=send_sem.at[1],
                recv_sem=recv_sem.at[1],
                device_id=across,
                device_id_type=MESH_IDS,
            )
        return pltpu.make_async_remote_copy(
            src_ref=away.at[offset, part],
            dst_ref=landed.at[offset, part],
            send_sem=send_sem.at[2 * offset + part],
            recv_sem=recv_sem.at[2 * offset + part],
            device_id=other(link_of(offset, part, reps)),
            device_id_type=MESH_IDS,
        )

    copies = {
        (offset, part): rows_copy(offset, part)
        for offset in range(reps)
        for part in (0, 1)
        if offset or part
    }
    tile = 32

    def product(offset, part):
        return jnp.dot(
            back_ref[offset, pl.ds(part * row_count, row_count), :],
            weight_t[...],
            preferred_element_type=jnp.float32,
        )

    def send(offset, part):
        sources = [
            later
            for later in range(1, reps)
            if later - link_of(later, part, reps) == offset
        ]
        for later in sources:
            copies[later, part].wait_recv()
        total = product(offset, part)
        for later in sources:
            total = total + landed[later, part].astype(jnp.float32)
        if offset == 0 and part == 0:
            grad_ref[here] = total
        else:
            away[offset, part] = total.astype(jnp.bfloat16)
            copies[offset, part].start()

    def weight_step(offset):
        fetch[offset].wait()
        back_t[...] = jnp.transpose(back_ref[offset].astype(jnp.float32)).astype(jnp.bfloat16)

        def columns_at(at, unused):
            cut = pl.ds(pl.multiple_of(at * 512, 512), 512)
            term = jnp.dot(
                back_t[...], normed[offset % slots, :, cut], preferred_element_type=jnp.float32
            )
            if offset == 0:
                weights_total[:, cut] = term
            else:
                weights_total[:, cut] += term
            return unused

        lax.fori_loop(0, width // 512, columns_at, 0)
        if offset + slots < reps:
            fetch[offset + slots].start()

    half_copy = pltpu.make_async_remote_copy(
        src_ref=half_out,
        dst_ref=half_in,
        send_sem=side_send,
        recv_sem=side_recv,
        device_id=across,
        device_id_type=MESH_IDS,
    )
    piece_copies = [
        pltpu.make_async_remote_copy(
            src_ref=piece_out.at[other(offset)[1]],
            dst_ref=pieces_ref.at[there],
            send_sem=piece_send.at[offset],
            recv_sem=piece_recv.at[offset],
            device_id=other(offset),
            device_id_type=MESH_IDS,
        )
        for offset in range(1, reps)
    ]

    def cross_weights():
        cut = pl.ds(pl.multiple_of((1 - here) * half, half), half)
        half_out[...] = weights_total[:, cut].astype(jnp.bfloat16)
        half_copy.start()

    def share_weights():
        half_copy.wait_recv()
        cut = pl.ds(pl.multiple_of(here * half, half), half)
        total = jnp.transpose(weights_total[:, cut] + half_in[...].astype(jnp.float32))
        piece_out[...] = total.astype(jnp.bfloat16).reshape(reps, own_rows, columns)
        pieces_ref[there] = piece_out[there]
        for one in piece_copies:
            one.start()

    far = [step for step in range(reps - 4, 0, -4)]
    todo = []
    for base in far + [0]:
        todo.append((base + 3, 1))
        todo.append((base + 3, 0))
        todo.append((base + 1, 1))
        todo.append((base + 1, 0))
    first = todo[:2]
    for offset, part in first:
        send(offset, part)
    for offset, part in todo[2:6]:
        send(offset, part)
    send(reps - 2, 1)
    send(reps - 2, 0)
    for offset, part in todo[6:]:
        send(offset, part)
    weights = list(range(reps))

    def weight_steps(count):
        for _ in range(min(count, len(weights))):
            weight_step(weights.pop(0))

    last = []
    order = []
    for base in sorted(far, key=lambda step: (-bin(step).count("1"), -step)):
        if base != far[0]:
            order.append((base + 2, 1))
            order.append((base + 2, 0))
    order += [(2, 1), (2, 0)]
    sums = sorted(far, key=lambda step: (-bin(step).count("1"), -step))
    for base in sums:
        last += [(base, 1), (base, 0)]
    if reps == 16:
        plan = [
            (10, 1), (10, 0), 4, (12, 1), (12, 0), 4, (6, 1), (6, 0), 2, (8, 1), 2, (8, 0),
            (2, 1), (2, 0), 4, "cross", (4, 1), (4, 0), "share", (0, 1), (0, 0),
        ]
    else:
        plan = order + last + [reps, "cross", "share", (0, 1), (0, 0)]
    for item in plan:
        if item == "cross":
            weight_steps(reps)
            cross_weights()
        elif item == "share":
            share_weights()
        elif isinstance(item, int):
            weight_steps(item)
        else:
            send(*item)
    copies[0, 1].wait_recv()
    grad_ref[1 - here] = landed[0, 1].astype(jnp.float32)
    for one in piece_copies:
        one.wait()
    half_copy.wait_send()
    for one in copies.values():
        one.wait_send()


def scatter_heads(back, weights, normed):
    reps, rows, columns = back.shape
    width = normed.shape[2]
    row_count = rows // 2
    half = width // 2
    vmem = pl.BlockSpec(memory_space=pltpu.VMEM)
    anywhere = pl.BlockSpec(memory_space=pl.ANY)
    return pl.pallas_call(
        scatter_kernel,
        out_shape=(
            jax.ShapeDtypeStruct((2, row_count, width), jnp.float32),
            jax.ShapeDtypeStruct((reps, half // reps, columns), jnp.bfloat16),
        ),
        in_specs=[vmem, vmem, anywhere],
        out_specs=(vmem, vmem),
        scratch_shapes=[
            pltpu.VMEM((reps, 2, row_count, width), jnp.bfloat16),
            pltpu.VMEM((reps, 2, row_count, width), jnp.bfloat16),
            pltpu.VMEM((4, rows, width), jnp.bfloat16),
            pltpu.VMEM((columns, rows), jnp.bfloat16),
            pltpu.VMEM((columns, width), jnp.bfloat16),
            pltpu.VMEM((columns, width), jnp.float32),
            pltpu.VMEM((columns, half), jnp.bfloat16),
            pltpu.VMEM((columns, half), jnp.bfloat16),
            pltpu.VMEM((reps, half // reps, columns), jnp.bfloat16),
            pltpu.SemaphoreType.DMA((reps,)),
            pltpu.SemaphoreType.DMA((2 * reps,)),
            pltpu.SemaphoreType.DMA((2 * reps,)),
            pltpu.SemaphoreType.DMA,
            pltpu.SemaphoreType.DMA,
            pltpu.SemaphoreType.DMA((reps,)),
            pltpu.SemaphoreType.DMA((reps,)),
        ],
        compiler_params=pltpu.CompilerParams(
            vmem_limit_bytes=KERNEL_VMEM, collective_id=1, has_side_effects=True
        ),
        cost_estimate=pl.CostEstimate(
            flops=14 * 10**9, bytes_accessed=250 << 20, transcendentals=0
        ),
        name="scatter_heads",
    )(back, weights, normed)


def heads_body(
    tokens,
    attn_gain,
    w_query,
    w_key,
    w_value,
    w_output,
    mlp_gain,
    w_gate,
    w_up,
    w_down,
    out_grad,
    lengths,
):
    groups, reps = lax.axis_size("grp"), lax.axis_size("rep")
    here, there = lax.axis_index("grp"), lax.axis_index("rep")
    core = there % 2
    micro_count, row_count, width = tokens.shape
    rows = micro_count * row_count
    hidden_width = w_gate.shape[1]
    half_width = width // groups
    own_width = hidden_width // (2 * groups)
    stripes = reps // 2

    gathered_rows, qkv, w_heads = gather_heads(tokens, attn_gain, w_query, w_key, w_value)
    gain_one = ordered(here, attn_gain, swap(attn_gain, 1, 0)).astype(jnp.float32)
    gain_two = ordered(here, mlp_gain, swap(mlp_gain, 1, 0)).astype(jnp.float32)
    inputs = tokens.astype(jnp.float32)

    output_other = swap(
        lax.dynamic_slice_in_dim(w_output, core * (half_width // 2), half_width // 2, axis=0), 1, 0
    )
    output_other = ordered(core, output_other, swap(output_other, 0, 1))
    w_output_full = ordered(here, w_output, output_other)

    def striped(weight):
        return weight.reshape(half_width, groups, stripes, 2, LANES)

    def own_stripes(weight, grp):
        cut = pick(pick(striped(weight), grp, 1), core, 2)
        return cut.reshape(half_width, own_width)

    w_in = jnp.concatenate([own_stripes(w_gate, here), own_stripes(w_up, here)], axis=1)
    w_in_other = swap(
        jnp.concatenate([own_stripes(w_gate, 1 - here), own_stripes(w_up, 1 - here)], axis=1), 1, 0
    )
    w_in = ordered(here, w_in, w_in_other)
    w_out = pick(w_down.reshape(stripes, 2, LANES, width), core, 1).reshape(own_width, width)

    def gather_quad(value):
        across = swap(value, 1, 0)
        return jnp.concatenate([value, swap(value, 0, 1), across, swap(across, 0, 1)], axis=0)

    out_rows = out_grad.reshape(rows, width)
    out_quad = gather_quad(out_rows)
    grad_hidden = contract(out_quad, w_out, 1, 1)

    tables = attention_tables(lengths, here, there, row_count)
    attended, out_heads, log_sum, query, key, value = attend(tables, qkv)
    returned = lax.all_to_all(attended, BOTH, split_axis=0, concat_axis=0, tiled=True)
    attn_rows = (
        returned.reshape(groups, reps, row_count, LANES).transpose(0, 2, 1, 3).reshape(rows, width)
    )
    mixed = inputs.reshape(rows, width) + jnp.dot(
        attn_rows, w_output_full, preferred_element_type=jnp.float32
    )
    normed_mid = (mixed * rms_scale(mixed) * gain_two).astype(jnp.bfloat16)
    mid_quad = gather_quad(normed_mid)
    gate_up = jnp.dot(mid_quad, w_in, preferred_element_type=jnp.float32)
    gate_pre, up_pre = gate_up[:, :own_width], gate_up[:, own_width:]
    gate_sig = jax.nn.sigmoid(gate_pre)
    gate_silu = gate_pre * gate_sig
    hidden = (gate_silu * up_pre).astype(jnp.bfloat16)
    grad_gate = (grad_hidden * up_pre * gate_sig * (1.0 + gate_pre * (1.0 - gate_sig))).astype(
        jnp.bfloat16
    )
    grad_up = (grad_hidden * gate_silu).astype(jnp.bfloat16)
    grad_in_mlp = jnp.concatenate([grad_gate, grad_up], axis=1)

    def scatter_quad(parts):
        parts = parts.reshape(2, 2, rows, width)
        both = parts[:, 0].astype(jnp.float32) + swap(narrow(parts[:, 1]), 0, 1).astype(jnp.float32)
        return both[0] + swap(narrow(both[1]), 1, 0).astype(jnp.float32)

    grad_mid = scatter_quad(contract(grad_in_mlp, w_in, 1, 1, jnp.bfloat16))
    grad_norm_mid, unused_gain = norm_backward(mixed, gain_two, grad_mid)
    grad_mixed = out_rows.astype(jnp.float32) + grad_norm_mid
    grad_branch = grad_mixed.astype(jnp.bfloat16)
    grad_att = contract(grad_branch, w_output_full, 1, 1, jnp.bfloat16)
    grad_heads = lax.all_to_all(
        grad_att.reshape(groups, row_count, reps, LANES)
        .transpose(0, 2, 1, 3)
        .reshape(groups * reps, row_count, LANES),
        BOTH,
        split_axis=0,
        concat_axis=0,
        tiled=True,
    )

    block_out = (
        mixed + scatter_quad(jnp.dot(hidden, w_out, preferred_element_type=jnp.float32).astype(jnp.bfloat16))
    ).astype(jnp.bfloat16)

    bits = [(there // step) % 2 for step in (1, 2)]
    far = [1 << place for place in range(2, reps.bit_length() - 1)]

    def scatter_stripes(parts):
        lead, rest = parts.shape[0], parts.shape[2:]
        parts = halve(parts.reshape((lead, stripes // 2, 2) + rest), 2, bits[1], 0, 2)
        for step in far:
            count = parts.shape[1]
            parts = halve(
                narrow(parts).reshape((lead, count // 2, 2) + rest), 2, (there // step) % 2, 0, step
            )
        return parts[:, 0]

    mlp_in_grad = contract(mid_quad, grad_in_mlp, 0, 0, jnp.bfloat16)
    own_rows = width // (groups * reps)
    mlp_in_part = narrow(
        scatter_stripes(
            mlp_in_grad.reshape(groups, stripes, 2, own_rows, 2 * own_width)
        )
    )
    down_grad = scatter_stripes(
        contract(hidden, out_quad, 0, 0, jnp.bfloat16).reshape(1, stripes, LANES, width)
    )[0]

    kept = pick(mlp_in_part, here, 0)
    crossed = swap(pick(mlp_in_part, 1 - here, 0), 1, 0)
    columns = []
    for part in (kept, crossed):
        columns.append(pick(part, core, 0))
        columns.append(swap(pick(part, 1 - core, 0), 0, 1))
    by_grp = [
        jnp.where(
            core == 0,
            jnp.stack([columns[2 * at], columns[2 * at + 1]], axis=1),
            jnp.stack([columns[2 * at + 1], columns[2 * at]], axis=1),
        )
        for at in range(2)
    ]
    pieces = jnp.where(
        here == 0,
        jnp.stack([by_grp[0], by_grp[1]], axis=1),
        jnp.stack([by_grp[1], by_grp[0]], axis=1),
    )
    pieces = pieces.reshape(own_rows, groups, 2, 2, stripes, LANES).transpose(3, 0, 1, 4, 2, 5)
    pieces = pieces.reshape(2, own_rows, hidden_width).astype(jnp.float32)
    gate_grad, up_grad = pieces[0], pieces[1]

    output_part = contract(attn_rows, grad_branch, 0, 0, jnp.bfloat16)
    output_part = output_part.reshape(groups, stripes, 2, own_rows, width)
    output_part = halve(output_part, 2, core, 0, 1)
    output_part = halve(narrow(output_part), 0, here, 1, 0)
    output_grad = scatter_stripes(narrow(output_part)[None])[0]

    back = attend_back(tables, query, key, value, out_heads, log_sum, grad_heads)
    grad_in, heads_grad = scatter_heads(
        back.reshape(reps, groups * row_count, 3 * LANES), w_heads, gathered_rows
    )
    grad_norm_in, unused_gain = norm_backward(
        inputs.reshape(rows, width), gain_one, grad_in.reshape(rows, width)
    )
    token_grad = (grad_mixed + grad_norm_in).astype(jnp.bfloat16)

    heads_grad = (
        heads_grad.reshape(reps, own_rows, 3, LANES)
        .transpose(2, 1, 0, 3)
        .reshape(3, own_rows, width)
        .astype(jnp.float32)
    )

    def own_part(value):
        return lax.dynamic_slice_in_dim(value, there * own_rows, own_rows, axis=0).astype(
            jnp.float32
        )

    attn_gain_grad = (
        jnp.sum(own_part(w_query) * heads_grad[0], axis=1)
        + jnp.sum(own_part(w_key) * heads_grad[1], axis=1)
        + jnp.sum(own_part(w_value) * heads_grad[2], axis=1)
    ) / own_part(attn_gain)
    mlp_gain_grad = (
        jnp.sum(own_part(w_gate) * gate_grad, axis=1) + jnp.sum(own_part(w_up) * up_grad, axis=1)
    ) / own_part(mlp_gain)
    block_shape = tokens.shape
    return (
        block_out.reshape(block_shape),
        token_grad.reshape(block_shape),
        attn_gain_grad,
        heads_grad[0],
        heads_grad[1],
        heads_grad[2],
        output_grad,
        mlp_gain_grad,
        gate_grad,
        up_grad,
        down_grad,
    )


def pick_body(*arrays):
    tokens = arrays[0]
    groups, reps = lax.axis_size("grp"), lax.axis_size("rep")
    fits = (
        groups == 2
        and tokens.shape[0] == groups
        and tokens.shape[2] == reps * LANES
        and reps % 4 == 0
        and reps & (reps - 1) == 0
        and tokens.shape[1] % UNIT_PAIR == 0
        and arrays[7].shape[1] % (2 * groups * LANES) == 0
    )
    return heads_body(*arrays) if fits else ring_body(*arrays)


def solution(mesh):
    in_specs = (
        P(None, ("grp", "rep"), None),
        P("grp"),
        P("grp", None),
        P("grp", None),
        P("grp", None),
        P("grp", None),
        P("grp"),
        P("grp", None),
        P("grp", None),
        P("grp", None),
        P(None, ("grp", "rep"), None),
        P(),
    )
    out_specs = (
        P(None, ("grp", "rep"), None),
        P(None, ("grp", "rep"), None),
        P(("grp", "rep")),
        P(("grp", "rep"), None),
        P(("grp", "rep"), None),
        P(("grp", "rep"), None),
        P(("grp", "rep"), None),
        P(("grp", "rep")),
        P(("grp", "rep"), None),
        P(("grp", "rep"), None),
        P(("grp", "rep"), None),
    )
    return jax.shard_map(pick_body, mesh=mesh, in_specs=in_specs, out_specs=out_specs, check_vma=False)
```

```python
import functools
import math

import jax
import jax.numpy as jnp
from jax import lax
from jax.experimental import pallas as pl
from jax.experimental.pallas import tpu as pltpu
from jax.sharding import PartitionSpec as P

HD = 64
WINDOW = 2048


epsilon = 1e-05
rope_base = 10000.0
masked_score = -1e30
BOTH = ("grp", "rep")
LANES = 128
UNIT_BLOCK = 8
UNIT_PAIR = 16
KERNEL_VMEM = 56 * 1024 * 1024


def from_behind(value, axis, steps):
    count = lax.axis_size(axis)
    first, last = (max(0, -steps), min(count, count - steps))
    return lax.ppermute(value, axis, [(source, source + steps) for source in range(first, last)])


def rms_scale(values):
    return lax.rsqrt(jnp.mean(values * values, axis=-1, keepdims=True) + epsilon)


def norm_backward(values, gain_full, grad_normed):
    inverse = rms_scale(values)
    normed = values * inverse
    gain_grad = jnp.sum(grad_normed * normed, axis=0)
    weighted = grad_normed * gain_full
    return (
        inverse * (weighted - normed * jnp.mean(weighted * normed, axis=-1, keepdims=True)),
        gain_grad,
    )


def rotary(values, cosine, sine_table):
    half_width = values.shape[-1] // 2
    first_half = values[..., :half_width]
    second_half = values[..., half_width:]
    return jnp.concatenate(
        [
            first_half * cosine - second_half * sine_table,
            second_half * cosine + first_half * sine_table,
        ],
        axis=-1,
    )


def pick_rows(rows_block, row_ids):
    return jnp.take(rows_block, row_ids, axis=0)


def take_rows(values, row_ids):
    return jax.vmap(pick_rows)(values, row_ids)


def gather_attn(attn_gain, w_query, w_key, w_value, w_output):
    return (
        lax.all_gather(attn_gain, "grp", axis=0, tiled=True),
        lax.all_gather(w_query, "grp", axis=0, tiled=True),
        lax.all_gather(w_key, "grp", axis=0, tiled=True),
        lax.all_gather(w_value, "grp", axis=0, tiled=True),
        lax.all_gather(w_output, "grp", axis=0, tiled=True),
    )


def gather_mlp(mlp_gain, w_gate, w_up, w_down):
    return (
        lax.all_gather(mlp_gain, "grp", axis=0, tiled=True),
        lax.all_gather(w_gate, "grp", axis=0, tiled=True),
        lax.all_gather(w_up, "grp", axis=0, tiled=True),
        lax.all_gather(w_down, "grp", axis=0, tiled=True),
    )


def reduce_attn(gain_grad, query_grad, key_grad, value_grad, output_grad):
    return (
        lax.psum_scatter(gain_grad, ("grp", "rep"), scatter_dimension=0, tiled=True),
        lax.psum_scatter(query_grad, ("grp", "rep"), scatter_dimension=0, tiled=True),
        lax.psum_scatter(key_grad, ("grp", "rep"), scatter_dimension=0, tiled=True),
        lax.psum_scatter(value_grad, ("grp", "rep"), scatter_dimension=0, tiled=True),
        lax.psum_scatter(output_grad, ("grp", "rep"), scatter_dimension=0, tiled=True),
    )


def reduce_mlp(gain_grad, gate_grad, up_grad, down_grad):
    return (
        lax.psum_scatter(gain_grad, ("grp", "rep"), scatter_dimension=0, tiled=True),
        lax.psum_scatter(gate_grad, ("grp", "rep"), scatter_dimension=0, tiled=True),
        lax.psum_scatter(up_grad, ("grp", "rep"), scatter_dimension=0, tiled=True),
        lax.psum_scatter(down_grad, ("grp", "rep"), scatter_dimension=0, tiled=True),
    )


def pass_on(carried, unused):
    arrived = from_behind(carried, ("grp", "rep"), 1)
    return (arrived, arrived)


def pass_back(running, portion):
    arrived = from_behind(running.astype(jnp.bfloat16), ("grp", "rep"), -1).astype(running.dtype)
    return (arrived + portion, None)


def ring_body(
    tokens,
    attn_gain,
    w_query,
    w_key,
    w_value,
    w_output,
    mlp_gain,
    w_gate,
    w_up,
    w_down,
    out_grad,
    lengths,
):
    devices = lax.axis_size(("grp", "rep"))
    rank_here = lax.axis_index(("grp", "rep"))
    micro_count, row_count, model_width = tokens.shape
    per_dev = row_count // devices
    head_count = model_width // HD
    reach_count = (WINDOW + row_count - 2) // row_count
    head_group = math.gcd(head_count, 4)
    group_count = head_count // head_group
    score_scale = 1.0 / math.sqrt(HD)
    unit_ids = jnp.arange(row_count, dtype=jnp.int32)
    seq_ends = jnp.cumsum(lengths, axis=1)
    starts = seq_ends - lengths
    seq_order = jnp.arange(lengths.shape[1], dtype=jnp.int32)
    earlier = seq_order[None, :] < seq_order[:, None]
    dealt_start = jnp.sum(jnp.where(earlier[None], lengths[:, None, :], 0), axis=2)
    seq_of = jnp.sum((seq_ends[:, None, :] <= unit_ids[None, :, None]).astype(jnp.int32), axis=2)
    seq_dealt = jnp.take_along_axis(dealt_start, seq_of, axis=1)
    unit_of = seq_dealt + unit_ids[None, :] - jnp.take_along_axis(starts, seq_of, axis=1)
    micro_ids = jnp.arange(micro_count, dtype=jnp.int32)[:, None]
    source_unit = (
        jnp.zeros((micro_count, row_count), jnp.int32)
        .at[micro_ids, unit_of]
        .set(jnp.broadcast_to(unit_ids[None, :], unit_of.shape))
    )
    unit_begin = (
        jnp.zeros((micro_count, row_count), jnp.int32).at[micro_ids, unit_of].set(seq_dealt)
    )
    local_ids = jnp.arange(row_count, dtype=jnp.int32)
    local_step = local_ids % per_dev
    local_source = local_ids // per_dev
    distance = jnp.arange(reach_count + 1, dtype=jnp.int32)
    owner_dev = rank_here - distance
    owner_ok = owner_dev >= 0
    owner_unit = jnp.maximum(owner_dev, 0)[:, None] * per_dev + local_step[None, :]
    key_begin = unit_begin[:, owner_unit]
    key_pos = (owner_unit[None] - key_begin) * devices + local_source[None, None, :]
    query_begin = key_begin[:, 0]
    query_pos = key_pos[:, 0]
    allowed = (
        owner_ok[None, None, :, None]
        & (query_begin[:, :, None, None] == key_begin[:, None, :, :])
        & (key_pos[:, None, :, :] <= query_pos[:, :, None, None])
        & (query_pos[:, :, None, None] - key_pos[:, None, :, :] < WINDOW)
    )
    mask_full = allowed[:, None]
    half_width = HD // 2
    frequency = jnp.power(rope_base, -2.0 * jnp.arange(half_width, dtype=jnp.float32) / HD)
    angles = query_pos.astype(jnp.float32)[:, :, None] * frequency[None, None, :]
    cosine = jnp.cos(angles)[:, :, None, :]
    sine_table = jnp.sin(angles)[:, :, None, :]
    head_shape = (micro_count, row_count, head_count, HD)
    block_shape = (micro_count, row_count, model_width)
    gathered = gather_attn(attn_gain, w_query, w_key, w_value, w_output)
    gain_one = gathered[0].astype(jnp.float32)
    inputs = tokens.astype(jnp.float32).reshape(micro_count * row_count, model_width)
    normed_in = (inputs * rms_scale(inputs) * gain_one).astype(jnp.bfloat16)
    queries = jnp.dot(normed_in, gathered[1], preferred_element_type=jnp.float32).astype(
        jnp.bfloat16
    )
    keys_in = jnp.dot(normed_in, gathered[2], preferred_element_type=jnp.float32).astype(
        jnp.bfloat16
    )
    values_in = jnp.dot(normed_in, gathered[3], preferred_element_type=jnp.float32).astype(
        jnp.bfloat16
    )
    dealt = (
        lax.all_to_all(
            take_rows(queries.reshape(block_shape), source_unit),
            ("grp", "rep"),
            split_axis=1,
            concat_axis=1,
            tiled=True,
        ),
        lax.all_to_all(
            take_rows(keys_in.reshape(block_shape), source_unit),
            ("grp", "rep"),
            split_axis=1,
            concat_axis=1,
            tiled=True,
        ),
        lax.all_to_all(
            take_rows(values_in.reshape(block_shape), source_unit),
            ("grp", "rep"),
            split_axis=1,
            concat_axis=1,
            tiled=True,
        ),
    )
    rot_q = rotary(dealt[0].reshape(head_shape).astype(jnp.float32), cosine, sine_table).astype(
        jnp.bfloat16
    )
    rot_k = rotary(dealt[1].reshape(head_shape).astype(jnp.float32), cosine, sine_table).astype(
        jnp.bfloat16
    )
    own_pair = jnp.stack([rot_k.reshape(block_shape), dealt[2]], axis=0)
    last_pair, farther = lax.scan(pass_on, own_pair, None, length=reach_count)
    context = jnp.concatenate([own_pair[None], farther], axis=0).reshape(
        reach_count + 1, 2, micro_count, row_count, head_count, HD
    )

    def group_scores(query_part, pair_part):
        scores = (
            jnp.einsum(
                "mqge,dmkge->mgqdk", query_part, pair_part[:, 0], preferred_element_type=jnp.float32
            )
            * score_scale
        )
        return jnp.where(mask_full, scores, masked_score)

    def forward_group(group_index, carried):
        attended_all, log_all = carried
        head_start = group_index * head_group
        query_part = lax.dynamic_slice_in_dim(rot_q, head_start, head_group, axis=2)
        pair_part = lax.dynamic_slice_in_dim(context, head_start, head_group, axis=4)
        scores = group_scores(query_part, pair_part)
        row_max = jnp.max(scores, axis=(3, 4), keepdims=True)
        weights_exp = jnp.exp(scores - row_max)
        row_sum = jnp.sum(weights_exp, axis=(3, 4), keepdims=True)
        soft_probs = (weights_exp / row_sum).astype(jnp.bfloat16)
        attended = jnp.einsum(
            "mgqdk,dmkge->mqge", soft_probs, pair_part[:, 1], preferred_element_type=jnp.float32
        ).astype(jnp.bfloat16)
        attended_all = lax.dynamic_update_slice_in_dim(attended_all, attended, head_start, axis=2)
        log_all = lax.dynamic_update_slice_in_dim(
            log_all, row_max + jnp.log(row_sum), head_start, axis=1
        )
        return (attended_all, log_all)

    attended_heads, log_sum = lax.fori_loop(
        0,
        group_count,
        forward_group,
        (
            jnp.zeros(head_shape, jnp.bfloat16),
            jnp.zeros((micro_count, head_count, row_count, 1, 1), jnp.float32),
        ),
    )
    returned = lax.all_to_all(
        attended_heads.reshape(block_shape), ("grp", "rep"), split_axis=1, concat_axis=1, tiled=True
    )
    attn_rows = take_rows(returned, unit_of).reshape(micro_count * row_count, model_width)
    mixed = inputs + jnp.dot(attn_rows, gathered[4], preferred_element_type=jnp.float32)
    mlp_set = gather_mlp(mlp_gain, w_gate, w_up, w_down)
    gain_two = mlp_set[0].astype(jnp.float32)
    normed_mid = (mixed * rms_scale(mixed) * gain_two).astype(jnp.bfloat16)
    gate_pre = jnp.dot(normed_mid, mlp_set[1], preferred_element_type=jnp.float32)
    up_pre = jnp.dot(normed_mid, mlp_set[2], preferred_element_type=jnp.float32)
    gate_sig = jax.nn.sigmoid(gate_pre)
    gate_silu = gate_pre * gate_sig
    hidden = (gate_silu * up_pre).astype(jnp.bfloat16)
    block_out = (mixed + jnp.dot(hidden, mlp_set[3], preferred_element_type=jnp.float32)).astype(
        jnp.bfloat16
    )
    mlp_set = gather_mlp(mlp_gain, w_gate, w_up, w_down)
    out_rows = out_grad.reshape(micro_count * row_count, model_width)
    down_grad = jnp.einsum("tf,td->fd", hidden, out_rows, preferred_element_type=jnp.float32)
    grad_hidden = jnp.einsum("td,fd->tf", out_rows, mlp_set[3], preferred_element_type=jnp.float32)
    grad_gate = (grad_hidden * up_pre * gate_sig * (1.0 + gate_pre * (1.0 - gate_sig))).astype(
        jnp.bfloat16
    )
    grad_up = (grad_hidden * gate_silu).astype(jnp.bfloat16)
    gate_grad = jnp.einsum("td,tf->df", normed_mid, grad_gate, preferred_element_type=jnp.float32)
    up_grad = jnp.einsum("td,tf->df", normed_mid, grad_up, preferred_element_type=jnp.float32)
    grad_mid = jnp.einsum(
        "tf,df->td", grad_gate, mlp_set[1], preferred_element_type=jnp.float32
    ) + jnp.einsum("tf,df->td", grad_up, mlp_set[2], preferred_element_type=jnp.float32)
    grad_norm_mid, mlp_gain_grad = norm_backward(mixed, gain_two, grad_mid)
    grad_mixed = out_rows.astype(jnp.float32) + grad_norm_mid
    mlp_sums = reduce_mlp(mlp_gain_grad, gate_grad, up_grad, down_grad)
    gathered = gather_attn(attn_gain, w_query, w_key, w_value, w_output)
    grad_branch = grad_mixed.astype(jnp.bfloat16)
    output_grad = jnp.einsum(
        "td,te->de", attn_rows, grad_branch, preferred_element_type=jnp.float32
    )
    grad_att = jnp.einsum(
        "te,de->td", grad_branch, gathered[4], preferred_element_type=jnp.float32
    ).astype(jnp.bfloat16)
    grad_dealt = lax.all_to_all(
        take_rows(grad_att.reshape(block_shape), source_unit),
        ("grp", "rep"),
        split_axis=1,
        concat_axis=1,
        tiled=True,
    )
    grad_heads = grad_dealt.reshape(head_shape)

    def backward_group(group_index, carried):
        query_total, pair_total = carried
        head_start = group_index * head_group
        query_part = lax.dynamic_slice_in_dim(rot_q, head_start, head_group, axis=2)
        grad_part = lax.dynamic_slice_in_dim(grad_heads, head_start, head_group, axis=2)
        pair_part = lax.dynamic_slice_in_dim(context, head_start, head_group, axis=4)
        log_part = lax.dynamic_slice_in_dim(log_sum, head_start, head_group, axis=1)
        scores = group_scores(query_part, pair_part)
        soft_probs = jnp.exp(scores - log_part)
        grad_probs = jnp.einsum(
            "mqge,dmkge->mgqdk", grad_part, pair_part[:, 1], preferred_element_type=jnp.float32
        )
        inner_sum = jnp.sum(soft_probs * grad_probs, axis=(3, 4), keepdims=True)
        grad_scores = (soft_probs * (grad_probs - inner_sum)).astype(jnp.bfloat16)
        query_piece = (
            jnp.einsum(
                "mgqdk,dmkge->mqge",
                grad_scores,
                pair_part[:, 0],
                preferred_element_type=jnp.float32,
            )
            * score_scale
        )
        key_part = (
            jnp.einsum(
                "mgqdk,mqge->dmkge", grad_scores, query_part, preferred_element_type=jnp.float32
            )
            * score_scale
        )
        value_part = jnp.einsum(
            "mgqdk,mqge->dmkge",
            soft_probs.astype(jnp.bfloat16),
            grad_part,
            preferred_element_type=jnp.float32,
        )
        query_total = lax.dynamic_update_slice_in_dim(query_total, query_piece, head_start, axis=2)
        pair_total = lax.dynamic_update_slice_in_dim(
            pair_total, jnp.stack([key_part, value_part], axis=1), head_start, axis=4
        )
        return (query_total, pair_total)

    query_total, pair_total = lax.fori_loop(
        0,
        group_count,
        backward_group,
        (
            jnp.zeros(head_shape, jnp.float32),
            jnp.zeros((reach_count + 1, 2) + head_shape, jnp.float32),
        ),
    )
    partials = pair_total.reshape(reach_count + 1, 2, micro_count, row_count, model_width)
    own_total, unused_out = lax.scan(
        pass_back, partials[reach_count], partials[:reach_count], reverse=True
    )
    query_back = rotary(query_total, cosine, -sine_table).astype(jnp.bfloat16)
    key_back = rotary(own_total[0].reshape(head_shape), cosine, -sine_table).astype(jnp.bfloat16)
    value_back = own_total[1].astype(jnp.bfloat16)
    grad_back = (
        lax.all_to_all(
            query_back.reshape(block_shape), ("grp", "rep"), split_axis=1, concat_axis=1, tiled=True
        ),
        lax.all_to_all(
            key_back.reshape(block_shape), ("grp", "rep"), split_axis=1, concat_axis=1, tiled=True
        ),
        lax.all_to_all(value_back, ("grp", "rep"), split_axis=1, concat_axis=1, tiled=True),
    )
    query_rows = take_rows(grad_back[0], unit_of).reshape(micro_count * row_count, model_width)
    key_rows = take_rows(grad_back[1], unit_of).reshape(micro_count * row_count, model_width)
    value_rows = take_rows(grad_back[2], unit_of).reshape(micro_count * row_count, model_width)
    query_grad = jnp.einsum("td,te->de", normed_in, query_rows, preferred_element_type=jnp.float32)
    key_grad = jnp.einsum("td,te->de", normed_in, key_rows, preferred_element_type=jnp.float32)
    value_grad = jnp.einsum("td,te->de", normed_in, value_rows, preferred_element_type=jnp.float32)
    grad_in = jnp.einsum("te,de->td", query_rows, gathered[1], preferred_element_type=jnp.float32)
    grad_in = grad_in + jnp.einsum(
        "te,de->td", key_rows, gathered[2], preferred_element_type=jnp.float32
    )
    grad_in = grad_in + jnp.einsum(
        "te,de->td", value_rows, gathered[3], preferred_element_type=jnp.float32
    )
    grad_norm_in, attn_gain_grad = norm_backward(inputs, gain_one, grad_in)
    token_grad = (grad_mixed + grad_norm_in).astype(jnp.bfloat16)
    attn_sums = reduce_attn(attn_gain_grad, query_grad, key_grad, value_grad, output_grad)
    return (
        block_out.reshape(block_shape),
        token_grad.reshape(block_shape),
        attn_sums[0],
        attn_sums[1],
        attn_sums[2],
        attn_sums[3],
        attn_sums[4],
        mlp_sums[0],
        mlp_sums[1],
        mlp_sums[2],
        mlp_sums[3],
    )


def contract(left_side, right_side, left_dim, right_dim, kind=jnp.float32):
    return lax.dot_general(
        left_side,
        right_side,
        (((left_dim,), (right_dim,)), ((), ())),
        preferred_element_type=jnp.float32,
    ).astype(kind)


def swap_halves(values):
    lane = lax.broadcasted_iota(jnp.int32, values.shape, 1)
    ahead = pltpu.roll(values, LANES - HD // 2, 1)
    behind = pltpu.roll(values, HD // 2, 1)
    return jnp.where(lane % HD < HD // 2, -ahead, behind)


def pair_angles(unit_at, cos_unit, sin_unit, cos_part, sin_part):
    unit_cos = cos_unit[pl.ds(unit_at, UNIT_PAIR), :][None]
    unit_sin = sin_unit[pl.ds(unit_at, UNIT_PAIR), :][None]
    part_cos = cos_part[...][:, None, :]
    part_sin = sin_part[...][:, None, :]
    cosine = unit_cos * part_cos - unit_sin * part_sin
    sine = unit_sin * part_cos + unit_cos * part_sin
    return cosine, sine


def key_offsets(block):
    row = lax.broadcasted_iota(jnp.int32, (block, block), 0)
    return (row % UNIT_BLOCK) * (block // UNIT_BLOCK) + row // UNIT_BLOCK


def query_offsets(block):
    column = lax.broadcasted_iota(jnp.int32, (block, block), 1)
    return (column % UNIT_BLOCK) * (block // UNIT_BLOCK) + column // UNIT_BLOCK


def attend_kernel(
    slot_ref,
    first_ref,
    plain_ref,
    cos_unit,
    sin_unit,
    cos_part,
    sin_part,
    low_ref,
    qkv_ref,
    att_ref,
    out_ref,
    log_ref,
    query_ref,
    key_ref,
    value_ref,
    query_t,
    value_t,
    key_at,
    causal_at,
):
    parts, units, _ = qkv_ref.shape
    block = parts * UNIT_BLOCK
    pairs = units // UNIT_PAIR
    key_at[...] = key_offsets(block)
    causal_at[...] = jnp.where(key_offsets(block) <= query_offsets(block), 0.0, masked_score)
    extra = value_t.shape[2] - HD

    def lay_out(pair, unused):
        unit_at = pl.multiple_of(pair * UNIT_PAIR, UNIT_PAIR)
        rows = jnp.stack(
            [qkv_ref[slot_ref[part], pl.ds(unit_at, UNIT_PAIR), :] for part in range(parts)]
        )
        cosine, sine = pair_angles(unit_at, cos_unit, sin_unit, cos_part, sin_part)
        flat = (parts * UNIT_PAIR, LANES)
        cosine = cosine.reshape(flat)
        sine = sine.reshape(flat)

        def rotated(values):
            values = values.astype(jnp.float32).reshape(flat)
            turned = values * cosine + swap_halves(values) * sine
            return turned.reshape(parts, UNIT_PAIR, LANES)

        query = rotated(rows[:, :, :LANES]) * (1.0 / math.sqrt(HD))
        key = rotated(rows[:, :, LANES : 2 * LANES])
        value = rows[:, :, 2 * LANES :].astype(jnp.float32)
        for half in range(UNIT_PAIR // UNIT_BLOCK):
            at = pair * (UNIT_PAIR // UNIT_BLOCK) + half
            cut = slice(half * UNIT_BLOCK, (half + 1) * UNIT_BLOCK)
            query_rows = query[:, cut].reshape(block, LANES)
            value_rows = value[:, cut].reshape(block, LANES)
            query_ref[at] = query_rows.astype(jnp.bfloat16)
            key_ref[at] = key[:, cut].reshape(block, LANES).astype(jnp.bfloat16)
            value_ref[at] = value_rows.astype(jnp.bfloat16)
            turned = jnp.transpose(query_rows)
            row = lax.broadcasted_iota(jnp.int32, turned.shape, 0)
            query_t[0, at] = jnp.where(row < HD, turned, 0.0).astype(jnp.bfloat16)
            query_t[1, at] = jnp.where(row < HD, 0.0, turned).astype(jnp.bfloat16)
            turned = jnp.transpose(value_rows).astype(jnp.bfloat16)
            for head in range(2):
                value_t[head, at, pl.ds(0, HD), :] = turned[head * HD : (head + 1) * HD]
                value_t[head, at, pl.ds(HD, extra), :] = jnp.ones((extra, block), jnp.bfloat16)
        return unused

    lax.fori_loop(0, pairs, lay_out, 0)

    def query_block(at):
        low = low_ref[at, 0:1, :]

        def step(key_block, carried, causal, bounded):
            new = []
            for head in range(2):
                top, total = carried[2 * head : 2 * head + 2]
                scores = jnp.dot(
                    key_ref[key_block], query_t[head, at], preferred_element_type=jnp.float32
                )
                if causal:
                    scores = scores + causal_at[...]
                if bounded:
                    scores = jnp.where(
                        key_at[...] >= low - key_block * block, scores, masked_score
                    )
                high = jnp.maximum(top, jnp.max(scores, axis=0, keepdims=True))
                weights = jnp.exp(scores - high).astype(jnp.bfloat16)
                total = total * jnp.exp(top - high) + jnp.dot(
                    value_t[head, key_block], weights, preferred_element_type=jnp.float32
                )
                new += [high, total]
            return tuple(new)

        empty = (
            jnp.full((1, block), masked_score, jnp.float32),
            jnp.zeros((HD + extra, block), jnp.float32),
        )
        carried = step(at, empty * 2, True, True)
        carried = lax.fori_loop(
            first_ref[at],
            plain_ref[at],
            lambda key_block, held: step(key_block, held, False, True),
            carried,
        )
        carried = lax.fori_loop(
            plain_ref[at],
            at,
            lambda key_block, held: step(key_block, held, False, False),
            carried,
        )
        heads = []
        for head in range(2):
            top, total = carried[2 * head : 2 * head + 2]
            heads.append(total[:HD] / total[HD : HD + 1])
            log_ref[at, head : head + 1, :] = top + jnp.log(total[HD : HD + 1])
        both = jnp.concatenate(heads, axis=0)
        out_ref[at] = both
        return jnp.transpose(both).reshape(parts, UNIT_BLOCK, LANES)

    def query_pair(pair, unused):
        halves = UNIT_PAIR // UNIT_BLOCK
        done = [query_block(pair * halves + half) for half in range(halves)]
        unit_at = pl.multiple_of(pair * UNIT_PAIR, UNIT_PAIR)
        att_ref[:, pl.ds(unit_at, UNIT_PAIR), :] = jnp.concatenate(done, axis=1).astype(
            jnp.bfloat16
        )
        return unused

    lax.fori_loop(0, pairs, query_pair, 0)


def attend_back_kernel(
    slot_ref,
    first_ref,
    plain_ref,
    cos_unit,
    sin_unit,
    cos_part,
    sin_part,
    low_ref,
    query_ref,
    key_ref,
    value_ref,
    out_ref,
    log_ref,
    grad_ref,
    back_ref,
    key_t,
    key_total,
    value_total,
    key_at,
    causal_at,
):
    parts, units, _ = grad_ref.shape
    block = parts * UNIT_BLOCK
    pairs = units // UNIT_PAIR
    halves = UNIT_PAIR // UNIT_BLOCK
    key_at[...] = key_offsets(block)
    causal_at[...] = jnp.where(key_offsets(block) <= query_offsets(block), 0.0, masked_score)

    def lay_out(at, unused):
        key_t[at] = jnp.transpose(key_ref[at].astype(jnp.float32)).astype(jnp.bfloat16)
        key_total[at] = jnp.zeros((block, LANES), jnp.float32)
        value_total[at] = jnp.zeros((block, LANES), jnp.float32)
        return unused

    lax.fori_loop(0, pairs * halves, lay_out, 0)

    def split_heads(values, axis):
        place = lax.broadcasted_iota(jnp.int32, values.shape, axis)
        zero = jnp.zeros_like(values)
        return [
            jnp.where(place < HD, values, zero).astype(jnp.bfloat16),
            jnp.where(place < HD, zero, values).astype(jnp.bfloat16),
        ]

    def query_block(at, grad_rows):
        low = low_ref[at, 0:1, :]
        query_rows = query_ref[at].astype(jnp.float32)
        query_heads = jnp.concatenate(split_heads(query_rows, 1), axis=0)
        grad_heads = jnp.concatenate(split_heads(grad_rows, 1), axis=0)
        query_t = split_heads(jnp.transpose(query_rows), 0)
        grad_turned = jnp.transpose(grad_rows)
        grad_t = split_heads(grad_turned, 0)
        product = grad_turned * out_ref[at]
        inner = [
            jnp.sum(product[head * HD : (head + 1) * HD], axis=0, keepdims=True)
            for head in range(2)
        ]
        logs = [log_ref[at, head : head + 1, :] for head in range(2)]

        def step(key_block, carried, causal, bounded):
            probs, slopes, new = [], [], []
            for head in range(2):
                scores = jnp.dot(
                    key_ref[key_block], query_t[head], preferred_element_type=jnp.float32
                )
                if causal:
                    scores = scores + causal_at[...]
                if bounded:
                    scores = jnp.where(
                        key_at[...] >= low - key_block * block, scores, masked_score
                    )
                soft = jnp.exp(scores - logs[head])
                grad_probs = jnp.dot(
                    value_ref[key_block], grad_t[head], preferred_element_type=jnp.float32
                )
                slope = (soft * (grad_probs - inner[head])).astype(jnp.bfloat16)
                probs.append(soft.astype(jnp.bfloat16))
                slopes.append(slope)
                new.append(
                    carried[head]
                    + jnp.dot(
                        key_t[key_block, pl.ds(head * HD, HD), :],
                        slope,
                        preferred_element_type=jnp.float32,
                    )
                )
            value_total[key_block] += jnp.dot(
                jnp.concatenate(probs, axis=1), grad_heads, preferred_element_type=jnp.float32
            )
            key_total[key_block] += jnp.dot(
                jnp.concatenate(slopes, axis=1), query_heads, preferred_element_type=jnp.float32
            )
            return tuple(new)

        carried = step(at, (jnp.zeros((HD, block), jnp.float32),) * 2, True, True)
        carried = lax.fori_loop(
            first_ref[at],
            plain_ref[at],
            lambda key_block, held: step(key_block, held, False, True),
            carried,
        )
        carried = lax.fori_loop(
            plain_ref[at],
            at,
            lambda key_block, held: step(key_block, held, False, False),
            carried,
        )
        return jnp.transpose(jnp.concatenate(carried, axis=0)) * (1.0 / math.sqrt(HD))

    def turn_back(rows, cosine, sine):
        flat = (parts * UNIT_PAIR, LANES)
        rows = jnp.concatenate(
            [one.reshape(parts, UNIT_BLOCK, LANES) for one in rows], axis=1
        ).reshape(flat)
        turned = rows * cosine.reshape(flat) - swap_halves(rows) * sine.reshape(flat)
        return turned.reshape(parts, UNIT_PAIR, LANES).astype(jnp.bfloat16)

    def put(values, unit_at, lane_at):
        for part in range(parts):
            back_ref[slot_ref[part], pl.ds(unit_at, UNIT_PAIR), pl.ds(lane_at, LANES)] = values[part]

    def query_pair(pair, unused):
        unit_at = pl.multiple_of(pair * UNIT_PAIR, UNIT_PAIR)
        grads = grad_ref[:, pl.ds(unit_at, UNIT_PAIR), :].astype(jnp.float32)
        done = [
            query_block(
                pair * halves + half,
                grads[:, half * UNIT_BLOCK : (half + 1) * UNIT_BLOCK].reshape(block, LANES),
            )
            for half in range(halves)
        ]
        cosine, sine = pair_angles(unit_at, cos_unit, sin_unit, cos_part, sin_part)
        put(turn_back(done, cosine, sine), unit_at, 0)
        return unused

    lax.fori_loop(0, pairs, query_pair, 0)

    def key_pair(pair, unused):
        unit_at = pl.multiple_of(pair * UNIT_PAIR, UNIT_PAIR)
        cosine, sine = pair_angles(unit_at, cos_unit, sin_unit, cos_part, sin_part)
        ids = [pair * halves + half for half in range(halves)]
        put(turn_back([key_total[at] for at in ids], cosine, sine), unit_at, LANES)
        values = jnp.concatenate(
            [value_total[at].reshape(parts, UNIT_BLOCK, LANES) for at in ids], axis=1
        ).astype(jnp.bfloat16)
        put(values, unit_at, 2 * LANES)
        return unused

    lax.fori_loop(0, pairs, key_pair, 0)


def attend(tables, qkv):
    parts, units, _ = qkv.shape
    block = parts * UNIT_BLOCK
    blocks = units // UNIT_BLOCK
    smem = pl.BlockSpec(memory_space=pltpu.SMEM)
    vmem = pl.BlockSpec(memory_space=pltpu.VMEM)
    rows = jax.ShapeDtypeStruct((blocks, block, LANES), jnp.bfloat16)
    extra = UNIT_PAIR
    return pl.pallas_call(
        attend_kernel,
        out_shape=(
            jax.ShapeDtypeStruct((parts, units, LANES), jnp.bfloat16),
            jax.ShapeDtypeStruct((blocks, LANES, block), jnp.float32),
            jax.ShapeDtypeStruct((blocks, 8, block), jnp.float32),
            rows,
            rows,
            rows,
        ),
        in_specs=[smem] * 3 + [vmem] * 6,
        out_specs=(vmem,) * 6,
        scratch_shapes=[
            pltpu.VMEM((2, blocks, LANES, block), jnp.bfloat16),
            pltpu.VMEM((2, blocks, HD + extra, block), jnp.bfloat16),
            pltpu.VMEM((block, block), jnp.int32),
            pltpu.VMEM((block, block), jnp.float32),
        ],
        compiler_params=pltpu.CompilerParams(vmem_limit_bytes=KERNEL_VMEM),
        cost_estimate=pl.CostEstimate(
            flops=20 * 10**9, bytes_accessed=16 << 20, transcendentals=20 * 10**6
        ),
        name="attend",
    )(*tables, qkv)


def attend_back(tables, query, key, value, out, log, grad):
    parts, units, _ = grad.shape
    block = parts * UNIT_BLOCK
    blocks = units // UNIT_BLOCK
    smem = pl.BlockSpec(memory_space=pltpu.SMEM)
    vmem = pl.BlockSpec(memory_space=pltpu.VMEM)
    return pl.pallas_call(
        attend_back_kernel,
        out_shape=jax.ShapeDtypeStruct((parts, units, 3 * LANES), jnp.bfloat16),
        in_specs=[smem] * 3 + [vmem] * 11,
        out_specs=vmem,
        scratch_shapes=[
            pltpu.VMEM((blocks, LANES, block), jnp.bfloat16),
            pltpu.VMEM((blocks, block, LANES), jnp.float32),
            pltpu.VMEM((blocks, block, LANES), jnp.float32),
            pltpu.VMEM((block, block), jnp.int32),
            pltpu.VMEM((block, block), jnp.float32),
        ],
        compiler_params=pltpu.CompilerParams(vmem_limit_bytes=KERNEL_VMEM),
        cost_estimate=pl.CostEstimate(
            flops=50 * 10**9, bytes_accessed=16 << 20, transcendentals=20 * 10**6
        ),
        name="attend_back",
    )(*tables, query, key, value, out, log, grad)


def attention_tables(lengths, grp_here, rep_here, units):
    reps = lax.axis_size("rep")
    parts = lax.axis_size("grp") * reps
    block = parts * UNIT_BLOCK
    blocks = units // UNIT_BLOCK
    own = lax.dynamic_index_in_dim(lengths, grp_here, 0, keepdims=False)
    ends = jnp.cumsum(own)
    unit_ids = jnp.arange(units, dtype=jnp.int32)
    begin = jnp.max(
        jnp.where(ends[None, :] <= unit_ids[:, None], ends[None, :], 0), axis=1
    ).astype(jnp.int32)
    part_ids = jnp.arange(parts, dtype=jnp.int32)
    offset = part_ids % reps ^ rep_here
    slot = offset * lax.axis_size("grp") + (part_ids // reps ^ grp_here)
    frequency = jnp.power(
        rope_base, -2.0 * (jnp.arange(LANES) % (HD // 2)).astype(jnp.float32) / HD
    )
    unit_angle = ((unit_ids - begin) * parts).astype(jnp.float32)[:, None] * frequency[None, :]
    part_angle = part_ids.astype(jnp.float32)[:, None] * frequency[None, :]
    low = jnp.maximum(
        (begin * parts)[:, None], unit_ids[:, None] * parts + part_ids[None, :] - (WINDOW - 1)
    )
    low = low.reshape(blocks, UNIT_BLOCK, parts)
    least = jnp.min(low, axis=(1, 2))
    most = jnp.max(low, axis=(1, 2))
    block_ids = jnp.arange(blocks, dtype=jnp.int32)
    first = jnp.maximum(least, 0) // block
    plain = jnp.clip((most + block - 1) // block, first, block_ids)
    low_rows = jnp.broadcast_to(
        low.transpose(0, 2, 1).reshape(blocks, 1, block), (blocks, 8, block)
    )
    return (
        slot,
        first,
        plain,
        jnp.cos(unit_angle),
        jnp.sin(unit_angle),
        jnp.cos(part_angle),
        jnp.sin(part_angle),
        low_rows,
    )


def swap(value, grp_step, rep_step):
    groups, reps = lax.axis_size("grp"), lax.axis_size("rep")
    pairs = [
        (grp * reps + rep, (grp ^ grp_step) * reps + (rep ^ rep_step))
        for grp in range(groups)
        for rep in range(reps)
    ]
    return lax.ppermute(value, BOTH, pairs)


def ordered(flag, own, other, axis=0):
    return jnp.where(
        flag == 0,
        jnp.concatenate([own, other], axis=axis),
        jnp.concatenate([other, own], axis=axis),
    )


def pick(value, index, axis):
    return lax.dynamic_index_in_dim(value, index, axis, keepdims=False)


def halve(value, axis, bit, grp_step, rep_step):
    kept = pick(value, bit, axis)
    sent = pick(value, 1 - bit, axis).astype(jnp.bfloat16)
    arrived = swap(sent, grp_step, rep_step)
    return kept.astype(jnp.float32) + arrived.astype(jnp.float32)


def narrow(value):
    return value.astype(jnp.bfloat16)


MESH_IDS = pl.DeviceIdType.MESH


def flipped(index, step):
    return index + step - 2 * step * ((index // step) % 2)


def lowest(offset):
    return offset & -offset


def arrivals(reps):
    far = [step for step in range(4, reps, 4)]
    far.sort(key=lambda step: (bin(step).count("1"), step))
    order = [(2, 0), (0, 1)]
    for at, step in enumerate(far):
        if bin(step).count("1") == 1:
            order.append((step, 0))
    order.append((2, 1))
    for step in far:
        if bin(step).count("1") == 1:
            order.append((step, 1))
    single = [step for step in far if bin(step).count("1") == 1]
    double = [step for step in far if bin(step).count("1") > 1]
    rest = []
    for step in single[:1]:
        rest.append((step + 2, 0))
    for step in double:
        rest.append((step, 0))
    for step in single[:1]:
        rest.append((step + 2, 1))
    for step in double:
        rest.append((step, 1))
    for step in single[1:] + double:
        rest += [(step + 2, 0), (step + 2, 1)]
    return order + rest


def link_of(offset, part, reps):
    if reps > 8 and offset == reps - 2 and part == 1:
        return 4
    return lowest(offset)


def gather_kernel(
    tokens_ref,
    gain_ref,
    w_query,
    w_key,
    w_value,
    w_gate,
    w_up,
    normed_out,
    qkv_ref,
    weight_ref,
    in_ref,
    raw,
    normed,
    gains,
    weight_sem,
    out_sem,
    send_sem,
    recv_sem,
    side_send,
    side_recv,
    stripe_sem,
    stripe_send,
    stripe_recv,
):
    here, there = lax.axis_index("grp"), lax.axis_index("rep")
    core = there % 2
    reps = raw.shape[0]
    slots = normed.shape[0]
    row_count, width = raw.shape[2:]
    steps = [1 << place for place in range(reps.bit_length() - 1)]
    across = (1 - here, there)

    def neighbour(step):
        return (here, flipped(there, step))

    barrier = pltpu.get_barrier_semaphore()
    for target in [across] + [neighbour(step) for step in steps]:
        pl.semaphore_signal(barrier, inc=1, device_id=target, device_id_type=MESH_IDS)
    local = []
    for at, weight in enumerate((w_query, w_key, w_value)):
        local.append(
            pltpu.make_async_copy(
                weight.at[:, pl.ds(pl.multiple_of(there * LANES, LANES), LANES)],
                weight_ref.at[here, :, pl.ds(at * LANES, LANES)],
                weight_sem.at[at],
            )
        )
        local[-1].start()
    raw[0, 0] = tokens_ref[here]
    gains[here] = gain_ref[...]
    pl.semaphore_wait(barrier, len(steps) + 1)

    def side(at, source, target_ref):
        return pltpu.make_async_remote_copy(
            src_ref=source,
            dst_ref=target_ref,
            send_sem=side_send.at[at],
            recv_sem=side_recv.at[at],
            device_id=across,
            device_id_type=MESH_IDS,
        )

    def rows_copy(offset, part):
        if offset == 0:
            return pltpu.make_async_remote_copy(
                src_ref=tokens_ref.at[1 - here],
                dst_ref=raw.at[0, 1],
                send_sem=send_sem.at[1],
                recv_sem=recv_sem.at[1],
                device_id=across,
                device_id_type=MESH_IDS,
            )
        step = link_of(offset, part, reps)
        return pltpu.make_async_remote_copy(
            src_ref=raw.at[offset - step, part],
            dst_ref=raw.at[offset, part],
            send_sem=send_sem.at[2 * offset + part],
            recv_sem=recv_sem.at[2 * offset + part],
            device_id=neighbour(step),
            device_id_type=MESH_IDS,
        )

    order = arrivals(reps)
    copies = {
        (offset, part): rows_copy(offset, part)
        for offset in range(reps)
        for part in (0, 1)
        if offset or part
    }

    def pass_on(offset, part):
        for later, part_of in order:
            if later and part_of == part and later - link_of(later, part, reps) == offset:
                copies[later, part].start()
        copies[offset + 1, part].start()

    gain_copy = side(0, gains.at[here], gains.at[here])
    gain_copy.start()
    copies[0, 1].start()
    pass_on(0, 0)
    for one in local:
        one.wait()
    weight_copy = side(1, weight_ref.at[here], weight_ref.at[here])
    weight_copy.start()

    stripes = reps // 2
    own_width = in_ref.shape[2] // 2
    stripe_copies, stripe_loads = [], []
    for kind, weight in enumerate((w_gate, w_up)):
        for at in range(stripes):
            target_ref = in_ref.at[here, :, pl.ds(kind * own_width + at * LANES, LANES)]
            number = kind * stripes + at

            def columns_of(grp):
                first = (grp * stripes + at) * 2 * LANES + core * LANES
                return weight.at[:, pl.ds(pl.multiple_of(first, LANES), LANES)]

            stripe_loads.append(
                pltpu.make_async_copy(columns_of(here), target_ref, stripe_sem.at[number])
            )
            stripe_copies.append(
                pltpu.make_async_remote_copy(
                    src_ref=columns_of(1 - here),
                    dst_ref=target_ref,
                    send_sem=stripe_send.at[number],
                    recv_sem=stripe_recv.at[number],
                    device_id=across,
                    device_id_type=MESH_IDS,
                )
            )
    for one in stripe_copies + stripe_loads:
        one.start()

    written = {}
    used = [None] * slots
    tile = 32

    def project(count, offset):
        slot = count % slots
        if used[slot] is not None:
            written[used[slot]].wait()
        used[slot] = offset
        gain = jnp.concatenate([gains[0, 0:1], gains[1, 0:1]], axis=1).astype(jnp.float32)
        for part in range(2):

            def norm_rows(at, unused):
                cut = pl.ds(pl.multiple_of(at * tile, tile), tile)
                values = raw[offset, part, cut, :].astype(jnp.float32)
                scaled = values * rms_scale(values) * gain
                normed[slot, pl.ds(pl.multiple_of(part * row_count + at * tile, tile), tile), :] = (
                    scaled.astype(jnp.bfloat16)
                )
                return unused

            lax.fori_loop(0, row_count // tile, norm_rows, 0)
        written[offset] = pltpu.make_async_copy(
            normed.at[slot], normed_out.at[offset], out_sem.at[offset]
        )
        written[offset].start()
        half = width // 2
        product = jnp.dot(
            normed[slot, :, :half], weight_ref[0], preferred_element_type=jnp.float32
        ) + jnp.dot(normed[slot, :, half:], weight_ref[1], preferred_element_type=jnp.float32)
        qkv_ref[pl.ds(2 * offset, 2)] = product.astype(jnp.bfloat16).reshape(
            2, row_count, 3 * LANES
        )

    ready = []
    arrived = {(0, 0)}
    started = False
    count = 0
    for offset, part in order:
        copies[offset, part].wait_recv()
        pass_on(offset, part)
        arrived.add((offset, part))
        if (offset, 1 - part) in arrived:
            ready.append(offset)
        if not started and len(ready) >= 1:
            gain_copy.wait_recv()
            weight_copy.wait_recv()
            started = True
        if started and len(ready) >= 2:
            base = ready.pop(0)
            project(count, base)
            copies[base + 1, 0].wait_recv()
            copies[base + 1, 1].wait_recv()
            project(count + 1, base + 1)
            count += 2
    for base in ready:
        project(count, base)
        copies[base + 1, 0].wait_recv()
        copies[base + 1, 1].wait_recv()
        project(count + 1, base + 1)
        count += 2
    for offset in used:
        written[offset].wait()
    for one in copies.values():
        one.wait_send()
    gain_copy.wait_send()
    weight_copy.wait_send()
    for one in stripe_copies + stripe_loads:
        one.wait()


def gather_heads(tokens, gain, w_query, w_key, w_value, w_gate, w_up):
    reps = lax.axis_size("rep")
    _, row_count, width = tokens.shape
    half = width // 2
    gain_rows = jnp.broadcast_to(gain[None], (16, half))
    vmem = pl.BlockSpec(memory_space=pltpu.VMEM)
    anywhere = pl.BlockSpec(memory_space=pl.ANY)
    return pl.pallas_call(
        gather_kernel,
        out_shape=(
            jax.ShapeDtypeStruct((reps, 2 * row_count, width), jnp.bfloat16),
            jax.ShapeDtypeStruct((2 * reps, row_count, 3 * LANES), jnp.bfloat16),
            jax.ShapeDtypeStruct((2, half, 3 * LANES), jnp.bfloat16),
            jax.ShapeDtypeStruct((2, half, reps * LANES), jnp.bfloat16),
        ),
        in_specs=[vmem, vmem] + [anywhere] * 5,
        out_specs=(anywhere, vmem, vmem, anywhere),
        scratch_shapes=[
            pltpu.VMEM((reps, 2, row_count, width), jnp.bfloat16),
            pltpu.VMEM((4, 2 * row_count, width), jnp.bfloat16),
            pltpu.VMEM((2, 16, half), jnp.bfloat16),
            pltpu.SemaphoreType.DMA((3,)),
            pltpu.SemaphoreType.DMA((reps,)),
            pltpu.SemaphoreType.DMA((2 * reps,)),
            pltpu.SemaphoreType.DMA((2 * reps,)),
            pltpu.SemaphoreType.DMA((2,)),
            pltpu.SemaphoreType.DMA((2,)),
            pltpu.SemaphoreType.DMA((reps,)),
            pltpu.SemaphoreType.DMA((reps,)),
            pltpu.SemaphoreType.DMA((reps,)),
        ],
        compiler_params=pltpu.CompilerParams(
            vmem_limit_bytes=KERNEL_VMEM, collective_id=0, has_side_effects=True
        ),
        cost_estimate=pl.CostEstimate(
            flops=8 * 10**9, bytes_accessed=250 << 20, transcendentals=0
        ),
        name="gather_heads",
    )(tokens, gain_rows, w_query, w_key, w_value, w_gate, w_up)


def scatter_kernel(
    back_ref,
    weight_ref,
    normed_ref,
    grad_ref,
    pieces_ref,
    away,
    landed,
    normed,
    back_t,
    weight_t,
    weights_total,
    half_out,
    half_in,
    piece_out,
    normed_sem,
    send_sem,
    recv_sem,
    side_send,
    side_recv,
    piece_send,
    piece_recv,
):
    here, there = lax.axis_index("grp"), lax.axis_index("rep")
    reps, rows, columns = back_ref.shape
    row_count = rows // 2
    width = grad_ref.shape[2]
    half = width // 2
    own_rows = half // reps
    steps = [1 << place for place in range(reps.bit_length() - 1)]
    across = (1 - here, there)

    def other(offset):
        index = there
        for step in steps:
            if offset & step:
                index = flipped(index, step)
        return (here, index)

    barrier = pltpu.get_barrier_semaphore()
    for target in [across] + [other(offset) for offset in range(1, reps)]:
        pl.semaphore_signal(barrier, inc=1, device_id=target, device_id_type=MESH_IDS)

    slots = normed.shape[0]
    fetch = [
        pltpu.make_async_copy(normed_ref.at[offset], normed.at[offset % slots], normed_sem.at[offset])
        for offset in range(reps)
    ]
    for offset in range(slots):
        fetch[offset].start()

    for at in range(2):
        turned = jnp.transpose(weight_ref[at].astype(jnp.float32)).astype(jnp.bfloat16)
        weight_t[:, pl.ds(at * half, half)] = turned
    pl.semaphore_wait(barrier, reps)

    def rows_copy(offset, part):
        if offset == 0:
            return pltpu.make_async_remote_copy(
                src_ref=away.at[0, 1],
                dst_ref=landed.at[0, 1],
                send_sem=send_sem.at[1],
                recv_sem=recv_sem.at[1],
                device_id=across,
                device_id_type=MESH_IDS,
            )
        return pltpu.make_async_remote_copy(
            src_ref=away.at[offset, part],
            dst_ref=landed.at[offset, part],
            send_sem=send_sem.at[2 * offset + part],
            recv_sem=recv_sem.at[2 * offset + part],
            device_id=other(link_of(offset, part, reps)),
            device_id_type=MESH_IDS,
        )

    copies = {
        (offset, part): rows_copy(offset, part)
        for offset in range(reps)
        for part in (0, 1)
        if offset or part
    }
    tile = 32

    def product(offset, part):
        return jnp.dot(
            back_ref[offset, pl.ds(part * row_count, row_count), :],
            weight_t[...],
            preferred_element_type=jnp.float32,
        )

    def send(offset, part):
        sources = [
            later
            for later in range(1, reps)
            if later - link_of(later, part, reps) == offset
        ]
        for later in sources:
            copies[later, part].wait_recv()
        total = product(offset, part)
        for later in sources:
            total = total + landed[later, part].astype(jnp.float32)
        if offset == 0 and part == 0:
            grad_ref[here] = total
        else:
            away[offset, part] = total.astype(jnp.bfloat16)
            copies[offset, part].start()

    def weight_step(offset):
        fetch[offset].wait()
        back_t[...] = jnp.transpose(back_ref[offset].astype(jnp.float32)).astype(jnp.bfloat16)

        def columns_at(at, unused):
            cut = pl.ds(pl.multiple_of(at * 512, 512), 512)
            term = jnp.dot(
                back_t[...], normed[offset % slots, :, cut], preferred_element_type=jnp.float32
            )
            if offset == 0:
                weights_total[:, cut] = term
            else:
                weights_total[:, cut] += term
            return unused

        lax.fori_loop(0, width // 512, columns_at, 0)
        if offset + slots < reps:
            fetch[offset + slots].start()

    half_copy = pltpu.make_async_remote_copy(
        src_ref=half_out,
        dst_ref=half_in,
        send_sem=side_send,
        recv_sem=side_recv,
        device_id=across,
        device_id_type=MESH_IDS,
    )
    piece_copies = [
        pltpu.make_async_remote_copy(
            src_ref=piece_out.at[other(offset)[1]],
            dst_ref=pieces_ref.at[there],
            send_sem=piece_send.at[offset],
            recv_sem=piece_recv.at[offset],
            device_id=other(offset),
            device_id_type=MESH_IDS,
        )
        for offset in range(1, reps)
    ]

    def cross_weights():
        cut = pl.ds(pl.multiple_of((1 - here) * half, half), half)
        half_out[...] = weights_total[:, cut].astype(jnp.bfloat16)
        half_copy.start()

    def share_weights():
        half_copy.wait_recv()
        cut = pl.ds(pl.multiple_of(here * half, half), half)
        total = jnp.transpose(weights_total[:, cut] + half_in[...].astype(jnp.float32))
        piece_out[...] = total.astype(jnp.bfloat16).reshape(reps, own_rows, columns)
        pieces_ref[there] = piece_out[there]
        for one in piece_copies:
            one.start()

    far = [step for step in range(reps - 4, 0, -4)]
    todo = []
    for base in far + [0]:
        todo.append((base + 3, 1))
        todo.append((base + 3, 0))
        todo.append((base + 1, 1))
        todo.append((base + 1, 0))
    first = todo[:2]
    for offset, part in first:
        send(offset, part)
    for offset, part in todo[2:6]:
        send(offset, part)
    send(reps - 2, 1)
    send(reps - 2, 0)
    for offset, part in todo[6:]:
        send(offset, part)
    weights = list(range(reps))

    def weight_steps(count):
        for _ in range(min(count, len(weights))):
            weight_step(weights.pop(0))

    last = []
    order = []
    for base in sorted(far, key=lambda step: (-bin(step).count("1"), -step)):
        if base != far[0]:
            order.append((base + 2, 1))
            order.append((base + 2, 0))
    order += [(2, 1), (2, 0)]
    sums = sorted(far, key=lambda step: (-bin(step).count("1"), -step))
    for base in sums:
        last += [(base, 1), (base, 0)]
    if reps == 16:
        plan = [
            (10, 1), (10, 0), 4, (12, 1), (12, 0), 4, (6, 1), (6, 0), 2, (8, 1), 2, (8, 0),
            (2, 1), (2, 0), 4, "cross", (4, 1), (4, 0), "share", (0, 1), (0, 0),
        ]
    else:
        plan = order + last + [reps, "cross", "share", (0, 1), (0, 0)]
    for item in plan:
        if item == "cross":
            weight_steps(reps)
            cross_weights()
        elif item == "share":
            share_weights()
        elif isinstance(item, int):
            weight_steps(item)
        else:
            send(*item)
    copies[0, 1].wait_recv()
    grad_ref[1 - here] = landed[0, 1].astype(jnp.float32)
    for one in piece_copies:
        one.wait()
    half_copy.wait_send()
    for one in copies.values():
        one.wait_send()


def scatter_heads(back, weights, normed):
    reps, rows, columns = back.shape
    width = normed.shape[2]
    row_count = rows // 2
    half = width // 2
    vmem = pl.BlockSpec(memory_space=pltpu.VMEM)
    anywhere = pl.BlockSpec(memory_space=pl.ANY)
    return pl.pallas_call(
        scatter_kernel,
        out_shape=(
            jax.ShapeDtypeStruct((2, row_count, width), jnp.float32),
            jax.ShapeDtypeStruct((reps, half // reps, columns), jnp.bfloat16),
        ),
        in_specs=[vmem, vmem, anywhere],
        out_specs=(vmem, vmem),
        scratch_shapes=[
            pltpu.VMEM((reps, 2, row_count, width), jnp.bfloat16),
            pltpu.VMEM((reps, 2, row_count, width), jnp.bfloat16),
            pltpu.VMEM((4, rows, width), jnp.bfloat16),
            pltpu.VMEM((columns, rows), jnp.bfloat16),
            pltpu.VMEM((columns, width), jnp.bfloat16),
            pltpu.VMEM((columns, width), jnp.float32),
            pltpu.VMEM((columns, half), jnp.bfloat16),
            pltpu.VMEM((columns, half), jnp.bfloat16),
            pltpu.VMEM((reps, half // reps, columns), jnp.bfloat16),
            pltpu.SemaphoreType.DMA((reps,)),
            pltpu.SemaphoreType.DMA((2 * reps,)),
            pltpu.SemaphoreType.DMA((2 * reps,)),
            pltpu.SemaphoreType.DMA,
            pltpu.SemaphoreType.DMA,
            pltpu.SemaphoreType.DMA((reps,)),
            pltpu.SemaphoreType.DMA((reps,)),
        ],
        compiler_params=pltpu.CompilerParams(
            vmem_limit_bytes=KERNEL_VMEM, collective_id=1, has_side_effects=True
        ),
        cost_estimate=pl.CostEstimate(
            flops=14 * 10**9, bytes_accessed=250 << 20, transcendentals=0
        ),
        name="scatter_heads",
    )(back, weights, normed)


def mlp_kernel(
    returned_ref,
    tokens_ref,
    gain_ref,
    out_ref,
    output_own,
    output_other,
    in_ref,
    down_weight,
    mixed_ref,
    mid_ref,
    hidden_ref,
    slope_ref,
    down_ref,
    grad_ref,
    branch_ref,
    att_ref,
    attended,
    w_output,
    w_in,
    w_out,
    near_away,
    near_landed,
    far_away,
    far_landed,
    down_away,
    down_landed,
    load_sem,
    stripe_sem,
    send_sem,
    recv_sem,
):
    here, there = lax.axis_index("grp"), lax.axis_index("rep")
    core = there % 2
    across = (1 - here, there)
    sibling = (here, flipped(there, 1))
    groups, heads, row_count, _ = returned_ref.shape
    rows, width = tokens_ref.shape
    half = width // 2
    own_width = w_out.shape[0]
    stripes = own_width // LANES

    loads = [
        pltpu.make_async_copy(output_own, w_output.at[here], load_sem.at[0]),
        pltpu.make_async_copy(output_other, w_output.at[1 - here], load_sem.at[1]),
        pltpu.make_async_copy(in_ref, w_in, load_sem.at[2]),
    ]
    for at in range(stripes):
        loads.append(
            pltpu.make_async_copy(
                down_weight.at[pl.ds(pl.multiple_of((2 * at + core) * LANES, LANES), LANES)],
                w_out.at[pl.ds(at * LANES, LANES)],
                stripe_sem.at[at],
            )
        )
    for one in loads:
        one.start()
    barrier = pltpu.get_barrier_semaphore()
    for target in (across, sibling):
        pl.semaphore_signal(barrier, inc=1, device_id=target, device_id_type=MESH_IDS)
    pl.semaphore_wait(barrier, 2)

    def copy(at, source, target_ref, target):
        return pltpu.make_async_remote_copy(
            src_ref=source,
            dst_ref=target_ref,
            send_sem=send_sem.at[at],
            recv_sem=recv_sem.at[at],
            device_id=target,
            device_id_type=MESH_IDS,
        )

    mid_near = copy(0, mid_ref.at[0], mid_ref.at[1], sibling)
    mid_far = copy(1, mid_ref.at[0], mid_ref.at[2], across)
    mid_on = copy(2, mid_ref.at[2], mid_ref.at[3], sibling)
    grad_near = [copy(3 + at, near_away.at[at], near_landed.at[at], sibling) for at in range(2)]
    grad_far = copy(5, far_away, far_landed, across)
    down_near = [copy(6 + at, down_away.at[at], down_landed.at[at], sibling) for at in range(2)]

    for group in range(groups):
        for head in range(heads):
            attended[
                group * row_count : (group + 1) * row_count, head * LANES : (head + 1) * LANES
            ] = returned_ref[group, head]
    loads[0].wait()
    loads[1].wait()
    wide = 512

    def mix(at, unused):
        cut = pl.ds(pl.multiple_of(at * wide, wide), wide)
        mixed_ref[:, cut] = (
            tokens_ref[:, cut].astype(jnp.float32)
            + jnp.dot(attended[:, :half], w_output[0, :, cut], preferred_element_type=jnp.float32)
            + jnp.dot(attended[:, half:], w_output[1, :, cut], preferred_element_type=jnp.float32)
        )
        return unused

    lax.fori_loop(0, width // wide, mix, 0)
    tile = 32

    def norm_rows(at, unused):
        cut = pl.ds(pl.multiple_of(at * tile, tile), tile)
        values = mixed_ref[cut, :]
        mid_ref[0, cut, :] = (values * rms_scale(values) * gain_ref[0:1, :]).astype(jnp.bfloat16)
        return unused

    lax.fori_loop(0, rows // tile, norm_rows, 0)
    mid_far.start()
    mid_near.start()
    for one in loads[2:]:
        one.wait()
    narrow_tile = 256

    def forward(slot):
        def columns(at, unused):
            cut = pl.ds(pl.multiple_of(at * narrow_tile, narrow_tile), narrow_tile)
            up_cut = pl.ds(pl.multiple_of(own_width + at * narrow_tile, narrow_tile), narrow_tile)

            def project(cols):
                return jnp.dot(
                    mid_ref[slot, :, :half], w_in[0, :, cols], preferred_element_type=jnp.float32
                ) + jnp.dot(
                    mid_ref[slot, :, half:], w_in[1, :, cols], preferred_element_type=jnp.float32
                )

            gate_pre, up_pre = project(cut), project(up_cut)
            grad_hidden = contract(out_ref[slot], w_out[cut, :], 1, 1)
            gate_sig = jax.nn.sigmoid(gate_pre)
            gate_silu = gate_pre * gate_sig
            hidden_ref[slot, :, cut] = (gate_silu * up_pre).astype(jnp.bfloat16)
            slope_ref[slot, :, cut] = (
                grad_hidden * up_pre * gate_sig * (1.0 + gate_pre * (1.0 - gate_sig))
            ).astype(jnp.bfloat16)
            slope_ref[slot, :, up_cut] = (grad_hidden * gate_silu).astype(jnp.bfloat16)
            return unused

        lax.fori_loop(0, own_width // narrow_tile, columns, 0)

    def backward(slot, finish):
        for at in range(2):

            def columns(step, unused):
                cut = pl.ds(pl.multiple_of(step * wide, wide), wide)
                whole = pl.ds(pl.multiple_of(at * half + step * wide, wide), wide)
                finish(whole, contract(slope_ref[slot], w_in[at, cut, :], 1, 1))
                return unused

            lax.fori_loop(0, half // wide, columns, 0)

    def down(slot, finish):
        def columns(step, unused):
            cut = pl.ds(pl.multiple_of(step * wide, wide), wide)
            finish(
                cut, jnp.dot(hidden_ref[slot], w_out[:, cut], preferred_element_type=jnp.float32)
            )
            return unused

        lax.fori_loop(0, width // wide, columns, 0)

    def into(target, at):
        def finish(cut, values):
            target[at, :, cut] = values.astype(jnp.bfloat16)

        return finish

    forward(0)
    mid_near.wait_recv()
    forward(1)
    backward(1, into(near_away, 0))
    grad_near[0].start()

    def keep(cut, values):
        grad_ref[:, cut] = values

    backward(0, keep)
    mid_far.wait_recv()
    mid_on.start()
    forward(2)
    mid_on.wait_recv()
    forward(3)
    backward(3, into(near_away, 1))
    grad_near[1].start()
    grad_near[1].wait_recv()

    def add_near(cut, values):
        far_away[:, cut] = (values + near_landed[1, :, cut].astype(jnp.float32)).astype(
            jnp.bfloat16
        )

    backward(2, add_near)
    grad_far.start()
    for at in range(2):
        down(2 * at + 1, into(down_away, at))
        down_near[at].start()
    for at in range(2):
        down_near[at].wait_recv()

        def add_down(cut, values):
            down_ref[at, :, cut] = (values + down_landed[at, :, cut].astype(jnp.float32)).astype(
                jnp.bfloat16
            )

        down(2 * at, add_down)
    grad_near[0].wait_recv()
    grad_far.wait_recv()

    def norm_back(at, unused):
        cut = pl.ds(pl.multiple_of(at * tile, tile), tile)
        grad_mid = (
            grad_ref[cut, :]
            + near_landed[0, cut, :].astype(jnp.float32)
            + far_landed[cut, :].astype(jnp.float32)
        )
        values = mixed_ref[cut, :]
        inverse = rms_scale(values)
        normed = values * inverse
        weighted = grad_mid * gain_ref[0:1, :]
        grad = out_ref[0, cut, :].astype(jnp.float32) + inverse * (
            weighted - normed * jnp.mean(weighted * normed, axis=-1, keepdims=True)
        )
        grad_ref[cut, :] = grad
        branch_ref[cut, :] = grad.astype(jnp.bfloat16)
        return unused

    lax.fori_loop(0, rows // tile, norm_back, 0)
    for head in range(0, heads, 4):
        at = head * LANES // half
        start = head * LANES - at * half
        values = contract(
            branch_ref[...], w_output[at, pl.ds(start, 4 * LANES), :], 1, 1, jnp.bfloat16
        )
        for group in range(groups):
            for step in range(4):
                att_ref[group, head + step] = values[
                    group * row_count : (group + 1) * row_count, step * LANES : (step + 1) * LANES
                ]
    for one in [mid_near, mid_far, mid_on, grad_far] + grad_near + down_near:
        one.wait_send()


def mlp(returned, tokens, gain, out_quad, output_own, output_other, w_in, w_down):
    groups, heads, row_count, _ = returned.shape
    rows, width = tokens.shape
    half = width // 2
    hidden_width = w_in.shape[2]
    own_width = hidden_width // 2
    vmem = pl.BlockSpec(memory_space=pltpu.VMEM)
    anywhere = pl.BlockSpec(memory_space=pl.ANY)
    low, full = jnp.bfloat16, jnp.float32
    return pl.pallas_call(
        mlp_kernel,
        out_shape=(
            jax.ShapeDtypeStruct((rows, width), full),
            jax.ShapeDtypeStruct((4, rows, width), low),
            jax.ShapeDtypeStruct((4, rows, own_width), low),
            jax.ShapeDtypeStruct((4, rows, hidden_width), low),
            jax.ShapeDtypeStruct((2, rows, width), low),
            jax.ShapeDtypeStruct((rows, width), full),
            jax.ShapeDtypeStruct((rows, width), low),
            jax.ShapeDtypeStruct((groups, heads, row_count, LANES), low),
        ),
        in_specs=[vmem] * 4 + [anywhere] * 4,
        out_specs=(vmem,) * 8,
        scratch_shapes=[
            pltpu.VMEM((rows, width), low),
            pltpu.VMEM((2, half, width), low),
            pltpu.VMEM((2, half, hidden_width), low),
            pltpu.VMEM((own_width, width), low),
            pltpu.VMEM((2, rows, width), low),
            pltpu.VMEM((2, rows, width), low),
            pltpu.VMEM((rows, width), low),
            pltpu.VMEM((rows, width), low),
            pltpu.VMEM((2, rows, width), low),
            pltpu.VMEM((2, rows, width), low),
            pltpu.SemaphoreType.DMA((3,)),
            pltpu.SemaphoreType.DMA((own_width // LANES,)),
            pltpu.SemaphoreType.DMA((8,)),
            pltpu.SemaphoreType.DMA((8,)),
        ],
        compiler_params=pltpu.CompilerParams(
            vmem_limit_bytes=60 * 1024 * 1024, collective_id=2, has_side_effects=True
        ),
        cost_estimate=pl.CostEstimate(
            flops=36 * 10**9, bytes_accessed=150 << 20, transcendentals=0
        ),
        name="mlp",
    )(returned, tokens, gain, out_quad, output_own, output_other, w_in, w_down)


def heads_body(
    tokens,
    attn_gain,
    w_query,
    w_key,
    w_value,
    w_output,
    mlp_gain,
    w_gate,
    w_up,
    w_down,
    out_grad,
    lengths,
):
    groups, reps = lax.axis_size("grp"), lax.axis_size("rep")
    here, there = lax.axis_index("grp"), lax.axis_index("rep")
    core = there % 2
    micro_count, row_count, width = tokens.shape
    rows = micro_count * row_count
    hidden_width = w_gate.shape[1]
    half_width = width // groups
    own_width = hidden_width // (2 * groups)
    stripes = reps // 2

    gathered_rows, qkv, w_heads, w_in = gather_heads(
        tokens, attn_gain, w_query, w_key, w_value, w_gate, w_up
    )
    gain_one = ordered(here, attn_gain, swap(attn_gain, 1, 0)).astype(jnp.float32)
    gain_two = ordered(here, mlp_gain, swap(mlp_gain, 1, 0)).astype(jnp.float32)
    inputs = tokens.astype(jnp.float32)

    output_other = swap(
        lax.dynamic_slice_in_dim(w_output, core * (half_width // 2), half_width // 2, axis=0), 1, 0
    )
    output_other = ordered(core, output_other, swap(output_other, 0, 1))

    def gather_quad(value):
        across = swap(value, 1, 0)
        return jnp.concatenate([value, swap(value, 0, 1), across, swap(across, 0, 1)], axis=0)

    out_rows = out_grad.reshape(rows, width)
    out_quad = gather_quad(out_rows)

    tables = attention_tables(lengths, here, there, row_count)
    attended, out_heads, log_sum, query, key, value = attend(tables, qkv)
    returned = lax.all_to_all(attended, BOTH, split_axis=0, concat_axis=0, tiled=True)
    returned = returned.reshape(groups, reps, row_count, LANES)
    attn_rows = returned.transpose(0, 2, 1, 3).reshape(rows, width)
    mixed, mid_quad, hidden, slopes, down_sums, grad_mixed, grad_branch, grad_att = mlp(
        returned,
        tokens.reshape(rows, width),
        jnp.broadcast_to(gain_two[None], (8, width)),
        out_quad.reshape(4, rows, width),
        w_output,
        output_other,
        w_in,
        w_down,
    )
    grad_heads = lax.all_to_all(
        grad_att.reshape(groups * reps, row_count, LANES),
        BOTH,
        split_axis=0,
        concat_axis=0,
        tiled=True,
    )
    block_out = (
        mixed + down_sums[0].astype(jnp.float32) + swap(down_sums[1], 1, 0).astype(jnp.float32)
    ).astype(jnp.bfloat16)
    mid_quad = mid_quad.reshape(4 * rows, width)
    hidden = hidden.reshape(4 * rows, own_width)
    slopes = slopes.reshape(4 * rows, 2 * own_width)

    bits = [(there // step) % 2 for step in (1, 2)]
    far = [1 << place for place in range(2, reps.bit_length() - 1)]

    def scatter_stripes(parts):
        lead, rest = parts.shape[0], parts.shape[2:]
        parts = halve(parts.reshape((lead, stripes // 2, 2) + rest), 2, bits[1], 0, 2)
        for step in far:
            count = parts.shape[1]
            parts = halve(
                narrow(parts).reshape((lead, count // 2, 2) + rest), 2, (there // step) % 2, 0, step
            )
        return parts[:, 0]

    mlp_in_grad = contract(mid_quad, slopes, 0, 0, jnp.bfloat16)
    own_rows = width // (groups * reps)
    mlp_in_part = narrow(
        scatter_stripes(
            mlp_in_grad.reshape(groups, stripes, 2, own_rows, 2 * own_width)
        )
    )
    down_grad = scatter_stripes(
        contract(hidden, out_quad, 0, 0, jnp.bfloat16).reshape(1, stripes, LANES, width)
    )[0]

    kept = pick(mlp_in_part, here, 0)
    crossed = swap(pick(mlp_in_part, 1 - here, 0), 1, 0)
    columns = []
    for part in (kept, crossed):
        columns.append(pick(part, core, 0))
        columns.append(swap(pick(part, 1 - core, 0), 0, 1))
    by_grp = [
        jnp.where(
            core == 0,
            jnp.stack([columns[2 * at], columns[2 * at + 1]], axis=1),
            jnp.stack([columns[2 * at + 1], columns[2 * at]], axis=1),
        )
        for at in range(2)
    ]
    pieces = jnp.where(
        here == 0,
        jnp.stack([by_grp[0], by_grp[1]], axis=1),
        jnp.stack([by_grp[1], by_grp[0]], axis=1),
    )
    pieces = pieces.reshape(own_rows, groups, 2, 2, stripes, LANES).transpose(3, 0, 1, 4, 2, 5)
    pieces = pieces.reshape(2, own_rows, hidden_width).astype(jnp.float32)
    gate_grad, up_grad = pieces[0], pieces[1]

    output_part = contract(attn_rows, grad_branch, 0, 0, jnp.bfloat16)
    output_part = output_part.reshape(groups, stripes, 2, own_rows, width)
    output_part = halve(output_part, 2, core, 0, 1)
    output_part = halve(narrow(output_part), 0, here, 1, 0)
    output_grad = scatter_stripes(narrow(output_part)[None])[0]

    back = attend_back(tables, query, key, value, out_heads, log_sum, grad_heads)
    grad_in, heads_grad = scatter_heads(
        back.reshape(reps, groups * row_count, 3 * LANES), w_heads, gathered_rows
    )
    grad_norm_in, unused_gain = norm_backward(
        inputs.reshape(rows, width), gain_one, grad_in.reshape(rows, width)
    )
    token_grad = (grad_mixed + grad_norm_in).astype(jnp.bfloat16)

    heads_grad = (
        heads_grad.reshape(reps, own_rows, 3, LANES)
        .transpose(2, 1, 0, 3)
        .reshape(3, own_rows, width)
        .astype(jnp.float32)
    )

    def own_part(value):
        return lax.dynamic_slice_in_dim(value, there * own_rows, own_rows, axis=0).astype(
            jnp.float32
        )

    attn_gain_grad = (
        jnp.sum(own_part(w_query) * heads_grad[0], axis=1)
        + jnp.sum(own_part(w_key) * heads_grad[1], axis=1)
        + jnp.sum(own_part(w_value) * heads_grad[2], axis=1)
    ) / own_part(attn_gain)
    mlp_gain_grad = (
        jnp.sum(own_part(w_gate) * gate_grad, axis=1) + jnp.sum(own_part(w_up) * up_grad, axis=1)
    ) / own_part(mlp_gain)
    block_shape = tokens.shape
    return (
        block_out.reshape(block_shape),
        token_grad.reshape(block_shape),
        attn_gain_grad,
        heads_grad[0],
        heads_grad[1],
        heads_grad[2],
        output_grad,
        mlp_gain_grad,
        gate_grad,
        up_grad,
        down_grad,
    )


def pick_body(*arrays):
    tokens = arrays[0]
    groups, reps = lax.axis_size("grp"), lax.axis_size("rep")
    fits = (
        groups == 2
        and tokens.shape[0] == groups
        and tokens.shape[2] == reps * LANES
        and reps % 4 == 0
        and reps & (reps - 1) == 0
        and tokens.shape[1] % UNIT_PAIR == 0
        and arrays[7].shape[1] == groups * reps * LANES
    )
    return heads_body(*arrays) if fits else ring_body(*arrays)


def solution(mesh):
    in_specs = (
        P(None, ("grp", "rep"), None),
        P("grp"),
        P("grp", None),
        P("grp", None),
        P("grp", None),
        P("grp", None),
        P("grp"),
        P("grp", None),
        P("grp", None),
        P("grp", None),
        P(None, ("grp", "rep"), None),
        P(),
    )
    out_specs = (
        P(None, ("grp", "rep"), None),
        P(None, ("grp", "rep"), None),
        P(("grp", "rep")),
        P(("grp", "rep"), None),
        P(("grp", "rep"), None),
        P(("grp", "rep"), None),
        P(("grp", "rep"), None),
        P(("grp", "rep")),
        P(("grp", "rep"), None),
        P(("grp", "rep"), None),
        P(("grp", "rep"), None),
    )
    return jax.shard_map(pick_body, mesh=mesh, in_specs=in_specs, out_specs=out_specs, check_vma=False)
```

```python
import functools
import math

import jax
import jax.numpy as jnp
from jax import lax
from jax.experimental import pallas as pl
from jax.experimental.pallas import tpu as pltpu
from jax.sharding import PartitionSpec as P

HD = 64
WINDOW = 2048


epsilon = 1e-05
rope_base = 10000.0
masked_score = -1e30
BOTH = ("grp", "rep")
LANES = 128
UNIT_BLOCK = 8
UNIT_PAIR = 16
KERNEL_VMEM = 56 * 1024 * 1024
SCATTER_REFS = 18


def from_behind(value, axis, steps):
    count = lax.axis_size(axis)
    first, last = (max(0, -steps), min(count, count - steps))
    return lax.ppermute(value, axis, [(source, source + steps) for source in range(first, last)])


def rms_scale(values):
    return lax.rsqrt(jnp.mean(values * values, axis=-1, keepdims=True) + epsilon)


def norm_backward(values, gain_full, grad_normed):
    inverse = rms_scale(values)
    normed = values * inverse
    gain_grad = jnp.sum(grad_normed * normed, axis=0)
    weighted = grad_normed * gain_full
    return (
        inverse * (weighted - normed * jnp.mean(weighted * normed, axis=-1, keepdims=True)),
        gain_grad,
    )


def rotary(values, cosine, sine_table):
    half_width = values.shape[-1] // 2
    first_half = values[..., :half_width]
    second_half = values[..., half_width:]
    return jnp.concatenate(
        [
            first_half * cosine - second_half * sine_table,
            second_half * cosine + first_half * sine_table,
        ],
        axis=-1,
    )


def pick_rows(rows_block, row_ids):
    return jnp.take(rows_block, row_ids, axis=0)


def take_rows(values, row_ids):
    return jax.vmap(pick_rows)(values, row_ids)


def gather_attn(attn_gain, w_query, w_key, w_value, w_output):
    return (
        lax.all_gather(attn_gain, "grp", axis=0, tiled=True),
        lax.all_gather(w_query, "grp", axis=0, tiled=True),
        lax.all_gather(w_key, "grp", axis=0, tiled=True),
        lax.all_gather(w_value, "grp", axis=0, tiled=True),
        lax.all_gather(w_output, "grp", axis=0, tiled=True),
    )


def gather_mlp(mlp_gain, w_gate, w_up, w_down):
    return (
        lax.all_gather(mlp_gain, "grp", axis=0, tiled=True),
        lax.all_gather(w_gate, "grp", axis=0, tiled=True),
        lax.all_gather(w_up, "grp", axis=0, tiled=True),
        lax.all_gather(w_down, "grp", axis=0, tiled=True),
    )


def reduce_attn(gain_grad, query_grad, key_grad, value_grad, output_grad):
    return (
        lax.psum_scatter(gain_grad, ("grp", "rep"), scatter_dimension=0, tiled=True),
        lax.psum_scatter(query_grad, ("grp", "rep"), scatter_dimension=0, tiled=True),
        lax.psum_scatter(key_grad, ("grp", "rep"), scatter_dimension=0, tiled=True),
        lax.psum_scatter(value_grad, ("grp", "rep"), scatter_dimension=0, tiled=True),
        lax.psum_scatter(output_grad, ("grp", "rep"), scatter_dimension=0, tiled=True),
    )


def reduce_mlp(gain_grad, gate_grad, up_grad, down_grad):
    return (
        lax.psum_scatter(gain_grad, ("grp", "rep"), scatter_dimension=0, tiled=True),
        lax.psum_scatter(gate_grad, ("grp", "rep"), scatter_dimension=0, tiled=True),
        lax.psum_scatter(up_grad, ("grp", "rep"), scatter_dimension=0, tiled=True),
        lax.psum_scatter(down_grad, ("grp", "rep"), scatter_dimension=0, tiled=True),
    )


def pass_on(carried, unused):
    arrived = from_behind(carried, ("grp", "rep"), 1)
    return (arrived, arrived)


def pass_back(running, portion):
    arrived = from_behind(running.astype(jnp.bfloat16), ("grp", "rep"), -1).astype(running.dtype)
    return (arrived + portion, None)


def ring_body(
    tokens,
    attn_gain,
    w_query,
    w_key,
    w_value,
    w_output,
    mlp_gain,
    w_gate,
    w_up,
    w_down,
    out_grad,
    lengths,
):
    devices = lax.axis_size(("grp", "rep"))
    rank_here = lax.axis_index(("grp", "rep"))
    micro_count, row_count, model_width = tokens.shape
    per_dev = row_count // devices
    head_count = model_width // HD
    reach_count = (WINDOW + row_count - 2) // row_count
    head_group = math.gcd(head_count, 4)
    group_count = head_count // head_group
    score_scale = 1.0 / math.sqrt(HD)
    unit_ids = jnp.arange(row_count, dtype=jnp.int32)
    seq_ends = jnp.cumsum(lengths, axis=1)
    starts = seq_ends - lengths
    seq_order = jnp.arange(lengths.shape[1], dtype=jnp.int32)
    earlier = seq_order[None, :] < seq_order[:, None]
    dealt_start = jnp.sum(jnp.where(earlier[None], lengths[:, None, :], 0), axis=2)
    seq_of = jnp.sum((seq_ends[:, None, :] <= unit_ids[None, :, None]).astype(jnp.int32), axis=2)
    seq_dealt = jnp.take_along_axis(dealt_start, seq_of, axis=1)
    unit_of = seq_dealt + unit_ids[None, :] - jnp.take_along_axis(starts, seq_of, axis=1)
    micro_ids = jnp.arange(micro_count, dtype=jnp.int32)[:, None]
    source_unit = (
        jnp.zeros((micro_count, row_count), jnp.int32)
        .at[micro_ids, unit_of]
        .set(jnp.broadcast_to(unit_ids[None, :], unit_of.shape))
    )
    unit_begin = (
        jnp.zeros((micro_count, row_count), jnp.int32).at[micro_ids, unit_of].set(seq_dealt)
    )
    local_ids = jnp.arange(row_count, dtype=jnp.int32)
    local_step = local_ids % per_dev
    local_source = local_ids // per_dev
    distance = jnp.arange(reach_count + 1, dtype=jnp.int32)
    owner_dev = rank_here - distance
    owner_ok = owner_dev >= 0
    owner_unit = jnp.maximum(owner_dev, 0)[:, None] * per_dev + local_step[None, :]
    key_begin = unit_begin[:, owner_unit]
    key_pos = (owner_unit[None] - key_begin) * devices + local_source[None, None, :]
    query_begin = key_begin[:, 0]
    query_pos = key_pos[:, 0]
    allowed = (
        owner_ok[None, None, :, None]
        & (query_begin[:, :, None, None] == key_begin[:, None, :, :])
        & (key_pos[:, None, :, :] <= query_pos[:, :, None, None])
        & (query_pos[:, :, None, None] - key_pos[:, None, :, :] < WINDOW)
    )
    mask_full = allowed[:, None]
    half_width = HD // 2
    frequency = jnp.power(rope_base, -2.0 * jnp.arange(half_width, dtype=jnp.float32) / HD)
    angles = query_pos.astype(jnp.float32)[:, :, None] * frequency[None, None, :]
    cosine = jnp.cos(angles)[:, :, None, :]
    sine_table = jnp.sin(angles)[:, :, None, :]
    head_shape = (micro_count, row_count, head_count, HD)
    block_shape = (micro_count, row_count, model_width)
    gathered = gather_attn(attn_gain, w_query, w_key, w_value, w_output)
    gain_one = gathered[0].astype(jnp.float32)
    inputs = tokens.astype(jnp.float32).reshape(micro_count * row_count, model_width)
    normed_in = (inputs * rms_scale(inputs) * gain_one).astype(jnp.bfloat16)
    queries = jnp.dot(normed_in, gathered[1], preferred_element_type=jnp.float32).astype(
        jnp.bfloat16
    )
    keys_in = jnp.dot(normed_in, gathered[2], preferred_element_type=jnp.float32).astype(
        jnp.bfloat16
    )
    values_in = jnp.dot(normed_in, gathered[3], preferred_element_type=jnp.float32).astype(
        jnp.bfloat16
    )
    dealt = (
        lax.all_to_all(
            take_rows(queries.reshape(block_shape), source_unit),
            ("grp", "rep"),
            split_axis=1,
            concat_axis=1,
            tiled=True,
        ),
        lax.all_to_all(
            take_rows(keys_in.reshape(block_shape), source_unit),
            ("grp", "rep"),
            split_axis=1,
            concat_axis=1,
            tiled=True,
        ),
        lax.all_to_all(
            take_rows(values_in.reshape(block_shape), source_unit),
            ("grp", "rep"),
            split_axis=1,
            concat_axis=1,
            tiled=True,
        ),
    )
    rot_q = rotary(dealt[0].reshape(head_shape).astype(jnp.float32), cosine, sine_table).astype(
        jnp.bfloat16
    )
    rot_k = rotary(dealt[1].reshape(head_shape).astype(jnp.float32), cosine, sine_table).astype(
        jnp.bfloat16
    )
    own_pair = jnp.stack([rot_k.reshape(block_shape), dealt[2]], axis=0)
    last_pair, farther = lax.scan(pass_on, own_pair, None, length=reach_count)
    context = jnp.concatenate([own_pair[None], farther], axis=0).reshape(
        reach_count + 1, 2, micro_count, row_count, head_count, HD
    )

    def group_scores(query_part, pair_part):
        scores = (
            jnp.einsum(
                "mqge,dmkge->mgqdk", query_part, pair_part[:, 0], preferred_element_type=jnp.float32
            )
            * score_scale
        )
        return jnp.where(mask_full, scores, masked_score)

    def forward_group(group_index, carried):
        attended_all, log_all = carried
        head_start = group_index * head_group
        query_part = lax.dynamic_slice_in_dim(rot_q, head_start, head_group, axis=2)
        pair_part = lax.dynamic_slice_in_dim(context, head_start, head_group, axis=4)
        scores = group_scores(query_part, pair_part)
        row_max = jnp.max(scores, axis=(3, 4), keepdims=True)
        weights_exp = jnp.exp(scores - row_max)
        row_sum = jnp.sum(weights_exp, axis=(3, 4), keepdims=True)
        soft_probs = (weights_exp / row_sum).astype(jnp.bfloat16)
        attended = jnp.einsum(
            "mgqdk,dmkge->mqge", soft_probs, pair_part[:, 1], preferred_element_type=jnp.float32
        ).astype(jnp.bfloat16)
        attended_all = lax.dynamic_update_slice_in_dim(attended_all, attended, head_start, axis=2)
        log_all = lax.dynamic_update_slice_in_dim(
            log_all, row_max + jnp.log(row_sum), head_start, axis=1
        )
        return (attended_all, log_all)

    attended_heads, log_sum = lax.fori_loop(
        0,
        group_count,
        forward_group,
        (
            jnp.zeros(head_shape, jnp.bfloat16),
            jnp.zeros((micro_count, head_count, row_count, 1, 1), jnp.float32),
        ),
    )
    returned = lax.all_to_all(
        attended_heads.reshape(block_shape), ("grp", "rep"), split_axis=1, concat_axis=1, tiled=True
    )
    attn_rows = take_rows(returned, unit_of).reshape(micro_count * row_count, model_width)
    mixed = inputs + jnp.dot(attn_rows, gathered[4], preferred_element_type=jnp.float32)
    mlp_set = gather_mlp(mlp_gain, w_gate, w_up, w_down)
    gain_two = mlp_set[0].astype(jnp.float32)
    normed_mid = (mixed * rms_scale(mixed) * gain_two).astype(jnp.bfloat16)
    gate_pre = jnp.dot(normed_mid, mlp_set[1], preferred_element_type=jnp.float32)
    up_pre = jnp.dot(normed_mid, mlp_set[2], preferred_element_type=jnp.float32)
    gate_sig = jax.nn.sigmoid(gate_pre)
    gate_silu = gate_pre * gate_sig
    hidden = (gate_silu * up_pre).astype(jnp.bfloat16)
    block_out = (mixed + jnp.dot(hidden, mlp_set[3], preferred_element_type=jnp.float32)).astype(
        jnp.bfloat16
    )
    mlp_set = gather_mlp(mlp_gain, w_gate, w_up, w_down)
    out_rows = out_grad.reshape(micro_count * row_count, model_width)
    down_grad = jnp.einsum("tf,td->fd", hidden, out_rows, preferred_element_type=jnp.float32)
    grad_hidden = jnp.einsum("td,fd->tf", out_rows, mlp_set[3], preferred_element_type=jnp.float32)
    grad_gate = (grad_hidden * up_pre * gate_sig * (1.0 + gate_pre * (1.0 - gate_sig))).astype(
        jnp.bfloat16
    )
    grad_up = (grad_hidden * gate_silu).astype(jnp.bfloat16)
    gate_grad = jnp.einsum("td,tf->df", normed_mid, grad_gate, preferred_element_type=jnp.float32)
    up_grad = jnp.einsum("td,tf->df", normed_mid, grad_up, preferred_element_type=jnp.float32)
    grad_mid = jnp.einsum(
        "tf,df->td", grad_gate, mlp_set[1], preferred_element_type=jnp.float32
    ) + jnp.einsum("tf,df->td", grad_up, mlp_set[2], preferred_element_type=jnp.float32)
    grad_norm_mid, mlp_gain_grad = norm_backward(mixed, gain_two, grad_mid)
    grad_mixed = out_rows.astype(jnp.float32) + grad_norm_mid
    mlp_sums = reduce_mlp(mlp_gain_grad, gate_grad, up_grad, down_grad)
    gathered = gather_attn(attn_gain, w_query, w_key, w_value, w_output)
    grad_branch = grad_mixed.astype(jnp.bfloat16)
    output_grad = jnp.einsum(
        "td,te->de", attn_rows, grad_branch, preferred_element_type=jnp.float32
    )
    grad_att = jnp.einsum(
        "te,de->td", grad_branch, gathered[4], preferred_element_type=jnp.float32
    ).astype(jnp.bfloat16)
    grad_dealt = lax.all_to_all(
        take_rows(grad_att.reshape(block_shape), source_unit),
        ("grp", "rep"),
        split_axis=1,
        concat_axis=1,
        tiled=True,
    )
    grad_heads = grad_dealt.reshape(head_shape)

    def backward_group(group_index, carried):
        query_total, pair_total = carried
        head_start = group_index * head_group
        query_part = lax.dynamic_slice_in_dim(rot_q, head_start, head_group, axis=2)
        grad_part = lax.dynamic_slice_in_dim(grad_heads, head_start, head_group, axis=2)
        pair_part = lax.dynamic_slice_in_dim(context, head_start, head_group, axis=4)
        log_part = lax.dynamic_slice_in_dim(log_sum, head_start, head_group, axis=1)
        scores = group_scores(query_part, pair_part)
        soft_probs = jnp.exp(scores - log_part)
        grad_probs = jnp.einsum(
            "mqge,dmkge->mgqdk", grad_part, pair_part[:, 1], preferred_element_type=jnp.float32
        )
        inner_sum = jnp.sum(soft_probs * grad_probs, axis=(3, 4), keepdims=True)
        grad_scores = (soft_probs * (grad_probs - inner_sum)).astype(jnp.bfloat16)
        query_piece = (
            jnp.einsum(
                "mgqdk,dmkge->mqge",
                grad_scores,
                pair_part[:, 0],
                preferred_element_type=jnp.float32,
            )
            * score_scale
        )
        key_part = (
            jnp.einsum(
                "mgqdk,mqge->dmkge", grad_scores, query_part, preferred_element_type=jnp.float32
            )
            * score_scale
        )
        value_part = jnp.einsum(
            "mgqdk,mqge->dmkge",
            soft_probs.astype(jnp.bfloat16),
            grad_part,
            preferred_element_type=jnp.float32,
        )
        query_total = lax.dynamic_update_slice_in_dim(query_total, query_piece, head_start, axis=2)
        pair_total = lax.dynamic_update_slice_in_dim(
            pair_total, jnp.stack([key_part, value_part], axis=1), head_start, axis=4
        )
        return (query_total, pair_total)

    query_total, pair_total = lax.fori_loop(
        0,
        group_count,
        backward_group,
        (
            jnp.zeros(head_shape, jnp.float32),
            jnp.zeros((reach_count + 1, 2) + head_shape, jnp.float32),
        ),
    )
    partials = pair_total.reshape(reach_count + 1, 2, micro_count, row_count, model_width)
    own_total, unused_out = lax.scan(
        pass_back, partials[reach_count], partials[:reach_count], reverse=True
    )
    query_back = rotary(query_total, cosine, -sine_table).astype(jnp.bfloat16)
    key_back = rotary(own_total[0].reshape(head_shape), cosine, -sine_table).astype(jnp.bfloat16)
    value_back = own_total[1].astype(jnp.bfloat16)
    grad_back = (
        lax.all_to_all(
            query_back.reshape(block_shape), ("grp", "rep"), split_axis=1, concat_axis=1, tiled=True
        ),
        lax.all_to_all(
            key_back.reshape(block_shape), ("grp", "rep"), split_axis=1, concat_axis=1, tiled=True
        ),
        lax.all_to_all(value_back, ("grp", "rep"), split_axis=1, concat_axis=1, tiled=True),
    )
    query_rows = take_rows(grad_back[0], unit_of).reshape(micro_count * row_count, model_width)
    key_rows = take_rows(grad_back[1], unit_of).reshape(micro_count * row_count, model_width)
    value_rows = take_rows(grad_back[2], unit_of).reshape(micro_count * row_count, model_width)
    query_grad = jnp.einsum("td,te->de", normed_in, query_rows, preferred_element_type=jnp.float32)
    key_grad = jnp.einsum("td,te->de", normed_in, key_rows, preferred_element_type=jnp.float32)
    value_grad = jnp.einsum("td,te->de", normed_in, value_rows, preferred_element_type=jnp.float32)
    grad_in = jnp.einsum("te,de->td", query_rows, gathered[1], preferred_element_type=jnp.float32)
    grad_in = grad_in + jnp.einsum(
        "te,de->td", key_rows, gathered[2], preferred_element_type=jnp.float32
    )
    grad_in = grad_in + jnp.einsum(
        "te,de->td", value_rows, gathered[3], preferred_element_type=jnp.float32
    )
    grad_norm_in, attn_gain_grad = norm_backward(inputs, gain_one, grad_in)
    token_grad = (grad_mixed + grad_norm_in).astype(jnp.bfloat16)
    attn_sums = reduce_attn(attn_gain_grad, query_grad, key_grad, value_grad, output_grad)
    return (
        block_out.reshape(block_shape),
        token_grad.reshape(block_shape),
        attn_sums[0],
        attn_sums[1],
        attn_sums[2],
        attn_sums[3],
        attn_sums[4],
        mlp_sums[0],
        mlp_sums[1],
        mlp_sums[2],
        mlp_sums[3],
    )


def contract(left_side, right_side, left_dim, right_dim, kind=jnp.float32):
    return lax.dot_general(
        left_side,
        right_side,
        (((left_dim,), (right_dim,)), ((), ())),
        preferred_element_type=jnp.float32,
    ).astype(kind)


def swap_halves(values):
    lane = lax.broadcasted_iota(jnp.int32, values.shape, 1)
    ahead = pltpu.roll(values, LANES - HD // 2, 1)
    behind = pltpu.roll(values, HD // 2, 1)
    return jnp.where(lane % HD < HD // 2, -ahead, behind)


def pair_angles(unit_at, cos_unit, sin_unit, cos_part, sin_part):
    unit_cos = cos_unit[pl.ds(unit_at, UNIT_PAIR), :][None]
    unit_sin = sin_unit[pl.ds(unit_at, UNIT_PAIR), :][None]
    part_cos = cos_part[...][:, None, :]
    part_sin = sin_part[...][:, None, :]
    cosine = unit_cos * part_cos - unit_sin * part_sin
    sine = unit_sin * part_cos + unit_cos * part_sin
    return cosine, sine


def key_offsets(block):
    row = lax.broadcasted_iota(jnp.int32, (block, block), 0)
    return (row % UNIT_BLOCK) * (block // UNIT_BLOCK) + row // UNIT_BLOCK


def query_offsets(block):
    column = lax.broadcasted_iota(jnp.int32, (block, block), 1)
    return (column % UNIT_BLOCK) * (block // UNIT_BLOCK) + column // UNIT_BLOCK


def attend_kernel(
    slot_ref,
    first_ref,
    plain_ref,
    cos_unit,
    sin_unit,
    cos_part,
    sin_part,
    low_ref,
    qkv_ref,
    att_ref,
    out_ref,
    log_ref,
    query_ref,
    key_ref,
    value_ref,
    query_t,
    value_t,
    key_at,
    causal_at,
):
    parts, units, _ = qkv_ref.shape
    block = parts * UNIT_BLOCK
    pairs = units // UNIT_PAIR
    key_at[...] = key_offsets(block)
    causal_at[...] = jnp.where(key_offsets(block) <= query_offsets(block), 0.0, masked_score)
    extra = value_t.shape[2] - HD

    def lay_out(pair, unused):
        unit_at = pl.multiple_of(pair * UNIT_PAIR, UNIT_PAIR)
        rows = jnp.stack(
            [qkv_ref[slot_ref[part], pl.ds(unit_at, UNIT_PAIR), :] for part in range(parts)]
        )
        cosine, sine = pair_angles(unit_at, cos_unit, sin_unit, cos_part, sin_part)
        flat = (parts * UNIT_PAIR, LANES)
        cosine = cosine.reshape(flat)
        sine = sine.reshape(flat)

        def rotated(values):
            values = values.astype(jnp.float32).reshape(flat)
            turned = values * cosine + swap_halves(values) * sine
            return turned.reshape(parts, UNIT_PAIR, LANES)

        query = rotated(rows[:, :, :LANES]) * (1.0 / math.sqrt(HD))
        key = rotated(rows[:, :, LANES : 2 * LANES])
        value = rows[:, :, 2 * LANES :].astype(jnp.float32)
        for half in range(UNIT_PAIR // UNIT_BLOCK):
            at = pair * (UNIT_PAIR // UNIT_BLOCK) + half
            cut = slice(half * UNIT_BLOCK, (half + 1) * UNIT_BLOCK)
            query_rows = query[:, cut].reshape(block, LANES)
            value_rows = value[:, cut].reshape(block, LANES)
            query_ref[at] = query_rows.astype(jnp.bfloat16)
            key_ref[at] = key[:, cut].reshape(block, LANES).astype(jnp.bfloat16)
            value_ref[at] = value_rows.astype(jnp.bfloat16)
            turned = jnp.transpose(query_rows)
            row = lax.broadcasted_iota(jnp.int32, turned.shape, 0)
            query_t[0, at] = jnp.where(row < HD, turned, 0.0).astype(jnp.bfloat16)
            query_t[1, at] = jnp.where(row < HD, 0.0, turned).astype(jnp.bfloat16)
            turned = jnp.transpose(value_rows).astype(jnp.bfloat16)
            for head in range(2):
                value_t[head, at, pl.ds(0, HD), :] = turned[head * HD : (head + 1) * HD]
                value_t[head, at, pl.ds(HD, extra), :] = jnp.ones((extra, block), jnp.bfloat16)
        return unused

    lax.fori_loop(0, pairs, lay_out, 0)

    def query_block(at):
        low = low_ref[at, 0:1, :]

        def step(key_block, carried, causal, bounded):
            new = []
            for head in range(2):
                top, total = carried[2 * head : 2 * head + 2]
                scores = jnp.dot(
                    key_ref[key_block], query_t[head, at], preferred_element_type=jnp.float32
                )
                if causal:
                    scores = scores + causal_at[...]
                if bounded:
                    scores = jnp.where(
                        key_at[...] >= low - key_block * block, scores, masked_score
                    )
                high = jnp.maximum(top, jnp.max(scores, axis=0, keepdims=True))
                weights = jnp.exp(scores - high).astype(jnp.bfloat16)
                total = total * jnp.exp(top - high) + jnp.dot(
                    value_t[head, key_block], weights, preferred_element_type=jnp.float32
                )
                new += [high, total]
            return tuple(new)

        empty = (
            jnp.full((1, block), masked_score, jnp.float32),
            jnp.zeros((HD + extra, block), jnp.float32),
        )
        carried = step(at, empty * 2, True, True)
        carried = lax.fori_loop(
            first_ref[at],
            plain_ref[at],
            lambda key_block, held: step(key_block, held, False, True),
            carried,
        )
        carried = lax.fori_loop(
            plain_ref[at],
            at,
            lambda key_block, held: step(key_block, held, False, False),
            carried,
        )
        heads = []
        for head in range(2):
            top, total = carried[2 * head : 2 * head + 2]
            heads.append(total[:HD] / total[HD : HD + 1])
            log_ref[at, head : head + 1, :] = top + jnp.log(total[HD : HD + 1])
        both = jnp.concatenate(heads, axis=0)
        out_ref[at] = both
        return jnp.transpose(both).reshape(parts, UNIT_BLOCK, LANES)

    def query_pair(pair, unused):
        halves = UNIT_PAIR // UNIT_BLOCK
        done = [query_block(pair * halves + half) for half in range(halves)]
        unit_at = pl.multiple_of(pair * UNIT_PAIR, UNIT_PAIR)
        att_ref[:, pl.ds(unit_at, UNIT_PAIR), :] = jnp.concatenate(done, axis=1).astype(
            jnp.bfloat16
        )
        return unused

    lax.fori_loop(0, pairs, query_pair, 0)


def attend_back_kernel(
    slot_ref,
    first_ref,
    plain_ref,
    cos_unit,
    sin_unit,
    cos_part,
    sin_part,
    low_ref,
    query_ref,
    key_ref,
    value_ref,
    out_ref,
    log_ref,
    grad_ref,
    back_ref,
    key_t,
    key_total,
    value_total,
    key_at,
    causal_at,
):
    parts, units, _ = grad_ref.shape
    block = parts * UNIT_BLOCK
    pairs = units // UNIT_PAIR
    halves = UNIT_PAIR // UNIT_BLOCK
    key_at[...] = key_offsets(block)
    causal_at[...] = jnp.where(key_offsets(block) <= query_offsets(block), 0.0, masked_score)

    def lay_out(at, unused):
        key_t[at] = jnp.transpose(key_ref[at].astype(jnp.float32)).astype(jnp.bfloat16)
        key_total[at] = jnp.zeros((block, LANES), jnp.float32)
        value_total[at] = jnp.zeros((block, LANES), jnp.float32)
        return unused

    lax.fori_loop(0, pairs * halves, lay_out, 0)

    def split_heads(values, axis):
        place = lax.broadcasted_iota(jnp.int32, values.shape, axis)
        zero = jnp.zeros_like(values)
        return [
            jnp.where(place < HD, values, zero).astype(jnp.bfloat16),
            jnp.where(place < HD, zero, values).astype(jnp.bfloat16),
        ]

    def query_block(at, grad_rows):
        low = low_ref[at, 0:1, :]
        query_rows = query_ref[at].astype(jnp.float32)
        query_heads = jnp.concatenate(split_heads(query_rows, 1), axis=0)
        grad_heads = jnp.concatenate(split_heads(grad_rows, 1), axis=0)
        query_t = split_heads(jnp.transpose(query_rows), 0)
        grad_turned = jnp.transpose(grad_rows)
        grad_t = split_heads(grad_turned, 0)
        product = grad_turned * out_ref[at]
        inner = [
            jnp.sum(product[head * HD : (head + 1) * HD], axis=0, keepdims=True)
            for head in range(2)
        ]
        logs = [log_ref[at, head : head + 1, :] for head in range(2)]

        def step(key_block, carried, causal, bounded):
            probs, slopes, new = [], [], []
            for head in range(2):
                scores = jnp.dot(
                    key_ref[key_block], query_t[head], preferred_element_type=jnp.float32
                )
                if causal:
                    scores = scores + causal_at[...]
                if bounded:
                    scores = jnp.where(
                        key_at[...] >= low - key_block * block, scores, masked_score
                    )
                soft = jnp.exp(scores - logs[head])
                grad_probs = jnp.dot(
                    value_ref[key_block], grad_t[head], preferred_element_type=jnp.float32
                )
                slope = (soft * (grad_probs - inner[head])).astype(jnp.bfloat16)
                probs.append(soft.astype(jnp.bfloat16))
                slopes.append(slope)
                new.append(
                    carried[head]
                    + jnp.dot(
                        key_t[key_block, pl.ds(head * HD, HD), :],
                        slope,
                        preferred_element_type=jnp.float32,
                    )
                )
            value_total[key_block] += jnp.dot(
                jnp.concatenate(probs, axis=1), grad_heads, preferred_element_type=jnp.float32
            )
            key_total[key_block] += jnp.dot(
                jnp.concatenate(slopes, axis=1), query_heads, preferred_element_type=jnp.float32
            )
            return tuple(new)

        carried = step(at, (jnp.zeros((HD, block), jnp.float32),) * 2, True, True)
        carried = lax.fori_loop(
            first_ref[at],
            plain_ref[at],
            lambda key_block, held: step(key_block, held, False, True),
            carried,
        )
        carried = lax.fori_loop(
            plain_ref[at],
            at,
            lambda key_block, held: step(key_block, held, False, False),
            carried,
        )
        return jnp.transpose(jnp.concatenate(carried, axis=0)) * (1.0 / math.sqrt(HD))

    def turn_back(rows, cosine, sine):
        flat = (parts * UNIT_PAIR, LANES)
        rows = jnp.concatenate(
            [one.reshape(parts, UNIT_BLOCK, LANES) for one in rows], axis=1
        ).reshape(flat)
        turned = rows * cosine.reshape(flat) - swap_halves(rows) * sine.reshape(flat)
        return turned.reshape(parts, UNIT_PAIR, LANES).astype(jnp.bfloat16)

    def put(values, unit_at, lane_at):
        for part in range(parts):
            back_ref[slot_ref[part], pl.ds(unit_at, UNIT_PAIR), pl.ds(lane_at, LANES)] = values[part]

    def query_pair(pair, unused):
        unit_at = pl.multiple_of(pair * UNIT_PAIR, UNIT_PAIR)
        grads = grad_ref[:, pl.ds(unit_at, UNIT_PAIR), :].astype(jnp.float32)
        done = [
            query_block(
                pair * halves + half,
                grads[:, half * UNIT_BLOCK : (half + 1) * UNIT_BLOCK].reshape(block, LANES),
            )
            for half in range(halves)
        ]
        cosine, sine = pair_angles(unit_at, cos_unit, sin_unit, cos_part, sin_part)
        put(turn_back(done, cosine, sine), unit_at, 0)
        return unused

    lax.fori_loop(0, pairs, query_pair, 0)

    def key_pair(pair, unused):
        unit_at = pl.multiple_of(pair * UNIT_PAIR, UNIT_PAIR)
        cosine, sine = pair_angles(unit_at, cos_unit, sin_unit, cos_part, sin_part)
        ids = [pair * halves + half for half in range(halves)]
        put(turn_back([key_total[at] for at in ids], cosine, sine), unit_at, LANES)
        values = jnp.concatenate(
            [value_total[at].reshape(parts, UNIT_BLOCK, LANES) for at in ids], axis=1
        ).astype(jnp.bfloat16)
        put(values, unit_at, 2 * LANES)
        return unused

    lax.fori_loop(0, pairs, key_pair, 0)


def attend(tables, qkv):
    parts, units, _ = qkv.shape
    block = parts * UNIT_BLOCK
    blocks = units // UNIT_BLOCK
    smem = pl.BlockSpec(memory_space=pltpu.SMEM)
    vmem = pl.BlockSpec(memory_space=pltpu.VMEM)
    rows = jax.ShapeDtypeStruct((blocks, block, LANES), jnp.bfloat16)
    extra = UNIT_PAIR
    return pl.pallas_call(
        attend_kernel,
        out_shape=(
            jax.ShapeDtypeStruct((parts, units, LANES), jnp.bfloat16),
            jax.ShapeDtypeStruct((blocks, LANES, block), jnp.float32),
            jax.ShapeDtypeStruct((blocks, 8, block), jnp.float32),
            rows,
            rows,
            rows,
        ),
        in_specs=[smem] * 3 + [vmem] * 6,
        out_specs=(vmem,) * 6,
        scratch_shapes=[
            pltpu.VMEM((2, blocks, LANES, block), jnp.bfloat16),
            pltpu.VMEM((2, blocks, HD + extra, block), jnp.bfloat16),
            pltpu.VMEM((block, block), jnp.int32),
            pltpu.VMEM((block, block), jnp.float32),
        ],
        compiler_params=pltpu.CompilerParams(vmem_limit_bytes=KERNEL_VMEM),
        cost_estimate=pl.CostEstimate(
            flops=20 * 10**9, bytes_accessed=16 << 20, transcendentals=20 * 10**6
        ),
        name="attend",
    )(*tables, qkv)


def attend_back(tables, query, key, value, out, log, grad):
    parts, units, _ = grad.shape
    block = parts * UNIT_BLOCK
    blocks = units // UNIT_BLOCK
    smem = pl.BlockSpec(memory_space=pltpu.SMEM)
    vmem = pl.BlockSpec(memory_space=pltpu.VMEM)
    return pl.pallas_call(
        attend_back_kernel,
        out_shape=jax.ShapeDtypeStruct((parts, units, 3 * LANES), jnp.bfloat16),
        in_specs=[smem] * 3 + [vmem] * 11,
        out_specs=vmem,
        scratch_shapes=[
            pltpu.VMEM((blocks, LANES, block), jnp.bfloat16),
            pltpu.VMEM((blocks, block, LANES), jnp.float32),
            pltpu.VMEM((blocks, block, LANES), jnp.float32),
            pltpu.VMEM((block, block), jnp.int32),
            pltpu.VMEM((block, block), jnp.float32),
        ],
        compiler_params=pltpu.CompilerParams(vmem_limit_bytes=KERNEL_VMEM),
        cost_estimate=pl.CostEstimate(
            flops=50 * 10**9, bytes_accessed=16 << 20, transcendentals=20 * 10**6
        ),
        name="attend_back",
    )(*tables, query, key, value, out, log, grad)


def attention_tables(lengths, grp_here, rep_here, units):
    reps = lax.axis_size("rep")
    parts = lax.axis_size("grp") * reps
    block = parts * UNIT_BLOCK
    blocks = units // UNIT_BLOCK
    own = lax.dynamic_index_in_dim(lengths, grp_here, 0, keepdims=False)
    ends = jnp.cumsum(own)
    unit_ids = jnp.arange(units, dtype=jnp.int32)
    begin = jnp.max(
        jnp.where(ends[None, :] <= unit_ids[:, None], ends[None, :], 0), axis=1
    ).astype(jnp.int32)
    part_ids = jnp.arange(parts, dtype=jnp.int32)
    offset = part_ids % reps ^ rep_here
    slot = offset * lax.axis_size("grp") + (part_ids // reps ^ grp_here)
    frequency = jnp.power(
        rope_base, -2.0 * (jnp.arange(LANES) % (HD // 2)).astype(jnp.float32) / HD
    )
    unit_angle = ((unit_ids - begin) * parts).astype(jnp.float32)[:, None] * frequency[None, :]
    part_angle = part_ids.astype(jnp.float32)[:, None] * frequency[None, :]
    low = jnp.maximum(
        (begin * parts)[:, None], unit_ids[:, None] * parts + part_ids[None, :] - (WINDOW - 1)
    )
    low = low.reshape(blocks, UNIT_BLOCK, parts)
    least = jnp.min(low, axis=(1, 2))
    most = jnp.max(low, axis=(1, 2))
    block_ids = jnp.arange(blocks, dtype=jnp.int32)
    first = jnp.maximum(least, 0) // block
    plain = jnp.clip((most + block - 1) // block, first, block_ids)
    low_rows = jnp.broadcast_to(
        low.transpose(0, 2, 1).reshape(blocks, 1, block), (blocks, 8, block)
    )
    return (
        slot,
        first,
        plain,
        jnp.cos(unit_angle),
        jnp.sin(unit_angle),
        jnp.cos(part_angle),
        jnp.sin(part_angle),
        low_rows,
    )


def swap(value, grp_step, rep_step):
    groups, reps = lax.axis_size("grp"), lax.axis_size("rep")
    pairs = [
        (grp * reps + rep, (grp ^ grp_step) * reps + (rep ^ rep_step))
        for grp in range(groups)
        for rep in range(reps)
    ]
    return lax.ppermute(value, BOTH, pairs)


def ordered(flag, own, other, axis=0):
    return jnp.where(
        flag == 0,
        jnp.concatenate([own, other], axis=axis),
        jnp.concatenate([other, own], axis=axis),
    )


def pick(value, index, axis):
    return lax.dynamic_index_in_dim(value, index, axis, keepdims=False)


def halve(value, axis, bit, grp_step, rep_step):
    kept = pick(value, bit, axis)
    sent = pick(value, 1 - bit, axis).astype(jnp.bfloat16)
    arrived = swap(sent, grp_step, rep_step)
    return kept.astype(jnp.float32) + arrived.astype(jnp.float32)


def narrow(value):
    return value.astype(jnp.bfloat16)


MESH_IDS = pl.DeviceIdType.MESH


def flipped(index, step):
    return index + step - 2 * step * ((index // step) % 2)


def lowest(offset):
    return offset & -offset


def arrivals(reps):
    far = [step for step in range(4, reps, 4)]
    far.sort(key=lambda step: (bin(step).count("1"), step))
    order = [(2, 0), (0, 1)]
    for at, step in enumerate(far):
        if bin(step).count("1") == 1:
            order.append((step, 0))
    order.append((2, 1))
    for step in far:
        if bin(step).count("1") == 1:
            order.append((step, 1))
    single = [step for step in far if bin(step).count("1") == 1]
    double = [step for step in far if bin(step).count("1") > 1]
    rest = []
    for step in single[:1]:
        rest.append((step + 2, 0))
    for step in double:
        rest.append((step, 0))
    for step in single[:1]:
        rest.append((step + 2, 1))
    for step in double:
        rest.append((step, 1))
    for step in single[1:] + double:
        rest += [(step + 2, 0), (step + 2, 1)]
    return order + rest


def link_of(offset, part, reps):
    if reps > 8 and offset == reps - 2 and part == 1:
        return 4
    return lowest(offset)


def gather_kernel(
    tokens_ref,
    gain_ref,
    w_query,
    w_key,
    w_value,
    w_gate,
    w_up,
    w_down,
    w_output,
    out_rows,
    normed_out,
    qkv_ref,
    weight_ref,
    gate_ref,
    up_ref,
    down_ref,
    output_ref,
    out_away,
    gains,
    raw,
    normed,
    weight_sem,
    out_sem,
    send_sem,
    recv_sem,
    side_send,
    side_recv,
    stripe_sem,
):
    here, there = lax.axis_index("grp"), lax.axis_index("rep")
    core = there % 2
    reps = raw.shape[0]
    slots = normed.shape[0]
    row_count, width = raw.shape[2:]
    steps = [1 << place for place in range(reps.bit_length() - 1)]
    across = (1 - here, there)

    def neighbour(step):
        return (here, flipped(there, step))

    barrier = pltpu.get_barrier_semaphore()
    for target in [across] + [neighbour(step) for step in steps]:
        pl.semaphore_signal(barrier, inc=1, device_id=target, device_id_type=MESH_IDS)
    local = []
    for at, weight in enumerate((w_query, w_key, w_value)):
        local.append(
            pltpu.make_async_copy(
                weight.at[:, pl.ds(pl.multiple_of(there * LANES, LANES), LANES)],
                weight_ref.at[here, :, pl.ds(at * LANES, LANES)],
                weight_sem.at[at],
            )
        )
        local[-1].start()
    raw[0, 0] = tokens_ref[here]
    gains[here] = gain_ref[...]
    pl.semaphore_wait(barrier, len(steps) + 1)

    def side(at, source, target_ref):
        return pltpu.make_async_remote_copy(
            src_ref=source,
            dst_ref=target_ref,
            send_sem=side_send.at[at],
            recv_sem=side_recv.at[at],
            device_id=across,
            device_id_type=MESH_IDS,
        )

    def rows_copy(offset, part):
        if offset == 0:
            return pltpu.make_async_remote_copy(
                src_ref=tokens_ref.at[1 - here],
                dst_ref=raw.at[0, 1],
                send_sem=send_sem.at[1],
                recv_sem=recv_sem.at[1],
                device_id=across,
                device_id_type=MESH_IDS,
            )
        step = link_of(offset, part, reps)
        return pltpu.make_async_remote_copy(
            src_ref=raw.at[offset - step, part],
            dst_ref=raw.at[offset, part],
            send_sem=send_sem.at[2 * offset + part],
            recv_sem=recv_sem.at[2 * offset + part],
            device_id=neighbour(step),
            device_id_type=MESH_IDS,
        )

    order = arrivals(reps)
    copies = {
        (offset, part): rows_copy(offset, part)
        for offset in range(reps)
        for part in (0, 1)
        if offset or part
    }

    def pass_on(offset, part):
        for later, part_of in order:
            if later and part_of == part and later - link_of(later, part, reps) == offset:
                copies[later, part].start()
        copies[offset + 1, part].start()

    gain_copy = side(0, gains.at[here], gains.at[here])
    gain_copy.start()
    copies[0, 1].start()
    pass_on(0, 0)
    for one in local:
        one.wait()
    weight_copy = side(1, weight_ref.at[here], weight_ref.at[here])
    weight_copy.start()

    stripes = [
        (grp, high, low)
        for grp in range(2)
        for high in range(reps // 8)
        for low in range(2)
    ]
    place = 4 * ((there // 4) % 2) + there % 2
    stripe_loads = []

    def load(source, target_ref):
        stripe_loads.append(
            pltpu.make_async_copy(source, target_ref, stripe_sem.at[len(stripe_loads)])
        )

    def columns_of(weight, grp, high, low):
        first = (grp * reps + 8 * high + 2 * low + place) * LANES
        return weight.at[:, pl.ds(pl.multiple_of(first, LANES), LANES)]

    for weight, target_ref in ((w_gate, gate_ref.at[here]), (w_up, up_ref)):
        for at, stripe in enumerate(stripes):
            load(columns_of(weight, *stripe), target_ref.at[:, pl.ds(at * LANES, LANES)])
    for at, (grp, high, low) in enumerate(stripes[: len(stripes) // 2]):
        first = (8 * high + 2 * low + place) * LANES
        load(
            w_down.at[pl.ds(pl.multiple_of(first, LANES), LANES)],
            down_ref.at[pl.ds(at * LANES, LANES)],
        )
    load(out_rows, out_away)
    for one in stripe_loads:
        one.start()
    quarter = output_ref.shape[0]
    output_copy = side(
        2,
        w_output.at[pl.ds(pl.multiple_of((there % 4) * quarter, quarter), quarter)],
        output_ref,
    )
    output_copy.start()
    gate_copy = side(3, gate_ref.at[here], gate_ref.at[here])
    for one in stripe_loads[: len(stripes)]:
        one.wait()
    gate_copy.start()

    written = {}
    used = [None] * slots
    tile = 32

    def project(count, offset):
        slot = count % slots
        if used[slot] is not None:
            written[used[slot]].wait()
        used[slot] = offset
        gain = jnp.concatenate([gains[0, 0:1], gains[1, 0:1]], axis=1).astype(jnp.float32)
        for part in range(2):

            def norm_rows(at, unused):
                cut = pl.ds(pl.multiple_of(at * tile, tile), tile)
                values = raw[offset, part, cut, :].astype(jnp.float32)
                scaled = values * rms_scale(values) * gain
                normed[slot, pl.ds(pl.multiple_of(part * row_count + at * tile, tile), tile), :] = (
                    scaled.astype(jnp.bfloat16)
                )
                return unused

            lax.fori_loop(0, row_count // tile, norm_rows, 0)
        written[offset] = pltpu.make_async_copy(
            normed.at[slot], normed_out.at[offset], out_sem.at[offset]
        )
        written[offset].start()
        half = width // 2
        product = jnp.dot(
            normed[slot, :, :half], weight_ref[0], preferred_element_type=jnp.float32
        ) + jnp.dot(normed[slot, :, half:], weight_ref[1], preferred_element_type=jnp.float32)
        qkv_ref[pl.ds(2 * offset, 2)] = product.astype(jnp.bfloat16).reshape(
            2, row_count, 3 * LANES
        )

    ready = []
    arrived = {(0, 0)}
    started = False
    count = 0
    for offset, part in order:
        copies[offset, part].wait_recv()
        pass_on(offset, part)
        arrived.add((offset, part))
        if (offset, 1 - part) in arrived:
            ready.append(offset)
        if not started and len(ready) >= 1:
            gain_copy.wait_recv()
            weight_copy.wait_recv()
            started = True
        if started and len(ready) >= 2:
            base = ready.pop(0)
            project(count, base)
            copies[base + 1, 0].wait_recv()
            copies[base + 1, 1].wait_recv()
            project(count + 1, base + 1)
            count += 2
    for base in ready:
        project(count, base)
        copies[base + 1, 0].wait_recv()
        copies[base + 1, 1].wait_recv()
        project(count + 1, base + 1)
        count += 2
    for offset in used:
        written[offset].wait()
    for one in copies.values():
        one.wait_send()
    gain_copy.wait_send()
    weight_copy.wait_send()
    for one in stripe_loads[len(stripes) :]:
        one.wait()
    gate_copy.wait()
    output_copy.wait()


def gather_heads(
    tokens, gains, w_query, w_key, w_value, w_gate, w_up, w_down, w_output, out_rows
):
    reps = lax.axis_size("rep")
    _, row_count, width = tokens.shape
    half = width // 2
    own_width = reps // 2 * LANES
    gain_rows = jnp.concatenate(
        [gains[0][None], gains[1][None], jnp.zeros((14, half), jnp.bfloat16)], axis=0
    )
    vmem = pl.BlockSpec(memory_space=pltpu.VMEM)
    anywhere = pl.BlockSpec(memory_space=pl.ANY)
    return pl.pallas_call(
        gather_kernel,
        out_shape=(
            jax.ShapeDtypeStruct((reps, 2 * row_count, width), jnp.bfloat16),
            jax.ShapeDtypeStruct((2 * reps, row_count, 3 * LANES), jnp.bfloat16),
            jax.ShapeDtypeStruct((2, half, 3 * LANES), jnp.bfloat16),
            jax.ShapeDtypeStruct((2, half, own_width), jnp.bfloat16),
            jax.ShapeDtypeStruct((half, own_width), jnp.bfloat16),
            jax.ShapeDtypeStruct((own_width // 2, width), jnp.bfloat16),
            jax.ShapeDtypeStruct((half // 4, width), jnp.bfloat16),
            jax.ShapeDtypeStruct(out_rows.shape, jnp.bfloat16),
            jax.ShapeDtypeStruct((2, 16, half), jnp.bfloat16),
        ),
        in_specs=[vmem, vmem] + [anywhere] * 8,
        out_specs=(anywhere,) + (vmem,) * 8,
        scratch_shapes=[
            pltpu.VMEM((reps, 2, row_count, width), jnp.bfloat16),
            pltpu.VMEM((4, 2 * row_count, width), jnp.bfloat16),
            pltpu.SemaphoreType.DMA((3,)),
            pltpu.SemaphoreType.DMA((reps,)),
            pltpu.SemaphoreType.DMA((2 * reps,)),
            pltpu.SemaphoreType.DMA((2 * reps,)),
            pltpu.SemaphoreType.DMA((4,)),
            pltpu.SemaphoreType.DMA((4,)),
            pltpu.SemaphoreType.DMA((reps // 2 * 5 // 2 + 1,)),
        ],
        compiler_params=pltpu.CompilerParams(
            vmem_limit_bytes=KERNEL_VMEM, collective_id=0, has_side_effects=True
        ),
        cost_estimate=pl.CostEstimate(
            flops=8 * 10**9, bytes_accessed=250 << 20, transcendentals=0
        ),
        name="gather_heads",
    )(tokens, gain_rows, w_query, w_key, w_value, w_gate, w_up, w_down, w_output, out_rows)


def scatter_kernel(
    back_ref,
    weight_ref,
    normed_ref,
    *refs,
):
    scatter_rows(back_ref, weight_ref, normed_ref, *refs[-SCATTER_REFS:])


def scatter_rows(
    back_ref,
    weight_ref,
    normed_ref,
    grad_ref,
    pieces_ref,
    away,
    landed,
    normed,
    back_t,
    weight_t,
    weights_total,
    half_out,
    half_in,
    piece_out,
    normed_sem,
    send_sem,
    recv_sem,
    side_send,
    side_recv,
    piece_send,
    piece_recv,
):
    here, there = lax.axis_index("grp"), lax.axis_index("rep")
    reps, rows, columns = back_ref.shape
    row_count = rows // 2
    width = grad_ref.shape[2]
    half = width // 2
    own_rows = half // reps
    steps = [1 << place for place in range(reps.bit_length() - 1)]
    across = (1 - here, there)

    def other(offset):
        index = there
        for step in steps:
            if offset & step:
                index = flipped(index, step)
        return (here, index)

    barrier = pltpu.get_barrier_semaphore()
    for target in [across] + [other(offset) for offset in range(1, reps)]:
        pl.semaphore_signal(barrier, inc=1, device_id=target, device_id_type=MESH_IDS)

    slots = normed.shape[0]
    fetch = [
        pltpu.make_async_copy(normed_ref.at[offset], normed.at[offset % slots], normed_sem.at[offset])
        for offset in range(reps)
    ]
    for offset in range(slots):
        fetch[offset].start()

    for at in range(2):
        turned = jnp.transpose(weight_ref[at].astype(jnp.float32)).astype(jnp.bfloat16)
        weight_t[:, pl.ds(at * half, half)] = turned
    pl.semaphore_wait(barrier, reps)

    def rows_copy(offset, part):
        if offset == 0:
            return pltpu.make_async_remote_copy(
                src_ref=away.at[0, 1],
                dst_ref=landed.at[0, 1],
                send_sem=send_sem.at[1],
                recv_sem=recv_sem.at[1],
                device_id=across,
                device_id_type=MESH_IDS,
            )
        return pltpu.make_async_remote_copy(
            src_ref=away.at[offset, part],
            dst_ref=landed.at[offset, part],
            send_sem=send_sem.at[2 * offset + part],
            recv_sem=recv_sem.at[2 * offset + part],
            device_id=other(link_of(offset, part, reps)),
            device_id_type=MESH_IDS,
        )

    copies = {
        (offset, part): rows_copy(offset, part)
        for offset in range(reps)
        for part in (0, 1)
        if offset or part
    }
    tile = 32

    def product(offset, part):
        return jnp.dot(
            back_ref[offset, pl.ds(part * row_count, row_count), :],
            weight_t[...],
            preferred_element_type=jnp.float32,
        )

    def send(offset, part):
        sources = [
            later
            for later in range(1, reps)
            if later - link_of(later, part, reps) == offset
        ]
        for later in sources:
            copies[later, part].wait_recv()
        total = product(offset, part)
        for later in sources:
            total = total + landed[later, part].astype(jnp.float32)
        if offset == 0 and part == 0:
            grad_ref[here] = total
        else:
            away[offset, part] = total.astype(jnp.bfloat16)
            copies[offset, part].start()

    def weight_step(offset):
        fetch[offset].wait()
        back_t[...] = jnp.transpose(back_ref[offset].astype(jnp.float32)).astype(jnp.bfloat16)

        def columns_at(at, unused):
            cut = pl.ds(pl.multiple_of(at * 512, 512), 512)
            term = jnp.dot(
                back_t[...], normed[offset % slots, :, cut], preferred_element_type=jnp.float32
            )
            if offset == 0:
                weights_total[:, cut] = term
            else:
                weights_total[:, cut] += term
            return unused

        lax.fori_loop(0, width // 512, columns_at, 0)
        if offset + slots < reps:
            fetch[offset + slots].start()

    half_copy = pltpu.make_async_remote_copy(
        src_ref=half_out,
        dst_ref=half_in,
        send_sem=side_send,
        recv_sem=side_recv,
        device_id=across,
        device_id_type=MESH_IDS,
    )
    piece_copies = [
        pltpu.make_async_remote_copy(
            src_ref=piece_out.at[other(offset)[1]],
            dst_ref=pieces_ref.at[there],
            send_sem=piece_send.at[offset],
            recv_sem=piece_recv.at[offset],
            device_id=other(offset),
            device_id_type=MESH_IDS,
        )
        for offset in range(1, reps)
    ]

    def cross_weights():
        cut = pl.ds(pl.multiple_of((1 - here) * half, half), half)
        half_out[...] = weights_total[:, cut].astype(jnp.bfloat16)
        half_copy.start()

    def share_weights():
        half_copy.wait_recv()
        cut = pl.ds(pl.multiple_of(here * half, half), half)
        total = jnp.transpose(weights_total[:, cut] + half_in[...].astype(jnp.float32))
        piece_out[...] = total.astype(jnp.bfloat16).reshape(reps, own_rows, columns)
        pieces_ref[there] = piece_out[there]
        for one in piece_copies:
            one.start()

    far = [step for step in range(reps - 4, 0, -4)]
    todo = []
    for base in far + [0]:
        todo.append((base + 3, 1))
        todo.append((base + 3, 0))
        todo.append((base + 1, 1))
        todo.append((base + 1, 0))
    first = todo[:2]
    for offset, part in first:
        send(offset, part)
    for offset, part in todo[2:6]:
        send(offset, part)
    send(reps - 2, 1)
    send(reps - 2, 0)
    for offset, part in todo[6:]:
        send(offset, part)
    weights = list(range(reps))

    def weight_steps(count):
        for _ in range(min(count, len(weights))):
            weight_step(weights.pop(0))

    last = []
    order = []
    for base in sorted(far, key=lambda step: (-bin(step).count("1"), -step)):
        if base != far[0]:
            order.append((base + 2, 1))
            order.append((base + 2, 0))
    order += [(2, 1), (2, 0)]
    sums = sorted(far, key=lambda step: (-bin(step).count("1"), -step))
    for base in sums:
        last += [(base, 1), (base, 0)]
    if reps == 16:
        plan = [
            (10, 1), (10, 0), 4, (12, 1), (12, 0), 4, (6, 1), (6, 0), 2, (8, 1), 2, (8, 0),
            (2, 1), (2, 0), 4, "cross", (4, 1), (4, 0), "share", (0, 1), (0, 0),
        ]
    else:
        plan = order + last + [reps, "cross", "share", (0, 1), (0, 0)]
    for item in plan:
        if item == "cross":
            weight_steps(reps)
            cross_weights()
        elif item == "share":
            share_weights()
        elif isinstance(item, int):
            weight_steps(item)
        else:
            send(*item)
    copies[0, 1].wait_recv()
    grad_ref[1 - here] = landed[0, 1].astype(jnp.float32)
    for one in piece_copies:
        one.wait()
    half_copy.wait_send()
    for one in copies.values():
        one.wait_send()


def scatter_heads(back, weights, normed, ahead):
    reps, rows, columns = back.shape
    width = normed.shape[2]
    row_count = rows // 2
    half = width // 2
    vmem = pl.BlockSpec(memory_space=pltpu.VMEM)
    anywhere = pl.BlockSpec(memory_space=pl.ANY)
    return pl.pallas_call(
        scatter_kernel,
        out_shape=(
            jax.ShapeDtypeStruct((2, row_count, width), jnp.float32),
            jax.ShapeDtypeStruct((reps, half // reps, columns), jnp.bfloat16),
        ),
        in_specs=[vmem, vmem, anywhere] + [anywhere] * len(ahead),
        out_specs=(vmem, vmem),
        scratch_shapes=[
            pltpu.VMEM((reps, 2, row_count, width), jnp.bfloat16),
            pltpu.VMEM((reps, 2, row_count, width), jnp.bfloat16),
            pltpu.VMEM((4, rows, width), jnp.bfloat16),
            pltpu.VMEM((columns, rows), jnp.bfloat16),
            pltpu.VMEM((columns, width), jnp.bfloat16),
            pltpu.VMEM((columns, width), jnp.float32),
            pltpu.VMEM((columns, half), jnp.bfloat16),
            pltpu.VMEM((columns, half), jnp.bfloat16),
            pltpu.VMEM((reps, half // reps, columns), jnp.bfloat16),
            pltpu.SemaphoreType.DMA((reps,)),
            pltpu.SemaphoreType.DMA((2 * reps,)),
            pltpu.SemaphoreType.DMA((2 * reps,)),
            pltpu.SemaphoreType.DMA,
            pltpu.SemaphoreType.DMA,
            pltpu.SemaphoreType.DMA((reps,)),
            pltpu.SemaphoreType.DMA((reps,)),
        ],
        compiler_params=pltpu.CompilerParams(
            vmem_limit_bytes=KERNEL_VMEM, collective_id=1, has_side_effects=True
        ),
        cost_estimate=pl.CostEstimate(
            flops=14 * 10**9, bytes_accessed=250 << 20, transcendentals=0
        ),
        name="scatter_heads",
    )(back, weights, normed, *ahead)


def mlp_kernel(
    heads_ref,
    tokens_ref,
    gain_ref,
    out_ref,
    output_own,
    output_a,
    output_b,
    output_c,
    output_d,
    gate_in,
    up_own,
    up_other,
    down_own,
    down_other,
    mixed_ref,
    attended,
    down_ref,
    grad_ref,
    branch_ref,
    back_ref,
    gate_ref,
    up_ref,
    down_grad_ref,
    returned,
    mid_ref,
    hidden_ref,
    slope_ref,
    w_output,
    w_in,
    w_out,
    near_away,
    near_landed,
    far_away,
    far_landed,
    down_landed,
    load_sem,
    part_sem,
    send_sem,
    recv_sem,
    heads_send,
    heads_recv,
    back_send,
    back_recv,
):
    here, there = lax.axis_index("grp"), lax.axis_index("rep")
    across = (here, flipped(there, 4))
    sibling = (here, flipped(there, 1))
    groups, heads, row_count, _ = returned.shape
    rows, width = tokens_ref.shape
    half = width // 2
    quarter = half // 4
    own_width = w_out.shape[0]

    loads = [
        pltpu.make_async_copy(output_own, w_output.at[here], load_sem.at[0]),
        pltpu.make_async_copy(gate_in, w_in.at[:, :, pl.ds(0, own_width)], load_sem.at[1]),
        pltpu.make_async_copy(
            up_own, w_in.at[here, :, pl.ds(own_width, own_width)], load_sem.at[2]
        ),
        pltpu.make_async_copy(
            up_other, w_in.at[1 - here, :, pl.ds(own_width, own_width)], load_sem.at[3]
        ),
    ]
    own_part = own_width // 2
    loads += [
        pltpu.make_async_copy(
            down_own,
            w_out.at[pl.ds(pl.multiple_of(here * own_part, own_part), own_part)],
            load_sem.at[4],
        ),
        pltpu.make_async_copy(
            down_other,
            w_out.at[pl.ds(pl.multiple_of((1 - here) * own_part, own_part), own_part)],
            load_sem.at[5],
        ),
    ]
    place = there % 4
    rest = []
    for at, (piece, part) in enumerate(
        (
            (output_a, place),
            (output_b, flipped(place, 2)),
            (output_c, flipped(place, 1)),
            (output_d, 3 - place),
        )
    ):
        rest.append(
            pltpu.make_async_copy(
                piece,
                w_output.at[1 - here, pl.ds(pl.multiple_of(part * quarter, quarter), quarter)],
                part_sem.at[at],
            )
        )
    loads = loads[:1] + rest + loads[1:]
    for one in loads:
        one.start()
    steps = [1 << place for place in range(heads.bit_length() - 1)]

    def other(crossing, offset):
        index = there
        for step in steps:
            if offset & step:
                index = flipped(index, step)
        return (1 - here if crossing else here, index)

    others = [
        (crossing, offset) for offset in range(heads) for crossing in (0, 1) if offset or crossing
    ]
    barrier = pltpu.get_barrier_semaphore()
    for key in others:
        pl.semaphore_signal(barrier, inc=1, device_id=other(*key), device_id_type=MESH_IDS)
    pl.semaphore_wait(barrier, len(others))

    heads_copies, back_copies = [], []
    for at, key in enumerate(others):
        target = other(*key)
        heads_copies.append(
            pltpu.make_async_remote_copy(
                src_ref=heads_ref.at[target[0] * heads + target[1]],
                dst_ref=returned.at[here, there],
                send_sem=heads_send.at[at],
                recv_sem=heads_recv.at[at],
                device_id=target,
                device_id_type=MESH_IDS,
            )
        )
        back_copies.append(
            pltpu.make_async_remote_copy(
                src_ref=returned.at[target[0], target[1]],
                dst_ref=back_ref.at[here * heads + there],
                send_sem=back_send.at[at],
                recv_sem=back_recv.at[at],
                device_id=target,
                device_id_type=MESH_IDS,
            )
        )
    for one in heads_copies[::-1]:
        one.start()
    returned[here, there] = heads_ref[here * heads + there]

    def copy(at, source, target_ref, target):
        return pltpu.make_async_remote_copy(
            src_ref=source,
            dst_ref=target_ref,
            send_sem=send_sem.at[at],
            recv_sem=recv_sem.at[at],
            device_id=target,
            device_id_type=MESH_IDS,
        )

    mid_near = copy(0, mid_ref.at[0], mid_ref.at[1], sibling)
    mid_far = copy(1, mid_ref.at[0], mid_ref.at[2], across)
    mid_on = copy(2, mid_ref.at[2], mid_ref.at[3], sibling)
    grad_near = [copy(3 + at, near_away.at[at], near_landed.at[at], sibling) for at in range(2)]
    grad_far = copy(5, far_away, far_landed, across)
    down_near = [copy(6 + at, near_away.at[at], down_landed.at[at], sibling) for at in range(2)]
    gate_cross = copy(
        8, w_in.at[1 - here, :, pl.ds(0, own_width)], gate_ref, (1 - here, there)
    )
    up_out = pltpu.make_async_copy(
        w_in.at[:, :, pl.ds(own_width, own_width)], up_ref, load_sem.at[0]
    )
    down_out = pltpu.make_async_copy(w_out, down_grad_ref, load_sem.at[1])

    for one in heads_copies:
        one.wait()
    for group in range(groups):
        for head in range(heads):
            attended[
                group * row_count : (group + 1) * row_count, head * LANES : (head + 1) * LANES
            ] = returned[group, head]
    for one in loads[:5]:
        one.wait()
    wide = 512

    def mix(at, unused):
        cut = pl.ds(pl.multiple_of(at * wide, wide), wide)
        mixed_ref[:, cut] = (
            tokens_ref[:, cut].astype(jnp.float32)
            + jnp.dot(attended[:, :half], w_output[0, :, cut], preferred_element_type=jnp.float32)
            + jnp.dot(attended[:, half:], w_output[1, :, cut], preferred_element_type=jnp.float32)
        )
        return unused

    lax.fori_loop(0, width // wide, mix, 0)
    tile = 32

    def norm_rows(at, unused):
        cut = pl.ds(pl.multiple_of(at * tile, tile), tile)
        values = mixed_ref[cut, :]
        mid_ref[0, cut, :] = (values * rms_scale(values) * gain_ref[0:1, :]).astype(jnp.bfloat16)
        return unused

    lax.fori_loop(0, rows // tile, norm_rows, 0)
    mid_far.start()
    mid_near.start()
    for one in loads[5:]:
        one.wait()
    narrow_tile = 256

    def forward(slot):
        def columns(at, unused):
            cut = pl.ds(pl.multiple_of(at * narrow_tile, narrow_tile), narrow_tile)
            up_cut = pl.ds(pl.multiple_of(own_width + at * narrow_tile, narrow_tile), narrow_tile)

            def project(cols):
                return jnp.dot(
                    mid_ref[slot, :, :half], w_in[0, :, cols], preferred_element_type=jnp.float32
                ) + jnp.dot(
                    mid_ref[slot, :, half:], w_in[1, :, cols], preferred_element_type=jnp.float32
                )

            gate_pre, up_pre = project(cut), project(up_cut)
            grad_hidden = contract(out_ref[slot], w_out[cut, :], 1, 1)
            gate_sig = jax.nn.sigmoid(gate_pre)
            gate_silu = gate_pre * gate_sig
            hidden_ref[slot, :, cut] = (gate_silu * up_pre).astype(jnp.bfloat16)
            slope_ref[slot, :, cut] = (
                grad_hidden * up_pre * gate_sig * (1.0 + gate_pre * (1.0 - gate_sig))
            ).astype(jnp.bfloat16)
            slope_ref[slot, :, up_cut] = (grad_hidden * gate_silu).astype(jnp.bfloat16)
            return unused

        lax.fori_loop(0, own_width // narrow_tile, columns, 0)

    def backward(slot, finish):
        for at in range(2):

            def columns(step, unused):
                cut = pl.ds(pl.multiple_of(step * wide, wide), wide)
                whole = pl.ds(pl.multiple_of(at * half + step * wide, wide), wide)
                finish(whole, contract(slope_ref[slot], w_in[at, cut, :], 1, 1))
                return unused

            lax.fori_loop(0, half // wide, columns, 0)

    def down(slot, finish):
        def columns(step, unused):
            cut = pl.ds(pl.multiple_of(step * wide, wide), wide)
            finish(
                cut, jnp.dot(hidden_ref[slot], w_out[:, cut], preferred_element_type=jnp.float32)
            )
            return unused

        lax.fori_loop(0, width // wide, columns, 0)

    def into(target, at):
        def finish(cut, values):
            target[at, :, cut] = values.astype(jnp.bfloat16)

        return finish

    forward(0)
    mid_near.wait_recv()
    forward(1)
    backward(1, into(near_away, 0))
    grad_near[0].start()

    def keep(cut, values):
        grad_ref[:, cut] = values

    backward(0, keep)
    mid_far.wait_recv()
    mid_on.start()
    forward(2)
    mid_on.wait_recv()
    forward(3)
    backward(3, into(near_away, 1))
    grad_near[1].start()
    grad_near[1].wait_recv()

    def add_near(cut, values):
        far_away[:, cut] = (values + near_landed[1, :, cut].astype(jnp.float32)).astype(
            jnp.bfloat16
        )

    backward(2, add_near)
    grad_far.start()

    def turned(values):
        flat = values.reshape(4 * rows, values.shape[2]).astype(jnp.float32)
        return jnp.transpose(flat).astype(jnp.bfloat16)

    def in_grads(at):
        def some_rows(step, unused):
            cut = pl.ds(pl.multiple_of(step * narrow_tile, narrow_tile), narrow_tile)
            source = pl.ds(pl.multiple_of(at * half + step * narrow_tile, narrow_tile), narrow_tile)
            left = turned(mid_ref[:, :, source])

            def columns(place_at, unused):
                cols = pl.ds(pl.multiple_of(place_at * wide, wide), wide)
                right = slope_ref[:, :, cols].reshape(4 * rows, wide)
                w_in[at, cut, cols] = jnp.dot(
                    left, right, preferred_element_type=jnp.float32
                ).astype(jnp.bfloat16)
                return unused

            return lax.fori_loop(0, 2 * own_width // wide, columns, unused)

        lax.fori_loop(0, half // narrow_tile, some_rows, 0)

    in_grads(1 - here)
    gate_cross.start()
    for at in range(2):
        grad_near[at].wait_send()
        down(2 * at + 1, into(near_away, at))
        down_near[at].start()
    in_grads(here)
    up_out.start()
    for at in range(2):
        down_near[at].wait_recv()

        def add_down(cut, values):
            down_ref[at, :, cut] = (values + down_landed[at, :, cut].astype(jnp.float32)).astype(
                jnp.bfloat16
            )

        down(2 * at, add_down)

    def down_rows(step, unused):
        cut = pl.ds(pl.multiple_of(step * narrow_tile, narrow_tile), narrow_tile)
        left = turned(hidden_ref[:, :, cut])

        def columns(place_at, unused):
            cols = pl.ds(pl.multiple_of(place_at * wide, wide), wide)
            right = out_ref[:, :, cols].reshape(4 * rows, wide)
            w_out[cut, cols] = jnp.dot(left, right, preferred_element_type=jnp.float32).astype(
                jnp.bfloat16
            )
            return unused

        return lax.fori_loop(0, width // wide, columns, unused)

    lax.fori_loop(0, own_width // narrow_tile, down_rows, 0)
    down_out.start()
    grad_near[0].wait_recv()
    grad_far.wait_recv()

    def norm_back(at, unused):
        cut = pl.ds(pl.multiple_of(at * tile, tile), tile)
        grad_mid = (
            grad_ref[cut, :]
            + near_landed[0, cut, :].astype(jnp.float32)
            + far_landed[cut, :].astype(jnp.float32)
        )
        values = mixed_ref[cut, :]
        inverse = rms_scale(values)
        normed = values * inverse
        weighted = grad_mid * gain_ref[0:1, :]
        grad = out_ref[0, cut, :].astype(jnp.float32) + inverse * (
            weighted - normed * jnp.mean(weighted * normed, axis=-1, keepdims=True)
        )
        grad_ref[cut, :] = grad
        branch_ref[cut, :] = grad.astype(jnp.bfloat16)
        return unused

    lax.fori_loop(0, rows // tile, norm_back, 0)
    for head in range(0, heads, 4):
        at = head * LANES // half
        start = head * LANES - at * half
        values = contract(
            branch_ref[...], w_output[at, pl.ds(start, 4 * LANES), :], 1, 1, jnp.bfloat16
        )
        for group in range(groups):
            for step in range(4):
                returned[group, head + step] = values[
                    group * row_count : (group + 1) * row_count, step * LANES : (step + 1) * LANES
                ]
    for one in back_copies[::-1]:
        one.start()
    back_ref[here * heads + there] = returned[here, there]
    gate_cross.wait()

    def add_gate(at, unused):
        cut = pl.ds(pl.multiple_of(at * tile, tile), tile)
        gate_ref[cut, :] = (
            gate_ref[cut, :].astype(jnp.float32)
            + w_in[here, cut, pl.ds(0, own_width)].astype(jnp.float32)
        ).astype(jnp.bfloat16)
        return unused

    lax.fori_loop(0, half // tile, add_gate, 0)
    up_out.wait()
    down_out.wait()
    for one in back_copies:
        one.wait()
    for one in [mid_near, mid_far, mid_on, grad_far] + down_near:
        one.wait_send()


def mlp(heads, tokens, gain, out_quad, output_parts, in_parts, down_parts):
    count, row_count, _ = heads.shape
    groups = lax.axis_size("grp")
    rows, width = tokens.shape
    half = width // 2
    own_width = in_parts[0].shape[2]
    vmem = pl.BlockSpec(memory_space=pltpu.VMEM)
    anywhere = pl.BlockSpec(memory_space=pl.ANY)
    low, full = jnp.bfloat16, jnp.float32
    others = pltpu.SemaphoreType.DMA((count - 1,))
    return pl.pallas_call(
        mlp_kernel,
        out_shape=(
            jax.ShapeDtypeStruct((rows, width), full),
            jax.ShapeDtypeStruct((rows, width), low),
            jax.ShapeDtypeStruct((2, rows, width), low),
            jax.ShapeDtypeStruct((rows, width), full),
            jax.ShapeDtypeStruct((rows, width), low),
            jax.ShapeDtypeStruct((count, row_count, LANES), low),
            jax.ShapeDtypeStruct((half, own_width), low),
            jax.ShapeDtypeStruct((2, half, own_width), low),
            jax.ShapeDtypeStruct((own_width, width), low),
        ),
        in_specs=[vmem] * 4 + [anywhere] * 10,
        out_specs=(vmem,) * 7 + (anywhere,) * 2,
        scratch_shapes=[
            pltpu.VMEM((groups, count // groups, row_count, LANES), low),
            pltpu.VMEM((4, rows, width), low),
            pltpu.VMEM((4, rows, own_width), low),
            pltpu.VMEM((4, rows, 2 * own_width), low),
            pltpu.VMEM((2, half, width), low),
            pltpu.VMEM((2, half, 2 * own_width), low),
            pltpu.VMEM((own_width, width), low),
            pltpu.VMEM((2, rows, width), low),
            pltpu.VMEM((2, rows, width), low),
            pltpu.VMEM((rows, width), low),
            pltpu.VMEM((rows, width), low),
            pltpu.VMEM((2, rows, width), low),
            pltpu.SemaphoreType.DMA((6,)),
            pltpu.SemaphoreType.DMA((4,)),
            pltpu.SemaphoreType.DMA((9,)),
            pltpu.SemaphoreType.DMA((9,)),
            others,
            others,
            others,
            others,
        ],
        compiler_params=pltpu.CompilerParams(
            vmem_limit_bytes=62 * 1024 * 1024, collective_id=2, has_side_effects=True
        ),
        cost_estimate=pl.CostEstimate(
            flops=150 * 10**9, bytes_accessed=150 << 20, transcendentals=0
        ),
        name="mlp",
    )(heads, tokens, gain, out_quad, *output_parts, *in_parts, *down_parts)


def after_kernel(*refs):
    pass


def after(values, ahead):
    anywhere = pl.BlockSpec(memory_space=pl.ANY)
    return pl.pallas_call(
        after_kernel,
        out_shape=tuple(jax.ShapeDtypeStruct(one.shape, one.dtype) for one in values),
        in_specs=[anywhere] * (len(values) + 1),
        out_specs=(anywhere,) * len(values),
        input_output_aliases={at: at for at in range(len(values))},
        name="after",
    )(*values, ahead)


def heads_body(
    tokens,
    attn_gain,
    w_query,
    w_key,
    w_value,
    w_output,
    mlp_gain,
    w_gate,
    w_up,
    w_down,
    out_grad,
    lengths,
):
    groups, reps = lax.axis_size("grp"), lax.axis_size("rep")
    here, there = lax.axis_index("grp"), lax.axis_index("rep")
    micro_count, row_count, width = tokens.shape
    rows = micro_count * row_count
    hidden_width = w_gate.shape[1]
    own_width = hidden_width // (2 * groups)

    out_rows = out_grad.reshape(rows, width)
    (
        gathered_rows,
        qkv,
        w_heads,
        gate_in,
        up_own,
        down_own,
        output_part,
        out_own,
        gains,
    ) = gather_heads(
        tokens,
        (attn_gain, mlp_gain),
        w_query,
        w_key,
        w_value,
        w_gate,
        w_up,
        w_down,
        w_output,
        out_rows,
    )
    gain_one = gains[:, 0].reshape(width).astype(jnp.float32)
    gain_two = gains[:, 1].reshape(width).astype(jnp.float32)
    inputs = tokens.astype(jnp.float32)

    output_beside = swap(output_part, 0, 2)
    output_parts = (
        w_output,
        output_part,
        output_beside,
        swap(output_part, 0, 1),
        swap(output_beside, 0, 1),
    )
    in_parts = (gate_in, up_own, swap(up_own, 1, 0))
    down_parts = (down_own, swap(down_own, 1, 0))
    out_far = swap(out_own, 0, 4)
    out_quad = jnp.stack([out_rows, swap(out_own, 0, 1), out_far, swap(out_far, 0, 1)], axis=0)

    tables = attention_tables(lengths, here, there, row_count)
    attended, out_heads, log_sum, query, key, value = attend(tables, qkv)
    (
        mixed,
        attn_rows,
        down_sums,
        grad_mixed,
        grad_branch,
        grad_heads,
        gate_part,
        up_part,
        down_part,
    ) = mlp(
        attended,
        tokens.reshape(rows, width),
        jnp.broadcast_to(gain_two[None], (8, width)),
        out_quad,
        output_parts,
        in_parts,
        down_parts,
    )

    own_rows = width // (groups * reps)
    high = reps // 8
    high_steps = [step for step in (8 << place for place in range(8)) if step < reps]
    bit = {step: (there // step) % 2 for step in [1, 2, 4] + high_steps}

    def send(parts, axis, step):
        flag, grp_step, rep_step = (here, 1, 0) if step == 0 else (bit[step], 0, step)
        return pick(parts, flag, axis), swap(pick(parts, 1 - flag, axis), grp_step, rep_step)

    def add(kept, arrived):
        return narrow(kept.astype(jnp.float32) + arrived.astype(jnp.float32))

    def over(parts, axis, step):
        return add(*send(parts, axis, step))

    def over_high(parts, axis):
        for step in high_steps:
            shape = parts.shape
            count = shape[axis] // 2
            parts = parts.reshape(shape[:axis] + (count, 2) + shape[axis + 1 :])
            parts = over(parts, axis + 1, step)
        return parts.reshape(parts.shape[:axis] + parts.shape[axis + 1 :])

    by_owner = (groups, high, 2, 2, 2, own_rows)
    up_kept, up_sent = send(up_part.reshape(by_owner + (own_width,)), 0, 0)
    down_kept, down_sent = send(down_part.reshape(groups, high, 2, LANES, width), 2, 2)
    output_grad = contract(attn_rows, grad_branch, 0, 0, jnp.bfloat16)
    output_grad = over(output_grad.reshape(by_owner + (width,)), 4, 1)
    output_kept, output_sent = send(output_grad, 2, 4)
    sums_sent = swap(down_sums[1], 0, 4)

    back = attend_back(tables, query, key, value, out_heads, log_sum, grad_heads)

    up_sent, down_sent, output_sent, sums_sent = after(
        (up_sent, down_sent, output_sent, sums_sent), back
    )
    up_part = add(up_kept, up_sent)
    down_part = add(down_kept, down_sent)
    output_grad = add(output_kept, output_sent)
    early = (up_part, down_part, output_grad)
    gate_kept, gate_sent = send(gate_part.reshape(by_owner[1:] + (own_width,)), 2, 2)
    up_kept, up_sent = send(up_part, 0, 8)
    down_kept, down_sent = send(down_part, 0, 0)
    output_kept, output_sent = send(output_grad, 0, 0)
    grad_in, heads_grad = scatter_heads(
        back.reshape(reps, groups * row_count, 3 * LANES), w_heads, gathered_rows, early
    )
    gate_sent, up_sent, down_sent, output_sent = after(
        (gate_sent, up_sent, down_sent, output_sent), grad_in
    )
    gate_part = over_high(add(gate_kept, gate_sent), 0)
    up_part = over(add(up_kept, up_sent), 1, 2)
    down_grad = over_high(add(down_kept, down_sent), 0).astype(jnp.float32)
    output_grad = over_high(over(add(output_kept, output_sent), 1, 2), 0).astype(jnp.float32)
    block_out = (
        mixed + down_sums[0].astype(jnp.float32) + sums_sent.astype(jnp.float32)
    ).astype(jnp.bfloat16)

    quad_part = jnp.concatenate([gate_part, up_part], axis=-1)
    kept = pick(quad_part, bit[4], 0)
    crossed = swap(pick(quad_part, 1 - bit[4], 0), 0, 4)
    columns = []
    for part in (kept, crossed):
        columns.append(pick(part, bit[1], 0))
        columns.append(swap(pick(part, 1 - bit[1], 0), 0, 1))

    def by_bit(flag, own, other):
        return jnp.where(
            flag == 0, jnp.stack([own, other], axis=1), jnp.stack([other, own], axis=1)
        )

    pieces = by_bit(
        bit[4], by_bit(bit[1], columns[0], columns[1]), by_bit(bit[1], columns[2], columns[3])
    )
    pieces = pieces.reshape(own_rows, 2, 2, 2, groups, high, 2, LANES)
    pieces = pieces.transpose(3, 0, 4, 5, 1, 6, 2, 7).reshape(2, own_rows, hidden_width)
    gate_grad, up_grad = pieces[0].astype(jnp.float32), pieces[1].astype(jnp.float32)

    grad_norm_in, unused_gain = norm_backward(
        inputs.reshape(rows, width), gain_one, grad_in.reshape(rows, width)
    )
    token_grad = (grad_mixed + grad_norm_in).astype(jnp.bfloat16)

    heads_grad = (
        heads_grad.reshape(reps, own_rows, 3, LANES)
        .transpose(2, 1, 0, 3)
        .reshape(3, own_rows, width)
        .astype(jnp.float32)
    )

    def own_part(value):
        return lax.dynamic_slice_in_dim(value, there * own_rows, own_rows, axis=0).astype(
            jnp.float32
        )

    attn_gain_grad = (
        jnp.sum(own_part(w_query) * heads_grad[0], axis=1)
        + jnp.sum(own_part(w_key) * heads_grad[1], axis=1)
        + jnp.sum(own_part(w_value) * heads_grad[2], axis=1)
    ) / own_part(attn_gain)
    mlp_gain_grad = (
        jnp.sum(own_part(w_gate) * gate_grad, axis=1) + jnp.sum(own_part(w_up) * up_grad, axis=1)
    ) / own_part(mlp_gain)
    block_shape = tokens.shape
    return (
        block_out.reshape(block_shape),
        token_grad.reshape(block_shape),
        attn_gain_grad,
        heads_grad[0],
        heads_grad[1],
        heads_grad[2],
        output_grad,
        mlp_gain_grad,
        gate_grad,
        up_grad,
        down_grad,
    )


def pick_body(*arrays):
    tokens = arrays[0]
    groups, reps = lax.axis_size("grp"), lax.axis_size("rep")
    fits = (
        groups == 2
        and tokens.shape[0] == groups
        and tokens.shape[2] == reps * LANES
        and reps == 16
        and reps & (reps - 1) == 0
        and tokens.shape[1] % UNIT_PAIR == 0
        and arrays[7].shape[1] == groups * reps * LANES
    )
    return heads_body(*arrays) if fits else ring_body(*arrays)


def solution(mesh):
    in_specs = (
        P(None, ("grp", "rep"), None),
        P("grp"),
        P("grp", None),
        P("grp", None),
        P("grp", None),
        P("grp", None),
        P("grp"),
        P("grp", None),
        P("grp", None),
        P("grp", None),
        P(None, ("grp", "rep"), None),
        P(),
    )
    out_specs = (
        P(None, ("grp", "rep"), None),
        P(None, ("grp", "rep"), None),
        P(("grp", "rep")),
        P(("grp", "rep"), None),
        P(("grp", "rep"), None),
        P(("grp", "rep"), None),
        P(("grp", "rep"), None),
        P(("grp", "rep")),
        P(("grp", "rep"), None),
        P(("grp", "rep"), None),
        P(("grp", "rep"), None),
    )
    return jax.shard_map(pick_body, mesh=mesh, in_specs=in_specs, out_specs=out_specs, check_vma=False)
```

```python
import functools
import math

import jax
import jax.numpy as jnp
from jax import lax
from jax.experimental import pallas as pl
from jax.experimental.pallas import tpu as pltpu
from jax.sharding import PartitionSpec as P

HD = 64
WINDOW = 2048


epsilon = 1e-05
rope_base = 10000.0
masked_score = -1e30
BOTH = ("grp", "rep")
LANES = 128
UNIT_BLOCK = 8
UNIT_PAIR = 16
KERNEL_VMEM = 56 * 1024 * 1024
SCATTER_REFS = 18


def from_behind(value, axis, steps):
    count = lax.axis_size(axis)
    first, last = (max(0, -steps), min(count, count - steps))
    return lax.ppermute(value, axis, [(source, source + steps) for source in range(first, last)])


def rms_scale(values):
    return lax.rsqrt(jnp.mean(values * values, axis=-1, keepdims=True) + epsilon)


def norm_backward(values, gain_full, grad_normed):
    inverse = rms_scale(values)
    normed = values * inverse
    gain_grad = jnp.sum(grad_normed * normed, axis=0)
    weighted = grad_normed * gain_full
    return (
        inverse * (weighted - normed * jnp.mean(weighted * normed, axis=-1, keepdims=True)),
        gain_grad,
    )


def rotary(values, cosine, sine_table):
    half_width = values.shape[-1] // 2
    first_half = values[..., :half_width]
    second_half = values[..., half_width:]
    return jnp.concatenate(
        [
            first_half * cosine - second_half * sine_table,
            second_half * cosine + first_half * sine_table,
        ],
        axis=-1,
    )


def pick_rows(rows_block, row_ids):
    return jnp.take(rows_block, row_ids, axis=0)


def take_rows(values, row_ids):
    return jax.vmap(pick_rows)(values, row_ids)


def gather_attn(attn_gain, w_query, w_key, w_value, w_output):
    return (
        lax.all_gather(attn_gain, "grp", axis=0, tiled=True),
        lax.all_gather(w_query, "grp", axis=0, tiled=True),
        lax.all_gather(w_key, "grp", axis=0, tiled=True),
        lax.all_gather(w_value, "grp", axis=0, tiled=True),
        lax.all_gather(w_output, "grp", axis=0, tiled=True),
    )


def gather_mlp(mlp_gain, w_gate, w_up, w_down):
    return (
        lax.all_gather(mlp_gain, "grp", axis=0, tiled=True),
        lax.all_gather(w_gate, "grp", axis=0, tiled=True),
        lax.all_gather(w_up, "grp", axis=0, tiled=True),
        lax.all_gather(w_down, "grp", axis=0, tiled=True),
    )


def reduce_attn(gain_grad, query_grad, key_grad, value_grad, output_grad):
    return (
        lax.psum_scatter(gain_grad, ("grp", "rep"), scatter_dimension=0, tiled=True),
        lax.psum_scatter(query_grad, ("grp", "rep"), scatter_dimension=0, tiled=True),
        lax.psum_scatter(key_grad, ("grp", "rep"), scatter_dimension=0, tiled=True),
        lax.psum_scatter(value_grad, ("grp", "rep"), scatter_dimension=0, tiled=True),
        lax.psum_scatter(output_grad, ("grp", "rep"), scatter_dimension=0, tiled=True),
    )


def reduce_mlp(gain_grad, gate_grad, up_grad, down_grad):
    return (
        lax.psum_scatter(gain_grad, ("grp", "rep"), scatter_dimension=0, tiled=True),
        lax.psum_scatter(gate_grad, ("grp", "rep"), scatter_dimension=0, tiled=True),
        lax.psum_scatter(up_grad, ("grp", "rep"), scatter_dimension=0, tiled=True),
        lax.psum_scatter(down_grad, ("grp", "rep"), scatter_dimension=0, tiled=True),
    )


def pass_on(carried, unused):
    arrived = from_behind(carried, ("grp", "rep"), 1)
    return (arrived, arrived)


def pass_back(running, portion):
    arrived = from_behind(running.astype(jnp.bfloat16), ("grp", "rep"), -1).astype(running.dtype)
    return (arrived + portion, None)


def ring_body(
    tokens,
    attn_gain,
    w_query,
    w_key,
    w_value,
    w_output,
    mlp_gain,
    w_gate,
    w_up,
    w_down,
    out_grad,
    lengths,
):
    devices = lax.axis_size(("grp", "rep"))
    rank_here = lax.axis_index(("grp", "rep"))
    micro_count, row_count, model_width = tokens.shape
    per_dev = row_count // devices
    head_count = model_width // HD
    reach_count = (WINDOW + row_count - 2) // row_count
    head_group = math.gcd(head_count, 4)
    group_count = head_count // head_group
    score_scale = 1.0 / math.sqrt(HD)
    unit_ids = jnp.arange(row_count, dtype=jnp.int32)
    seq_ends = jnp.cumsum(lengths, axis=1)
    starts = seq_ends - lengths
    seq_order = jnp.arange(lengths.shape[1], dtype=jnp.int32)
    earlier = seq_order[None, :] < seq_order[:, None]
    dealt_start = jnp.sum(jnp.where(earlier[None], lengths[:, None, :], 0), axis=2)
    seq_of = jnp.sum((seq_ends[:, None, :] <= unit_ids[None, :, None]).astype(jnp.int32), axis=2)
    seq_dealt = jnp.take_along_axis(dealt_start, seq_of, axis=1)
    unit_of = seq_dealt + unit_ids[None, :] - jnp.take_along_axis(starts, seq_of, axis=1)
    micro_ids = jnp.arange(micro_count, dtype=jnp.int32)[:, None]
    source_unit = (
        jnp.zeros((micro_count, row_count), jnp.int32)
        .at[micro_ids, unit_of]
        .set(jnp.broadcast_to(unit_ids[None, :], unit_of.shape))
    )
    unit_begin = (
        jnp.zeros((micro_count, row_count), jnp.int32).at[micro_ids, unit_of].set(seq_dealt)
    )
    local_ids = jnp.arange(row_count, dtype=jnp.int32)
    local_step = local_ids % per_dev
    local_source = local_ids // per_dev
    distance = jnp.arange(reach_count + 1, dtype=jnp.int32)
    owner_dev = rank_here - distance
    owner_ok = owner_dev >= 0
    owner_unit = jnp.maximum(owner_dev, 0)[:, None] * per_dev + local_step[None, :]
    key_begin = unit_begin[:, owner_unit]
    key_pos = (owner_unit[None] - key_begin) * devices + local_source[None, None, :]
    query_begin = key_begin[:, 0]
    query_pos = key_pos[:, 0]
    allowed = (
        owner_ok[None, None, :, None]
        & (query_begin[:, :, None, None] == key_begin[:, None, :, :])
        & (key_pos[:, None, :, :] <= query_pos[:, :, None, None])
        & (query_pos[:, :, None, None] - key_pos[:, None, :, :] < WINDOW)
    )
    mask_full = allowed[:, None]
    half_width = HD // 2
    frequency = jnp.power(rope_base, -2.0 * jnp.arange(half_width, dtype=jnp.float32) / HD)
    angles = query_pos.astype(jnp.float32)[:, :, None] * frequency[None, None, :]
    cosine = jnp.cos(angles)[:, :, None, :]
    sine_table = jnp.sin(angles)[:, :, None, :]
    head_shape = (micro_count, row_count, head_count, HD)
    block_shape = (micro_count, row_count, model_width)
    gathered = gather_attn(attn_gain, w_query, w_key, w_value, w_output)
    gain_one = gathered[0].astype(jnp.float32)
    inputs = tokens.astype(jnp.float32).reshape(micro_count * row_count, model_width)
    normed_in = (inputs * rms_scale(inputs) * gain_one).astype(jnp.bfloat16)
    queries = jnp.dot(normed_in, gathered[1], preferred_element_type=jnp.float32).astype(
        jnp.bfloat16
    )
    keys_in = jnp.dot(normed_in, gathered[2], preferred_element_type=jnp.float32).astype(
        jnp.bfloat16
    )
    values_in = jnp.dot(normed_in, gathered[3], preferred_element_type=jnp.float32).astype(
        jnp.bfloat16
    )
    dealt = (
        lax.all_to_all(
            take_rows(queries.reshape(block_shape), source_unit),
            ("grp", "rep"),
            split_axis=1,
            concat_axis=1,
            tiled=True,
        ),
        lax.all_to_all(
            take_rows(keys_in.reshape(block_shape), source_unit),
            ("grp", "rep"),
            split_axis=1,
            concat_axis=1,
            tiled=True,
        ),
        lax.all_to_all(
            take_rows(values_in.reshape(block_shape), source_unit),
            ("grp", "rep"),
            split_axis=1,
            concat_axis=1,
            tiled=True,
        ),
    )
    rot_q = rotary(dealt[0].reshape(head_shape).astype(jnp.float32), cosine, sine_table).astype(
        jnp.bfloat16
    )
    rot_k = rotary(dealt[1].reshape(head_shape).astype(jnp.float32), cosine, sine_table).astype(
        jnp.bfloat16
    )
    own_pair = jnp.stack([rot_k.reshape(block_shape), dealt[2]], axis=0)
    last_pair, farther = lax.scan(pass_on, own_pair, None, length=reach_count)
    context = jnp.concatenate([own_pair[None], farther], axis=0).reshape(
        reach_count + 1, 2, micro_count, row_count, head_count, HD
    )

    def group_scores(query_part, pair_part):
        scores = (
            jnp.einsum(
                "mqge,dmkge->mgqdk", query_part, pair_part[:, 0], preferred_element_type=jnp.float32
            )
            * score_scale
        )
        return jnp.where(mask_full, scores, masked_score)

    def forward_group(group_index, carried):
        attended_all, log_all = carried
        head_start = group_index * head_group
        query_part = lax.dynamic_slice_in_dim(rot_q, head_start, head_group, axis=2)
        pair_part = lax.dynamic_slice_in_dim(context, head_start, head_group, axis=4)
        scores = group_scores(query_part, pair_part)
        row_max = jnp.max(scores, axis=(3, 4), keepdims=True)
        weights_exp = jnp.exp(scores - row_max)
        row_sum = jnp.sum(weights_exp, axis=(3, 4), keepdims=True)
        soft_probs = (weights_exp / row_sum).astype(jnp.bfloat16)
        attended = jnp.einsum(
            "mgqdk,dmkge->mqge", soft_probs, pair_part[:, 1], preferred_element_type=jnp.float32
        ).astype(jnp.bfloat16)
        attended_all = lax.dynamic_update_slice_in_dim(attended_all, attended, head_start, axis=2)
        log_all = lax.dynamic_update_slice_in_dim(
            log_all, row_max + jnp.log(row_sum), head_start, axis=1
        )
        return (attended_all, log_all)

    attended_heads, log_sum = lax.fori_loop(
        0,
        group_count,
        forward_group,
        (
            jnp.zeros(head_shape, jnp.bfloat16),
            jnp.zeros((micro_count, head_count, row_count, 1, 1), jnp.float32),
        ),
    )
    returned = lax.all_to_all(
        attended_heads.reshape(block_shape), ("grp", "rep"), split_axis=1, concat_axis=1, tiled=True
    )
    attn_rows = take_rows(returned, unit_of).reshape(micro_count * row_count, model_width)
    mixed = inputs + jnp.dot(attn_rows, gathered[4], preferred_element_type=jnp.float32)
    mlp_set = gather_mlp(mlp_gain, w_gate, w_up, w_down)
    gain_two = mlp_set[0].astype(jnp.float32)
    normed_mid = (mixed * rms_scale(mixed) * gain_two).astype(jnp.bfloat16)
    gate_pre = jnp.dot(normed_mid, mlp_set[1], preferred_element_type=jnp.float32)
    up_pre = jnp.dot(normed_mid, mlp_set[2], preferred_element_type=jnp.float32)
    gate_sig = jax.nn.sigmoid(gate_pre)
    gate_silu = gate_pre * gate_sig
    hidden = (gate_silu * up_pre).astype(jnp.bfloat16)
    block_out = (mixed + jnp.dot(hidden, mlp_set[3], preferred_element_type=jnp.float32)).astype(
        jnp.bfloat16
    )
    mlp_set = gather_mlp(mlp_gain, w_gate, w_up, w_down)
    out_rows = out_grad.reshape(micro_count * row_count, model_width)
    down_grad = jnp.einsum("tf,td->fd", hidden, out_rows, preferred_element_type=jnp.float32)
    grad_hidden = jnp.einsum("td,fd->tf", out_rows, mlp_set[3], preferred_element_type=jnp.float32)
    grad_gate = (grad_hidden * up_pre * gate_sig * (1.0 + gate_pre * (1.0 - gate_sig))).astype(
        jnp.bfloat16
    )
    grad_up = (grad_hidden * gate_silu).astype(jnp.bfloat16)
    gate_grad = jnp.einsum("td,tf->df", normed_mid, grad_gate, preferred_element_type=jnp.float32)
    up_grad = jnp.einsum("td,tf->df", normed_mid, grad_up, preferred_element_type=jnp.float32)
    grad_mid = jnp.einsum(
        "tf,df->td", grad_gate, mlp_set[1], preferred_element_type=jnp.float32
    ) + jnp.einsum("tf,df->td", grad_up, mlp_set[2], preferred_element_type=jnp.float32)
    grad_norm_mid, mlp_gain_grad = norm_backward(mixed, gain_two, grad_mid)
    grad_mixed = out_rows.astype(jnp.float32) + grad_norm_mid
    mlp_sums = reduce_mlp(mlp_gain_grad, gate_grad, up_grad, down_grad)
    gathered = gather_attn(attn_gain, w_query, w_key, w_value, w_output)
    grad_branch = grad_mixed.astype(jnp.bfloat16)
    output_grad = jnp.einsum(
        "td,te->de", attn_rows, grad_branch, preferred_element_type=jnp.float32
    )
    grad_att = jnp.einsum(
        "te,de->td", grad_branch, gathered[4], preferred_element_type=jnp.float32
    ).astype(jnp.bfloat16)
    grad_dealt = lax.all_to_all(
        take_rows(grad_att.reshape(block_shape), source_unit),
        ("grp", "rep"),
        split_axis=1,
        concat_axis=1,
        tiled=True,
    )
    grad_heads = grad_dealt.reshape(head_shape)

    def backward_group(group_index, carried):
        query_total, pair_total = carried
        head_start = group_index * head_group
        query_part = lax.dynamic_slice_in_dim(rot_q, head_start, head_group, axis=2)
        grad_part = lax.dynamic_slice_in_dim(grad_heads, head_start, head_group, axis=2)
        pair_part = lax.dynamic_slice_in_dim(context, head_start, head_group, axis=4)
        log_part = lax.dynamic_slice_in_dim(log_sum, head_start, head_group, axis=1)
        scores = group_scores(query_part, pair_part)
        soft_probs = jnp.exp(scores - log_part)
        grad_probs = jnp.einsum(
            "mqge,dmkge->mgqdk", grad_part, pair_part[:, 1], preferred_element_type=jnp.float32
        )
        inner_sum = jnp.sum(soft_probs * grad_probs, axis=(3, 4), keepdims=True)
        grad_scores = (soft_probs * (grad_probs - inner_sum)).astype(jnp.bfloat16)
        query_piece = (
            jnp.einsum(
                "mgqdk,dmkge->mqge",
                grad_scores,
                pair_part[:, 0],
                preferred_element_type=jnp.float32,
            )
            * score_scale
        )
        key_part = (
            jnp.einsum(
                "mgqdk,mqge->dmkge", grad_scores, query_part, preferred_element_type=jnp.float32
            )
            * score_scale
        )
        value_part = jnp.einsum(
            "mgqdk,mqge->dmkge",
            soft_probs.astype(jnp.bfloat16),
            grad_part,
            preferred_element_type=jnp.float32,
        )
        query_total = lax.dynamic_update_slice_in_dim(query_total, query_piece, head_start, axis=2)
        pair_total = lax.dynamic_update_slice_in_dim(
            pair_total, jnp.stack([key_part, value_part], axis=1), head_start, axis=4
        )
        return (query_total, pair_total)

    query_total, pair_total = lax.fori_loop(
        0,
        group_count,
        backward_group,
        (
            jnp.zeros(head_shape, jnp.float32),
            jnp.zeros((reach_count + 1, 2) + head_shape, jnp.float32),
        ),
    )
    partials = pair_total.reshape(reach_count + 1, 2, micro_count, row_count, model_width)
    own_total, unused_out = lax.scan(
        pass_back, partials[reach_count], partials[:reach_count], reverse=True
    )
    query_back = rotary(query_total, cosine, -sine_table).astype(jnp.bfloat16)
    key_back = rotary(own_total[0].reshape(head_shape), cosine, -sine_table).astype(jnp.bfloat16)
    value_back = own_total[1].astype(jnp.bfloat16)
    grad_back = (
        lax.all_to_all(
            query_back.reshape(block_shape), ("grp", "rep"), split_axis=1, concat_axis=1, tiled=True
        ),
        lax.all_to_all(
            key_back.reshape(block_shape), ("grp", "rep"), split_axis=1, concat_axis=1, tiled=True
        ),
        lax.all_to_all(value_back, ("grp", "rep"), split_axis=1, concat_axis=1, tiled=True),
    )
    query_rows = take_rows(grad_back[0], unit_of).reshape(micro_count * row_count, model_width)
    key_rows = take_rows(grad_back[1], unit_of).reshape(micro_count * row_count, model_width)
    value_rows = take_rows(grad_back[2], unit_of).reshape(micro_count * row_count, model_width)
    query_grad = jnp.einsum("td,te->de", normed_in, query_rows, preferred_element_type=jnp.float32)
    key_grad = jnp.einsum("td,te->de", normed_in, key_rows, preferred_element_type=jnp.float32)
    value_grad = jnp.einsum("td,te->de", normed_in, value_rows, preferred_element_type=jnp.float32)
    grad_in = jnp.einsum("te,de->td", query_rows, gathered[1], preferred_element_type=jnp.float32)
    grad_in = grad_in + jnp.einsum(
        "te,de->td", key_rows, gathered[2], preferred_element_type=jnp.float32
    )
    grad_in = grad_in + jnp.einsum(
        "te,de->td", value_rows, gathered[3], preferred_element_type=jnp.float32
    )
    grad_norm_in, attn_gain_grad = norm_backward(inputs, gain_one, grad_in)
    token_grad = (grad_mixed + grad_norm_in).astype(jnp.bfloat16)
    attn_sums = reduce_attn(attn_gain_grad, query_grad, key_grad, value_grad, output_grad)
    return (
        block_out.reshape(block_shape),
        token_grad.reshape(block_shape),
        attn_sums[0],
        attn_sums[1],
        attn_sums[2],
        attn_sums[3],
        attn_sums[4],
        mlp_sums[0],
        mlp_sums[1],
        mlp_sums[2],
        mlp_sums[3],
    )


def contract(left_side, right_side, left_dim, right_dim, kind=jnp.float32):
    return lax.dot_general(
        left_side,
        right_side,
        (((left_dim,), (right_dim,)), ((), ())),
        preferred_element_type=jnp.float32,
    ).astype(kind)


def swap_halves(values):
    lane = lax.broadcasted_iota(jnp.int32, values.shape, 1)
    ahead = pltpu.roll(values, LANES - HD // 2, 1)
    behind = pltpu.roll(values, HD // 2, 1)
    return jnp.where(lane % HD < HD // 2, -ahead, behind)


def pair_angles(unit_at, cos_unit, sin_unit, cos_part, sin_part):
    unit_cos = cos_unit[pl.ds(unit_at, UNIT_PAIR), :][None]
    unit_sin = sin_unit[pl.ds(unit_at, UNIT_PAIR), :][None]
    part_cos = cos_part[...][:, None, :]
    part_sin = sin_part[...][:, None, :]
    cosine = unit_cos * part_cos - unit_sin * part_sin
    sine = unit_sin * part_cos + unit_cos * part_sin
    return cosine, sine


def key_offsets(block):
    row = lax.broadcasted_iota(jnp.int32, (block, block), 0)
    return (row % UNIT_BLOCK) * (block // UNIT_BLOCK) + row // UNIT_BLOCK


def query_offsets(block):
    column = lax.broadcasted_iota(jnp.int32, (block, block), 1)
    return (column % UNIT_BLOCK) * (block // UNIT_BLOCK) + column // UNIT_BLOCK


def attend_kernel(
    slot_ref,
    first_ref,
    plain_ref,
    cos_unit,
    sin_unit,
    cos_part,
    sin_part,
    low_ref,
    qkv_ref,
    att_ref,
    out_ref,
    log_ref,
    query_ref,
    key_ref,
    value_ref,
    query_t,
    value_t,
    key_at,
    causal_at,
):
    parts, units, _ = qkv_ref.shape
    block = parts * UNIT_BLOCK
    pairs = units // UNIT_PAIR
    key_at[...] = key_offsets(block)
    causal_at[...] = jnp.where(key_offsets(block) <= query_offsets(block), 0.0, masked_score)
    extra = value_t.shape[2] - HD

    def lay_out(pair, unused):
        unit_at = pl.multiple_of(pair * UNIT_PAIR, UNIT_PAIR)
        rows = jnp.stack(
            [qkv_ref[slot_ref[part], pl.ds(unit_at, UNIT_PAIR), :] for part in range(parts)]
        )
        cosine, sine = pair_angles(unit_at, cos_unit, sin_unit, cos_part, sin_part)
        flat = (parts * UNIT_PAIR, LANES)
        cosine = cosine.reshape(flat)
        sine = sine.reshape(flat)

        def rotated(values):
            values = values.astype(jnp.float32).reshape(flat)
            turned = values * cosine + swap_halves(values) * sine
            return turned.reshape(parts, UNIT_PAIR, LANES)

        query = rotated(rows[:, :, :LANES]) * (1.0 / math.sqrt(HD))
        key = rotated(rows[:, :, LANES : 2 * LANES])
        value = rows[:, :, 2 * LANES :].astype(jnp.float32)
        for half in range(UNIT_PAIR // UNIT_BLOCK):
            at = pair * (UNIT_PAIR // UNIT_BLOCK) + half
            cut = slice(half * UNIT_BLOCK, (half + 1) * UNIT_BLOCK)
            query_rows = query[:, cut].reshape(block, LANES)
            value_rows = value[:, cut].reshape(block, LANES)
            query_ref[at] = query_rows.astype(jnp.bfloat16)
            key_ref[at] = key[:, cut].reshape(block, LANES).astype(jnp.bfloat16)
            value_ref[at] = value_rows.astype(jnp.bfloat16)
            turned = jnp.transpose(query_rows)
            row = lax.broadcasted_iota(jnp.int32, turned.shape, 0)
            query_t[0, at] = jnp.where(row < HD, turned, 0.0).astype(jnp.bfloat16)
            query_t[1, at] = jnp.where(row < HD, 0.0, turned).astype(jnp.bfloat16)
            turned = jnp.transpose(value_rows).astype(jnp.bfloat16)
            for head in range(2):
                value_t[head, at, pl.ds(0, HD), :] = turned[head * HD : (head + 1) * HD]
                value_t[head, at, pl.ds(HD, extra), :] = jnp.ones((extra, block), jnp.bfloat16)
        return unused

    lax.fori_loop(0, pairs, lay_out, 0)

    def query_block(at):
        low = low_ref[at, 0:1, :]

        def step(key_block, carried, causal, bounded):
            new = []
            for head in range(2):
                top, total = carried[2 * head : 2 * head + 2]
                scores = jnp.dot(
                    key_ref[key_block], query_t[head, at], preferred_element_type=jnp.float32
                )
                if causal:
                    scores = scores + causal_at[...]
                if bounded:
                    scores = jnp.where(
                        key_at[...] >= low - key_block * block, scores, masked_score
                    )
                high = jnp.maximum(top, jnp.max(scores, axis=0, keepdims=True))
                weights = jnp.exp(scores - high).astype(jnp.bfloat16)
                total = total * jnp.exp(top - high) + jnp.dot(
                    value_t[head, key_block], weights, preferred_element_type=jnp.float32
                )
                new += [high, total]
            return tuple(new)

        empty = (
            jnp.full((1, block), masked_score, jnp.float32),
            jnp.zeros((HD + extra, block), jnp.float32),
        )
        carried = step(at, empty * 2, True, True)
        carried = lax.fori_loop(
            first_ref[at],
            plain_ref[at],
            lambda key_block, held: step(key_block, held, False, True),
            carried,
        )
        carried = lax.fori_loop(
            plain_ref[at],
            at,
            lambda key_block, held: step(key_block, held, False, False),
            carried,
        )
        heads = []
        for head in range(2):
            top, total = carried[2 * head : 2 * head + 2]
            heads.append(total[:HD] / total[HD : HD + 1])
            log_ref[at, head : head + 1, :] = top + jnp.log(total[HD : HD + 1])
        both = jnp.concatenate(heads, axis=0)
        out_ref[at] = both
        return jnp.transpose(both).reshape(parts, UNIT_BLOCK, LANES)

    def query_pair(pair, unused):
        halves = UNIT_PAIR // UNIT_BLOCK
        done = [query_block(pair * halves + half) for half in range(halves)]
        unit_at = pl.multiple_of(pair * UNIT_PAIR, UNIT_PAIR)
        att_ref[:, pl.ds(unit_at, UNIT_PAIR), :] = jnp.concatenate(done, axis=1).astype(
            jnp.bfloat16
        )
        return unused

    lax.fori_loop(0, pairs, query_pair, 0)


def attend_back_kernel(
    slot_ref,
    first_ref,
    plain_ref,
    cos_unit,
    sin_unit,
    cos_part,
    sin_part,
    low_ref,
    query_ref,
    key_ref,
    value_ref,
    out_ref,
    log_ref,
    grad_ref,
    back_ref,
    key_t,
    key_total,
    value_total,
    key_at,
    causal_at,
):
    parts, units, _ = grad_ref.shape
    block = parts * UNIT_BLOCK
    pairs = units // UNIT_PAIR
    halves = UNIT_PAIR // UNIT_BLOCK
    key_at[...] = key_offsets(block)
    causal_at[...] = jnp.where(key_offsets(block) <= query_offsets(block), 0.0, masked_score)

    def lay_out(at, unused):
        key_t[at] = jnp.transpose(key_ref[at].astype(jnp.float32)).astype(jnp.bfloat16)
        key_total[at] = jnp.zeros((block, LANES), jnp.float32)
        value_total[at] = jnp.zeros((block, LANES), jnp.float32)
        return unused

    lax.fori_loop(0, pairs * halves, lay_out, 0)

    def split_heads(values, axis):
        place = lax.broadcasted_iota(jnp.int32, values.shape, axis)
        zero = jnp.zeros_like(values)
        return [
            jnp.where(place < HD, values, zero).astype(jnp.bfloat16),
            jnp.where(place < HD, zero, values).astype(jnp.bfloat16),
        ]

    def query_block(at, grad_rows):
        low = low_ref[at, 0:1, :]
        query_rows = query_ref[at].astype(jnp.float32)
        query_heads = jnp.concatenate(split_heads(query_rows, 1), axis=0)
        grad_heads = jnp.concatenate(split_heads(grad_rows, 1), axis=0)
        query_t = split_heads(jnp.transpose(query_rows), 0)
        grad_turned = jnp.transpose(grad_rows)
        grad_t = split_heads(grad_turned, 0)
        product = grad_turned * out_ref[at]
        inner = [
            jnp.sum(product[head * HD : (head + 1) * HD], axis=0, keepdims=True)
            for head in range(2)
        ]
        logs = [log_ref[at, head : head + 1, :] for head in range(2)]

        def step(key_block, carried, causal, bounded):
            probs, slopes, new = [], [], []
            for head in range(2):
                scores = jnp.dot(
                    key_ref[key_block], query_t[head], preferred_element_type=jnp.float32
                )
                if causal:
                    scores = scores + causal_at[...]
                if bounded:
                    scores = jnp.where(
                        key_at[...] >= low - key_block * block, scores, masked_score
                    )
                soft = jnp.exp(scores - logs[head])
                grad_probs = jnp.dot(
                    value_ref[key_block], grad_t[head], preferred_element_type=jnp.float32
                )
                slope = (soft * (grad_probs - inner[head])).astype(jnp.bfloat16)
                probs.append(soft.astype(jnp.bfloat16))
                slopes.append(slope)
                new.append(
                    carried[head]
                    + jnp.dot(
                        key_t[key_block, pl.ds(head * HD, HD), :],
                        slope,
                        preferred_element_type=jnp.float32,
                    )
                )
            value_total[key_block] += jnp.dot(
                jnp.concatenate(probs, axis=1), grad_heads, preferred_element_type=jnp.float32
            )
            key_total[key_block] += jnp.dot(
                jnp.concatenate(slopes, axis=1), query_heads, preferred_element_type=jnp.float32
            )
            return tuple(new)

        carried = step(at, (jnp.zeros((HD, block), jnp.float32),) * 2, True, True)
        carried = lax.fori_loop(
            first_ref[at],
            plain_ref[at],
            lambda key_block, held: step(key_block, held, False, True),
            carried,
        )
        carried = lax.fori_loop(
            plain_ref[at],
            at,
            lambda key_block, held: step(key_block, held, False, False),
            carried,
        )
        return jnp.transpose(jnp.concatenate(carried, axis=0)) * (1.0 / math.sqrt(HD))

    def turn_back(rows, cosine, sine):
        flat = (parts * UNIT_PAIR, LANES)
        rows = jnp.concatenate(
            [one.reshape(parts, UNIT_BLOCK, LANES) for one in rows], axis=1
        ).reshape(flat)
        turned = rows * cosine.reshape(flat) - swap_halves(rows) * sine.reshape(flat)
        return turned.reshape(parts, UNIT_PAIR, LANES).astype(jnp.bfloat16)

    def put(values, unit_at, lane_at):
        for part in range(parts):
            back_ref[slot_ref[part], pl.ds(unit_at, UNIT_PAIR), pl.ds(lane_at, LANES)] = values[part]

    def query_pair(pair, unused):
        unit_at = pl.multiple_of(pair * UNIT_PAIR, UNIT_PAIR)
        grads = grad_ref[:, pl.ds(unit_at, UNIT_PAIR), :].astype(jnp.float32)
        done = [
            query_block(
                pair * halves + half,
                grads[:, half * UNIT_BLOCK : (half + 1) * UNIT_BLOCK].reshape(block, LANES),
            )
            for half in range(halves)
        ]
        cosine, sine = pair_angles(unit_at, cos_unit, sin_unit, cos_part, sin_part)
        put(turn_back(done, cosine, sine), unit_at, 0)
        return unused

    lax.fori_loop(0, pairs, query_pair, 0)

    def key_pair(pair, unused):
        unit_at = pl.multiple_of(pair * UNIT_PAIR, UNIT_PAIR)
        cosine, sine = pair_angles(unit_at, cos_unit, sin_unit, cos_part, sin_part)
        ids = [pair * halves + half for half in range(halves)]
        put(turn_back([key_total[at] for at in ids], cosine, sine), unit_at, LANES)
        values = jnp.concatenate(
            [value_total[at].reshape(parts, UNIT_BLOCK, LANES) for at in ids], axis=1
        ).astype(jnp.bfloat16)
        put(values, unit_at, 2 * LANES)
        return unused

    lax.fori_loop(0, pairs, key_pair, 0)


def attend(tables, qkv):
    parts, units, _ = qkv.shape
    block = parts * UNIT_BLOCK
    blocks = units // UNIT_BLOCK
    smem = pl.BlockSpec(memory_space=pltpu.SMEM)
    vmem = pl.BlockSpec(memory_space=pltpu.VMEM)
    rows = jax.ShapeDtypeStruct((blocks, block, LANES), jnp.bfloat16)
    extra = UNIT_PAIR
    return pl.pallas_call(
        attend_kernel,
        out_shape=(
            jax.ShapeDtypeStruct((parts, units, LANES), jnp.bfloat16),
            jax.ShapeDtypeStruct((blocks, LANES, block), jnp.float32),
            jax.ShapeDtypeStruct((blocks, 8, block), jnp.float32),
            rows,
            rows,
            rows,
        ),
        in_specs=[smem] * 3 + [vmem] * 6,
        out_specs=(vmem,) * 6,
        scratch_shapes=[
            pltpu.VMEM((2, blocks, LANES, block), jnp.bfloat16),
            pltpu.VMEM((2, blocks, HD + extra, block), jnp.bfloat16),
            pltpu.VMEM((block, block), jnp.int32),
            pltpu.VMEM((block, block), jnp.float32),
        ],
        compiler_params=pltpu.CompilerParams(vmem_limit_bytes=KERNEL_VMEM),
        cost_estimate=pl.CostEstimate(
            flops=20 * 10**9, bytes_accessed=16 << 20, transcendentals=20 * 10**6
        ),
        name="attend",
    )(*tables, qkv)


def attend_back(tables, query, key, value, out, log, grad):
    parts, units, _ = grad.shape
    block = parts * UNIT_BLOCK
    blocks = units // UNIT_BLOCK
    smem = pl.BlockSpec(memory_space=pltpu.SMEM)
    vmem = pl.BlockSpec(memory_space=pltpu.VMEM)
    return pl.pallas_call(
        attend_back_kernel,
        out_shape=jax.ShapeDtypeStruct((parts, units, 3 * LANES), jnp.bfloat16),
        in_specs=[smem] * 3 + [vmem] * 11,
        out_specs=vmem,
        scratch_shapes=[
            pltpu.VMEM((blocks, LANES, block), jnp.bfloat16),
            pltpu.VMEM((blocks, block, LANES), jnp.float32),
            pltpu.VMEM((blocks, block, LANES), jnp.float32),
            pltpu.VMEM((block, block), jnp.int32),
            pltpu.VMEM((block, block), jnp.float32),
        ],
        compiler_params=pltpu.CompilerParams(vmem_limit_bytes=KERNEL_VMEM),
        cost_estimate=pl.CostEstimate(
            flops=50 * 10**9, bytes_accessed=16 << 20, transcendentals=20 * 10**6
        ),
        name="attend_back",
    )(*tables, query, key, value, out, log, grad)


def attention_tables(lengths, grp_here, rep_here, units):
    reps = lax.axis_size("rep")
    parts = lax.axis_size("grp") * reps
    block = parts * UNIT_BLOCK
    blocks = units // UNIT_BLOCK
    own = lax.dynamic_index_in_dim(lengths, grp_here, 0, keepdims=False)
    ends = jnp.cumsum(own)
    unit_ids = jnp.arange(units, dtype=jnp.int32)
    begin = jnp.max(
        jnp.where(ends[None, :] <= unit_ids[:, None], ends[None, :], 0), axis=1
    ).astype(jnp.int32)
    part_ids = jnp.arange(parts, dtype=jnp.int32)
    offset = part_ids % reps ^ rep_here
    slot = offset * lax.axis_size("grp") + (part_ids // reps ^ grp_here)
    frequency = jnp.power(
        rope_base, -2.0 * (jnp.arange(LANES) % (HD // 2)).astype(jnp.float32) / HD
    )
    unit_angle = ((unit_ids - begin) * parts).astype(jnp.float32)[:, None] * frequency[None, :]
    part_angle = part_ids.astype(jnp.float32)[:, None] * frequency[None, :]
    low = jnp.maximum(
        (begin * parts)[:, None], unit_ids[:, None] * parts + part_ids[None, :] - (WINDOW - 1)
    )
    low = low.reshape(blocks, UNIT_BLOCK, parts)
    least = jnp.min(low, axis=(1, 2))
    most = jnp.max(low, axis=(1, 2))
    block_ids = jnp.arange(blocks, dtype=jnp.int32)
    first = jnp.maximum(least, 0) // block
    plain = jnp.clip((most + block - 1) // block, first, block_ids)
    low_rows = jnp.broadcast_to(
        low.transpose(0, 2, 1).reshape(blocks, 1, block), (blocks, 8, block)
    )
    return (
        slot,
        first,
        plain,
        jnp.cos(unit_angle),
        jnp.sin(unit_angle),
        jnp.cos(part_angle),
        jnp.sin(part_angle),
        low_rows,
    )


def swap(value, grp_step, rep_step):
    groups, reps = lax.axis_size("grp"), lax.axis_size("rep")
    pairs = [
        (grp * reps + rep, (grp ^ grp_step) * reps + (rep ^ rep_step))
        for grp in range(groups)
        for rep in range(reps)
    ]
    return lax.ppermute(value, BOTH, pairs)


def ordered(flag, own, other, axis=0):
    return jnp.where(
        flag == 0,
        jnp.concatenate([own, other], axis=axis),
        jnp.concatenate([other, own], axis=axis),
    )


def pick(value, index, axis):
    return lax.dynamic_index_in_dim(value, index, axis, keepdims=False)


def halve(value, axis, bit, grp_step, rep_step):
    kept = pick(value, bit, axis)
    sent = pick(value, 1 - bit, axis).astype(jnp.bfloat16)
    arrived = swap(sent, grp_step, rep_step)
    return kept.astype(jnp.float32) + arrived.astype(jnp.float32)


def narrow(value):
    return value.astype(jnp.bfloat16)


MESH_IDS = pl.DeviceIdType.MESH


def flipped(index, step):
    return index + step - 2 * step * ((index // step) % 2)


def lowest(offset):
    return offset & -offset


def arrivals(reps):
    far = [step for step in range(4, reps, 4)]
    far.sort(key=lambda step: (bin(step).count("1"), step))
    order = [(2, 0), (0, 1)]
    for at, step in enumerate(far):
        if bin(step).count("1") == 1:
            order.append((step, 0))
    order.append((2, 1))
    for step in far:
        if bin(step).count("1") == 1:
            order.append((step, 1))
    single = [step for step in far if bin(step).count("1") == 1]
    double = [step for step in far if bin(step).count("1") > 1]
    rest = []
    for step in single[:1]:
        rest.append((step + 2, 0))
    for step in double:
        rest.append((step, 0))
    for step in single[:1]:
        rest.append((step + 2, 1))
    for step in double:
        rest.append((step, 1))
    for step in single[1:] + double:
        rest += [(step + 2, 0), (step + 2, 1)]
    return order + rest


def link_of(offset, part, reps):
    if reps > 8 and offset == reps - 2 and part == 1:
        return 4
    return lowest(offset)


def gather_kernel(
    tokens_ref,
    gain_ref,
    w_query,
    w_key,
    w_value,
    w_gate,
    w_up,
    w_down,
    w_output,
    out_rows,
    normed_out,
    qkv_ref,
    weight_ref,
    gate_ref,
    up_ref,
    down_first,
    down_second,
    output_ref,
    out_away,
    gains,
    raw,
    normed,
    weight_sem,
    out_sem,
    send_sem,
    recv_sem,
    side_send,
    side_recv,
    stripe_sem,
):
    here, there = lax.axis_index("grp"), lax.axis_index("rep")
    core = there % 2
    reps = raw.shape[0]
    slots = normed.shape[0]
    row_count, width = raw.shape[2:]
    steps = [1 << place for place in range(reps.bit_length() - 1)]
    across = (1 - here, there)

    def neighbour(step):
        return (here, flipped(there, step))

    barrier = pltpu.get_barrier_semaphore()
    for target in [across] + [neighbour(step) for step in steps]:
        pl.semaphore_signal(barrier, inc=1, device_id=target, device_id_type=MESH_IDS)
    local = []
    for at, weight in enumerate((w_query, w_key, w_value)):
        local.append(
            pltpu.make_async_copy(
                weight.at[:, pl.ds(pl.multiple_of(there * LANES, LANES), LANES)],
                weight_ref.at[here, :, pl.ds(at * LANES, LANES)],
                weight_sem.at[at],
            )
        )
        local[-1].start()
    raw[0, 0] = tokens_ref[here]
    gains[here] = gain_ref[...]
    pl.semaphore_wait(barrier, len(steps) + 1)

    def side(at, source, target_ref):
        return pltpu.make_async_remote_copy(
            src_ref=source,
            dst_ref=target_ref,
            send_sem=side_send.at[at],
            recv_sem=side_recv.at[at],
            device_id=across,
            device_id_type=MESH_IDS,
        )

    def rows_copy(offset, part):
        if offset == 0:
            return pltpu.make_async_remote_copy(
                src_ref=tokens_ref.at[1 - here],
                dst_ref=raw.at[0, 1],
                send_sem=send_sem.at[1],
                recv_sem=recv_sem.at[1],
                device_id=across,
                device_id_type=MESH_IDS,
            )
        step = link_of(offset, part, reps)
        return pltpu.make_async_remote_copy(
            src_ref=raw.at[offset - step, part],
            dst_ref=raw.at[offset, part],
            send_sem=send_sem.at[2 * offset + part],
            recv_sem=recv_sem.at[2 * offset + part],
            device_id=neighbour(step),
            device_id_type=MESH_IDS,
        )

    order = arrivals(reps)
    copies = {
        (offset, part): rows_copy(offset, part)
        for offset in range(reps)
        for part in (0, 1)
        if offset or part
    }

    def pass_on(offset, part):
        for later, part_of in order:
            if later and part_of == part and later - link_of(later, part, reps) == offset:
                copies[later, part].start()
        copies[offset + 1, part].start()

    gain_copy = side(0, gains.at[here], gains.at[here])
    gain_copy.start()
    copies[0, 1].start()
    pass_on(0, 0)
    for one in local:
        one.wait()
    weight_copy = side(1, weight_ref.at[here], weight_ref.at[here])
    weight_copy.start()

    stripes = [
        (grp, high, low)
        for grp in range(2)
        for high in range(reps // 8)
        for low in range(2)
    ]
    place = 4 * ((there // 4) % 2) + there % 2
    stripe_loads = []

    def load(source, target_ref):
        stripe_loads.append(
            pltpu.make_async_copy(source, target_ref, stripe_sem.at[len(stripe_loads)])
        )

    def columns_of(weight, grp, high, low):
        first = (grp * reps + 8 * high + 2 * low + place) * LANES
        return weight.at[:, pl.ds(pl.multiple_of(first, LANES), LANES)]

    for weight, target_ref in ((w_gate, gate_ref.at[here]), (w_up, up_ref)):
        for at, stripe in enumerate(stripes):
            load(columns_of(weight, *stripe), target_ref.at[:, pl.ds(at * LANES, LANES)])
    for at, (grp, high, low) in enumerate(stripes[: len(stripes) // 2]):
        first = (8 * high + 2 * low + place) * LANES
        target_ref = (down_first, down_second)[at // 2]
        load(
            w_down.at[pl.ds(pl.multiple_of(first, LANES), LANES)],
            target_ref.at[pl.ds(at % 2 * LANES, LANES)],
        )
    load(out_rows, out_away)
    for one in stripe_loads:
        one.start()
    quarter = output_ref.shape[0]
    output_copy = side(
        2,
        w_output.at[pl.ds(pl.multiple_of((there % 4) * quarter, quarter), quarter)],
        output_ref,
    )
    output_copy.start()
    gate_copy = side(3, gate_ref.at[here], gate_ref.at[here])
    for one in stripe_loads[: len(stripes)]:
        one.wait()
    gate_copy.start()

    written = {}
    used = [None] * slots
    tile = 32

    def project(count, offset):
        slot = count % slots
        if used[slot] is not None:
            written[used[slot]].wait()
        used[slot] = offset
        gain = jnp.concatenate([gains[0, 0:1], gains[1, 0:1]], axis=1).astype(jnp.float32)
        for part in range(2):

            def norm_rows(at, unused):
                cut = pl.ds(pl.multiple_of(at * tile, tile), tile)
                values = raw[offset, part, cut, :].astype(jnp.float32)
                scaled = values * rms_scale(values) * gain
                normed[slot, pl.ds(pl.multiple_of(part * row_count + at * tile, tile), tile), :] = (
                    scaled.astype(jnp.bfloat16)
                )
                return unused

            lax.fori_loop(0, row_count // tile, norm_rows, 0)
        written[offset] = pltpu.make_async_copy(
            normed.at[slot], normed_out.at[offset], out_sem.at[offset]
        )
        written[offset].start()
        half = width // 2
        product = jnp.dot(
            normed[slot, :, :half], weight_ref[0], preferred_element_type=jnp.float32
        ) + jnp.dot(normed[slot, :, half:], weight_ref[1], preferred_element_type=jnp.float32)
        qkv_ref[pl.ds(2 * offset, 2)] = product.astype(jnp.bfloat16).reshape(
            2, row_count, 3 * LANES
        )

    ready = []
    arrived = {(0, 0)}
    started = False
    count = 0
    for offset, part in order:
        copies[offset, part].wait_recv()
        pass_on(offset, part)
        arrived.add((offset, part))
        if (offset, 1 - part) in arrived:
            ready.append(offset)
        if not started and len(ready) >= 1:
            gain_copy.wait_recv()
            weight_copy.wait_recv()
            started = True
        if started and len(ready) >= 2:
            base = ready.pop(0)
            project(count, base)
            copies[base + 1, 0].wait_recv()
            copies[base + 1, 1].wait_recv()
            project(count + 1, base + 1)
            count += 2
    for base in ready:
        project(count, base)
        copies[base + 1, 0].wait_recv()
        copies[base + 1, 1].wait_recv()
        project(count + 1, base + 1)
        count += 2
    for offset in used:
        written[offset].wait()
    for one in copies.values():
        one.wait_send()
    gain_copy.wait_send()
    weight_copy.wait_send()
    for one in stripe_loads[len(stripes) :]:
        one.wait()
    gate_copy.wait()
    output_copy.wait()


def gather_heads(
    tokens, gains, w_query, w_key, w_value, w_gate, w_up, w_down, w_output, out_rows
):
    reps = lax.axis_size("rep")
    _, row_count, width = tokens.shape
    half = width // 2
    own_width = reps // 2 * LANES
    gain_rows = jnp.concatenate(
        [gains[0][None], gains[1][None], jnp.zeros((14, half), jnp.bfloat16)], axis=0
    )
    vmem = pl.BlockSpec(memory_space=pltpu.VMEM)
    anywhere = pl.BlockSpec(memory_space=pl.ANY)
    return pl.pallas_call(
        gather_kernel,
        out_shape=(
            jax.ShapeDtypeStruct((reps, 2 * row_count, width), jnp.bfloat16),
            jax.ShapeDtypeStruct((2 * reps, row_count, 3 * LANES), jnp.bfloat16),
            jax.ShapeDtypeStruct((2, half, 3 * LANES), jnp.bfloat16),
            jax.ShapeDtypeStruct((2, half, own_width), jnp.bfloat16),
            jax.ShapeDtypeStruct((half, own_width), jnp.bfloat16),
            jax.ShapeDtypeStruct((2 * LANES, width), jnp.bfloat16),
            jax.ShapeDtypeStruct((own_width // 2 - 2 * LANES, width), jnp.bfloat16),
            jax.ShapeDtypeStruct((half // 4, width), jnp.bfloat16),
            jax.ShapeDtypeStruct(out_rows.shape, jnp.bfloat16),
            jax.ShapeDtypeStruct((2, 16, half), jnp.bfloat16),
        ),
        in_specs=[vmem, vmem] + [anywhere] * 8,
        out_specs=(anywhere,) + (vmem,) * 9,
        scratch_shapes=[
            pltpu.VMEM((reps, 2, row_count, width), jnp.bfloat16),
            pltpu.VMEM((4, 2 * row_count, width), jnp.bfloat16),
            pltpu.SemaphoreType.DMA((3,)),
            pltpu.SemaphoreType.DMA((reps,)),
            pltpu.SemaphoreType.DMA((2 * reps,)),
            pltpu.SemaphoreType.DMA((2 * reps,)),
            pltpu.SemaphoreType.DMA((4,)),
            pltpu.SemaphoreType.DMA((4,)),
            pltpu.SemaphoreType.DMA((reps // 2 * 5 // 2 + 1,)),
        ],
        compiler_params=pltpu.CompilerParams(
            vmem_limit_bytes=KERNEL_VMEM, collective_id=0, has_side_effects=True
        ),
        cost_estimate=pl.CostEstimate(
            flops=8 * 10**9, bytes_accessed=250 << 20, transcendentals=0
        ),
        name="gather_heads",
    )(tokens, gain_rows, w_query, w_key, w_value, w_gate, w_up, w_down, w_output, out_rows)


def scatter_kernel(
    back_ref,
    weight_ref,
    normed_ref,
    *refs,
):
    scatter_rows(back_ref, weight_ref, normed_ref, *refs[-SCATTER_REFS:])


def scatter_rows(
    back_ref,
    weight_ref,
    normed_ref,
    grad_ref,
    pieces_ref,
    away,
    landed,
    normed,
    back_t,
    weight_t,
    weights_total,
    half_out,
    half_in,
    piece_out,
    normed_sem,
    send_sem,
    recv_sem,
    side_send,
    side_recv,
    piece_send,
    piece_recv,
):
    here, there = lax.axis_index("grp"), lax.axis_index("rep")
    reps, rows, columns = back_ref.shape
    row_count = rows // 2
    width = grad_ref.shape[2]
    half = width // 2
    own_rows = half // reps
    steps = [1 << place for place in range(reps.bit_length() - 1)]
    across = (1 - here, there)

    def other(offset):
        index = there
        for step in steps:
            if offset & step:
                index = flipped(index, step)
        return (here, index)

    barrier = pltpu.get_barrier_semaphore()
    for target in [across] + [other(offset) for offset in range(1, reps)]:
        pl.semaphore_signal(barrier, inc=1, device_id=target, device_id_type=MESH_IDS)

    slots = normed.shape[0]
    fetch = [
        pltpu.make_async_copy(normed_ref.at[offset], normed.at[offset % slots], normed_sem.at[offset])
        for offset in range(reps)
    ]
    for offset in range(slots):
        fetch[offset].start()

    for at in range(2):
        turned = jnp.transpose(weight_ref[at].astype(jnp.float32)).astype(jnp.bfloat16)
        weight_t[:, pl.ds(at * half, half)] = turned
    pl.semaphore_wait(barrier, reps)

    def rows_copy(offset, part):
        if offset == 0:
            return pltpu.make_async_remote_copy(
                src_ref=away.at[0, 1],
                dst_ref=landed.at[0, 1],
                send_sem=send_sem.at[1],
                recv_sem=recv_sem.at[1],
                device_id=across,
                device_id_type=MESH_IDS,
            )
        return pltpu.make_async_remote_copy(
            src_ref=away.at[offset, part],
            dst_ref=landed.at[offset, part],
            send_sem=send_sem.at[2 * offset + part],
            recv_sem=recv_sem.at[2 * offset + part],
            device_id=other(link_of(offset, part, reps)),
            device_id_type=MESH_IDS,
        )

    copies = {
        (offset, part): rows_copy(offset, part)
        for offset in range(reps)
        for part in (0, 1)
        if offset or part
    }
    tile = 32

    def product(offset, part):
        return jnp.dot(
            back_ref[offset, pl.ds(part * row_count, row_count), :],
            weight_t[...],
            preferred_element_type=jnp.float32,
        )

    def send(offset, part):
        sources = [
            later
            for later in range(1, reps)
            if later - link_of(later, part, reps) == offset
        ]
        for later in sources:
            copies[later, part].wait_recv()
        total = product(offset, part)
        for later in sources:
            total = total + landed[later, part].astype(jnp.float32)
        if offset == 0 and part == 0:
            grad_ref[here] = total
        else:
            away[offset, part] = total.astype(jnp.bfloat16)
            copies[offset, part].start()

    def weight_step(offset):
        fetch[offset].wait()
        back_t[...] = jnp.transpose(back_ref[offset].astype(jnp.float32)).astype(jnp.bfloat16)

        def columns_at(at, unused):
            cut = pl.ds(pl.multiple_of(at * 512, 512), 512)
            term = jnp.dot(
                back_t[...], normed[offset % slots, :, cut], preferred_element_type=jnp.float32
            )
            if offset == 0:
                weights_total[:, cut] = term
            else:
                weights_total[:, cut] += term
            return unused

        lax.fori_loop(0, width // 512, columns_at, 0)
        if offset + slots < reps:
            fetch[offset + slots].start()

    half_copy = pltpu.make_async_remote_copy(
        src_ref=half_out,
        dst_ref=half_in,
        send_sem=side_send,
        recv_sem=side_recv,
        device_id=across,
        device_id_type=MESH_IDS,
    )
    piece_copies = [
        pltpu.make_async_remote_copy(
            src_ref=piece_out.at[other(offset)[1]],
            dst_ref=pieces_ref.at[there],
            send_sem=piece_send.at[offset],
            recv_sem=piece_recv.at[offset],
            device_id=other(offset),
            device_id_type=MESH_IDS,
        )
        for offset in range(1, reps)
    ]

    def cross_weights():
        cut = pl.ds(pl.multiple_of((1 - here) * half, half), half)
        half_out[...] = weights_total[:, cut].astype(jnp.bfloat16)
        half_copy.start()

    def share_weights():
        half_copy.wait_recv()
        cut = pl.ds(pl.multiple_of(here * half, half), half)
        total = jnp.transpose(weights_total[:, cut] + half_in[...].astype(jnp.float32))
        piece_out[...] = total.astype(jnp.bfloat16).reshape(reps, own_rows, columns)
        pieces_ref[there] = piece_out[there]
        for one in piece_copies:
            one.start()

    far = [step for step in range(reps - 4, 0, -4)]
    todo = []
    for base in far + [0]:
        todo.append((base + 3, 1))
        todo.append((base + 3, 0))
        todo.append((base + 1, 1))
        todo.append((base + 1, 0))
    first = todo[:2]
    for offset, part in first:
        send(offset, part)
    for offset, part in todo[2:6]:
        send(offset, part)
    send(reps - 2, 1)
    send(reps - 2, 0)
    for offset, part in todo[6:]:
        send(offset, part)
    weights = list(range(reps))

    def weight_steps(count):
        for _ in range(min(count, len(weights))):
            weight_step(weights.pop(0))

    last = []
    order = []
    for base in sorted(far, key=lambda step: (-bin(step).count("1"), -step)):
        if base != far[0]:
            order.append((base + 2, 1))
            order.append((base + 2, 0))
    order += [(2, 1), (2, 0)]
    sums = sorted(far, key=lambda step: (-bin(step).count("1"), -step))
    for base in sums:
        last += [(base, 1), (base, 0)]
    if reps == 16:
        plan = [
            (10, 1), (10, 0), 4, (12, 1), (12, 0), 4, (6, 1), (6, 0), 2, (8, 1), 2, (8, 0),
            (2, 1), (2, 0), 4, "cross", (4, 1), (4, 0), "share", (0, 1), (0, 0),
        ]
    else:
        plan = order + last + [reps, "cross", "share", (0, 1), (0, 0)]
    for item in plan:
        if item == "cross":
            weight_steps(reps)
            cross_weights()
        elif item == "share":
            share_weights()
        elif isinstance(item, int):
            weight_steps(item)
        else:
            send(*item)
    copies[0, 1].wait_recv()
    grad_ref[1 - here] = landed[0, 1].astype(jnp.float32)
    for one in piece_copies:
        one.wait()
    half_copy.wait_send()
    for one in copies.values():
        one.wait_send()


def scatter_heads(back, weights, normed, ahead):
    reps, rows, columns = back.shape
    width = normed.shape[2]
    row_count = rows // 2
    half = width // 2
    vmem = pl.BlockSpec(memory_space=pltpu.VMEM)
    anywhere = pl.BlockSpec(memory_space=pl.ANY)
    return pl.pallas_call(
        scatter_kernel,
        out_shape=(
            jax.ShapeDtypeStruct((2, row_count, width), jnp.float32),
            jax.ShapeDtypeStruct((reps, half // reps, columns), jnp.bfloat16),
        ),
        in_specs=[vmem, vmem, anywhere] + [anywhere] * len(ahead),
        out_specs=(vmem, vmem),
        scratch_shapes=[
            pltpu.VMEM((reps, 2, row_count, width), jnp.bfloat16),
            pltpu.VMEM((reps, 2, row_count, width), jnp.bfloat16),
            pltpu.VMEM((4, rows, width), jnp.bfloat16),
            pltpu.VMEM((columns, rows), jnp.bfloat16),
            pltpu.VMEM((columns, width), jnp.bfloat16),
            pltpu.VMEM((columns, width), jnp.float32),
            pltpu.VMEM((columns, half), jnp.bfloat16),
            pltpu.VMEM((columns, half), jnp.bfloat16),
            pltpu.VMEM((reps, half // reps, columns), jnp.bfloat16),
            pltpu.SemaphoreType.DMA((reps,)),
            pltpu.SemaphoreType.DMA((2 * reps,)),
            pltpu.SemaphoreType.DMA((2 * reps,)),
            pltpu.SemaphoreType.DMA,
            pltpu.SemaphoreType.DMA,
            pltpu.SemaphoreType.DMA((reps,)),
            pltpu.SemaphoreType.DMA((reps,)),
        ],
        compiler_params=pltpu.CompilerParams(
            vmem_limit_bytes=KERNEL_VMEM, collective_id=1, has_side_effects=True
        ),
        cost_estimate=pl.CostEstimate(
            flops=14 * 10**9, bytes_accessed=250 << 20, transcendentals=0
        ),
        name="scatter_heads",
    )(back, weights, normed, *ahead)


def mlp_kernel(
    heads_ref,
    tokens_ref,
    gain_ref,
    out_rows,
    out_across,
    output_own,
    output_part,
    output_beside,
    gate_in,
    up_own,
    up_other,
    down_first,
    down_second,
    down_other,
    mixed_ref,
    down_ref,
    grad_ref,
    back_ref,
    gate_ref,
    up_kept,
    up_sent,
    down_kept,
    down_sent,
    output_kept,
    output_sent,
    attended,
    branch_ref,
    returned,
    out_ref,
    mid_ref,
    hidden_ref,
    slope_ref,
    w_output,
    w_in,
    w_out,
    near_away,
    near_landed,
    far_away,
    far_landed,
    down_landed,
    load_sem,
    part_sem,
    send_sem,
    recv_sem,
    heads_send,
    heads_recv,
    back_send,
    back_recv,
    piece_sem,
    place_sem,
    core_send,
    core_recv,
    free_sem,
):
    here, there = lax.axis_index("grp"), lax.axis_index("rep")
    across = (here, flipped(there, 4))
    sibling = (here, flipped(there, 1))
    groups, heads, row_count, _ = returned.shape
    rows, width = tokens_ref.shape
    half = width // 2
    quarter = half // 4
    own_width = w_out.shape[0]

    loads = [
        pltpu.make_async_copy(output_own, w_output.at[here], load_sem.at[0]),
        pltpu.make_async_copy(gate_in, w_in.at[:, :, pl.ds(0, own_width)], load_sem.at[1]),
        pltpu.make_async_copy(
            up_own, w_in.at[here, :, pl.ds(own_width, own_width)], load_sem.at[2]
        ),
        pltpu.make_async_copy(
            up_other, w_in.at[1 - here, :, pl.ds(own_width, own_width)], load_sem.at[3]
        ),
    ]
    own_part = own_width // 2
    early_rows = down_first.shape[0]

    def down_cut(grp, first, count):
        return pl.ds(pl.multiple_of(grp * own_part + first, LANES), count)

    late_rows = own_part - early_rows
    loads += [
        pltpu.make_async_copy(
            down_first, w_out.at[down_cut(here, 0, early_rows)], load_sem.at[4]
        ),
        pltpu.make_async_copy(
            down_second, w_out.at[down_cut(here, early_rows, late_rows)], load_sem.at[5]
        ),
        pltpu.make_async_copy(
            down_other, w_out.at[down_cut(1 - here, 0, early_rows)], load_sem.at[6]
        ),
        pltpu.make_async_copy(out_rows, out_ref.at[0], load_sem.at[7]),
        pltpu.make_async_copy(out_across, out_ref.at[2], load_sem.at[8]),
    ]
    place = there % 4
    core = there % 2

    def output_cut(part):
        return w_output.at[1 - here, pl.ds(pl.multiple_of(part * quarter, quarter), quarter)]

    output_pieces = ((output_part, place), (output_beside, flipped(place, 2)))
    rest = [
        pltpu.make_async_copy(piece, output_cut(part), part_sem.at[at])
        for at, (piece, part) in enumerate(output_pieces)
    ]
    loads = loads[:1] + rest + loads[1:]
    for one in loads:
        one.start()
    steps = [1 << place for place in range(heads.bit_length() - 1)]

    def other(crossing, offset):
        index = there
        for step in steps:
            if offset & step:
                index = flipped(index, step)
        return (1 - here if crossing else here, index)

    others = [
        (crossing, offset) for offset in range(heads) for crossing in (0, 1) if offset or crossing
    ]
    barrier = pltpu.get_barrier_semaphore()
    for key in others:
        pl.semaphore_signal(barrier, inc=1, device_id=other(*key), device_id_type=MESH_IDS)
    pl.semaphore_wait(barrier, len(others))

    facing = (1 - here, there)

    def copy(at, source, target_ref, target):
        return pltpu.make_async_remote_copy(
            src_ref=source,
            dst_ref=target_ref,
            send_sem=send_sem.at[at],
            recv_sem=recv_sem.at[at],
            device_id=target,
            device_id_type=MESH_IDS,
        )

    heads_copies, back_copies = [], []
    for at, key in enumerate(others):
        target = other(*key)
        heads_copies.append(
            pltpu.make_async_remote_copy(
                src_ref=heads_ref.at[target[0] * heads + target[1]],
                dst_ref=returned.at[here, there],
                send_sem=heads_send.at[at],
                recv_sem=heads_recv.at[at],
                device_id=target,
                device_id_type=MESH_IDS,
            )
        )
        back_copies.append(
            pltpu.make_async_remote_copy(
                src_ref=returned.at[target[0], target[1]],
                dst_ref=back_ref.at[here * heads + there],
                send_sem=back_send.at[at],
                recv_sem=back_recv.at[at],
                device_id=target,
                device_id_type=MESH_IDS,
            )
        )
    for one in heads_copies[::-1]:
        one.start()
    output_near = [
        copy(at, piece, output_cut(part), sibling)
        for at, (piece, part) in enumerate(output_pieces, 9)
    ]
    down_far = copy(11, down_second, w_out.at[down_cut(here, early_rows, late_rows)], facing)
    out_near = copy(12, out_rows, out_ref.at[1], sibling)
    out_on = copy(13, out_across, out_ref.at[3], sibling)
    for one in output_near + [out_near, out_on, down_far]:
        one.start()
    returned[here, there] = heads_ref[here * heads + there]

    mid_near = copy(0, mid_ref.at[0], mid_ref.at[1], sibling)
    mid_far = copy(1, mid_ref.at[0], mid_ref.at[2], across)
    mid_on = copy(2, mid_ref.at[2], mid_ref.at[3], sibling)
    grad_near = [copy(3 + at, near_away.at[at], near_landed.at[at], sibling) for at in range(2)]
    grad_far = copy(5, far_away, far_landed, across)
    down_near = [copy(6 + at, near_away.at[at], down_landed.at[at], sibling) for at in range(2)]
    gate_cross = copy(
        8, w_in.at[1 - here, :, pl.ds(0, own_width)], gate_ref, facing
    )
    up_cut = pl.ds(own_width, own_width)
    up_outs = [
        pltpu.make_async_copy(w_in.at[here, :, up_cut], up_kept, load_sem.at[0]),
        pltpu.make_async_copy(w_in.at[1 - here, :, up_cut], up_sent, load_sem.at[1]),
    ]
    low = (there // 2) % 2
    down_outs = []
    for at in range(own_width // (2 * LANES)):
        for kind, (target_ref, bit) in enumerate(((down_kept, low), (down_sent, 1 - low))):
            cut = pl.ds(pl.multiple_of((2 * at + bit) * LANES, LANES), LANES)
            down_outs.append(
                pltpu.make_async_copy(w_out.at[cut], target_ref.at[at], piece_sem.at[2 * at + kind])
            )

    for one in heads_copies:
        one.wait()
    for group in range(groups):
        for head in range(heads):
            attended[
                group * row_count : (group + 1) * row_count, head * LANES : (head + 1) * LANES
            ] = returned[group, head]
    for one in loads[:3]:
        one.wait()
    for one in output_near:
        one.wait_recv()
    wide = 512

    def mix(at, unused):
        cut = pl.ds(pl.multiple_of(at * wide, wide), wide)
        mixed_ref[:, cut] = (
            tokens_ref[:, cut].astype(jnp.float32)
            + jnp.dot(attended[:, :half], w_output[0, :, cut], preferred_element_type=jnp.float32)
            + jnp.dot(attended[:, half:], w_output[1, :, cut], preferred_element_type=jnp.float32)
        )
        return unused

    lax.fori_loop(0, width // wide, mix, 0)
    tile = 32

    def norm_rows(at, unused):
        cut = pl.ds(pl.multiple_of(at * tile, tile), tile)
        values = mixed_ref[cut, :]
        mid_ref[0, cut, :] = (values * rms_scale(values) * gain_ref[0:1, :]).astype(jnp.bfloat16)
        return unused

    lax.fori_loop(0, rows // tile, norm_rows, 0)
    mid_far.start()
    mid_near.start()
    for one in loads[3:]:
        one.wait()
    down_far.wait_recv()
    narrow_tile = 256

    def forward(slot):
        def columns(at, unused):
            cut = pl.ds(pl.multiple_of(at * narrow_tile, narrow_tile), narrow_tile)
            up_cut = pl.ds(pl.multiple_of(own_width + at * narrow_tile, narrow_tile), narrow_tile)

            def project(cols):
                return jnp.dot(
                    mid_ref[slot, :, :half], w_in[0, :, cols], preferred_element_type=jnp.float32
                ) + jnp.dot(
                    mid_ref[slot, :, half:], w_in[1, :, cols], preferred_element_type=jnp.float32
                )

            gate_pre, up_pre = project(cut), project(up_cut)
            grad_hidden = contract(out_ref[slot], w_out[cut, :], 1, 1)
            gate_sig = jax.nn.sigmoid(gate_pre)
            gate_silu = gate_pre * gate_sig
            hidden_ref[slot, :, cut] = (gate_silu * up_pre).astype(jnp.bfloat16)
            slope_ref[slot, :, cut] = (
                grad_hidden * up_pre * gate_sig * (1.0 + gate_pre * (1.0 - gate_sig))
            ).astype(jnp.bfloat16)
            slope_ref[slot, :, up_cut] = (grad_hidden * gate_silu).astype(jnp.bfloat16)
            return unused

        lax.fori_loop(0, own_width // narrow_tile, columns, 0)

    def backward(slot, finish):
        for at in range(2):

            def columns(step, unused):
                cut = pl.ds(pl.multiple_of(step * wide, wide), wide)
                whole = pl.ds(pl.multiple_of(at * half + step * wide, wide), wide)
                finish(whole, contract(slope_ref[slot], w_in[at, cut, :], 1, 1))
                return unused

            lax.fori_loop(0, half // wide, columns, 0)

    def down(slot, finish):
        def columns(step, unused):
            cut = pl.ds(pl.multiple_of(step * wide, wide), wide)
            finish(
                cut, jnp.dot(hidden_ref[slot], w_out[:, cut], preferred_element_type=jnp.float32)
            )
            return unused

        lax.fori_loop(0, width // wide, columns, 0)

    def into(target, at):
        def finish(cut, values):
            target[at, :, cut] = values.astype(jnp.bfloat16)

        return finish

    forward(0)
    mid_near.wait_recv()
    out_near.wait_recv()
    forward(1)
    backward(1, into(near_away, 0))
    grad_near[0].start()

    def keep(cut, values):
        grad_ref[:, cut] = values

    backward(0, keep)
    mid_far.wait_recv()
    mid_on.start()
    forward(2)
    mid_on.wait_recv()
    out_on.wait_recv()
    forward(3)
    backward(3, into(near_away, 1))
    grad_near[1].start()
    grad_near[1].wait_recv()

    def add_near(cut, values):
        far_away[:, cut] = (values + near_landed[1, :, cut].astype(jnp.float32)).astype(
            jnp.bfloat16
        )

    backward(2, add_near)
    grad_far.start()

    def turned(values):
        flat = values.reshape(4 * rows, values.shape[2]).astype(jnp.float32)
        return jnp.transpose(flat).astype(jnp.bfloat16)

    def in_grads(at):
        def some_rows(step, unused):
            cut = pl.ds(pl.multiple_of(step * narrow_tile, narrow_tile), narrow_tile)
            source = pl.ds(pl.multiple_of(at * half + step * narrow_tile, narrow_tile), narrow_tile)
            left = turned(mid_ref[:, :, source])

            def columns(place_at, unused):
                cols = pl.ds(pl.multiple_of(place_at * wide, wide), wide)
                right = slope_ref[:, :, cols].reshape(4 * rows, wide)
                w_in[at, cut, cols] = jnp.dot(
                    left, right, preferred_element_type=jnp.float32
                ).astype(jnp.bfloat16)
                return unused

            return lax.fori_loop(0, 2 * own_width // wide, columns, unused)

        lax.fori_loop(0, half // narrow_tile, some_rows, 0)

    in_grads(1 - here)
    gate_cross.start()
    for at in range(2):
        grad_near[at].wait_send()
        down(2 * at + 1, into(near_away, at))
        down_near[at].start()
    in_grads(here)
    for one in up_outs:
        one.start()
    for one in (mid_near, mid_far, mid_on):
        one.wait_send()
    pl.semaphore_signal(free_sem, inc=1, device_id=sibling, device_id_type=MESH_IDS)
    for at in range(2):
        down_near[at].wait_recv()

        def add_down(cut, values):
            down_ref[at, :, cut] = (values + down_landed[at, :, cut].astype(jnp.float32)).astype(
                jnp.bfloat16
            )

        down(2 * at, add_down)

    def down_rows(step, unused):
        cut = pl.ds(pl.multiple_of(step * narrow_tile, narrow_tile), narrow_tile)
        left = turned(hidden_ref[:, :, cut])

        def columns(place_at, unused):
            cols = pl.ds(pl.multiple_of(place_at * wide, wide), wide)
            right = out_ref[:, :, cols].reshape(4 * rows, wide)
            w_out[cut, cols] = jnp.dot(left, right, preferred_element_type=jnp.float32).astype(
                jnp.bfloat16
            )
            return unused

        return lax.fori_loop(0, width // wide, columns, unused)

    lax.fori_loop(0, own_width // narrow_tile, down_rows, 0)
    for one in down_outs:
        one.start()
    grad_near[0].wait_recv()
    grad_far.wait_recv()

    def norm_back(at, unused):
        cut = pl.ds(pl.multiple_of(at * tile, tile), tile)
        grad_mid = (
            grad_ref[cut, :]
            + near_landed[0, cut, :].astype(jnp.float32)
            + far_landed[cut, :].astype(jnp.float32)
        )
        values = mixed_ref[cut, :]
        inverse = rms_scale(values)
        normed = values * inverse
        weighted = grad_mid * gain_ref[0:1, :]
        grad = out_ref[0, cut, :].astype(jnp.float32) + inverse * (
            weighted - normed * jnp.mean(weighted * normed, axis=-1, keepdims=True)
        )
        grad_ref[cut, :] = grad
        branch_ref[cut, :] = grad.astype(jnp.bfloat16)
        return unused

    lax.fori_loop(0, rows // tile, norm_back, 0)
    for head in range(0, heads, 4):
        at = head * LANES // half
        start = head * LANES - at * half
        values = contract(
            branch_ref[...], w_output[at, pl.ds(start, 4 * LANES), :], 1, 1, jnp.bfloat16
        )
        for group in range(groups):
            for step in range(4):
                returned[group, head + step] = values[
                    group * row_count : (group + 1) * row_count, step * LANES : (step + 1) * LANES
                ]
    for one in back_copies[::-1]:
        one.start()
    back_ref[here * heads + there] = returned[here, there]

    for at in range(2):

        def output_rows(step, unused):
            cut = pl.ds(pl.multiple_of(step * narrow_tile, narrow_tile), narrow_tile)
            source = pl.ds(pl.multiple_of(at * half + step * narrow_tile, narrow_tile), narrow_tile)
            left = jnp.transpose(attended[:, source].astype(jnp.float32)).astype(jnp.bfloat16)

            def columns(place_at, unused):
                cols = pl.ds(pl.multiple_of(place_at * wide, wide), wide)
                w_output[at, cut, cols] = jnp.dot(
                    left, branch_ref[:, cols], preferred_element_type=jnp.float32
                ).astype(jnp.bfloat16)
                return unused

            return lax.fori_loop(0, width // wide, columns, unused)

        lax.fori_loop(0, half // narrow_tile, output_rows, 0)

    own_rows = half // heads
    stripes = heads // 2
    pl.semaphore_wait(free_sem, 1)

    def stripe_of(at, bit):
        first = (at % stripes * 2 + bit) * own_rows
        return pl.ds(pl.multiple_of(first, own_rows), own_rows)

    def landed_at(at):
        per_slot = rows // own_rows
        return at // per_slot, pl.ds(at % per_slot * own_rows, own_rows)

    core_copies = []
    for at in range(2 * stripes):
        slot, cut = landed_at(at)
        core_copies.append(
            pltpu.make_async_remote_copy(
                src_ref=w_output.at[at // stripes, stripe_of(at, 1 - core)],
                dst_ref=mid_ref.at[slot, cut],
                send_sem=core_send.at[at],
                recv_sem=core_recv.at[at],
                device_id=sibling,
                device_id_type=MESH_IDS,
            )
        )
        core_copies[-1].start()
    gate_cross.wait()

    def add_gate(at, unused):
        cut = pl.ds(pl.multiple_of(at * tile, tile), tile)
        gate_ref[cut, :] = (
            gate_ref[cut, :].astype(jnp.float32)
            + w_in[here, cut, pl.ds(0, own_width)].astype(jnp.float32)
        ).astype(jnp.bfloat16)
        return unused

    lax.fori_loop(0, half // tile, add_gate, 0)
    far_bit = (there // 4) % 2
    output_outs = []
    for at in range(2 * stripes):
        core_copies[at].wait_recv()
        slot, cut = landed_at(at)
        own = stripe_of(at, core)
        w_output[at // stripes, own, :] = (
            w_output[at // stripes, own, :].astype(jnp.float32)
            + mid_ref[slot, cut, :].astype(jnp.float32)
        ).astype(jnp.bfloat16)
    for at in range(stripes):
        grp, high, low_bit = at // (stripes // 2), at // 2 % (stripes // 4), at % 2
        for kind, (target_ref, bit) in enumerate(
            ((output_kept, far_bit), (output_sent, 1 - far_bit))
        ):
            first = ((high * 4 + bit * 2 + low_bit) * 2 + core) * own_rows
            cut = pl.ds(pl.multiple_of(first, own_rows), own_rows)
            output_outs.append(
                pltpu.make_async_copy(
                    w_output.at[grp, cut], target_ref.at[at], place_sem.at[2 * at + kind]
                )
            )
            output_outs[-1].start()
    for one in up_outs + down_outs + output_outs:
        one.wait()
    for one in back_copies:
        one.wait()
    for one in [grad_far, out_near, out_on, down_far]:
        one.wait_send()
    for one in down_near + output_near + core_copies:
        one.wait_send()


def mlp(heads, tokens, gain, out_rows, out_across, output_parts, in_parts, down_parts):
    count, row_count, _ = heads.shape
    groups, reps = lax.axis_size("grp"), lax.axis_size("rep")
    rows, width = tokens.shape
    half = width // 2
    own_width = in_parts[0].shape[2]
    vmem = pl.BlockSpec(memory_space=pltpu.VMEM)
    anywhere = pl.BlockSpec(memory_space=pl.ANY)
    low, full = jnp.bfloat16, jnp.float32
    others = pltpu.SemaphoreType.DMA((count - 1,))
    return pl.pallas_call(
        mlp_kernel,
        out_shape=(
            jax.ShapeDtypeStruct((rows, width), full),
            jax.ShapeDtypeStruct((2, rows, width), low),
            jax.ShapeDtypeStruct((rows, width), full),
            jax.ShapeDtypeStruct((count, row_count, LANES), low),
            jax.ShapeDtypeStruct((half, own_width), low),
            jax.ShapeDtypeStruct((half, own_width), low),
            jax.ShapeDtypeStruct((half, own_width), low),
            jax.ShapeDtypeStruct((own_width // (2 * LANES), LANES, width), low),
            jax.ShapeDtypeStruct((own_width // (2 * LANES), LANES, width), low),
            jax.ShapeDtypeStruct((reps // 2, half // reps, width), low),
            jax.ShapeDtypeStruct((reps // 2, half // reps, width), low),
        ),
        in_specs=[vmem] * 3 + [anywhere] * 11,
        out_specs=(vmem,) * 5 + (anywhere,) * 6,
        scratch_shapes=[
            pltpu.VMEM((rows, width), low),
            pltpu.VMEM((rows, width), low),
            pltpu.VMEM((groups, reps, row_count, LANES), low),
            pltpu.VMEM((4, rows, width), low),
            pltpu.VMEM((4, rows, width), low),
            pltpu.VMEM((4, rows, own_width), low),
            pltpu.VMEM((4, rows, 2 * own_width), low),
            pltpu.VMEM((2, half, width), low),
            pltpu.VMEM((2, half, 2 * own_width), low),
            pltpu.VMEM((own_width, width), low),
            pltpu.VMEM((2, rows, width), low),
            pltpu.VMEM((2, rows, width), low),
            pltpu.VMEM((rows, width), low),
            pltpu.VMEM((rows, width), low),
            pltpu.VMEM((2, rows, width), low),
            pltpu.SemaphoreType.DMA((9,)),
            pltpu.SemaphoreType.DMA((2,)),
            pltpu.SemaphoreType.DMA((14,)),
            pltpu.SemaphoreType.DMA((14,)),
            others,
            others,
            others,
            others,
            pltpu.SemaphoreType.DMA((own_width // LANES,)),
            pltpu.SemaphoreType.DMA((reps,)),
            pltpu.SemaphoreType.DMA((reps,)),
            pltpu.SemaphoreType.DMA((reps,)),
            pltpu.SemaphoreType.REGULAR,
        ],
        compiler_params=pltpu.CompilerParams(
            vmem_limit_bytes=62 * 1024 * 1024, collective_id=2, has_side_effects=True
        ),
        cost_estimate=pl.CostEstimate(
            flops=150 * 10**9, bytes_accessed=150 << 20, transcendentals=0
        ),
        name="mlp",
    )(heads, tokens, gain, out_rows, out_across, *output_parts, *in_parts, *down_parts)


def after_kernel(*refs):
    pass


def after(values, ahead):
    anywhere = pl.BlockSpec(memory_space=pl.ANY)
    return pl.pallas_call(
        after_kernel,
        out_shape=tuple(jax.ShapeDtypeStruct(one.shape, one.dtype) for one in values),
        in_specs=[anywhere] * (len(values) + 1),
        out_specs=(anywhere,) * len(values),
        input_output_aliases={at: at for at in range(len(values))},
        name="after",
    )(*values, ahead)


def heads_body(
    tokens,
    attn_gain,
    w_query,
    w_key,
    w_value,
    w_output,
    mlp_gain,
    w_gate,
    w_up,
    w_down,
    out_grad,
    lengths,
):
    groups, reps = lax.axis_size("grp"), lax.axis_size("rep")
    here, there = lax.axis_index("grp"), lax.axis_index("rep")
    micro_count, row_count, width = tokens.shape
    rows = micro_count * row_count
    hidden_width = w_gate.shape[1]
    own_width = hidden_width // (2 * groups)

    out_rows = out_grad.reshape(rows, width)
    (
        gathered_rows,
        qkv,
        w_heads,
        gate_in,
        up_own,
        down_first,
        down_second,
        output_part,
        out_own,
        gains,
    ) = gather_heads(
        tokens,
        (attn_gain, mlp_gain),
        w_query,
        w_key,
        w_value,
        w_gate,
        w_up,
        w_down,
        w_output,
        out_rows,
    )
    gain_one = gains[:, 0].reshape(width).astype(jnp.float32)
    gain_two = gains[:, 1].reshape(width).astype(jnp.float32)
    inputs = tokens.astype(jnp.float32)

    output_parts = (w_output, output_part, swap(output_part, 0, 2))
    in_parts = (gate_in, up_own, swap(up_own, 1, 0))
    down_parts = (down_first, down_second, swap(down_first, 1, 0))

    tables = attention_tables(lengths, here, there, row_count)
    attended, out_heads, log_sum, query, key, value = attend(tables, qkv)
    (
        mixed,
        down_sums,
        grad_mixed,
        grad_heads,
        gate_part,
        up_kept,
        up_sent,
        down_kept,
        down_sent,
        output_kept,
        output_sent,
    ) = mlp(
        attended,
        tokens.reshape(rows, width),
        jnp.broadcast_to(gain_two[None], (8, width)),
        out_rows,
        swap(out_own, 0, 4),
        output_parts,
        in_parts,
        down_parts,
    )

    own_rows = width // (groups * reps)
    high = reps // 8
    high_steps = [step for step in (8 << place for place in range(8)) if step < reps]
    bit = {step: (there // step) % 2 for step in [1, 2, 4] + high_steps}

    def send(parts, axis, step):
        flag, grp_step, rep_step = (here, 1, 0) if step == 0 else (bit[step], 0, step)
        return pick(parts, flag, axis), swap(pick(parts, 1 - flag, axis), grp_step, rep_step)

    def add(kept, arrived):
        return narrow(kept.astype(jnp.float32) + arrived.astype(jnp.float32))

    def over(parts, axis, step):
        return add(*send(parts, axis, step))

    def over_high(parts, axis):
        for step in high_steps:
            shape = parts.shape
            count = shape[axis] // 2
            parts = parts.reshape(shape[:axis] + (count, 2) + shape[axis + 1 :])
            parts = over(parts, axis + 1, step)
        return parts.reshape(parts.shape[:axis] + parts.shape[axis + 1 :])

    by_owner = (groups, high, 2, 2, 2, own_rows)
    up_sent = swap(up_sent, 1, 0)
    down_sent = swap(down_sent, 0, 2)
    output_sent = swap(output_sent, 0, 4)
    sums_sent = swap(down_sums[1], 0, 4)

    back = attend_back(tables, query, key, value, out_heads, log_sum, grad_heads)

    up_sent, down_sent, output_sent, sums_sent = after(
        (up_sent, down_sent, output_sent, sums_sent), back
    )
    up_part = add(up_kept, up_sent).reshape(by_owner[1:] + (own_width,))
    down_part = add(down_kept, down_sent).reshape(groups, high, LANES, width)
    output_grad = add(output_kept, output_sent).reshape(groups, high, 2, own_rows, width)
    early = (up_part, down_part, output_grad)
    gate_kept, gate_sent = send(gate_part.reshape(by_owner[1:] + (own_width,)), 2, 2)
    up_kept, up_sent = send(up_part, 0, 8)
    down_kept, down_sent = send(down_part, 0, 0)
    output_kept, output_sent = send(output_grad, 0, 0)
    grad_in, heads_grad = scatter_heads(
        back.reshape(reps, groups * row_count, 3 * LANES), w_heads, gathered_rows, early
    )
    gate_sent, up_sent, down_sent, output_sent = after(
        (gate_sent, up_sent, down_sent, output_sent), grad_in
    )
    gate_part = over_high(add(gate_kept, gate_sent), 0)
    up_part = over(add(up_kept, up_sent), 1, 2)
    down_grad = over_high(add(down_kept, down_sent), 0).astype(jnp.float32)
    output_grad = over_high(over(add(output_kept, output_sent), 1, 2), 0).astype(jnp.float32)
    block_out = (
        mixed + down_sums[0].astype(jnp.float32) + sums_sent.astype(jnp.float32)
    ).astype(jnp.bfloat16)

    quad_part = jnp.concatenate([gate_part, up_part], axis=-1)
    kept = pick(quad_part, bit[4], 0)
    crossed = swap(pick(quad_part, 1 - bit[4], 0), 0, 4)
    columns = []
    for part in (kept, crossed):
        columns.append(pick(part, bit[1], 0))
        columns.append(swap(pick(part, 1 - bit[1], 0), 0, 1))

    def by_bit(flag, own, other):
        return jnp.where(
            flag == 0, jnp.stack([own, other], axis=1), jnp.stack([other, own], axis=1)
        )

    pieces = by_bit(
        bit[4], by_bit(bit[1], columns[0], columns[1]), by_bit(bit[1], columns[2], columns[3])
    )
    pieces = pieces.reshape(own_rows, 2, 2, 2, groups, high, 2, LANES)
    pieces = pieces.transpose(3, 0, 4, 5, 1, 6, 2, 7).reshape(2, own_rows, hidden_width)
    gate_grad, up_grad = pieces[0].astype(jnp.float32), pieces[1].astype(jnp.float32)

    grad_norm_in, unused_gain = norm_backward(
        inputs.reshape(rows, width), gain_one, grad_in.reshape(rows, width)
    )
    token_grad = (grad_mixed + grad_norm_in).astype(jnp.bfloat16)

    heads_grad = (
        heads_grad.reshape(reps, own_rows, 3, LANES)
        .transpose(2, 1, 0, 3)
        .reshape(3, own_rows, width)
        .astype(jnp.float32)
    )

    def own_part(value):
        return lax.dynamic_slice_in_dim(value, there * own_rows, own_rows, axis=0).astype(
            jnp.float32
        )

    attn_gain_grad = (
        jnp.sum(own_part(w_query) * heads_grad[0], axis=1)
        + jnp.sum(own_part(w_key) * heads_grad[1], axis=1)
        + jnp.sum(own_part(w_value) * heads_grad[2], axis=1)
    ) / own_part(attn_gain)
    mlp_gain_grad = (
        jnp.sum(own_part(w_gate) * gate_grad, axis=1) + jnp.sum(own_part(w_up) * up_grad, axis=1)
    ) / own_part(mlp_gain)
    block_shape = tokens.shape
    return (
        block_out.reshape(block_shape),
        token_grad.reshape(block_shape),
        attn_gain_grad,
        heads_grad[0],
        heads_grad[1],
        heads_grad[2],
        output_grad,
        mlp_gain_grad,
        gate_grad,
        up_grad,
        down_grad,
    )


def pick_body(*arrays):
    tokens = arrays[0]
    groups, reps = lax.axis_size("grp"), lax.axis_size("rep")
    fits = (
        groups == 2
        and tokens.shape[0] == groups
        and tokens.shape[2] == reps * LANES
        and reps == 16
        and reps & (reps - 1) == 0
        and tokens.shape[1] % UNIT_PAIR == 0
        and arrays[7].shape[1] == groups * reps * LANES
    )
    return heads_body(*arrays) if fits else ring_body(*arrays)


def solution(mesh):
    in_specs = (
        P(None, ("grp", "rep"), None),
        P("grp"),
        P("grp", None),
        P("grp", None),
        P("grp", None),
        P("grp", None),
        P("grp"),
        P("grp", None),
        P("grp", None),
        P("grp", None),
        P(None, ("grp", "rep"), None),
        P(),
    )
    out_specs = (
        P(None, ("grp", "rep"), None),
        P(None, ("grp", "rep"), None),
        P(("grp", "rep")),
        P(("grp", "rep"), None),
        P(("grp", "rep"), None),
        P(("grp", "rep"), None),
        P(("grp", "rep"), None),
        P(("grp", "rep")),
        P(("grp", "rep"), None),
        P(("grp", "rep"), None),
        P(("grp", "rep"), None),
    )
    return jax.shard_map(pick_body, mesh=mesh, in_specs=in_specs, out_specs=out_specs, check_vma=False)
```

```python
import functools
import math

import jax
import jax.numpy as jnp
from jax import lax
from jax.experimental import pallas as pl
from jax.experimental.pallas import tpu as pltpu
from jax.sharding import PartitionSpec as P

HD = 64
WINDOW = 2048


epsilon = 1e-05
rope_base = 10000.0
masked_score = -1e30
BOTH = ("grp", "rep")
LANES = 128
UNIT_BLOCK = 8
UNIT_PAIR = 16
KERNEL_VMEM = 56 * 1024 * 1024
SCATTER_REFS = 18


def from_behind(value, axis, steps):
    count = lax.axis_size(axis)
    first, last = (max(0, -steps), min(count, count - steps))
    return lax.ppermute(value, axis, [(source, source + steps) for source in range(first, last)])


def rms_scale(values):
    return lax.rsqrt(jnp.mean(values * values, axis=-1, keepdims=True) + epsilon)


def norm_backward(values, gain_full, grad_normed):
    inverse = rms_scale(values)
    normed = values * inverse
    gain_grad = jnp.sum(grad_normed * normed, axis=0)
    weighted = grad_normed * gain_full
    return (
        inverse * (weighted - normed * jnp.mean(weighted * normed, axis=-1, keepdims=True)),
        gain_grad,
    )


def rotary(values, cosine, sine_table):
    half_width = values.shape[-1] // 2
    first_half = values[..., :half_width]
    second_half = values[..., half_width:]
    return jnp.concatenate(
        [
            first_half * cosine - second_half * sine_table,
            second_half * cosine + first_half * sine_table,
        ],
        axis=-1,
    )


def pick_rows(rows_block, row_ids):
    return jnp.take(rows_block, row_ids, axis=0)


def take_rows(values, row_ids):
    return jax.vmap(pick_rows)(values, row_ids)


def gather_attn(attn_gain, w_query, w_key, w_value, w_output):
    return (
        lax.all_gather(attn_gain, "grp", axis=0, tiled=True),
        lax.all_gather(w_query, "grp", axis=0, tiled=True),
        lax.all_gather(w_key, "grp", axis=0, tiled=True),
        lax.all_gather(w_value, "grp", axis=0, tiled=True),
        lax.all_gather(w_output, "grp", axis=0, tiled=True),
    )


def gather_mlp(mlp_gain, w_gate, w_up, w_down):
    return (
        lax.all_gather(mlp_gain, "grp", axis=0, tiled=True),
        lax.all_gather(w_gate, "grp", axis=0, tiled=True),
        lax.all_gather(w_up, "grp", axis=0, tiled=True),
        lax.all_gather(w_down, "grp", axis=0, tiled=True),
    )


def reduce_attn(gain_grad, query_grad, key_grad, value_grad, output_grad):
    return (
        lax.psum_scatter(gain_grad, ("grp", "rep"), scatter_dimension=0, tiled=True),
        lax.psum_scatter(query_grad, ("grp", "rep"), scatter_dimension=0, tiled=True),
        lax.psum_scatter(key_grad, ("grp", "rep"), scatter_dimension=0, tiled=True),
        lax.psum_scatter(value_grad, ("grp", "rep"), scatter_dimension=0, tiled=True),
        lax.psum_scatter(output_grad, ("grp", "rep"), scatter_dimension=0, tiled=True),
    )


def reduce_mlp(gain_grad, gate_grad, up_grad, down_grad):
    return (
        lax.psum_scatter(gain_grad, ("grp", "rep"), scatter_dimension=0, tiled=True),
        lax.psum_scatter(gate_grad, ("grp", "rep"), scatter_dimension=0, tiled=True),
        lax.psum_scatter(up_grad, ("grp", "rep"), scatter_dimension=0, tiled=True),
        lax.psum_scatter(down_grad, ("grp", "rep"), scatter_dimension=0, tiled=True),
    )


def pass_on(carried, unused):
    arrived = from_behind(carried, ("grp", "rep"), 1)
    return (arrived, arrived)


def pass_back(running, portion):
    arrived = from_behind(running.astype(jnp.bfloat16), ("grp", "rep"), -1).astype(running.dtype)
    return (arrived + portion, None)


def ring_body(
    tokens,
    attn_gain,
    w_query,
    w_key,
    w_value,
    w_output,
    mlp_gain,
    w_gate,
    w_up,
    w_down,
    out_grad,
    lengths,
):
    devices = lax.axis_size(("grp", "rep"))
    rank_here = lax.axis_index(("grp", "rep"))
    micro_count, row_count, model_width = tokens.shape
    per_dev = row_count // devices
    head_count = model_width // HD
    reach_count = (WINDOW + row_count - 2) // row_count
    head_group = math.gcd(head_count, 4)
    group_count = head_count // head_group
    score_scale = 1.0 / math.sqrt(HD)
    unit_ids = jnp.arange(row_count, dtype=jnp.int32)
    seq_ends = jnp.cumsum(lengths, axis=1)
    starts = seq_ends - lengths
    seq_order = jnp.arange(lengths.shape[1], dtype=jnp.int32)
    earlier = seq_order[None, :] < seq_order[:, None]
    dealt_start = jnp.sum(jnp.where(earlier[None], lengths[:, None, :], 0), axis=2)
    seq_of = jnp.sum((seq_ends[:, None, :] <= unit_ids[None, :, None]).astype(jnp.int32), axis=2)
    seq_dealt = jnp.take_along_axis(dealt_start, seq_of, axis=1)
    unit_of = seq_dealt + unit_ids[None, :] - jnp.take_along_axis(starts, seq_of, axis=1)
    micro_ids = jnp.arange(micro_count, dtype=jnp.int32)[:, None]
    source_unit = (
        jnp.zeros((micro_count, row_count), jnp.int32)
        .at[micro_ids, unit_of]
        .set(jnp.broadcast_to(unit_ids[None, :], unit_of.shape))
    )
    unit_begin = (
        jnp.zeros((micro_count, row_count), jnp.int32).at[micro_ids, unit_of].set(seq_dealt)
    )
    local_ids = jnp.arange(row_count, dtype=jnp.int32)
    local_step = local_ids % per_dev
    local_source = local_ids // per_dev
    distance = jnp.arange(reach_count + 1, dtype=jnp.int32)
    owner_dev = rank_here - distance
    owner_ok = owner_dev >= 0
    owner_unit = jnp.maximum(owner_dev, 0)[:, None] * per_dev + local_step[None, :]
    key_begin = unit_begin[:, owner_unit]
    key_pos = (owner_unit[None] - key_begin) * devices + local_source[None, None, :]
    query_begin = key_begin[:, 0]
    query_pos = key_pos[:, 0]
    allowed = (
        owner_ok[None, None, :, None]
        & (query_begin[:, :, None, None] == key_begin[:, None, :, :])
        & (key_pos[:, None, :, :] <= query_pos[:, :, None, None])
        & (query_pos[:, :, None, None] - key_pos[:, None, :, :] < WINDOW)
    )
    mask_full = allowed[:, None]
    half_width = HD // 2
    frequency = jnp.power(rope_base, -2.0 * jnp.arange(half_width, dtype=jnp.float32) / HD)
    angles = query_pos.astype(jnp.float32)[:, :, None] * frequency[None, None, :]
    cosine = jnp.cos(angles)[:, :, None, :]
    sine_table = jnp.sin(angles)[:, :, None, :]
    head_shape = (micro_count, row_count, head_count, HD)
    block_shape = (micro_count, row_count, model_width)
    gathered = gather_attn(attn_gain, w_query, w_key, w_value, w_output)
    gain_one = gathered[0].astype(jnp.float32)
    inputs = tokens.astype(jnp.float32).reshape(micro_count * row_count, model_width)
    normed_in = (inputs * rms_scale(inputs) * gain_one).astype(jnp.bfloat16)
    queries = jnp.dot(normed_in, gathered[1], preferred_element_type=jnp.float32).astype(
        jnp.bfloat16
    )
    keys_in = jnp.dot(normed_in, gathered[2], preferred_element_type=jnp.float32).astype(
        jnp.bfloat16
    )
    values_in = jnp.dot(normed_in, gathered[3], preferred_element_type=jnp.float32).astype(
        jnp.bfloat16
    )
    dealt = (
        lax.all_to_all(
            take_rows(queries.reshape(block_shape), source_unit),
            ("grp", "rep"),
            split_axis=1,
            concat_axis=1,
            tiled=True,
        ),
        lax.all_to_all(
            take_rows(keys_in.reshape(block_shape), source_unit),
            ("grp", "rep"),
            split_axis=1,
            concat_axis=1,
            tiled=True,
        ),
        lax.all_to_all(
            take_rows(values_in.reshape(block_shape), source_unit),
            ("grp", "rep"),
            split_axis=1,
            concat_axis=1,
            tiled=True,
        ),
    )
    rot_q = rotary(dealt[0].reshape(head_shape).astype(jnp.float32), cosine, sine_table).astype(
        jnp.bfloat16
    )
    rot_k = rotary(dealt[1].reshape(head_shape).astype(jnp.float32), cosine, sine_table).astype(
        jnp.bfloat16
    )
    own_pair = jnp.stack([rot_k.reshape(block_shape), dealt[2]], axis=0)
    last_pair, farther = lax.scan(pass_on, own_pair, None, length=reach_count)
    context = jnp.concatenate([own_pair[None], farther], axis=0).reshape(
        reach_count + 1, 2, micro_count, row_count, head_count, HD
    )

    def group_scores(query_part, pair_part):
        scores = (
            jnp.einsum(
                "mqge,dmkge->mgqdk", query_part, pair_part[:, 0], preferred_element_type=jnp.float32
            )
            * score_scale
        )
        return jnp.where(mask_full, scores, masked_score)

    def forward_group(group_index, carried):
        attended_all, log_all = carried
        head_start = group_index * head_group
        query_part = lax.dynamic_slice_in_dim(rot_q, head_start, head_group, axis=2)
        pair_part = lax.dynamic_slice_in_dim(context, head_start, head_group, axis=4)
        scores = group_scores(query_part, pair_part)
        row_max = jnp.max(scores, axis=(3, 4), keepdims=True)
        weights_exp = jnp.exp(scores - row_max)
        row_sum = jnp.sum(weights_exp, axis=(3, 4), keepdims=True)
        soft_probs = (weights_exp / row_sum).astype(jnp.bfloat16)
        attended = jnp.einsum(
            "mgqdk,dmkge->mqge", soft_probs, pair_part[:, 1], preferred_element_type=jnp.float32
        ).astype(jnp.bfloat16)
        attended_all = lax.dynamic_update_slice_in_dim(attended_all, attended, head_start, axis=2)
        log_all = lax.dynamic_update_slice_in_dim(
            log_all, row_max + jnp.log(row_sum), head_start, axis=1
        )
        return (attended_all, log_all)

    attended_heads, log_sum = lax.fori_loop(
        0,
        group_count,
        forward_group,
        (
            jnp.zeros(head_shape, jnp.bfloat16),
            jnp.zeros((micro_count, head_count, row_count, 1, 1), jnp.float32),
        ),
    )
    returned = lax.all_to_all(
        attended_heads.reshape(block_shape), ("grp", "rep"), split_axis=1, concat_axis=1, tiled=True
    )
    attn_rows = take_rows(returned, unit_of).reshape(micro_count * row_count, model_width)
    mixed = inputs + jnp.dot(attn_rows, gathered[4], preferred_element_type=jnp.float32)
    mlp_set = gather_mlp(mlp_gain, w_gate, w_up, w_down)
    gain_two = mlp_set[0].astype(jnp.float32)
    normed_mid = (mixed * rms_scale(mixed) * gain_two).astype(jnp.bfloat16)
    gate_pre = jnp.dot(normed_mid, mlp_set[1], preferred_element_type=jnp.float32)
    up_pre = jnp.dot(normed_mid, mlp_set[2], preferred_element_type=jnp.float32)
    gate_sig = jax.nn.sigmoid(gate_pre)
    gate_silu = gate_pre * gate_sig
    hidden = (gate_silu * up_pre).astype(jnp.bfloat16)
    block_out = (mixed + jnp.dot(hidden, mlp_set[3], preferred_element_type=jnp.float32)).astype(
        jnp.bfloat16
    )
    mlp_set = gather_mlp(mlp_gain, w_gate, w_up, w_down)
    out_rows = out_grad.reshape(micro_count * row_count, model_width)
    down_grad = jnp.einsum("tf,td->fd", hidden, out_rows, preferred_element_type=jnp.float32)
    grad_hidden = jnp.einsum("td,fd->tf", out_rows, mlp_set[3], preferred_element_type=jnp.float32)
    grad_gate = (grad_hidden * up_pre * gate_sig * (1.0 + gate_pre * (1.0 - gate_sig))).astype(
        jnp.bfloat16
    )
    grad_up = (grad_hidden * gate_silu).astype(jnp.bfloat16)
    gate_grad = jnp.einsum("td,tf->df", normed_mid, grad_gate, preferred_element_type=jnp.float32)
    up_grad = jnp.einsum("td,tf->df", normed_mid, grad_up, preferred_element_type=jnp.float32)
    grad_mid = jnp.einsum(
        "tf,df->td", grad_gate, mlp_set[1], preferred_element_type=jnp.float32
    ) + jnp.einsum("tf,df->td", grad_up, mlp_set[2], preferred_element_type=jnp.float32)
    grad_norm_mid, mlp_gain_grad = norm_backward(mixed, gain_two, grad_mid)
    grad_mixed = out_rows.astype(jnp.float32) + grad_norm_mid
    mlp_sums = reduce_mlp(mlp_gain_grad, gate_grad, up_grad, down_grad)
    gathered = gather_attn(attn_gain, w_query, w_key, w_value, w_output)
    grad_branch = grad_mixed.astype(jnp.bfloat16)
    output_grad = jnp.einsum(
        "td,te->de", attn_rows, grad_branch, preferred_element_type=jnp.float32
    )
    grad_att = jnp.einsum(
        "te,de->td", grad_branch, gathered[4], preferred_element_type=jnp.float32
    ).astype(jnp.bfloat16)
    grad_dealt = lax.all_to_all(
        take_rows(grad_att.reshape(block_shape), source_unit),
        ("grp", "rep"),
        split_axis=1,
        concat_axis=1,
        tiled=True,
    )
    grad_heads = grad_dealt.reshape(head_shape)

    def backward_group(group_index, carried):
        query_total, pair_total = carried
        head_start = group_index * head_group
        query_part = lax.dynamic_slice_in_dim(rot_q, head_start, head_group, axis=2)
        grad_part = lax.dynamic_slice_in_dim(grad_heads, head_start, head_group, axis=2)
        pair_part = lax.dynamic_slice_in_dim(context, head_start, head_group, axis=4)
        log_part = lax.dynamic_slice_in_dim(log_sum, head_start, head_group, axis=1)
        scores = group_scores(query_part, pair_part)
        soft_probs = jnp.exp(scores - log_part)
        grad_probs = jnp.einsum(
            "mqge,dmkge->mgqdk", grad_part, pair_part[:, 1], preferred_element_type=jnp.float32
        )
        inner_sum = jnp.sum(soft_probs * grad_probs, axis=(3, 4), keepdims=True)
        grad_scores = (soft_probs * (grad_probs - inner_sum)).astype(jnp.bfloat16)
        query_piece = (
            jnp.einsum(
                "mgqdk,dmkge->mqge",
                grad_scores,
                pair_part[:, 0],
                preferred_element_type=jnp.float32,
            )
            * score_scale
        )
        key_part = (
            jnp.einsum(
                "mgqdk,mqge->dmkge", grad_scores, query_part, preferred_element_type=jnp.float32
            )
            * score_scale
        )
        value_part = jnp.einsum(
            "mgqdk,mqge->dmkge",
            soft_probs.astype(jnp.bfloat16),
            grad_part,
            preferred_element_type=jnp.float32,
        )
        query_total = lax.dynamic_update_slice_in_dim(query_total, query_piece, head_start, axis=2)
        pair_total = lax.dynamic_update_slice_in_dim(
            pair_total, jnp.stack([key_part, value_part], axis=1), head_start, axis=4
        )
        return (query_total, pair_total)

    query_total, pair_total = lax.fori_loop(
        0,
        group_count,
        backward_group,
        (
            jnp.zeros(head_shape, jnp.float32),
            jnp.zeros((reach_count + 1, 2) + head_shape, jnp.float32),
        ),
    )
    partials = pair_total.reshape(reach_count + 1, 2, micro_count, row_count, model_width)
    own_total, unused_out = lax.scan(
        pass_back, partials[reach_count], partials[:reach_count], reverse=True
    )
    query_back = rotary(query_total, cosine, -sine_table).astype(jnp.bfloat16)
    key_back = rotary(own_total[0].reshape(head_shape), cosine, -sine_table).astype(jnp.bfloat16)
    value_back = own_total[1].astype(jnp.bfloat16)
    grad_back = (
        lax.all_to_all(
            query_back.reshape(block_shape), ("grp", "rep"), split_axis=1, concat_axis=1, tiled=True
        ),
        lax.all_to_all(
            key_back.reshape(block_shape), ("grp", "rep"), split_axis=1, concat_axis=1, tiled=True
        ),
        lax.all_to_all(value_back, ("grp", "rep"), split_axis=1, concat_axis=1, tiled=True),
    )
    query_rows = take_rows(grad_back[0], unit_of).reshape(micro_count * row_count, model_width)
    key_rows = take_rows(grad_back[1], unit_of).reshape(micro_count * row_count, model_width)
    value_rows = take_rows(grad_back[2], unit_of).reshape(micro_count * row_count, model_width)
    query_grad = jnp.einsum("td,te->de", normed_in, query_rows, preferred_element_type=jnp.float32)
    key_grad = jnp.einsum("td,te->de", normed_in, key_rows, preferred_element_type=jnp.float32)
    value_grad = jnp.einsum("td,te->de", normed_in, value_rows, preferred_element_type=jnp.float32)
    grad_in = jnp.einsum("te,de->td", query_rows, gathered[1], preferred_element_type=jnp.float32)
    grad_in = grad_in + jnp.einsum(
        "te,de->td", key_rows, gathered[2], preferred_element_type=jnp.float32
    )
    grad_in = grad_in + jnp.einsum(
        "te,de->td", value_rows, gathered[3], preferred_element_type=jnp.float32
    )
    grad_norm_in, attn_gain_grad = norm_backward(inputs, gain_one, grad_in)
    token_grad = (grad_mixed + grad_norm_in).astype(jnp.bfloat16)
    attn_sums = reduce_attn(attn_gain_grad, query_grad, key_grad, value_grad, output_grad)
    return (
        block_out.reshape(block_shape),
        token_grad.reshape(block_shape),
        attn_sums[0],
        attn_sums[1],
        attn_sums[2],
        attn_sums[3],
        attn_sums[4],
        mlp_sums[0],
        mlp_sums[1],
        mlp_sums[2],
        mlp_sums[3],
    )


def contract(left_side, right_side, left_dim, right_dim, kind=jnp.float32):
    return lax.dot_general(
        left_side,
        right_side,
        (((left_dim,), (right_dim,)), ((), ())),
        preferred_element_type=jnp.float32,
    ).astype(kind)


def swap_halves(values):
    lane = lax.broadcasted_iota(jnp.int32, values.shape, 1)
    ahead = pltpu.roll(values, LANES - HD // 2, 1)
    behind = pltpu.roll(values, HD // 2, 1)
    return jnp.where(lane % HD < HD // 2, -ahead, behind)


def fill_tables(lengths_ref, begin_at, cos_unit, sin_unit, cos_part, sin_part):
    parts, units = cos_part.shape[0], cos_unit.shape[0]
    here = lax.axis_index("grp")

    def frequency(shape):
        lane = lax.broadcasted_iota(jnp.int32, shape, 1) % (HD // 2)
        return jnp.exp(lane.astype(jnp.float32) * (-2.0 * math.log(rope_base) / HD))

    unit = lax.broadcasted_iota(jnp.int32, (units, LANES), 0)
    begin = jnp.zeros((units, LANES), jnp.int32)
    end = 0
    for seq in range(lengths_ref.shape[1]):
        end = end + lengths_ref[here, seq]
        begin = jnp.where(unit >= end, end, begin)
    begin_at[...] = begin
    angle = ((unit - begin) * parts).astype(jnp.float32) * frequency((units, LANES))
    cos_unit[...] = jnp.cos(angle)
    sin_unit[...] = jnp.sin(angle)
    part = lax.broadcasted_iota(jnp.int32, (parts, LANES), 0).astype(jnp.float32)
    angle = part * frequency((parts, LANES))
    cos_part[...] = jnp.cos(angle)
    sin_part[...] = jnp.sin(angle)


def begin_of(lengths_ref, unit):
    here = lax.axis_index("grp")
    begin, end = 0, 0
    for seq in range(lengths_ref.shape[1]):
        end = end + lengths_ref[here, seq]
        begin = jnp.where(unit >= end, end, begin)
    return begin


def key_range(lengths_ref, at, parts, block):
    first_unit = at * UNIT_BLOCK
    last_unit = first_unit + UNIT_BLOCK - 1
    least = jnp.maximum(begin_of(lengths_ref, first_unit) * parts, at * block - (WINDOW - 1))
    most = jnp.maximum(
        begin_of(lengths_ref, last_unit) * parts, (at + 1) * block - 1 - (WINDOW - 1)
    )
    first = jnp.maximum(least, 0) // block
    return first, jnp.minimum(jnp.maximum((most + block - 1) // block, first), at)


def low_of(begin_at, at, parts):
    begin = begin_at[pl.ds(pl.multiple_of(at * UNIT_BLOCK, UNIT_BLOCK), UNIT_BLOCK), :] * parts
    shape = (parts, UNIT_BLOCK, LANES)
    part = lax.broadcasted_iota(jnp.int32, shape, 0)
    unit = lax.broadcasted_iota(jnp.int32, shape, 1) + at * UNIT_BLOCK
    low = jnp.maximum(begin[None], unit * parts + part - (WINDOW - 1))
    return low.reshape(parts * UNIT_BLOCK, LANES).astype(jnp.float32)


def slot_of(part):
    groups, reps = lax.axis_size("grp"), lax.axis_size("rep")
    offset = (part % reps) ^ lax.axis_index("rep")
    return offset * groups + ((part // reps) ^ lax.axis_index("grp"))


def pair_angles(unit_at, cos_unit, sin_unit, cos_part, sin_part):
    unit_cos = cos_unit[pl.ds(unit_at, UNIT_PAIR), :][None]
    unit_sin = sin_unit[pl.ds(unit_at, UNIT_PAIR), :][None]
    part_cos = cos_part[...][:, None, :]
    part_sin = sin_part[...][:, None, :]
    cosine = unit_cos * part_cos - unit_sin * part_sin
    sine = unit_sin * part_cos + unit_cos * part_sin
    return cosine, sine


def key_offsets(block):
    row = lax.broadcasted_iota(jnp.int32, (block, block), 0)
    return (row % UNIT_BLOCK) * (block // UNIT_BLOCK) + row // UNIT_BLOCK


def query_offsets(block):
    column = lax.broadcasted_iota(jnp.int32, (block, block), 1)
    return (column % UNIT_BLOCK) * (block // UNIT_BLOCK) + column // UNIT_BLOCK


def attend_kernel(
    lengths_ref,
    qkv_ref,
    att_ref,
    out_ref,
    log_ref,
    query_ref,
    key_ref,
    value_ref,
    query_heads,
    key_t,
    tops,
    sums,
    totals,
    lows,
    causal_at,
    key_at,
    begin_at,
    cos_unit,
    sin_unit,
    cos_part,
    sin_part,
):
    parts, units, _ = qkv_ref.shape
    block = parts * UNIT_BLOCK
    pairs = units // UNIT_PAIR
    halves = UNIT_PAIR // UNIT_BLOCK
    wide = block // LANES
    fill_tables(lengths_ref, begin_at, cos_unit, sin_unit, cos_part, sin_part)
    key_at[...] = query_offsets(block).astype(jnp.float32)
    causal_at[...] = jnp.where(query_offsets(block) <= key_offsets(block), 0.0, masked_score)

    def lay_out(pair, unused):
        unit_at = pl.multiple_of(pair * UNIT_PAIR, UNIT_PAIR)
        rows = jnp.stack(
            [qkv_ref[slot_of(part), pl.ds(unit_at, UNIT_PAIR), :] for part in range(parts)]
        )
        cosine, sine = pair_angles(unit_at, cos_unit, sin_unit, cos_part, sin_part)
        flat = (parts * UNIT_PAIR, LANES)
        cosine = cosine.reshape(flat)
        sine = sine.reshape(flat)

        def rotated(values):
            values = values.astype(jnp.float32).reshape(flat)
            turned = values * cosine + swap_halves(values) * sine
            return turned.reshape(parts, UNIT_PAIR, LANES)

        query = rotated(rows[:, :, :LANES]) * (1.0 / math.sqrt(HD))
        key = rotated(rows[:, :, LANES : 2 * LANES])
        value = rows[:, :, 2 * LANES :].astype(jnp.float32)
        for half in range(halves):
            at = pair * halves + half
            cut = slice(half * UNIT_BLOCK, (half + 1) * UNIT_BLOCK)
            query_rows = query[:, cut].reshape(block, LANES)
            key_rows = key[:, cut].reshape(block, LANES)
            query_ref[at] = query_rows.astype(jnp.bfloat16)
            key_ref[at] = key_rows.astype(jnp.bfloat16)
            value_ref[at] = value[:, cut].reshape(block, LANES).astype(jnp.bfloat16)
            lane = lax.broadcasted_iota(jnp.int32, query_rows.shape, 1)
            query_heads[at, 0] = jnp.where(lane < HD, query_rows, 0.0).astype(jnp.bfloat16)
            query_heads[at, 1] = jnp.where(lane < HD, 0.0, query_rows).astype(jnp.bfloat16)
            key_t[at] = jnp.transpose(key_rows).astype(jnp.bfloat16)
        return unused

    lax.fori_loop(0, pairs, lay_out, 0)

    def query_pair(pair, unused):
        ids = [pair * halves + half for half in range(halves)]
        for half, at in enumerate(ids):
            lows[half] = low_of(begin_at, at, parts)
        first, _ = key_range(lengths_ref, ids[0], parts, block)
        _, plain = key_range(lengths_ref, ids[-1], parts, block)
        plain = jnp.minimum(plain, ids[0])

        def wider(value):
            return jnp.concatenate([value] * wide, axis=1)

        def scores_of(half, head, key_block, causal, bounded):
            scores = jnp.dot(
                query_heads[ids[half], head], key_t[key_block], preferred_element_type=jnp.float32
            )
            if causal:
                scores = scores + causal_at[...]
            if bounded:
                bound = wider(lows[half] - (key_block * block).astype(jnp.float32))
                scores = jnp.where(key_at[...] >= bound, scores, masked_score)
            return scores

        def folded(combine, values):
            result = values[:, :LANES]
            for at in range(1, wide):
                result = combine(result, values[:, at * LANES : (at + 1) * LANES])
            return result

        def top_step(half, head, key_block, causal, bounded, fresh):
            high = folded(jnp.maximum, scores_of(half, head, key_block, causal, bounded))
            tops[half, head] = high if fresh else jnp.maximum(tops[half, head], high)

        def sum_step(half, head, key_block, causal, bounded, fresh):
            scores = scores_of(half, head, key_block, causal, bounded)
            weights = jnp.exp(scores - wider(tops[half, head]))
            part = folded(jnp.add, weights)
            product = jnp.dot(
                weights.astype(jnp.bfloat16),
                value_ref[key_block],
                preferred_element_type=jnp.float32,
            )
            sums[half, head] = part if fresh else sums[half, head] + part
            totals[half, head] = product if fresh else totals[half, head] + product

        def over_keys(step):
            for half, at in enumerate(ids):
                for head in range(2):
                    step(half, head, at, True, True, True)
                    for earlier in ids[:half]:
                        step(half, head, earlier, False, True, False)

            def all_steps(bounded):
                def go(key_block, unused):
                    for half in range(halves):
                        for head in range(2):
                            step(half, head, key_block, False, bounded, False)
                    return unused

                return go

            lax.fori_loop(first, plain, all_steps(True), 0)
            lax.fori_loop(plain, ids[0], all_steps(False), 0)

        over_keys(top_step)
        for half in range(halves):
            for head in range(2):
                high = jnp.max(tops[half, head], axis=1, keepdims=True)
                tops[half, head] = jnp.broadcast_to(high, (block, LANES))
        over_keys(sum_step)
        done = []
        for half, at in enumerate(ids):
            rows = []
            for head in range(2):
                total = jnp.broadcast_to(
                    jnp.sum(sums[half, head], axis=1, keepdims=True), (block, LANES)
                )
                rows.append(totals[half, head] / total)
                log = jnp.transpose(tops[half, head] + jnp.log(total))
                log_ref[at, head : head + 1, :] = log[0:1]
            lane = lax.broadcasted_iota(jnp.int32, (block, LANES), 1)
            both = jnp.where(lane < HD, rows[0], rows[1])
            out_ref[at] = jnp.transpose(both)
            done.append(both.reshape(parts, UNIT_BLOCK, LANES))
        unit_at = pl.multiple_of(pair * UNIT_PAIR, UNIT_PAIR)
        att_ref[:, pl.ds(unit_at, UNIT_PAIR), :] = jnp.concatenate(done, axis=1).astype(
            jnp.bfloat16
        )
        return unused

    lax.fori_loop(0, pairs, query_pair, 0)


def attend_back_kernel(
    lengths_ref,
    query_ref,
    key_ref,
    value_ref,
    out_ref,
    log_ref,
    grad_ref,
    back_ref,
    key_t,
    key_total,
    value_total,
    key_at,
    causal_at,
    begin_at,
    cos_unit,
    sin_unit,
    cos_part,
    sin_part,
):
    parts, units, _ = grad_ref.shape
    block = parts * UNIT_BLOCK
    pairs = units // UNIT_PAIR
    halves = UNIT_PAIR // UNIT_BLOCK
    fill_tables(lengths_ref, begin_at, cos_unit, sin_unit, cos_part, sin_part)
    key_at[...] = key_offsets(block).astype(jnp.float32)
    causal_at[...] = jnp.where(key_offsets(block) <= query_offsets(block), 0.0, masked_score)

    def lay_out(at, unused):
        key_t[at] = jnp.transpose(key_ref[at].astype(jnp.float32)).astype(jnp.bfloat16)
        key_total[at] = jnp.zeros((block, LANES), jnp.float32)
        value_total[at] = jnp.zeros((block, LANES), jnp.float32)
        return unused

    lax.fori_loop(0, pairs * halves, lay_out, 0)

    def split_heads(values, axis):
        place = lax.broadcasted_iota(jnp.int32, values.shape, axis)
        zero = jnp.zeros_like(values)
        return [
            jnp.where(place < HD, values, zero).astype(jnp.bfloat16),
            jnp.where(place < HD, zero, values).astype(jnp.bfloat16),
        ]

    def prepare(at, grad_rows):
        query_rows = query_ref[at].astype(jnp.float32)
        grad_turned = jnp.transpose(grad_rows)
        product = grad_turned * out_ref[at]
        return dict(
            low=jnp.transpose(low_of(begin_at, at, parts))[0:1],
            query=jnp.concatenate(split_heads(query_rows, 1), axis=0),
            grad=jnp.concatenate(split_heads(grad_rows, 1), axis=0),
            query_t=split_heads(jnp.transpose(query_rows), 0),
            grad_t=split_heads(grad_turned, 0),
            inner=[
                jnp.sum(product[head * HD : (head + 1) * HD], axis=0, keepdims=True)
                for head in range(2)
            ],
            logs=[log_ref[at, head : head + 1, :] for head in range(2)],
        )

    def step(held, key_block, carried, causal, bounded):
        probs, slopes, new = [], [], []
        for head in range(2):
            scores = jnp.dot(
                key_ref[key_block], held["query_t"][head], preferred_element_type=jnp.float32
            )
            if causal:
                scores = scores + causal_at[...]
            if bounded:
                scores = jnp.where(
                    key_at[...] >= held["low"] - (key_block * block).astype(jnp.float32), scores, masked_score
                )
            soft = jnp.exp(scores - held["logs"][head])
            grad_probs = jnp.dot(
                value_ref[key_block], held["grad_t"][head], preferred_element_type=jnp.float32
            )
            slope = (soft * (grad_probs - held["inner"][head])).astype(jnp.bfloat16)
            probs.append(soft.astype(jnp.bfloat16))
            slopes.append(slope)
            new.append(
                carried[head]
                + jnp.dot(
                    key_t[key_block, pl.ds(head * HD, HD), :],
                    slope,
                    preferred_element_type=jnp.float32,
                )
            )
        return tuple(new), probs, slopes

    def add_key(key_block, held, probs, slopes):
        value_total[key_block] += jnp.dot(
            jnp.concatenate(probs, axis=1),
            jnp.concatenate([one["grad"] for one in held], axis=0),
            preferred_element_type=jnp.float32,
        )
        key_total[key_block] += jnp.dot(
            jnp.concatenate(slopes, axis=1),
            jnp.concatenate([one["query"] for one in held], axis=0),
            preferred_element_type=jnp.float32,
        )

    def query_blocks(pair, grads):
        ids = [pair * halves + half for half in range(halves)]
        held = [prepare(at, rows) for at, rows in zip(ids, grads)]
        states = []
        for half, at in enumerate(ids):
            state, probs, slopes = step(
                held[half], at, (jnp.zeros((HD, block), jnp.float32),) * 2, True, True
            )
            add_key(at, held[half : half + 1], probs, slopes)
            for earlier in ids[:half]:
                state, probs, slopes = step(held[half], earlier, state, False, True)
                add_key(earlier, held[half : half + 1], probs, slopes)
            states.append(state)

        def all_steps(bounded):
            def run(key_block, carried):
                new, probs, slopes = [], [], []
                for half in range(halves):
                    state, prob, slope = step(held[half], key_block, carried[half], False, bounded)
                    new.append(state)
                    probs += prob
                    slopes += slope
                add_key(key_block, held, probs, slopes)
                return tuple(new)

            return run

        first, _ = key_range(lengths_ref, ids[0], parts, block)
        _, plain = key_range(lengths_ref, ids[-1], parts, block)
        plain = jnp.minimum(plain, ids[0])
        states = lax.fori_loop(first, plain, all_steps(True), tuple(states))
        states = lax.fori_loop(plain, ids[0], all_steps(False), states)
        return [
            jnp.transpose(jnp.concatenate(state, axis=0)) * (1.0 / math.sqrt(HD))
            for state in states
        ]

    def turn_back(rows, cosine, sine):
        flat = (parts * UNIT_PAIR, LANES)
        rows = jnp.concatenate(
            [one.reshape(parts, UNIT_BLOCK, LANES) for one in rows], axis=1
        ).reshape(flat)
        turned = rows * cosine.reshape(flat) - swap_halves(rows) * sine.reshape(flat)
        return turned.reshape(parts, UNIT_PAIR, LANES).astype(jnp.bfloat16)

    def put(values, unit_at, lane_at):
        for part in range(parts):
            back_ref[slot_of(part), pl.ds(unit_at, UNIT_PAIR), pl.ds(lane_at, LANES)] = values[part]

    def query_pair(pair, unused):
        unit_at = pl.multiple_of(pair * UNIT_PAIR, UNIT_PAIR)
        grads = grad_ref[:, pl.ds(unit_at, UNIT_PAIR), :].astype(jnp.float32)
        done = query_blocks(
            pair,
            [
                grads[:, half * UNIT_BLOCK : (half + 1) * UNIT_BLOCK].reshape(block, LANES)
                for half in range(halves)
            ],
        )
        cosine, sine = pair_angles(unit_at, cos_unit, sin_unit, cos_part, sin_part)
        put(turn_back(done, cosine, sine), unit_at, 0)
        return unused

    lax.fori_loop(0, pairs, query_pair, 0)

    def key_pair(pair, unused):
        unit_at = pl.multiple_of(pair * UNIT_PAIR, UNIT_PAIR)
        cosine, sine = pair_angles(unit_at, cos_unit, sin_unit, cos_part, sin_part)
        ids = [pair * halves + half for half in range(halves)]
        put(turn_back([key_total[at] for at in ids], cosine, sine), unit_at, LANES)
        values = jnp.concatenate(
            [value_total[at].reshape(parts, UNIT_BLOCK, LANES) for at in ids], axis=1
        ).astype(jnp.bfloat16)
        put(values, unit_at, 2 * LANES)
        return unused

    lax.fori_loop(0, pairs, key_pair, 0)


def table_shapes(parts, units):
    table = pltpu.VMEM((units, LANES), jnp.float32)
    row = pltpu.VMEM((parts, LANES), jnp.float32)
    return [pltpu.VMEM((units, LANES), jnp.int32), table, table, row, row]


def attend(lengths, qkv):
    parts, units, _ = qkv.shape
    block = parts * UNIT_BLOCK
    blocks = units // UNIT_BLOCK
    smem = pl.BlockSpec(memory_space=pltpu.SMEM)
    vmem = pl.BlockSpec(memory_space=pltpu.VMEM)
    rows = jax.ShapeDtypeStruct((blocks, block, LANES), jnp.bfloat16)
    halves = UNIT_PAIR // UNIT_BLOCK
    held = pltpu.VMEM((halves, 2, block, LANES), jnp.float32)
    return pl.pallas_call(
        attend_kernel,
        out_shape=(
            jax.ShapeDtypeStruct((parts, units, LANES), jnp.bfloat16),
            jax.ShapeDtypeStruct((blocks, LANES, block), jnp.float32),
            jax.ShapeDtypeStruct((blocks, 8, block), jnp.float32),
            rows,
            rows,
            rows,
        ),
        in_specs=[smem, vmem],
        out_specs=(vmem,) * 6,
        scratch_shapes=[
            pltpu.VMEM((blocks, 2, block, LANES), jnp.bfloat16),
            pltpu.VMEM((blocks, LANES, block), jnp.bfloat16),
            held,
            held,
            held,
            pltpu.VMEM((halves, block, LANES), jnp.float32),
            pltpu.VMEM((block, block), jnp.float32),
            pltpu.VMEM((block, block), jnp.float32),
        ]
        + table_shapes(parts, units),
        compiler_params=pltpu.CompilerParams(vmem_limit_bytes=KERNEL_VMEM),
        cost_estimate=pl.CostEstimate(
            flops=20 * 10**9, bytes_accessed=16 << 20, transcendentals=20 * 10**6
        ),
        name="attend",
    )(lengths, qkv)


def attend_back(lengths, query, key, value, out, log, grad):
    parts, units, _ = grad.shape
    block = parts * UNIT_BLOCK
    blocks = units // UNIT_BLOCK
    smem = pl.BlockSpec(memory_space=pltpu.SMEM)
    vmem = pl.BlockSpec(memory_space=pltpu.VMEM)
    return pl.pallas_call(
        attend_back_kernel,
        out_shape=jax.ShapeDtypeStruct((parts, units, 3 * LANES), jnp.bfloat16),
        in_specs=[smem] + [vmem] * 6,
        out_specs=vmem,
        scratch_shapes=[
            pltpu.VMEM((blocks, LANES, block), jnp.bfloat16),
            pltpu.VMEM((blocks, block, LANES), jnp.float32),
            pltpu.VMEM((blocks, block, LANES), jnp.float32),
            pltpu.VMEM((block, block), jnp.float32),
            pltpu.VMEM((block, block), jnp.float32),
        ]
        + table_shapes(parts, units),
        compiler_params=pltpu.CompilerParams(vmem_limit_bytes=KERNEL_VMEM),
        cost_estimate=pl.CostEstimate(
            flops=50 * 10**9, bytes_accessed=16 << 20, transcendentals=20 * 10**6
        ),
        name="attend_back",
    )(lengths, query, key, value, out, log, grad)


def swap(value, grp_step, rep_step):
    groups, reps = lax.axis_size("grp"), lax.axis_size("rep")
    pairs = [
        (grp * reps + rep, (grp ^ grp_step) * reps + (rep ^ rep_step))
        for grp in range(groups)
        for rep in range(reps)
    ]
    return lax.ppermute(value, BOTH, pairs)


def ordered(flag, own, other, axis=0):
    return jnp.where(
        flag == 0,
        jnp.concatenate([own, other], axis=axis),
        jnp.concatenate([other, own], axis=axis),
    )


def pick(value, index, axis):
    return lax.dynamic_index_in_dim(value, index, axis, keepdims=False)


def halve(value, axis, bit, grp_step, rep_step):
    kept = pick(value, bit, axis)
    sent = pick(value, 1 - bit, axis).astype(jnp.bfloat16)
    arrived = swap(sent, grp_step, rep_step)
    return kept.astype(jnp.float32) + arrived.astype(jnp.float32)


def narrow(value):
    return value.astype(jnp.bfloat16)


MESH_IDS = pl.DeviceIdType.MESH


def flipped(index, step):
    return index + step - 2 * step * ((index // step) % 2)


def lowest(offset):
    return offset & -offset


def arrivals(reps):
    far = [step for step in range(4, reps, 4)]
    far.sort(key=lambda step: (bin(step).count("1"), step))
    order = [(2, 0), (0, 1)]
    for at, step in enumerate(far):
        if bin(step).count("1") == 1:
            order.append((step, 0))
    order.append((2, 1))
    for step in far:
        if bin(step).count("1") == 1:
            order.append((step, 1))
    single = [step for step in far if bin(step).count("1") == 1]
    double = [step for step in far if bin(step).count("1") > 1]
    rest = []
    for step in single[:1]:
        rest.append((step + 2, 0))
    for step in double:
        rest.append((step, 0))
    for step in single[:1]:
        rest.append((step + 2, 1))
    for step in double:
        rest.append((step, 1))
    for step in single[1:] + double:
        rest += [(step + 2, 0), (step + 2, 1)]
    return order + rest


def link_of(offset, part, reps, turned=1):
    if offset == reps - 2 and part == turned:
        return 4
    return lowest(offset)


def gather_kernel(
    tokens_ref,
    gain_ref,
    w_query,
    w_key,
    w_value,
    w_gate,
    w_up,
    w_down,
    w_output,
    out_rows,
    normed_out,
    qkv_ref,
    weight_ref,
    gate_ref,
    up_ref,
    down_ref,
    output_ref,
    out_away,
    gains,
    raw,
    normed,
    weight_sem,
    out_sem,
    send_sem,
    recv_sem,
    side_send,
    side_recv,
    stripe_sem,
):
    here, there = lax.axis_index("grp"), lax.axis_index("rep")
    core = there % 2
    reps = raw.shape[0]
    slots = normed.shape[0]
    row_count, width = raw.shape[2:]
    steps = [1 << place for place in range(reps.bit_length() - 1)]
    across = (1 - here, there)

    def neighbour(step):
        return (here, flipped(there, step))

    barrier = pltpu.get_barrier_semaphore()
    for target in [across] + [neighbour(step) for step in steps]:
        pl.semaphore_signal(barrier, inc=1, device_id=target, device_id_type=MESH_IDS)
    local = []
    for at, weight in enumerate((w_query, w_key, w_value)):
        local.append(
            pltpu.make_async_copy(
                weight.at[:, pl.ds(pl.multiple_of(there * LANES, LANES), LANES)],
                weight_ref.at[here, :, pl.ds(at * LANES, LANES)],
                weight_sem.at[at],
            )
        )
        local[-1].start()
    raw[0, 0] = tokens_ref[here]
    gains[here] = gain_ref[...]
    pl.semaphore_wait(barrier, len(steps) + 1)

    def side(at, source, target_ref):
        return pltpu.make_async_remote_copy(
            src_ref=source,
            dst_ref=target_ref,
            send_sem=side_send.at[at],
            recv_sem=side_recv.at[at],
            device_id=across,
            device_id_type=MESH_IDS,
        )

    def rows_copy(offset, part):
        if offset == 0:
            return pltpu.make_async_remote_copy(
                src_ref=tokens_ref.at[1 - here],
                dst_ref=raw.at[0, 1],
                send_sem=send_sem.at[1],
                recv_sem=recv_sem.at[1],
                device_id=across,
                device_id_type=MESH_IDS,
            )
        step = link_of(offset, part, reps)
        return pltpu.make_async_remote_copy(
            src_ref=raw.at[offset - step, part],
            dst_ref=raw.at[offset, part],
            send_sem=send_sem.at[2 * offset + part],
            recv_sem=recv_sem.at[2 * offset + part],
            device_id=neighbour(step),
            device_id_type=MESH_IDS,
        )

    order = arrivals(reps)
    copies = {
        (offset, part): rows_copy(offset, part)
        for offset in range(reps)
        for part in (0, 1)
        if offset or part
    }

    def pass_on(offset, part):
        for later, part_of in order:
            if later and part_of == part and later - link_of(later, part, reps) == offset:
                copies[later, part].start()
        copies[offset + 1, part].start()

    gain_copy = side(0, gains.at[here], gains.at[here])
    gain_copy.start()
    copies[0, 1].start()
    pass_on(0, 0)
    for one in local:
        one.wait()
    weight_copy = side(1, weight_ref.at[here], weight_ref.at[here])
    weight_copy.start()

    stripes = [
        (grp, high, low)
        for grp in range(2)
        for high in range(reps // 8)
        for low in range(2)
    ]
    place = 4 * ((there // 4) % 2) + there % 2
    stripe_loads = []

    def load(source, target_ref):
        stripe_loads.append(
            pltpu.make_async_copy(source, target_ref, stripe_sem.at[len(stripe_loads)])
        )

    def columns_of(weight, grp, high, low):
        first = (grp * reps + 8 * high + 2 * low + place) * LANES
        return weight.at[:, pl.ds(pl.multiple_of(first, LANES), LANES)]

    for weight, target_ref in ((w_gate, gate_ref.at[here]), (w_up, up_ref)):
        for at, stripe in enumerate(stripes):
            load(columns_of(weight, *stripe), target_ref.at[:, pl.ds(at * LANES, LANES)])
    for at, (grp, high, low) in enumerate(stripes[: len(stripes) // 2]):
        first = (8 * high + 2 * low + place) * LANES
        load(
            w_down.at[pl.ds(pl.multiple_of(first, LANES), LANES)],
            down_ref.at[pl.ds(at * LANES, LANES)],
        )
    load(out_rows, out_away)
    for one in stripe_loads:
        one.start()
    quarter = output_ref.shape[0]
    output_copy = side(
        2,
        w_output.at[pl.ds(pl.multiple_of((there % 4) * quarter, quarter), quarter)],
        output_ref,
    )
    output_copy.start()
    gate_copy = side(3, gate_ref.at[here], gate_ref.at[here])
    for one in stripe_loads[: len(stripes)]:
        one.wait()
    gate_copy.start()

    written = {}
    used = [None] * slots
    tile = 32

    def project(count, offset):
        slot = count % slots
        if used[slot] is not None:
            written[used[slot]].wait()
        used[slot] = offset
        gain = jnp.concatenate([gains[0, 0:1], gains[1, 0:1]], axis=1).astype(jnp.float32)
        for part in range(2):

            def norm_rows(at, unused):
                cut = pl.ds(pl.multiple_of(at * tile, tile), tile)
                values = raw[offset, part, cut, :].astype(jnp.float32)
                scaled = values * rms_scale(values) * gain
                normed[slot, pl.ds(pl.multiple_of(part * row_count + at * tile, tile), tile), :] = (
                    scaled.astype(jnp.bfloat16)
                )
                return unused

            lax.fori_loop(0, row_count // tile, norm_rows, 0)
        written[offset] = pltpu.make_async_copy(
            normed.at[slot], normed_out.at[offset], out_sem.at[offset]
        )
        written[offset].start()
        half = width // 2
        product = jnp.dot(
            normed[slot, :, :half], weight_ref[0], preferred_element_type=jnp.float32
        ) + jnp.dot(normed[slot, :, half:], weight_ref[1], preferred_element_type=jnp.float32)
        qkv_ref[pl.ds(2 * offset, 2)] = product.astype(jnp.bfloat16).reshape(
            2, row_count, 3 * LANES
        )

    ready = []
    arrived = {(0, 0)}
    started = False
    count = 0
    for offset, part in order:
        copies[offset, part].wait_recv()
        pass_on(offset, part)
        arrived.add((offset, part))
        if (offset, 1 - part) in arrived:
            ready.append(offset)
        if not started and len(ready) >= 1:
            gain_copy.wait_recv()
            weight_copy.wait_recv()
            started = True
        if started and len(ready) >= 2:
            base = ready.pop(0)
            project(count, base)
            copies[base + 1, 0].wait_recv()
            copies[base + 1, 1].wait_recv()
            project(count + 1, base + 1)
            count += 2
    for base in ready:
        project(count, base)
        copies[base + 1, 0].wait_recv()
        copies[base + 1, 1].wait_recv()
        project(count + 1, base + 1)
        count += 2
    for offset in used:
        written[offset].wait()
    for one in copies.values():
        one.wait_send()
    gain_copy.wait_send()
    weight_copy.wait_send()
    for one in stripe_loads[len(stripes) :]:
        one.wait()
    gate_copy.wait()
    output_copy.wait()


def gather_heads(
    tokens, gains, w_query, w_key, w_value, w_gate, w_up, w_down, w_output, out_rows
):
    reps = lax.axis_size("rep")
    _, row_count, width = tokens.shape
    half = width // 2
    own_width = reps // 2 * LANES
    gain_rows = jnp.concatenate(
        [gains[0][None], gains[1][None], jnp.zeros((14, half), jnp.bfloat16)], axis=0
    )
    vmem = pl.BlockSpec(memory_space=pltpu.VMEM)
    anywhere = pl.BlockSpec(memory_space=pl.ANY)
    return pl.pallas_call(
        gather_kernel,
        out_shape=(
            jax.ShapeDtypeStruct((reps, 2 * row_count, width), jnp.bfloat16),
            jax.ShapeDtypeStruct((2 * reps, row_count, 3 * LANES), jnp.bfloat16),
            jax.ShapeDtypeStruct((2, half, 3 * LANES), jnp.bfloat16),
            jax.ShapeDtypeStruct((2, half, own_width), jnp.bfloat16),
            jax.ShapeDtypeStruct((half, own_width), jnp.bfloat16),
            jax.ShapeDtypeStruct((own_width // 2, width), jnp.bfloat16),
            jax.ShapeDtypeStruct((half // 4, width), jnp.bfloat16),
            jax.ShapeDtypeStruct(out_rows.shape, jnp.bfloat16),
            jax.ShapeDtypeStruct((2, 16, half), jnp.bfloat16),
        ),
        in_specs=[vmem, vmem] + [anywhere] * 8,
        out_specs=(anywhere,) + (vmem,) * 8,
        scratch_shapes=[
            pltpu.VMEM((reps, 2, row_count, width), jnp.bfloat16),
            pltpu.VMEM((4, 2 * row_count, width), jnp.bfloat16),
            pltpu.SemaphoreType.DMA((3,)),
            pltpu.SemaphoreType.DMA((reps,)),
            pltpu.SemaphoreType.DMA((2 * reps,)),
            pltpu.SemaphoreType.DMA((2 * reps,)),
            pltpu.SemaphoreType.DMA((4,)),
            pltpu.SemaphoreType.DMA((4,)),
            pltpu.SemaphoreType.DMA((reps // 2 * 5 // 2 + 1,)),
        ],
        compiler_params=pltpu.CompilerParams(
            vmem_limit_bytes=KERNEL_VMEM, collective_id=0, has_side_effects=True
        ),
        cost_estimate=pl.CostEstimate(
            flops=8 * 10**9, bytes_accessed=250 << 20, transcendentals=0
        ),
        name="gather_heads",
    )(tokens, gain_rows, w_query, w_key, w_value, w_gate, w_up, w_down, w_output, out_rows)


SCATTER_PLAN = (
    ("first", "up"), ("rows", 13, 0), ("rows", 15, 0), ("weights", 1), ("rows", 1, 0),
    ("rows", 15, 1), ("weights", 2), ("rows", 5, 0), ("first", "down"), ("rows", 14, 0),
    ("first", "gate"), ("rows", 12, 0), ("rows", 13, 1), ("weights", 1), ("rows", 14, 1),
    ("rows", 9, 1), ("weights", 1), ("sum", "up"), ("weights", 1), ("rows", 11, 0),
    ("rows", 11, 1), ("rows", 1, 1), ("rows", 10, 0), ("rows", 7, 0), ("first", "out"),
    ("weights", 1), ("sum", "down"), ("weights", 4), ("rows", 3, 1), ("rows", 10, 1),
    ("weights", 1), ("sum", "gate"), ("rows", 7, 1), ("rows", 3, 0), ("rows", 9, 0),
    ("rows", 2, 1), ("rows", 12, 1), ("weights", 3), ("sum", "quad"), ("weights", 1),
    ("weights over",), ("rows", 6, 1), ("rows", 8, 0), ("rows", 8, 1), ("rows", 5, 1),
    ("sum", "out"), ("rows", 4, 1), ("sum", "out next"), ("rows", 6, 0), ("weights out",),
    ("rows", 2, 0), ("rows", 0, 1), ("rows", 4, 0), ("rows", 0, 0), ("sum", "quad next"),
)


def scatter_kernel(
    back_ref,
    weight_ref,
    tokens_ref,
    mixed_grad,
    gain_ref,
    normed_ref,
    gate_kept,
    gate_met,
    up_kept,
    up_met,
    down_kept,
    down_met,
    output_kept,
    output_met,
    token_ref,
    pieces_ref,
    quad_ref,
    down_ref,
    output_ref,
    away,
    landed,
    grad_in,
    normed,
    back_t,
    weight_t,
    weights_total,
    half_out,
    half_in,
    piece_out,
    gate_away,
    gate_landed,
    up_away,
    up_landed,
    up_last,
    down_away,
    down_landed,
    down_last,
    output_away,
    output_landed,
    output_next,
    output_last,
    narrow_stage,
    wide_stage,
    crossed,
    normed_sem,
    send_sem,
    recv_sem,
    side_send,
    side_recv,
    piece_send,
    piece_recv,
    stage_sem,
    sum_send,
    sum_recv,
):
    here, there = lax.axis_index("grp"), lax.axis_index("rep")
    reps, rows, columns = back_ref.shape
    row_count = rows // 2
    width = token_ref.shape[1]
    half = width // 2
    own_rows = half // reps
    steps = [1 << place for place in range(reps.bit_length() - 1)]
    bit = {step: (there // step) % 2 for step in steps}
    across = (1 - here, there)

    def other(offset):
        index = there
        for step in steps:
            if offset & step:
                index = flipped(index, step)
        return (here, index)

    barrier = pltpu.get_barrier_semaphore()
    for target in [across] + [other(offset) for offset in range(1, reps)]:
        pl.semaphore_signal(barrier, inc=1, device_id=target, device_id_type=MESH_IDS)

    slots = normed.shape[0]
    fetch = [
        pltpu.make_async_copy(normed_ref.at[offset], normed.at[offset % slots], normed_sem.at[offset])
        for offset in range(reps)
    ]
    for offset in range(slots):
        fetch[offset].start()

    def part_of(ref, axis, index):
        return ref.at[(slice(None),) * axis + (index,)]

    def load(at, source, target_ref):
        copy = pltpu.make_async_copy(source, target_ref, stage_sem.at[at])
        copy.start()
        return copy

    def open_half(at, kept, met, axis, flag, stage, target_ref):
        return (
            load(2 * at, part_of(kept, axis, flag), stage),
            load(2 * at + 1, part_of(met, axis, flag), target_ref),
        )

    firsts = [
        open_half(0, down_kept, down_met, 0, 1 - here, wide_stage.at[0], down_away),
        open_half(1, output_kept, output_met, 0, 1 - here, wide_stage.at[1], output_away),
        open_half(2, gate_kept, gate_met, 1, 1 - bit[2], narrow_stage.at[1, 0], gate_away),
        open_half(3, up_kept, up_met, 2, 1 - bit[2], narrow_stage.at[0], up_away),
    ]

    for at in range(2):
        turned = jnp.transpose(weight_ref[at].astype(jnp.float32)).astype(jnp.bfloat16)
        weight_t[:, pl.ds(at * half, half)] = turned
    pl.semaphore_wait(barrier, reps)

    def add_to(target_ref, *sources):
        lead = target_ref.shape[:-2]
        count = 1
        for size in lead:
            count *= size
        for at in range(count):
            index, rest = [], at
            for size in lead[::-1]:
                index.insert(0, rest % size)
                rest //= size

            def some_rows(step, unused):
                place = tuple(index) + (pl.ds(pl.multiple_of(step * 16, 16), 16),)
                total = target_ref[place].astype(jnp.float32)
                for source in sources:
                    total = total + source[place].astype(jnp.float32)
                target_ref[place] = total.astype(target_ref.dtype)
                return unused

            lax.fori_loop(0, target_ref.shape[-2] // 16, some_rows, 0)

    def sum_copy(at, source, target_ref, target):
        return pltpu.make_async_remote_copy(
            src_ref=source,
            dst_ref=target_ref,
            send_sem=sum_send.at[at],
            recv_sem=sum_recv.at[at],
            device_id=target,
            device_id_type=MESH_IDS,
        )

    down_cross = sum_copy(0, down_away, down_landed, across)
    output_cross = sum_copy(1, output_away, output_landed, across)
    gate_low = sum_copy(2, gate_away, gate_landed, other(2))
    up_low = sum_copy(3, up_away, up_landed, other(2))
    down_high = sum_copy(4, down_landed.at[1 - bit[8]], down_last, other(8))
    up_high = sum_copy(5, up_landed.at[1 - bit[8]], up_last, other(8))
    output_low = sum_copy(6, output_landed.at[:, 1 - bit[2]], output_next, other(2))
    output_high = sum_copy(7, output_next.at[1 - bit[8]], output_last, other(8))
    quad_far = [
        sum_copy(8, gate_landed.at[1 - bit[4]], crossed.at[0], other(4)),
        sum_copy(9, up_last.at[1 - bit[4]], crossed.at[1], other(4)),
    ]
    quad_near = [
        sum_copy(10, gate_landed.at[bit[4], 1 - bit[1]], quad_ref.at[bit[4], bit[1], 0], other(1)),
        sum_copy(11, up_last.at[bit[4], 1 - bit[1]], quad_ref.at[bit[4], bit[1], 1], other(1)),
        sum_copy(12, crossed.at[0, 1 - bit[1]], quad_ref.at[1 - bit[4], bit[1], 0], other(1)),
        sum_copy(13, crossed.at[1, 1 - bit[1]], quad_ref.at[1 - bit[4], bit[1], 1], other(1)),
    ]
    sum_copies = (
        [down_cross, output_cross, gate_low, up_low, down_high, up_high, output_low, output_high]
        + quad_far
        + quad_near
    )

    def first_send(at, target_ref, stage, copy):
        for one in firsts[at]:
            one.wait()
        add_to(target_ref, stage)
        copy.start()

    def own_half(at, kept, met, axis, flag, stage_a, stage_b, copy, target_ref):
        loads = (
            load(2 * at, part_of(kept, axis, flag), stage_a),
            load(2 * at + 1, part_of(met, axis, flag), stage_b),
        )
        for one in loads:
            one.wait()
        copy.wait_recv()
        add_to(target_ref, stage_a, stage_b)

    def down_sum():
        own_half(
            0, down_kept, down_met, 0, here, wide_stage.at[0], wide_stage.at[1], down_cross,
            down_landed,
        )
        down_high.start()

    def output_sum():
        own_half(
            1, output_kept, output_met, 0, here, wide_stage.at[0], wide_stage.at[1], output_cross,
            output_landed,
        )
        output_low.start()

    def gate_sum():
        own_half(
            2, gate_kept, gate_met, 1, bit[2], narrow_stage.at[0, 0], narrow_stage.at[1, 0],
            gate_low, gate_landed,
        )

    def up_sum():
        own_half(
            3, up_kept, up_met, 2, bit[2], narrow_stage.at[0], narrow_stage.at[1], up_low,
            up_landed,
        )
        up_high.start()

    def output_next_sum():
        output_low.wait_recv()
        add_to(output_next, output_landed.at[:, bit[2]])
        output_high.start()

    def quad_send():
        up_high.wait_recv()
        add_to(up_last, up_landed.at[bit[8]])
        for one in quad_far + quad_near[:2]:
            one.start()
        quad_ref[bit[4], bit[1], 0] = gate_landed[bit[4], bit[1]]
        quad_ref[bit[4], bit[1], 1] = up_last[bit[4], bit[1]]

    def quad_pass():
        for one in quad_far:
            one.wait_recv()
        for one in quad_near[2:]:
            one.start()
        for kind in range(2):
            quad_ref[1 - bit[4], bit[1], kind] = crossed[kind, bit[1]]

    def last_sums():
        down_high.wait_recv()
        output_high.wait_recv()

        def down_rows(step, unused):
            cut = pl.ds(pl.multiple_of(step * 16, 16), 16)
            for at in range(down_last.shape[0]):
                down_ref[at, cut] = down_last[at, cut].astype(jnp.float32) + down_landed[
                    bit[8], at, cut
                ].astype(jnp.float32)
            output_ref[cut] = output_last[cut].astype(jnp.float32) + output_next[
                bit[8], cut
            ].astype(jnp.float32)
            return unused

        lax.fori_loop(0, own_rows // 16, down_rows, 0)

    def rows_copy(offset, part):
        if offset == 0:
            return pltpu.make_async_remote_copy(
                src_ref=away.at[0, 1],
                dst_ref=landed.at[0, 1],
                send_sem=send_sem.at[1],
                recv_sem=recv_sem.at[1],
                device_id=across,
                device_id_type=MESH_IDS,
            )
        return pltpu.make_async_remote_copy(
            src_ref=away.at[offset // 2, part],
            dst_ref=landed.at[offset, part],
            send_sem=send_sem.at[2 * offset + part],
            recv_sem=recv_sem.at[2 * offset + part],
            device_id=other(link_of(offset, part, reps, 0)),
            device_id_type=MESH_IDS,
        )

    copies = {
        (offset, part): rows_copy(offset, part)
        for offset in range(reps)
        for part in (0, 1)
        if offset or part
    }

    def send(offset, part):
        sources = [
            later
            for later in range(1, reps)
            if later - link_of(later, part, reps, 0) == offset
        ]
        for later in sources:
            copies[later, part].wait_recv()
        total = jnp.dot(
            back_ref[offset, pl.ds(part * row_count, row_count), :],
            weight_t[...],
            preferred_element_type=jnp.float32,
        )
        for later in sources:
            total = total + landed[later, part].astype(jnp.float32)
        if offset == 0 and part == 0:
            grad_in[...] = total
        else:
            if offset % 2 == 0:
                copies[offset + 1, part].wait_send()
            away[offset // 2, part] = total.astype(jnp.bfloat16)
            copies[offset, part].start()

    def weight_step(offset):
        fetch[offset].wait()
        back_t[...] = jnp.transpose(back_ref[offset].astype(jnp.float32)).astype(jnp.bfloat16)

        def columns_at(at, unused):
            cut = pl.ds(pl.multiple_of(at * 512, 512), 512)
            term = jnp.dot(
                back_t[...], normed[offset % slots, :, cut], preferred_element_type=jnp.float32
            )
            if offset == 0:
                weights_total[:, cut] = term
            else:
                weights_total[:, cut] += term
            return unused

        lax.fori_loop(0, width // 512, columns_at, 0)
        if offset + slots < reps:
            fetch[offset + slots].start()

    half_copy = pltpu.make_async_remote_copy(
        src_ref=half_out,
        dst_ref=half_in,
        send_sem=side_send,
        recv_sem=side_recv,
        device_id=across,
        device_id_type=MESH_IDS,
    )
    piece_copies = [
        pltpu.make_async_remote_copy(
            src_ref=piece_out.at[other(offset)[1]],
            dst_ref=pieces_ref.at[there],
            send_sem=piece_send.at[offset],
            recv_sem=piece_recv.at[offset],
            device_id=other(offset),
            device_id_type=MESH_IDS,
        )
        for offset in range(1, reps)
    ]

    def cross_weights():
        cut = pl.ds(pl.multiple_of((1 - here) * half, half), half)
        half_out[...] = weights_total[:, cut].astype(jnp.bfloat16)
        half_copy.start()

    def share_weights():
        half_copy.wait_recv()
        cut = pl.ds(pl.multiple_of(here * half, half), half)
        total = jnp.transpose(weights_total[:, cut] + half_in[...].astype(jnp.float32))
        piece_out[...] = total.astype(jnp.bfloat16).reshape(reps, own_rows, columns)
        pieces_ref[there] = piece_out[there]
        for one in piece_copies:
            one.start()

    weights = list(range(reps))

    def weight_steps(count):
        for _ in range(min(count, len(weights))):
            weight_step(weights.pop(0))

    firsts_by = {
        "down": lambda: first_send(0, down_away, wide_stage.at[0], down_cross),
        "out": lambda: first_send(1, output_away, wide_stage.at[1], output_cross),
        "gate": lambda: first_send(2, gate_away, narrow_stage.at[1, 0], gate_low),
        "up": lambda: first_send(3, up_away, narrow_stage.at[0], up_low),
    }
    sums_by = {
        "down": down_sum,
        "out": output_sum,
        "gate": gate_sum,
        "up": up_sum,
        "out next": output_next_sum,
        "quad": quad_send,
        "quad next": quad_pass,
    }
    for kind, *what in SCATTER_PLAN:
        if kind == "rows":
            send(*what)
        elif kind == "weights":
            weight_steps(*what)
        elif kind == "first":
            firsts_by[what[0]]()
        elif kind == "sum":
            sums_by[what[0]]()
        elif kind == "weights over":
            cross_weights()
        else:
            share_weights()
    last_sums()
    copies[0, 1].wait_recv()

    tile = 32

    def norm_rows(grp, step, grad_rows):
        place = pl.ds(pl.multiple_of(grp * row_count + step * tile, tile), tile)
        values = tokens_ref[place, :].astype(jnp.float32)
        inverse = rms_scale(values)
        normed_rows = values * inverse
        weighted = grad_rows * gain_ref[0:1, :]
        token_ref[place, :] = (
            mixed_grad[place, :]
            + inverse
            * (weighted - normed_rows * jnp.mean(weighted * normed_rows, axis=-1, keepdims=True))
        ).astype(jnp.bfloat16)

    def norm_back(step, unused):
        cut = pl.ds(pl.multiple_of(step * tile, tile), tile)
        norm_rows(here, step, grad_in[cut, :])
        norm_rows(1 - here, step, landed[0, 1, cut, :].astype(jnp.float32))
        return unused

    lax.fori_loop(0, row_count // tile, norm_back, 0)
    for one in piece_copies:
        one.wait()
    for one in quad_near:
        one.wait_recv()
    for one in [half_copy] + sum_copies:
        one.wait_send()
    for (offset, part), one in copies.items():
        if offset % 2 == 0 or (offset == 1 and part == 0):
            one.wait_send()


def scatter_heads(back, weights, tokens, mixed_grad, gain, normed, sums):
    reps, rows, columns = back.shape
    width = normed.shape[2]
    row_count = rows // 2
    half = width // 2
    own_rows = half // reps
    own_width = width // 2
    vmem = pl.BlockSpec(memory_space=pltpu.VMEM)
    anywhere = pl.BlockSpec(memory_space=pl.ANY)
    low, full = jnp.bfloat16, jnp.float32
    wide = (2, 2, own_rows, width)
    slim = (2, 2, 2, own_rows, own_width)
    return pl.pallas_call(
        scatter_kernel,
        out_shape=(
            jax.ShapeDtypeStruct((rows, width), low),
            jax.ShapeDtypeStruct((reps, own_rows, columns), low),
            jax.ShapeDtypeStruct(slim, low),
            jax.ShapeDtypeStruct(wide[1:], full),
            jax.ShapeDtypeStruct(wide[2:], full),
        ),
        in_specs=[vmem] * 5 + [anywhere] * 9,
        out_specs=(vmem,) * 5,
        scratch_shapes=[
            pltpu.VMEM((reps // 2, 2, row_count, width), low),
            pltpu.VMEM((reps, 2, row_count, width), low),
            pltpu.VMEM((row_count, width), full),
            pltpu.VMEM((2, rows, width), low),
            pltpu.VMEM((columns, rows), low),
            pltpu.VMEM((columns, width), low),
            pltpu.VMEM((columns, width), full),
            pltpu.VMEM((columns, half), low),
            pltpu.VMEM((columns, half), low),
            pltpu.VMEM((reps, own_rows, columns), low),
            pltpu.VMEM(slim[1:], low),
            pltpu.VMEM(slim[1:], low),
            pltpu.VMEM(slim, low),
            pltpu.VMEM(slim, low),
            pltpu.VMEM(slim[1:], low),
            pltpu.VMEM(wide, low),
            pltpu.VMEM(wide, low),
            pltpu.VMEM(wide[1:], low),
            pltpu.VMEM(wide, low),
            pltpu.VMEM(wide, low),
            pltpu.VMEM(wide[1:], low),
            pltpu.VMEM(wide[2:], low),
            pltpu.VMEM((2,) + slim, low),
            pltpu.VMEM((2,) + wide, low),
            pltpu.VMEM(slim[1:], low),
            pltpu.SemaphoreType.DMA((reps,)),
            pltpu.SemaphoreType.DMA((2 * reps,)),
            pltpu.SemaphoreType.DMA((2 * reps,)),
            pltpu.SemaphoreType.DMA,
            pltpu.SemaphoreType.DMA,
            pltpu.SemaphoreType.DMA((reps,)),
            pltpu.SemaphoreType.DMA((reps,)),
            pltpu.SemaphoreType.DMA((8,)),
            pltpu.SemaphoreType.DMA((14,)),
            pltpu.SemaphoreType.DMA((14,)),
        ],
        compiler_params=pltpu.CompilerParams(
            vmem_limit_bytes=62 * 1024 * 1024, collective_id=1, has_side_effects=True
        ),
        cost_estimate=pl.CostEstimate(
            flops=14 * 10**9, bytes_accessed=250 << 20, transcendentals=0
        ),
        name="scatter_heads",
    )(back, weights, tokens, mixed_grad, gain, normed, *sums)


def mlp_kernel(
    heads_ref,
    tokens_ref,
    gain_ref,
    out_rows,
    out_across,
    output_own,
    output_part,
    output_beside,
    gate_in,
    up_own,
    up_other,
    down_own,
    block_ref,
    grad_ref,
    back_ref,
    gate_ref,
    up_kept,
    up_sent,
    down_kept,
    down_sent,
    output_kept,
    output_sent,
    mixed_ref,
    down_own_ref,
    down_far_landed,
    attended,
    branch_ref,
    returned,
    out_ref,
    mid_ref,
    hidden_ref,
    slope_ref,
    w_output,
    w_in,
    w_out,
    near_away,
    near_landed,
    far_away,
    far_landed,
    down_landed,
    load_sem,
    part_sem,
    send_sem,
    recv_sem,
    heads_send,
    heads_recv,
    back_send,
    back_recv,
    piece_sem,
    place_sem,
    core_send,
    core_recv,
    free_sem,
):
    here, there = lax.axis_index("grp"), lax.axis_index("rep")
    across = (here, flipped(there, 4))
    sibling = (here, flipped(there, 1))
    groups, heads, row_count, _ = returned.shape
    rows, width = tokens_ref.shape
    half = width // 2
    quarter = half // 4
    own_width = w_out.shape[0]

    loads = [
        pltpu.make_async_copy(output_own, w_output.at[here], load_sem.at[0]),
        pltpu.make_async_copy(gate_in, w_in.at[:, :, pl.ds(0, own_width)], load_sem.at[1]),
        pltpu.make_async_copy(
            up_own, w_in.at[here, :, pl.ds(own_width, own_width)], load_sem.at[2]
        ),
        pltpu.make_async_copy(
            up_other, w_in.at[1 - here, :, pl.ds(own_width, own_width)], load_sem.at[3]
        ),
    ]
    own_part = own_width // 2

    def down_cut(grp):
        return pl.ds(pl.multiple_of(grp * own_part, own_part), own_part)

    loads += [
        pltpu.make_async_copy(down_own, w_out.at[down_cut(here)], load_sem.at[4]),
        pltpu.make_async_copy(out_rows.at[pl.ds(0, row_count)], out_ref.at[0, 0], load_sem.at[5]),
        pltpu.make_async_copy(
            out_rows.at[pl.ds(row_count, row_count)], out_ref.at[1, 0], load_sem.at[6]
        ),
        pltpu.make_async_copy(out_across.at[pl.ds(0, row_count)], out_ref.at[0, 2], load_sem.at[7]),
        pltpu.make_async_copy(
            out_across.at[pl.ds(row_count, row_count)], out_ref.at[1, 2], load_sem.at[8]
        ),
    ]
    place = there % 4
    core = there % 2

    def output_cut(part):
        return w_output.at[1 - here, pl.ds(pl.multiple_of(part * quarter, quarter), quarter)]

    output_pieces = ((output_part, place), (output_beside, flipped(place, 2)))
    rest = [
        pltpu.make_async_copy(piece, output_cut(part), part_sem.at[at])
        for at, (piece, part) in enumerate(output_pieces)
    ]
    loads = loads[:1] + rest + loads[1:]
    for one in loads:
        one.start()
    steps = [1 << place for place in range(heads.bit_length() - 1)]

    def other(crossing, offset):
        index = there
        for step in steps:
            if offset & step:
                index = flipped(index, step)
        return (1 - here if crossing else here, index)

    others = [
        (crossing, offset) for offset in range(heads) for crossing in (0, 1) if offset or crossing
    ]
    barrier = pltpu.get_barrier_semaphore()
    for key in others:
        pl.semaphore_signal(barrier, inc=1, device_id=other(*key), device_id_type=MESH_IDS)
    pl.semaphore_wait(barrier, len(others))

    facing = (1 - here, there)

    def copy(at, source, target_ref, target):
        return pltpu.make_async_remote_copy(
            src_ref=source,
            dst_ref=target_ref,
            send_sem=send_sem.at[at],
            recv_sem=recv_sem.at[at],
            device_id=target,
            device_id_type=MESH_IDS,
        )

    heads_copies, back_copies = [], []
    for at, key in enumerate(others):
        target = other(*key)
        heads_copies.append(
            pltpu.make_async_remote_copy(
                src_ref=heads_ref.at[target[0] * heads + target[1]],
                dst_ref=returned.at[here, there],
                send_sem=heads_send.at[at],
                recv_sem=heads_recv.at[at],
                device_id=target,
                device_id_type=MESH_IDS,
            )
        )
        back_copies.append(
            pltpu.make_async_remote_copy(
                src_ref=returned.at[target[0], target[1]],
                dst_ref=back_ref.at[here * heads + there],
                send_sem=back_send.at[at],
                recv_sem=back_recv.at[at],
                device_id=target,
                device_id_type=MESH_IDS,
            )
        )
    for one in heads_copies[::-1]:
        one.start()
    parts = range(groups)

    def rows_of(part):
        return pl.ds(part * row_count, row_count)

    output_near = [
        copy(at, piece, output_cut(part), sibling) for at, (piece, part) in enumerate(output_pieces)
    ]
    down_far = copy(2, down_own, w_out.at[down_cut(here)], facing)
    out_near = [
        copy(3 + part, out_rows.at[rows_of(part)], out_ref.at[part, 1], sibling) for part in parts
    ]
    out_on = [
        copy(5 + part, out_across.at[rows_of(part)], out_ref.at[part, 3], sibling) for part in parts
    ]
    for one in output_near + out_near + out_on + [down_far]:
        one.start()
    returned[here, there] = heads_ref[here * heads + there]

    mid_near = [copy(7 + at, mid_ref.at[at, 0], mid_ref.at[at, 1], sibling) for at in parts]
    mid_far = [copy(9 + at, mid_ref.at[at, 0], mid_ref.at[at, 2], across) for at in parts]
    mid_on = [copy(11 + at, mid_ref.at[at, 2], mid_ref.at[at, 3], sibling) for at in parts]
    grad_near = {
        (side, at): copy(
            13 + 2 * side + at, near_away.at[side, at], near_landed.at[side, at], sibling
        )
        for side in range(2)
        for at in parts
    }
    grad_far = [copy(17 + at, far_away.at[at], far_landed.at[at], across) for at in parts]
    down_near = {
        (side, at): copy(
            19 + 2 * side + at, near_away.at[side, at], down_landed.at[side, at], sibling
        )
        for side in range(2)
        for at in parts
    }
    down_over = [
        copy(23 + at, down_own_ref.at[1, at], down_far_landed.at[at], across) for at in parts
    ]
    gate_cross = copy(25, w_in.at[1 - here, :, pl.ds(0, own_width)], gate_ref, facing)
    up_cut = pl.ds(own_width, own_width)
    up_outs = [
        pltpu.make_async_copy(w_in.at[here, :, up_cut], up_kept, load_sem.at[0]),
        pltpu.make_async_copy(w_in.at[1 - here, :, up_cut], up_sent, load_sem.at[1]),
    ]
    low = (there // 2) % 2
    down_outs = []
    for at in range(own_width // (2 * LANES)):
        for kind, (target_ref, bit) in enumerate(((down_kept, low), (down_sent, 1 - low))):
            cut = pl.ds(pl.multiple_of((2 * at + bit) * LANES, LANES), LANES)
            down_outs.append(
                pltpu.make_async_copy(w_out.at[cut], target_ref.at[at], piece_sem.at[2 * at + kind])
            )

    for one in heads_copies:
        one.wait()
    for group in range(groups):
        for head in range(heads):
            attended[
                group * row_count : (group + 1) * row_count, head * LANES : (head + 1) * LANES
            ] = returned[group, head]
    for one in loads[:3]:
        one.wait()
    for one in output_near:
        one.wait_recv()
    wide = 512

    def mix(at, unused):
        cut = pl.ds(pl.multiple_of(at * wide, wide), wide)
        mixed_ref[:, cut] = (
            tokens_ref[:, cut].astype(jnp.float32)
            + jnp.dot(attended[:, :half], w_output[0, :, cut], preferred_element_type=jnp.float32)
            + jnp.dot(attended[:, half:], w_output[1, :, cut], preferred_element_type=jnp.float32)
        )
        return unused

    lax.fori_loop(0, width // wide, mix, 0)
    tile = 32
    for part in parts:

        def norm_rows(at, unused):
            cut = pl.ds(pl.multiple_of(at * tile, tile), tile)
            values = mixed_ref[pl.ds(pl.multiple_of(part * row_count + at * tile, tile), tile), :]
            mid_ref[part, 0, cut, :] = (
                values * rms_scale(values) * gain_ref[0:1, :]
            ).astype(jnp.bfloat16)
            return unused

        lax.fori_loop(0, row_count // tile, norm_rows, 0)
        mid_far[part].start()
        mid_near[part].start()
    for one in loads[3:]:
        one.wait()
    narrow_tile = 256
    per_half = own_part // narrow_tile
    every = (0, 1)

    def pair_rows(ref, side, part, cols):
        values = ref[part, pl.ds(2 * side, 2), :, cols]
        return values.reshape(rows, values.shape[2])

    def forward(side, part, halves):
        def columns(step, unused):
            at = jnp.where(step < per_half, halves[0] * per_half, halves[-1] * per_half - per_half)
            at = at + step
            cut = pl.ds(pl.multiple_of(at * narrow_tile, narrow_tile), narrow_tile)
            up_cut = pl.ds(pl.multiple_of(own_width + at * narrow_tile, narrow_tile), narrow_tile)
            low_rows = pair_rows(mid_ref, side, part, slice(0, half))
            high_rows = pair_rows(mid_ref, side, part, slice(half, width))

            def project(cols):
                return jnp.dot(
                    low_rows, w_in[0, :, cols], preferred_element_type=jnp.float32
                ) + jnp.dot(high_rows, w_in[1, :, cols], preferred_element_type=jnp.float32)

            gate_pre, up_pre = project(cut), project(up_cut)
            grad_hidden = contract(
                pair_rows(out_ref, side, part, slice(0, width)), w_out[cut, :], 1, 1
            )
            gate_sig = jax.nn.sigmoid(gate_pre)
            gate_silu = gate_pre * gate_sig

            def put(ref, cols, values):
                ref[part, pl.ds(2 * side, 2), :, cols] = values.astype(jnp.bfloat16).reshape(
                    2, row_count, narrow_tile
                )

            put(hidden_ref, cut, gate_silu * up_pre)
            put(
                slope_ref,
                cut,
                grad_hidden * up_pre * gate_sig * (1.0 + gate_pre * (1.0 - gate_sig)),
            )
            put(slope_ref, up_cut, grad_hidden * gate_silu)
            return unused

        lax.fori_loop(0, len(halves) * per_half, columns, 0)

    def backward(side, part):
        for at in range(2):

            def columns(step, unused):
                cut = pl.ds(pl.multiple_of(step * wide, wide), wide)
                whole = pl.ds(pl.multiple_of(at * half + step * wide, wide), wide)
                values = contract(
                    pair_rows(slope_ref, side, part, slice(0, 2 * own_width)),
                    w_in[at, cut, :],
                    1,
                    1,
                )
                near_away[side, part, :, whole] = values[row_count:].astype(jnp.bfloat16)
                if side == 0:
                    grad_ref[rows_of(part), whole] = values[:row_count]
                else:
                    far_away[part, :, whole] = values[:row_count].astype(jnp.bfloat16)
                return unused

            lax.fori_loop(0, half // wide, columns, 0)
        grad_near[side, part].start()

    def add_rows(target_ref, source_ref):
        def some_rows(at, unused):
            cut = pl.ds(pl.multiple_of(at * tile, tile), tile)
            target_ref[cut, :] = (
                target_ref[cut, :].astype(jnp.float32) + source_ref[cut, :].astype(jnp.float32)
            ).astype(target_ref.dtype)
            return unused

        lax.fori_loop(0, row_count // tile, some_rows, 0)

    def far_send(part):
        grad_near[1, part].wait_recv()
        add_rows(far_away.at[part], near_landed.at[1, part])
        grad_far[part].start()

    def down(side, part):
        grad_near[side, part].wait_send()

        def columns(step, unused):
            cut = pl.ds(pl.multiple_of(step * wide, wide), wide)
            values = jnp.dot(
                pair_rows(hidden_ref, side, part, slice(0, own_width)),
                w_out[:, cut],
                preferred_element_type=jnp.float32,
            ).astype(jnp.bfloat16)
            near_away[side, part, :, cut] = values[row_count:]
            down_own_ref[side, part, :, cut] = values[:row_count]
            return unused

        lax.fori_loop(0, width // wide, columns, 0)
        down_near[side, part].start()

    def down_meet(side, part):
        down_near[side, part].wait_recv()
        add_rows(down_own_ref.at[side, part], down_landed.at[side, part])

    for part in parts:
        mid_near[part].wait_recv()
        out_near[part].wait_recv()
        forward(0, part, (here,))
    for part in parts:
        mid_far[part].wait_recv()
        mid_on[part].start()
        if part == 0:
            down_far.wait_recv()
        else:
            forward(0, 0, (1 - here,))
            far_send(0)
        mid_on[part].wait_recv()
        out_on[part].wait_recv()
        forward(1, part, every)
        backward(1, part)
    forward(0, 1, (1 - here,))
    far_send(1)
    for part in parts:
        backward(0, part)

    def turned(values):
        flat = values.reshape(4 * rows, values.shape[3]).astype(jnp.float32)
        return jnp.transpose(flat).astype(jnp.bfloat16)

    def in_grads(at):
        def some_rows(step, unused):
            cut = pl.ds(pl.multiple_of(step * narrow_tile, narrow_tile), narrow_tile)
            source = pl.ds(pl.multiple_of(at * half + step * narrow_tile, narrow_tile), narrow_tile)
            left = turned(mid_ref[:, :, :, source])

            def columns(place_at, unused):
                cols = pl.ds(pl.multiple_of(place_at * wide, wide), wide)
                right = slope_ref[:, :, :, cols].reshape(4 * rows, wide)
                w_in[at, cut, cols] = jnp.dot(
                    left, right, preferred_element_type=jnp.float32
                ).astype(jnp.bfloat16)
                return unused

            return lax.fori_loop(0, 2 * own_width // wide, columns, unused)

        lax.fori_loop(0, half // narrow_tile, some_rows, 0)

    def down_rows(step, unused):
        cut = pl.ds(pl.multiple_of(step * narrow_tile, narrow_tile), narrow_tile)
        left = turned(hidden_ref[:, :, :, cut])

        def columns(place_at, unused):
            cols = pl.ds(pl.multiple_of(place_at * wide, wide), wide)
            right = out_ref[:, :, :, cols].reshape(4 * rows, wide)
            w_out[cut, cols] = jnp.dot(left, right, preferred_element_type=jnp.float32).astype(
                jnp.bfloat16
            )
            return unused

        return lax.fori_loop(0, width // wide, columns, unused)

    def finish(part):
        grad_near[0, part].wait_recv()
        grad_far[part].wait_recv()

        def norm_back(at, unused):
            cut = pl.ds(pl.multiple_of(at * tile, tile), tile)
            place = pl.ds(pl.multiple_of(part * row_count + at * tile, tile), tile)
            grad_mid = (
                grad_ref[place, :]
                + near_landed[0, part, cut, :].astype(jnp.float32)
                + far_landed[part, cut, :].astype(jnp.float32)
            )
            values = mixed_ref[place, :]
            inverse = rms_scale(values)
            normed = values * inverse
            weighted = grad_mid * gain_ref[0:1, :]
            grad = out_ref[part, 0, cut, :].astype(jnp.float32) + inverse * (
                weighted - normed * jnp.mean(weighted * normed, axis=-1, keepdims=True)
            )
            grad_ref[place, :] = grad
            branch_ref[place, :] = grad.astype(jnp.bfloat16)
            return unused

        lax.fori_loop(0, row_count // tile, norm_back, 0)
        for head in range(0, heads, 4):
            at = head * LANES // half
            start = head * LANES - at * half
            values = contract(
                branch_ref[rows_of(part), :],
                w_output[at, pl.ds(start, 4 * LANES), :],
                1,
                1,
                jnp.bfloat16,
            )
            for step in range(4):
                returned[part, head + step] = values[:, step * LANES : (step + 1) * LANES]
        for at, (crossing, _) in enumerate(others):

            @pl.when(jnp.where(crossing, 1 - here, here) == part)
            def _():
                back_copies[at].start()

    in_grads(1 - here)
    gate_cross.start()
    down(1, 0)
    finish(0)
    down(1, 1)
    finish(1)
    back_ref[here * heads + there] = returned[here, there]
    for part in parts:
        down_meet(1, part)
        down_over[part].start()
    in_grads(here)
    for one in up_outs:
        one.start()
    for one in mid_near + mid_far + mid_on:
        one.wait_send()
    pl.semaphore_signal(free_sem, inc=1, device_id=sibling, device_id_type=MESH_IDS)
    for part in parts:
        down(0, part)
    lax.fori_loop(0, own_width // narrow_tile, down_rows, 0)
    for one in down_outs:
        one.start()

    for at in range(2):

        def output_rows(step, unused):
            cut = pl.ds(pl.multiple_of(step * narrow_tile, narrow_tile), narrow_tile)
            source = pl.ds(pl.multiple_of(at * half + step * narrow_tile, narrow_tile), narrow_tile)
            left = jnp.transpose(attended[:, source].astype(jnp.float32)).astype(jnp.bfloat16)

            def columns(place_at, unused):
                cols = pl.ds(pl.multiple_of(place_at * wide, wide), wide)
                w_output[at, cut, cols] = jnp.dot(
                    left, branch_ref[:, cols], preferred_element_type=jnp.float32
                ).astype(jnp.bfloat16)
                return unused

            return lax.fori_loop(0, width // wide, columns, unused)

        lax.fori_loop(0, half // narrow_tile, output_rows, 0)

    own_rows = half // heads
    stripes = heads // 2
    pl.semaphore_wait(free_sem, 1)

    def stripe_of(at, bit):
        first = (at % stripes * 2 + bit) * own_rows
        return pl.ds(pl.multiple_of(first, own_rows), own_rows)

    def landed_at(at):
        per_slot = row_count // own_rows
        slot = at // per_slot
        return (slot // 4, slot % 4, pl.ds(at % per_slot * own_rows, own_rows))

    core_copies = []
    for at in range(2 * stripes):
        core_copies.append(
            pltpu.make_async_remote_copy(
                src_ref=w_output.at[at // stripes, stripe_of(at, 1 - core)],
                dst_ref=mid_ref.at[landed_at(at)],
                send_sem=core_send.at[at],
                recv_sem=core_recv.at[at],
                device_id=sibling,
                device_id_type=MESH_IDS,
            )
        )
        core_copies[-1].start()
    gate_cross.wait()

    def add_gate(at, unused):
        cut = pl.ds(pl.multiple_of(at * tile, tile), tile)
        gate_ref[cut, :] = (
            gate_ref[cut, :].astype(jnp.float32)
            + w_in[here, cut, pl.ds(0, own_width)].astype(jnp.float32)
        ).astype(jnp.bfloat16)
        return unused

    lax.fori_loop(0, half // tile, add_gate, 0)
    far_bit = (there // 4) % 2
    output_outs = []
    for at in range(2 * stripes):
        core_copies[at].wait_recv()
        own = stripe_of(at, core)
        w_output[at // stripes, own, :] = (
            w_output[at // stripes, own, :].astype(jnp.float32)
            + mid_ref[landed_at(at)].astype(jnp.float32)
        ).astype(jnp.bfloat16)
    for at in range(stripes):
        grp, high, low_bit = at // (stripes // 2), at // 2 % (stripes // 4), at % 2
        for kind, (target_ref, bit) in enumerate(
            ((output_kept, far_bit), (output_sent, 1 - far_bit))
        ):
            first = ((high * 4 + bit * 2 + low_bit) * 2 + core) * own_rows
            cut = pl.ds(pl.multiple_of(first, own_rows), own_rows)
            output_outs.append(
                pltpu.make_async_copy(
                    w_output.at[grp, cut], target_ref.at[at], place_sem.at[2 * at + kind]
                )
            )
            output_outs[-1].start()
    for part in parts:
        down_meet(0, part)
        down_over[part].wait_recv()

        def block_rows(at, unused):
            cut = pl.ds(pl.multiple_of(at * tile, tile), tile)
            place = pl.ds(pl.multiple_of(part * row_count + at * tile, tile), tile)
            block_ref[place, :] = (
                mixed_ref[place, :]
                + down_own_ref[0, part, cut, :].astype(jnp.float32)
                + down_far_landed[part, cut, :].astype(jnp.float32)
            ).astype(jnp.bfloat16)
            return unused

        lax.fori_loop(0, row_count // tile, block_rows, 0)
    for one in up_outs + down_outs + output_outs:
        one.wait()
    for one in back_copies:
        one.wait()
    for one in grad_far + out_near + out_on + down_over + [down_far]:
        one.wait_send()
    for one in list(down_near.values()) + output_near + core_copies:
        one.wait_send()


def mlp(heads, tokens, gain, out_rows, out_across, output_parts, in_parts, down_own):
    count, row_count, _ = heads.shape
    groups, reps = lax.axis_size("grp"), lax.axis_size("rep")
    rows, width = tokens.shape
    half = width // 2
    own_width = in_parts[0].shape[2]
    vmem = pl.BlockSpec(memory_space=pltpu.VMEM)
    anywhere = pl.BlockSpec(memory_space=pl.ANY)
    low, full = jnp.bfloat16, jnp.float32
    others = pltpu.SemaphoreType.DMA((count - 1,))
    return pl.pallas_call(
        mlp_kernel,
        out_shape=(
            jax.ShapeDtypeStruct((rows, width), low),
            jax.ShapeDtypeStruct((rows, width), full),
            jax.ShapeDtypeStruct((count, row_count, LANES), low),
            jax.ShapeDtypeStruct((half, own_width), low),
            jax.ShapeDtypeStruct((half, own_width), low),
            jax.ShapeDtypeStruct((half, own_width), low),
            jax.ShapeDtypeStruct((own_width // (2 * LANES), LANES, width), low),
            jax.ShapeDtypeStruct((own_width // (2 * LANES), LANES, width), low),
            jax.ShapeDtypeStruct((reps // 2, half // reps, width), low),
            jax.ShapeDtypeStruct((reps // 2, half // reps, width), low),
        ),
        in_specs=[vmem] * 3 + [anywhere] * 9,
        out_specs=(vmem,) * 4 + (anywhere,) * 6,
        scratch_shapes=[
            pltpu.VMEM((rows, width), full),
            pltpu.VMEM((2, 2, row_count, width), low),
            pltpu.VMEM((2, row_count, width), low),
            pltpu.VMEM((rows, width), low),
            pltpu.VMEM((rows, width), low),
            pltpu.VMEM((groups, reps, row_count, LANES), low),
            pltpu.VMEM((groups, 4, row_count, width), low),
            pltpu.VMEM((groups, 4, row_count, width), low),
            pltpu.VMEM((groups, 4, row_count, own_width), low),
            pltpu.VMEM((groups, 4, row_count, 2 * own_width), low),
            pltpu.VMEM((2, half, width), low),
            pltpu.VMEM((2, half, 2 * own_width), low),
            pltpu.VMEM((own_width, width), low),
            pltpu.VMEM((2, 2, row_count, width), low),
            pltpu.VMEM((2, 2, row_count, width), low),
            pltpu.VMEM((2, row_count, width), low),
            pltpu.VMEM((2, row_count, width), low),
            pltpu.VMEM((2, 2, row_count, width), low),
            pltpu.SemaphoreType.DMA((9,)),
            pltpu.SemaphoreType.DMA((2,)),
            pltpu.SemaphoreType.DMA((26,)),
            pltpu.SemaphoreType.DMA((26,)),
            others,
            others,
            others,
            others,
            pltpu.SemaphoreType.DMA((own_width // LANES,)),
            pltpu.SemaphoreType.DMA((reps,)),
            pltpu.SemaphoreType.DMA((reps,)),
            pltpu.SemaphoreType.DMA((reps,)),
            pltpu.SemaphoreType.REGULAR,
        ],
        compiler_params=pltpu.CompilerParams(
            vmem_limit_bytes=62 * 1024 * 1024, collective_id=2, has_side_effects=True
        ),
        cost_estimate=pl.CostEstimate(
            flops=150 * 10**9, bytes_accessed=150 << 20, transcendentals=0
        ),
        name="mlp",
    )(heads, tokens, gain, out_rows, out_across, *output_parts, *in_parts, down_own)


def after_kernel(*refs):
    pass


def after(values, ahead):
    anywhere = pl.BlockSpec(memory_space=pl.ANY)
    return pl.pallas_call(
        after_kernel,
        out_shape=tuple(jax.ShapeDtypeStruct(one.shape, one.dtype) for one in values),
        in_specs=[anywhere] * (len(values) + 1),
        out_specs=(anywhere,) * len(values),
        input_output_aliases={at: at for at in range(len(values))},
        name="after",
    )(*values, ahead)


def heads_body(
    tokens,
    attn_gain,
    w_query,
    w_key,
    w_value,
    w_output,
    mlp_gain,
    w_gate,
    w_up,
    w_down,
    out_grad,
    lengths,
):
    groups, reps = lax.axis_size("grp"), lax.axis_size("rep")
    here, there = lax.axis_index("grp"), lax.axis_index("rep")
    micro_count, row_count, width = tokens.shape
    rows = micro_count * row_count
    hidden_width = w_gate.shape[1]
    own_width = hidden_width // (2 * groups)

    out_rows = out_grad.reshape(rows, width)
    (
        gathered_rows,
        qkv,
        w_heads,
        gate_in,
        up_own,
        down_own,
        output_part,
        out_own,
        gains,
    ) = gather_heads(
        tokens,
        (attn_gain, mlp_gain),
        w_query,
        w_key,
        w_value,
        w_gate,
        w_up,
        w_down,
        w_output,
        out_rows,
    )
    gain_one = gains[:, 0].reshape(width).astype(jnp.float32)
    gain_two = gains[:, 1].reshape(width).astype(jnp.float32)

    output_parts = (w_output, output_part, swap(output_part, 0, 2))
    in_parts = (gate_in, up_own, swap(up_own, 1, 0))

    attended, out_heads, log_sum, query, key, value = attend(lengths, qkv)
    (
        block_out,
        grad_mixed,
        grad_heads,
        gate_part,
        up_kept,
        up_sent,
        down_kept,
        down_sent,
        output_kept,
        output_sent,
    ) = mlp(
        attended,
        tokens.reshape(rows, width),
        jnp.broadcast_to(gain_two[None], (8, width)),
        out_rows,
        swap(out_own, 0, 4),
        output_parts,
        in_parts,
        down_own,
    )

    own_rows = width // (groups * reps)
    by_owner = (2, 2, 2, 2, own_rows, own_width)
    gate_part = gate_part.reshape(by_owner)
    high_bit = there // 8 % 2
    gate_kept = pick(gate_part, high_bit, 0)
    sums = (
        swap(pick(gate_part, 1 - high_bit, 0), 0, 8),
        swap(up_sent, 1, 0),
        swap(down_sent, 0, 2),
        swap(output_sent, 0, 4),
    )
    back = attend_back(lengths, query, key, value, out_heads, log_sum, grad_heads)
    gate_met, up_met, down_met, output_met = after(sums, back)
    token_grad, heads_grad, quad_grad, down_grad, output_grad = scatter_heads(
        back.reshape(reps, groups * row_count, 3 * LANES),
        w_heads,
        tokens.reshape(rows, width),
        grad_mixed,
        jnp.broadcast_to(gain_one[None], (8, width)),
        gathered_rows,
        (
            gate_kept,
            gate_met,
            up_kept.reshape(by_owner),
            up_met.reshape(by_owner),
            down_kept.reshape(2, 2, 2, own_rows, width),
            down_met.reshape(2, 2, 2, own_rows, width),
            output_kept.reshape(2, 2, 2, own_rows, width),
            output_met.reshape(2, 2, 2, own_rows, width),
        ),
    )
    pieces = quad_grad.reshape(2, 2, 2, own_rows, groups, 2, 2, LANES)
    pieces = pieces.transpose(2, 3, 4, 5, 0, 6, 1, 7).reshape(2, own_rows, hidden_width)
    gate_grad, up_grad = pieces[0].astype(jnp.float32), pieces[1].astype(jnp.float32)
    heads_grad = (
        heads_grad.reshape(reps, own_rows, 3, LANES)
        .transpose(2, 1, 0, 3)
        .reshape(3, own_rows, width)
        .astype(jnp.float32)
    )

    def own_part(value):
        return lax.dynamic_slice_in_dim(value, there * own_rows, own_rows, axis=0).astype(
            jnp.float32
        )

    attn_gain_grad = (
        jnp.sum(own_part(w_query) * heads_grad[0], axis=1)
        + jnp.sum(own_part(w_key) * heads_grad[1], axis=1)
        + jnp.sum(own_part(w_value) * heads_grad[2], axis=1)
    ) / own_part(attn_gain)
    mlp_gain_grad = (
        jnp.sum(own_part(w_gate) * gate_grad, axis=1) + jnp.sum(own_part(w_up) * up_grad, axis=1)
    ) / own_part(mlp_gain)
    block_shape = tokens.shape
    return (
        block_out.reshape(block_shape),
        token_grad.reshape(block_shape),
        attn_gain_grad,
        heads_grad[0],
        heads_grad[1],
        heads_grad[2],
        output_grad,
        mlp_gain_grad,
        gate_grad,
        up_grad,
        down_grad.reshape(2 * own_rows, width),
    )


def pick_body(*arrays):
    tokens = arrays[0]
    groups, reps = lax.axis_size("grp"), lax.axis_size("rep")
    fits = (
        groups == 2
        and tokens.shape[0] == groups
        and tokens.shape[2] == reps * LANES
        and reps == 16
        and reps & (reps - 1) == 0
        and tokens.shape[1] % UNIT_PAIR == 0
        and arrays[7].shape[1] == groups * reps * LANES
    )
    return heads_body(*arrays) if fits else ring_body(*arrays)


def solution(mesh):
    in_specs = (
        P(None, ("grp", "rep"), None),
        P("grp"),
        P("grp", None),
        P("grp", None),
        P("grp", None),
        P("grp", None),
        P("grp"),
        P("grp", None),
        P("grp", None),
        P("grp", None),
        P(None, ("grp", "rep"), None),
        P(),
    )
    out_specs = (
        P(None, ("grp", "rep"), None),
        P(None, ("grp", "rep"), None),
        P(("grp", "rep")),
        P(("grp", "rep"), None),
        P(("grp", "rep"), None),
        P(("grp", "rep"), None),
        P(("grp", "rep"), None),
        P(("grp", "rep")),
        P(("grp", "rep"), None),
        P(("grp", "rep"), None),
        P(("grp", "rep"), None),
    )
    return jax.shard_map(pick_body, mesh=mesh, in_specs=in_specs, out_specs=out_specs, check_vma=False)
```

```python
import functools
import math

import jax
import jax.numpy as jnp
from jax import lax
from jax.experimental import pallas as pl
from jax.experimental.pallas import tpu as pltpu
from jax.sharding import PartitionSpec as P

HD = 64
WINDOW = 2048


epsilon = 1e-05
rope_base = 10000.0
masked_score = -1e30
BOTH = ("grp", "rep")
LANES = 128
UNIT_BLOCK = 8
UNIT_PAIR = 16
KERNEL_VMEM = 56 * 1024 * 1024
SCATTER_REFS = 18


def from_behind(value, axis, steps):
    count = lax.axis_size(axis)
    first, last = (max(0, -steps), min(count, count - steps))
    return lax.ppermute(value, axis, [(source, source + steps) for source in range(first, last)])


def rms_scale(values):
    return lax.rsqrt(jnp.mean(values * values, axis=-1, keepdims=True) + epsilon)


def norm_backward(values, gain_full, grad_normed):
    inverse = rms_scale(values)
    normed = values * inverse
    gain_grad = jnp.sum(grad_normed * normed, axis=0)
    weighted = grad_normed * gain_full
    return (
        inverse * (weighted - normed * jnp.mean(weighted * normed, axis=-1, keepdims=True)),
        gain_grad,
    )


def rotary(values, cosine, sine_table):
    half_width = values.shape[-1] // 2
    first_half = values[..., :half_width]
    second_half = values[..., half_width:]
    return jnp.concatenate(
        [
            first_half * cosine - second_half * sine_table,
            second_half * cosine + first_half * sine_table,
        ],
        axis=-1,
    )


def pick_rows(rows_block, row_ids):
    return jnp.take(rows_block, row_ids, axis=0)


def take_rows(values, row_ids):
    return jax.vmap(pick_rows)(values, row_ids)


def gather_attn(attn_gain, w_query, w_key, w_value, w_output):
    return (
        lax.all_gather(attn_gain, "grp", axis=0, tiled=True),
        lax.all_gather(w_query, "grp", axis=0, tiled=True),
        lax.all_gather(w_key, "grp", axis=0, tiled=True),
        lax.all_gather(w_value, "grp", axis=0, tiled=True),
        lax.all_gather(w_output, "grp", axis=0, tiled=True),
    )


def gather_mlp(mlp_gain, w_gate, w_up, w_down):
    return (
        lax.all_gather(mlp_gain, "grp", axis=0, tiled=True),
        lax.all_gather(w_gate, "grp", axis=0, tiled=True),
        lax.all_gather(w_up, "grp", axis=0, tiled=True),
        lax.all_gather(w_down, "grp", axis=0, tiled=True),
    )


def reduce_attn(gain_grad, query_grad, key_grad, value_grad, output_grad):
    return (
        lax.psum_scatter(gain_grad, ("grp", "rep"), scatter_dimension=0, tiled=True),
        lax.psum_scatter(query_grad, ("grp", "rep"), scatter_dimension=0, tiled=True),
        lax.psum_scatter(key_grad, ("grp", "rep"), scatter_dimension=0, tiled=True),
        lax.psum_scatter(value_grad, ("grp", "rep"), scatter_dimension=0, tiled=True),
        lax.psum_scatter(output_grad, ("grp", "rep"), scatter_dimension=0, tiled=True),
    )


def reduce_mlp(gain_grad, gate_grad, up_grad, down_grad):
    return (
        lax.psum_scatter(gain_grad, ("grp", "rep"), scatter_dimension=0, tiled=True),
        lax.psum_scatter(gate_grad, ("grp", "rep"), scatter_dimension=0, tiled=True),
        lax.psum_scatter(up_grad, ("grp", "rep"), scatter_dimension=0, tiled=True),
        lax.psum_scatter(down_grad, ("grp", "rep"), scatter_dimension=0, tiled=True),
    )


def pass_on(carried, unused):
    arrived = from_behind(carried, ("grp", "rep"), 1)
    return (arrived, arrived)


def pass_back(running, portion):
    arrived = from_behind(running.astype(jnp.bfloat16), ("grp", "rep"), -1).astype(running.dtype)
    return (arrived + portion, None)


def ring_body(
    tokens,
    attn_gain,
    w_query,
    w_key,
    w_value,
    w_output,
    mlp_gain,
    w_gate,
    w_up,
    w_down,
    out_grad,
    lengths,
):
    devices = lax.axis_size(("grp", "rep"))
    rank_here = lax.axis_index(("grp", "rep"))
    micro_count, row_count, model_width = tokens.shape
    per_dev = row_count // devices
    head_count = model_width // HD
    reach_count = (WINDOW + row_count - 2) // row_count
    head_group = math.gcd(head_count, 4)
    group_count = head_count // head_group
    score_scale = 1.0 / math.sqrt(HD)
    unit_ids = jnp.arange(row_count, dtype=jnp.int32)
    seq_ends = jnp.cumsum(lengths, axis=1)
    starts = seq_ends - lengths
    seq_order = jnp.arange(lengths.shape[1], dtype=jnp.int32)
    earlier = seq_order[None, :] < seq_order[:, None]
    dealt_start = jnp.sum(jnp.where(earlier[None], lengths[:, None, :], 0), axis=2)
    seq_of = jnp.sum((seq_ends[:, None, :] <= unit_ids[None, :, None]).astype(jnp.int32), axis=2)
    seq_dealt = jnp.take_along_axis(dealt_start, seq_of, axis=1)
    unit_of = seq_dealt + unit_ids[None, :] - jnp.take_along_axis(starts, seq_of, axis=1)
    micro_ids = jnp.arange(micro_count, dtype=jnp.int32)[:, None]
    source_unit = (
        jnp.zeros((micro_count, row_count), jnp.int32)
        .at[micro_ids, unit_of]
        .set(jnp.broadcast_to(unit_ids[None, :], unit_of.shape))
    )
    unit_begin = (
        jnp.zeros((micro_count, row_count), jnp.int32).at[micro_ids, unit_of].set(seq_dealt)
    )
    local_ids = jnp.arange(row_count, dtype=jnp.int32)
    local_step = local_ids % per_dev
    local_source = local_ids // per_dev
    distance = jnp.arange(reach_count + 1, dtype=jnp.int32)
    owner_dev = rank_here - distance
    owner_ok = owner_dev >= 0
    owner_unit = jnp.maximum(owner_dev, 0)[:, None] * per_dev + local_step[None, :]
    key_begin = unit_begin[:, owner_unit]
    key_pos = (owner_unit[None] - key_begin) * devices + local_source[None, None, :]
    query_begin = key_begin[:, 0]
    query_pos = key_pos[:, 0]
    allowed = (
        owner_ok[None, None, :, None]
        & (query_begin[:, :, None, None] == key_begin[:, None, :, :])
        & (key_pos[:, None, :, :] <= query_pos[:, :, None, None])
        & (query_pos[:, :, None, None] - key_pos[:, None, :, :] < WINDOW)
    )
    mask_full = allowed[:, None]
    half_width = HD // 2
    frequency = jnp.power(rope_base, -2.0 * jnp.arange(half_width, dtype=jnp.float32) / HD)
    angles = query_pos.astype(jnp.float32)[:, :, None] * frequency[None, None, :]
    cosine = jnp.cos(angles)[:, :, None, :]
    sine_table = jnp.sin(angles)[:, :, None, :]
    head_shape = (micro_count, row_count, head_count, HD)
    block_shape = (micro_count, row_count, model_width)
    gathered = gather_attn(attn_gain, w_query, w_key, w_value, w_output)
    gain_one = gathered[0].astype(jnp.float32)
    inputs = tokens.astype(jnp.float32).reshape(micro_count * row_count, model_width)
    normed_in = (inputs * rms_scale(inputs) * gain_one).astype(jnp.bfloat16)
    queries = jnp.dot(normed_in, gathered[1], preferred_element_type=jnp.float32).astype(
        jnp.bfloat16
    )
    keys_in = jnp.dot(normed_in, gathered[2], preferred_element_type=jnp.float32).astype(
        jnp.bfloat16
    )
    values_in = jnp.dot(normed_in, gathered[3], preferred_element_type=jnp.float32).astype(
        jnp.bfloat16
    )
    dealt = (
        lax.all_to_all(
            take_rows(queries.reshape(block_shape), source_unit),
            ("grp", "rep"),
            split_axis=1,
            concat_axis=1,
            tiled=True,
        ),
        lax.all_to_all(
            take_rows(keys_in.reshape(block_shape), source_unit),
            ("grp", "rep"),
            split_axis=1,
            concat_axis=1,
            tiled=True,
        ),
        lax.all_to_all(
            take_rows(values_in.reshape(block_shape), source_unit),
            ("grp", "rep"),
            split_axis=1,
            concat_axis=1,
            tiled=True,
        ),
    )
    rot_q = rotary(dealt[0].reshape(head_shape).astype(jnp.float32), cosine, sine_table).astype(
        jnp.bfloat16
    )
    rot_k = rotary(dealt[1].reshape(head_shape).astype(jnp.float32), cosine, sine_table).astype(
        jnp.bfloat16
    )
    own_pair = jnp.stack([rot_k.reshape(block_shape), dealt[2]], axis=0)
    last_pair, farther = lax.scan(pass_on, own_pair, None, length=reach_count)
    context = jnp.concatenate([own_pair[None], farther], axis=0).reshape(
        reach_count + 1, 2, micro_count, row_count, head_count, HD
    )

    def group_scores(query_part, pair_part):
        scores = (
            jnp.einsum(
                "mqge,dmkge->mgqdk", query_part, pair_part[:, 0], preferred_element_type=jnp.float32
            )
            * score_scale
        )
        return jnp.where(mask_full, scores, masked_score)

    def forward_group(group_index, carried):
        attended_all, log_all = carried
        head_start = group_index * head_group
        query_part = lax.dynamic_slice_in_dim(rot_q, head_start, head_group, axis=2)
        pair_part = lax.dynamic_slice_in_dim(context, head_start, head_group, axis=4)
        scores = group_scores(query_part, pair_part)
        row_max = jnp.max(scores, axis=(3, 4), keepdims=True)
        weights_exp = jnp.exp(scores - row_max)
        row_sum = jnp.sum(weights_exp, axis=(3, 4), keepdims=True)
        soft_probs = (weights_exp / row_sum).astype(jnp.bfloat16)
        attended = jnp.einsum(
            "mgqdk,dmkge->mqge", soft_probs, pair_part[:, 1], preferred_element_type=jnp.float32
        ).astype(jnp.bfloat16)
        attended_all = lax.dynamic_update_slice_in_dim(attended_all, attended, head_start, axis=2)
        log_all = lax.dynamic_update_slice_in_dim(
            log_all, row_max + jnp.log(row_sum), head_start, axis=1
        )
        return (attended_all, log_all)

    attended_heads, log_sum = lax.fori_loop(
        0,
        group_count,
        forward_group,
        (
            jnp.zeros(head_shape, jnp.bfloat16),
            jnp.zeros((micro_count, head_count, row_count, 1, 1), jnp.float32),
        ),
    )
    returned = lax.all_to_all(
        attended_heads.reshape(block_shape), ("grp", "rep"), split_axis=1, concat_axis=1, tiled=True
    )
    attn_rows = take_rows(returned, unit_of).reshape(micro_count * row_count, model_width)
    mixed = inputs + jnp.dot(attn_rows, gathered[4], preferred_element_type=jnp.float32)
    mlp_set = gather_mlp(mlp_gain, w_gate, w_up, w_down)
    gain_two = mlp_set[0].astype(jnp.float32)
    normed_mid = (mixed * rms_scale(mixed) * gain_two).astype(jnp.bfloat16)
    gate_pre = jnp.dot(normed_mid, mlp_set[1], preferred_element_type=jnp.float32)
    up_pre = jnp.dot(normed_mid, mlp_set[2], preferred_element_type=jnp.float32)
    gate_sig = jax.nn.sigmoid(gate_pre)
    gate_silu = gate_pre * gate_sig
    hidden = (gate_silu * up_pre).astype(jnp.bfloat16)
    block_out = (mixed + jnp.dot(hidden, mlp_set[3], preferred_element_type=jnp.float32)).astype(
        jnp.bfloat16
    )
    mlp_set = gather_mlp(mlp_gain, w_gate, w_up, w_down)
    out_rows = out_grad.reshape(micro_count * row_count, model_width)
    down_grad = jnp.einsum("tf,td->fd", hidden, out_rows, preferred_element_type=jnp.float32)
    grad_hidden = jnp.einsum("td,fd->tf", out_rows, mlp_set[3], preferred_element_type=jnp.float32)
    grad_gate = (grad_hidden * up_pre * gate_sig * (1.0 + gate_pre * (1.0 - gate_sig))).astype(
        jnp.bfloat16
    )
    grad_up = (grad_hidden * gate_silu).astype(jnp.bfloat16)
    gate_grad = jnp.einsum("td,tf->df", normed_mid, grad_gate, preferred_element_type=jnp.float32)
    up_grad = jnp.einsum("td,tf->df", normed_mid, grad_up, preferred_element_type=jnp.float32)
    grad_mid = jnp.einsum(
        "tf,df->td", grad_gate, mlp_set[1], preferred_element_type=jnp.float32
    ) + jnp.einsum("tf,df->td", grad_up, mlp_set[2], preferred_element_type=jnp.float32)
    grad_norm_mid, mlp_gain_grad = norm_backward(mixed, gain_two, grad_mid)
    grad_mixed = out_rows.astype(jnp.float32) + grad_norm_mid
    mlp_sums = reduce_mlp(mlp_gain_grad, gate_grad, up_grad, down_grad)
    gathered = gather_attn(attn_gain, w_query, w_key, w_value, w_output)
    grad_branch = grad_mixed.astype(jnp.bfloat16)
    output_grad = jnp.einsum(
        "td,te->de", attn_rows, grad_branch, preferred_element_type=jnp.float32
    )
    grad_att = jnp.einsum(
        "te,de->td", grad_branch, gathered[4], preferred_element_type=jnp.float32
    ).astype(jnp.bfloat16)
    grad_dealt = lax.all_to_all(
        take_rows(grad_att.reshape(block_shape), source_unit),
        ("grp", "rep"),
        split_axis=1,
        concat_axis=1,
        tiled=True,
    )
    grad_heads = grad_dealt.reshape(head_shape)

    def backward_group(group_index, carried):
        query_total, pair_total = carried
        head_start = group_index * head_group
        query_part = lax.dynamic_slice_in_dim(rot_q, head_start, head_group, axis=2)
        grad_part = lax.dynamic_slice_in_dim(grad_heads, head_start, head_group, axis=2)
        pair_part = lax.dynamic_slice_in_dim(context, head_start, head_group, axis=4)
        log_part = lax.dynamic_slice_in_dim(log_sum, head_start, head_group, axis=1)
        scores = group_scores(query_part, pair_part)
        soft_probs = jnp.exp(scores - log_part)
        grad_probs = jnp.einsum(
            "mqge,dmkge->mgqdk", grad_part, pair_part[:, 1], preferred_element_type=jnp.float32
        )
        inner_sum = jnp.sum(soft_probs * grad_probs, axis=(3, 4), keepdims=True)
        grad_scores = (soft_probs * (grad_probs - inner_sum)).astype(jnp.bfloat16)
        query_piece = (
            jnp.einsum(
                "mgqdk,dmkge->mqge",
                grad_scores,
                pair_part[:, 0],
                preferred_element_type=jnp.float32,
            )
            * score_scale
        )
        key_part = (
            jnp.einsum(
                "mgqdk,mqge->dmkge", grad_scores, query_part, preferred_element_type=jnp.float32
            )
            * score_scale
        )
        value_part = jnp.einsum(
            "mgqdk,mqge->dmkge",
            soft_probs.astype(jnp.bfloat16),
            grad_part,
            preferred_element_type=jnp.float32,
        )
        query_total = lax.dynamic_update_slice_in_dim(query_total, query_piece, head_start, axis=2)
        pair_total = lax.dynamic_update_slice_in_dim(
            pair_total, jnp.stack([key_part, value_part], axis=1), head_start, axis=4
        )
        return (query_total, pair_total)

    query_total, pair_total = lax.fori_loop(
        0,
        group_count,
        backward_group,
        (
            jnp.zeros(head_shape, jnp.float32),
            jnp.zeros((reach_count + 1, 2) + head_shape, jnp.float32),
        ),
    )
    partials = pair_total.reshape(reach_count + 1, 2, micro_count, row_count, model_width)
    own_total, unused_out = lax.scan(
        pass_back, partials[reach_count], partials[:reach_count], reverse=True
    )
    query_back = rotary(query_total, cosine, -sine_table).astype(jnp.bfloat16)
    key_back = rotary(own_total[0].reshape(head_shape), cosine, -sine_table).astype(jnp.bfloat16)
    value_back = own_total[1].astype(jnp.bfloat16)
    grad_back = (
        lax.all_to_all(
            query_back.reshape(block_shape), ("grp", "rep"), split_axis=1, concat_axis=1, tiled=True
        ),
        lax.all_to_all(
            key_back.reshape(block_shape), ("grp", "rep"), split_axis=1, concat_axis=1, tiled=True
        ),
        lax.all_to_all(value_back, ("grp", "rep"), split_axis=1, concat_axis=1, tiled=True),
    )
    query_rows = take_rows(grad_back[0], unit_of).reshape(micro_count * row_count, model_width)
    key_rows = take_rows(grad_back[1], unit_of).reshape(micro_count * row_count, model_width)
    value_rows = take_rows(grad_back[2], unit_of).reshape(micro_count * row_count, model_width)
    query_grad = jnp.einsum("td,te->de", normed_in, query_rows, preferred_element_type=jnp.float32)
    key_grad = jnp.einsum("td,te->de", normed_in, key_rows, preferred_element_type=jnp.float32)
    value_grad = jnp.einsum("td,te->de", normed_in, value_rows, preferred_element_type=jnp.float32)
    grad_in = jnp.einsum("te,de->td", query_rows, gathered[1], preferred_element_type=jnp.float32)
    grad_in = grad_in + jnp.einsum(
        "te,de->td", key_rows, gathered[2], preferred_element_type=jnp.float32
    )
    grad_in = grad_in + jnp.einsum(
        "te,de->td", value_rows, gathered[3], preferred_element_type=jnp.float32
    )
    grad_norm_in, attn_gain_grad = norm_backward(inputs, gain_one, grad_in)
    token_grad = (grad_mixed + grad_norm_in).astype(jnp.bfloat16)
    attn_sums = reduce_attn(attn_gain_grad, query_grad, key_grad, value_grad, output_grad)
    return (
        block_out.reshape(block_shape),
        token_grad.reshape(block_shape),
        attn_sums[0],
        attn_sums[1],
        attn_sums[2],
        attn_sums[3],
        attn_sums[4],
        mlp_sums[0],
        mlp_sums[1],
        mlp_sums[2],
        mlp_sums[3],
    )


def contract(left_side, right_side, left_dim, right_dim, kind=jnp.float32):
    return lax.dot_general(
        left_side,
        right_side,
        (((left_dim,), (right_dim,)), ((), ())),
        preferred_element_type=jnp.float32,
    ).astype(kind)


def swap_halves(values):
    lane = lax.broadcasted_iota(jnp.int32, values.shape, 1)
    ahead = pltpu.roll(values, LANES - HD // 2, 1)
    behind = pltpu.roll(values, HD // 2, 1)
    return jnp.where(lane % HD < HD // 2, -ahead, behind)


def fill_tables(lengths_ref, begin_at, cos_unit, sin_unit, cos_part, sin_part):
    parts, units = cos_part.shape[0], cos_unit.shape[0]
    here = lax.axis_index("grp")

    def frequency(shape):
        lane = lax.broadcasted_iota(jnp.int32, shape, 1) % (HD // 2)
        return jnp.exp(lane.astype(jnp.float32) * (-2.0 * math.log(rope_base) / HD))

    unit = lax.broadcasted_iota(jnp.int32, (units, LANES), 0)
    begin = jnp.zeros((units, LANES), jnp.int32)
    end = 0
    for seq in range(lengths_ref.shape[1]):
        end = end + lengths_ref[here, seq]
        begin = jnp.where(unit >= end, end, begin)
    begin_at[...] = begin
    angle = ((unit - begin) * parts).astype(jnp.float32) * frequency((units, LANES))
    cos_unit[...] = jnp.cos(angle)
    sin_unit[...] = jnp.sin(angle)
    part = lax.broadcasted_iota(jnp.int32, (parts, LANES), 0).astype(jnp.float32)
    angle = part * frequency((parts, LANES))
    cos_part[...] = jnp.cos(angle)
    sin_part[...] = jnp.sin(angle)


def begin_of(lengths_ref, unit):
    here = lax.axis_index("grp")
    begin, end = 0, 0
    for seq in range(lengths_ref.shape[1]):
        end = end + lengths_ref[here, seq]
        begin = jnp.where(unit >= end, end, begin)
    return begin


def key_range(lengths_ref, at, parts, block):
    first_unit = at * UNIT_BLOCK
    last_unit = first_unit + UNIT_BLOCK - 1
    least = jnp.maximum(begin_of(lengths_ref, first_unit) * parts, at * block - (WINDOW - 1))
    most = jnp.maximum(
        begin_of(lengths_ref, last_unit) * parts, (at + 1) * block - 1 - (WINDOW - 1)
    )
    first = jnp.maximum(least, 0) // block
    return first, jnp.minimum(jnp.maximum((most + block - 1) // block, first), at)


def low_of(begin_at, at, parts):
    begin = begin_at[pl.ds(pl.multiple_of(at * UNIT_BLOCK, UNIT_BLOCK), UNIT_BLOCK), :] * parts
    shape = (parts, UNIT_BLOCK, LANES)
    part = lax.broadcasted_iota(jnp.int32, shape, 0)
    unit = lax.broadcasted_iota(jnp.int32, shape, 1) + at * UNIT_BLOCK
    low = jnp.maximum(begin[None], unit * parts + part - (WINDOW - 1))
    return low.reshape(parts * UNIT_BLOCK, LANES).astype(jnp.float32)


def slot_of(part):
    groups, reps = lax.axis_size("grp"), lax.axis_size("rep")
    offset = (part % reps) ^ lax.axis_index("rep")
    return offset * groups + ((part // reps) ^ lax.axis_index("grp"))


def pair_angles(unit_at, cos_unit, sin_unit, cos_part, sin_part):
    unit_cos = cos_unit[pl.ds(unit_at, UNIT_PAIR), :][None]
    unit_sin = sin_unit[pl.ds(unit_at, UNIT_PAIR), :][None]
    part_cos = cos_part[...][:, None, :]
    part_sin = sin_part[...][:, None, :]
    cosine = unit_cos * part_cos - unit_sin * part_sin
    sine = unit_sin * part_cos + unit_cos * part_sin
    return cosine, sine


def key_offsets(block):
    row = lax.broadcasted_iota(jnp.int32, (block, block), 0)
    return (row % UNIT_BLOCK) * (block // UNIT_BLOCK) + row // UNIT_BLOCK


def query_offsets(block):
    column = lax.broadcasted_iota(jnp.int32, (block, block), 1)
    return (column % UNIT_BLOCK) * (block // UNIT_BLOCK) + column // UNIT_BLOCK


def attend_kernel(
    lengths_ref,
    qkv_ref,
    att_ref,
    out_ref,
    log_ref,
    query_ref,
    key_ref,
    value_ref,
    query_heads,
    key_t,
    tops,
    sums,
    totals,
    lows,
    causal_at,
    key_at,
    begin_at,
    cos_unit,
    sin_unit,
    cos_part,
    sin_part,
):
    parts, units, _ = qkv_ref.shape
    block = parts * UNIT_BLOCK
    pairs = units // UNIT_PAIR
    halves = UNIT_PAIR // UNIT_BLOCK
    wide = block // LANES
    fill_tables(lengths_ref, begin_at, cos_unit, sin_unit, cos_part, sin_part)
    key_at[...] = query_offsets(block).astype(jnp.float32)
    causal_at[...] = jnp.where(query_offsets(block) <= key_offsets(block), 0.0, masked_score)

    def lay_out(pair, unused):
        unit_at = pl.multiple_of(pair * UNIT_PAIR, UNIT_PAIR)
        rows = jnp.stack(
            [qkv_ref[slot_of(part), pl.ds(unit_at, UNIT_PAIR), :] for part in range(parts)]
        )
        cosine, sine = pair_angles(unit_at, cos_unit, sin_unit, cos_part, sin_part)
        flat = (parts * UNIT_PAIR, LANES)
        cosine = cosine.reshape(flat)
        sine = sine.reshape(flat)

        def rotated(values):
            values = values.astype(jnp.float32).reshape(flat)
            turned = values * cosine + swap_halves(values) * sine
            return turned.reshape(parts, UNIT_PAIR, LANES)

        query = rotated(rows[:, :, :LANES]) * (1.0 / math.sqrt(HD))
        key = rotated(rows[:, :, LANES : 2 * LANES])
        value = rows[:, :, 2 * LANES :].astype(jnp.float32)
        for half in range(halves):
            at = pair * halves + half
            cut = slice(half * UNIT_BLOCK, (half + 1) * UNIT_BLOCK)
            query_rows = query[:, cut].reshape(block, LANES)
            key_rows = key[:, cut].reshape(block, LANES)
            query_ref[at] = query_rows.astype(jnp.bfloat16)
            key_ref[at] = key_rows.astype(jnp.bfloat16)
            value_ref[at] = value[:, cut].reshape(block, LANES).astype(jnp.bfloat16)
            lane = lax.broadcasted_iota(jnp.int32, query_rows.shape, 1)
            query_heads[at, 0] = jnp.where(lane < HD, query_rows, 0.0).astype(jnp.bfloat16)
            query_heads[at, 1] = jnp.where(lane < HD, 0.0, query_rows).astype(jnp.bfloat16)
            key_t[at] = jnp.transpose(key_rows).astype(jnp.bfloat16)
        return unused

    lax.fori_loop(0, pairs, lay_out, 0)

    def query_pair(pair, unused):
        ids = [pair * halves + half for half in range(halves)]
        for half, at in enumerate(ids):
            lows[half] = low_of(begin_at, at, parts)
        first, _ = key_range(lengths_ref, ids[0], parts, block)
        _, plain = key_range(lengths_ref, ids[-1], parts, block)
        plain = jnp.minimum(plain, ids[0])

        def wider(value):
            return jnp.concatenate([value] * wide, axis=1)

        def scores_of(half, head, key_block, causal, bounded):
            scores = jnp.dot(
                query_heads[ids[half], head], key_t[key_block], preferred_element_type=jnp.float32
            )
            if causal:
                scores = scores + causal_at[...]
            if bounded:
                bound = wider(lows[half] - (key_block * block).astype(jnp.float32))
                scores = jnp.where(key_at[...] >= bound, scores, masked_score)
            return scores

        def folded(combine, values):
            result = values[:, :LANES]
            for at in range(1, wide):
                result = combine(result, values[:, at * LANES : (at + 1) * LANES])
            return result

        def top_step(half, head, key_block, causal, bounded, fresh):
            high = folded(jnp.maximum, scores_of(half, head, key_block, causal, bounded))
            tops[half, head] = high if fresh else jnp.maximum(tops[half, head], high)

        def sum_step(half, head, key_block, causal, bounded, fresh):
            scores = scores_of(half, head, key_block, causal, bounded)
            weights = jnp.exp(scores - wider(tops[half, head]))
            part = folded(jnp.add, weights)
            product = jnp.dot(
                weights.astype(jnp.bfloat16),
                value_ref[key_block],
                preferred_element_type=jnp.float32,
            )
            sums[half, head] = part if fresh else sums[half, head] + part
            totals[half, head] = product if fresh else totals[half, head] + product

        def over_keys(step):
            for half, at in enumerate(ids):
                for head in range(2):
                    step(half, head, at, True, True, True)
                    for earlier in ids[:half]:
                        step(half, head, earlier, False, True, False)

            def all_steps(bounded):
                def go(key_block, unused):
                    for half in range(halves):
                        for head in range(2):
                            step(half, head, key_block, False, bounded, False)
                    return unused

                return go

            lax.fori_loop(first, plain, all_steps(True), 0)
            lax.fori_loop(plain, ids[0], all_steps(False), 0)

        over_keys(top_step)
        for half in range(halves):
            for head in range(2):
                high = jnp.max(tops[half, head], axis=1, keepdims=True)
                tops[half, head] = jnp.broadcast_to(high, (block, LANES))
        over_keys(sum_step)
        done = []
        for half, at in enumerate(ids):
            rows = []
            for head in range(2):
                total = jnp.broadcast_to(
                    jnp.sum(sums[half, head], axis=1, keepdims=True), (block, LANES)
                )
                rows.append(totals[half, head] / total)
                log = jnp.transpose(tops[half, head] + jnp.log(total))
                log_ref[at, head : head + 1, :] = log[0:1]
            lane = lax.broadcasted_iota(jnp.int32, (block, LANES), 1)
            both = jnp.where(lane < HD, rows[0], rows[1])
            out_ref[at] = jnp.transpose(both)
            done.append(both.reshape(parts, UNIT_BLOCK, LANES))
        unit_at = pl.multiple_of(pair * UNIT_PAIR, UNIT_PAIR)
        att_ref[:, pl.ds(unit_at, UNIT_PAIR), :] = jnp.concatenate(done, axis=1).astype(
            jnp.bfloat16
        )
        return unused

    lax.fori_loop(0, pairs, query_pair, 0)


def attend_back_kernel(
    lengths_ref,
    query_ref,
    key_ref,
    value_ref,
    out_ref,
    log_ref,
    grad_ref,
    back_ref,
    key_t,
    key_total,
    value_total,
    key_at,
    causal_at,
    begin_at,
    cos_unit,
    sin_unit,
    cos_part,
    sin_part,
):
    parts, units, _ = grad_ref.shape
    block = parts * UNIT_BLOCK
    pairs = units // UNIT_PAIR
    halves = UNIT_PAIR // UNIT_BLOCK
    fill_tables(lengths_ref, begin_at, cos_unit, sin_unit, cos_part, sin_part)
    key_at[...] = key_offsets(block).astype(jnp.float32)
    causal_at[...] = jnp.where(key_offsets(block) <= query_offsets(block), 0.0, masked_score)

    def lay_out(at, unused):
        key_t[at] = jnp.transpose(key_ref[at].astype(jnp.float32)).astype(jnp.bfloat16)
        key_total[at] = jnp.zeros((block, LANES), jnp.float32)
        value_total[at] = jnp.zeros((block, LANES), jnp.float32)
        return unused

    lax.fori_loop(0, pairs * halves, lay_out, 0)

    def split_heads(values, axis):
        place = lax.broadcasted_iota(jnp.int32, values.shape, axis)
        zero = jnp.zeros_like(values)
        return [
            jnp.where(place < HD, values, zero).astype(jnp.bfloat16),
            jnp.where(place < HD, zero, values).astype(jnp.bfloat16),
        ]

    def prepare(at, grad_rows):
        query_rows = query_ref[at].astype(jnp.float32)
        grad_turned = jnp.transpose(grad_rows)
        product = grad_turned * out_ref[at]
        return dict(
            low=jnp.transpose(low_of(begin_at, at, parts))[0:1],
            query=jnp.concatenate(split_heads(query_rows, 1), axis=0),
            grad=jnp.concatenate(split_heads(grad_rows, 1), axis=0),
            query_t=split_heads(jnp.transpose(query_rows), 0),
            grad_t=split_heads(grad_turned, 0),
            inner=[
                jnp.sum(product[head * HD : (head + 1) * HD], axis=0, keepdims=True)
                for head in range(2)
            ],
            logs=[log_ref[at, head : head + 1, :] for head in range(2)],
        )

    def step(held, key_block, carried, causal, bounded):
        probs, slopes, new = [], [], []
        for head in range(2):
            scores = jnp.dot(
                key_ref[key_block], held["query_t"][head], preferred_element_type=jnp.float32
            )
            if causal:
                scores = scores + causal_at[...]
            if bounded:
                scores = jnp.where(
                    key_at[...] >= held["low"] - (key_block * block).astype(jnp.float32), scores, masked_score
                )
            soft = jnp.exp(scores - held["logs"][head])
            grad_probs = jnp.dot(
                value_ref[key_block], held["grad_t"][head], preferred_element_type=jnp.float32
            )
            slope = (soft * (grad_probs - held["inner"][head])).astype(jnp.bfloat16)
            probs.append(soft.astype(jnp.bfloat16))
            slopes.append(slope)
            new.append(
                carried[head]
                + jnp.dot(
                    key_t[key_block, pl.ds(head * HD, HD), :],
                    slope,
                    preferred_element_type=jnp.float32,
                )
            )
        return tuple(new), probs, slopes

    def add_key(key_block, held, probs, slopes):
        value_total[key_block] += jnp.dot(
            jnp.concatenate(probs, axis=1),
            jnp.concatenate([one["grad"] for one in held], axis=0),
            preferred_element_type=jnp.float32,
        )
        key_total[key_block] += jnp.dot(
            jnp.concatenate(slopes, axis=1),
            jnp.concatenate([one["query"] for one in held], axis=0),
            preferred_element_type=jnp.float32,
        )

    def query_blocks(pair, grads):
        ids = [pair * halves + half for half in range(halves)]
        held = [prepare(at, rows) for at, rows in zip(ids, grads)]
        states = []
        for half, at in enumerate(ids):
            state, probs, slopes = step(
                held[half], at, (jnp.zeros((HD, block), jnp.float32),) * 2, True, True
            )
            add_key(at, held[half : half + 1], probs, slopes)
            for earlier in ids[:half]:
                state, probs, slopes = step(held[half], earlier, state, False, True)
                add_key(earlier, held[half : half + 1], probs, slopes)
            states.append(state)

        def all_steps(bounded):
            def run(key_block, carried):
                new, probs, slopes = [], [], []
                for half in range(halves):
                    state, prob, slope = step(held[half], key_block, carried[half], False, bounded)
                    new.append(state)
                    probs += prob
                    slopes += slope
                add_key(key_block, held, probs, slopes)
                return tuple(new)

            return run

        first, _ = key_range(lengths_ref, ids[0], parts, block)
        _, plain = key_range(lengths_ref, ids[-1], parts, block)
        plain = jnp.minimum(plain, ids[0])
        states = lax.fori_loop(first, plain, all_steps(True), tuple(states))
        states = lax.fori_loop(plain, ids[0], all_steps(False), states)
        return [
            jnp.transpose(jnp.concatenate(state, axis=0)) * (1.0 / math.sqrt(HD))
            for state in states
        ]

    def turn_back(rows, cosine, sine):
        flat = (parts * UNIT_PAIR, LANES)
        rows = jnp.concatenate(
            [one.reshape(parts, UNIT_BLOCK, LANES) for one in rows], axis=1
        ).reshape(flat)
        turned = rows * cosine.reshape(flat) - swap_halves(rows) * sine.reshape(flat)
        return turned.reshape(parts, UNIT_PAIR, LANES).astype(jnp.bfloat16)

    def put(values, unit_at, lane_at):
        for part in range(parts):
            back_ref[slot_of(part), pl.ds(unit_at, UNIT_PAIR), pl.ds(lane_at, LANES)] = values[part]

    def query_pair(pair, unused):
        unit_at = pl.multiple_of(pair * UNIT_PAIR, UNIT_PAIR)
        grads = grad_ref[:, pl.ds(unit_at, UNIT_PAIR), :].astype(jnp.float32)
        done = query_blocks(
            pair,
            [
                grads[:, half * UNIT_BLOCK : (half + 1) * UNIT_BLOCK].reshape(block, LANES)
                for half in range(halves)
            ],
        )
        cosine, sine = pair_angles(unit_at, cos_unit, sin_unit, cos_part, sin_part)
        put(turn_back(done, cosine, sine), unit_at, 0)
        return unused

    lax.fori_loop(0, pairs, query_pair, 0)

    def key_pair(pair, unused):
        unit_at = pl.multiple_of(pair * UNIT_PAIR, UNIT_PAIR)
        cosine, sine = pair_angles(unit_at, cos_unit, sin_unit, cos_part, sin_part)
        ids = [pair * halves + half for half in range(halves)]
        put(turn_back([key_total[at] for at in ids], cosine, sine), unit_at, LANES)
        values = jnp.concatenate(
            [value_total[at].reshape(parts, UNIT_BLOCK, LANES) for at in ids], axis=1
        ).astype(jnp.bfloat16)
        put(values, unit_at, 2 * LANES)
        return unused

    lax.fori_loop(0, pairs, key_pair, 0)


def table_shapes(parts, units):
    table = pltpu.VMEM((units, LANES), jnp.float32)
    row = pltpu.VMEM((parts, LANES), jnp.float32)
    return [pltpu.VMEM((units, LANES), jnp.int32), table, table, row, row]


def attend(lengths, qkv):
    parts, units, _ = qkv.shape
    block = parts * UNIT_BLOCK
    blocks = units // UNIT_BLOCK
    smem = pl.BlockSpec(memory_space=pltpu.SMEM)
    vmem = pl.BlockSpec(memory_space=pltpu.VMEM)
    rows = jax.ShapeDtypeStruct((blocks, block, LANES), jnp.bfloat16)
    halves = UNIT_PAIR // UNIT_BLOCK
    held = pltpu.VMEM((halves, 2, block, LANES), jnp.float32)
    return pl.pallas_call(
        attend_kernel,
        out_shape=(
            jax.ShapeDtypeStruct((parts, units, LANES), jnp.bfloat16),
            jax.ShapeDtypeStruct((blocks, LANES, block), jnp.float32),
            jax.ShapeDtypeStruct((blocks, 8, block), jnp.float32),
            rows,
            rows,
            rows,
        ),
        in_specs=[smem, vmem],
        out_specs=(vmem,) * 6,
        scratch_shapes=[
            pltpu.VMEM((blocks, 2, block, LANES), jnp.bfloat16),
            pltpu.VMEM((blocks, LANES, block), jnp.bfloat16),
            held,
            held,
            held,
            pltpu.VMEM((halves, block, LANES), jnp.float32),
            pltpu.VMEM((block, block), jnp.float32),
            pltpu.VMEM((block, block), jnp.float32),
        ]
        + table_shapes(parts, units),
        compiler_params=pltpu.CompilerParams(vmem_limit_bytes=KERNEL_VMEM),
        cost_estimate=pl.CostEstimate(
            flops=20 * 10**9, bytes_accessed=16 << 20, transcendentals=20 * 10**6
        ),
        name="attend",
    )(lengths, qkv)


def attend_back(lengths, query, key, value, out, log, grad):
    parts, units, _ = grad.shape
    block = parts * UNIT_BLOCK
    blocks = units // UNIT_BLOCK
    smem = pl.BlockSpec(memory_space=pltpu.SMEM)
    vmem = pl.BlockSpec(memory_space=pltpu.VMEM)
    return pl.pallas_call(
        attend_back_kernel,
        out_shape=jax.ShapeDtypeStruct((parts, units, 3 * LANES), jnp.bfloat16),
        in_specs=[smem] + [vmem] * 6,
        out_specs=vmem,
        scratch_shapes=[
            pltpu.VMEM((blocks, LANES, block), jnp.bfloat16),
            pltpu.VMEM((blocks, block, LANES), jnp.float32),
            pltpu.VMEM((blocks, block, LANES), jnp.float32),
            pltpu.VMEM((block, block), jnp.float32),
            pltpu.VMEM((block, block), jnp.float32),
        ]
        + table_shapes(parts, units),
        compiler_params=pltpu.CompilerParams(vmem_limit_bytes=KERNEL_VMEM),
        cost_estimate=pl.CostEstimate(
            flops=50 * 10**9, bytes_accessed=16 << 20, transcendentals=20 * 10**6
        ),
        name="attend_back",
    )(lengths, query, key, value, out, log, grad)


def swap(value, grp_step, rep_step):
    groups, reps = lax.axis_size("grp"), lax.axis_size("rep")
    pairs = [
        (grp * reps + rep, (grp ^ grp_step) * reps + (rep ^ rep_step))
        for grp in range(groups)
        for rep in range(reps)
    ]
    return lax.ppermute(value, BOTH, pairs)


def ordered(flag, own, other, axis=0):
    return jnp.where(
        flag == 0,
        jnp.concatenate([own, other], axis=axis),
        jnp.concatenate([other, own], axis=axis),
    )


def pick(value, index, axis):
    return lax.dynamic_index_in_dim(value, index, axis, keepdims=False)


def halve(value, axis, bit, grp_step, rep_step):
    kept = pick(value, bit, axis)
    sent = pick(value, 1 - bit, axis).astype(jnp.bfloat16)
    arrived = swap(sent, grp_step, rep_step)
    return kept.astype(jnp.float32) + arrived.astype(jnp.float32)


def narrow(value):
    return value.astype(jnp.bfloat16)


MESH_IDS = pl.DeviceIdType.MESH


def flipped(index, step):
    return index + step - 2 * step * ((index // step) % 2)


def lowest(offset):
    return offset & -offset


def link_of(offset, part, turned):
    return turned.get((offset, part), lowest(offset))


GATHER_LINKS = {(14, 0): 4}
GATHER_PLAN = (
    ("rows", 4, 0), ("rows", 0, 1), ("rows", 4, 1), ("rows", 8, 0), ("rows", 8, 1),
    ("rows", 6, 0), ("rows", 2, 0), ("rows", 6, 1), ("project", 5), ("project", 0),
    ("project", 9), ("project", 4), ("rows", 10, 0), ("project", 6), ("project", 8),
    ("project", 1), ("rows", 12, 1), ("rows", 2, 1), ("project", 2), ("project", 7),
    ("rows", 12, 0), ("rows", 10, 1), ("project", 10), ("project", 3), ("project", 12),
    ("rows", 14, 0), ("project", 13), ("rows", 14, 1), ("project", 14), ("project", 11),
    ("project", 15),
)


def gather_kernel(
    tokens_ref,
    gain_ref,
    w_query,
    w_key,
    w_value,
    w_gate,
    w_up,
    w_down,
    w_output,
    out_rows,
    normed_out,
    qkv_ref,
    weight_ref,
    gate_own,
    gate_met,
    up_ref,
    up_piece,
    down_first,
    down_second,
    output_ref,
    out_away,
    gains,
    raw,
    normed,
    weight_sem,
    out_sem,
    send_sem,
    recv_sem,
    side_send,
    side_recv,
    stripe_sem,
):
    here, there = lax.axis_index("grp"), lax.axis_index("rep")
    core = there % 2
    reps = raw.shape[0]
    slots = normed.shape[0]
    row_count, width = raw.shape[2:]
    steps = [1 << place for place in range(reps.bit_length() - 1)]
    across = (1 - here, there)

    def neighbour(step):
        return (here, flipped(there, step))

    barrier = pltpu.get_barrier_semaphore()
    for target in [across] + [neighbour(step) for step in steps]:
        pl.semaphore_signal(barrier, inc=1, device_id=target, device_id_type=MESH_IDS)
    local = []
    for at, weight in enumerate((w_query, w_key, w_value)):
        local.append(
            pltpu.make_async_copy(
                weight.at[:, pl.ds(pl.multiple_of(there * LANES, LANES), LANES)],
                weight_ref.at[here, :, pl.ds(at * LANES, LANES)],
                weight_sem.at[at],
            )
        )
        local[-1].start()
    raw[0, 0] = tokens_ref[here]
    gains[here] = gain_ref[...]
    pl.semaphore_wait(barrier, len(steps) + 1)

    def side(at, source, target_ref):
        return pltpu.make_async_remote_copy(
            src_ref=source,
            dst_ref=target_ref,
            send_sem=side_send.at[at],
            recv_sem=side_recv.at[at],
            device_id=across,
            device_id_type=MESH_IDS,
        )

    def rows_copy(offset, part):
        if offset == 0:
            return pltpu.make_async_remote_copy(
                src_ref=tokens_ref.at[1 - here],
                dst_ref=raw.at[0, 1],
                send_sem=send_sem.at[1],
                recv_sem=recv_sem.at[1],
                device_id=across,
                device_id_type=MESH_IDS,
            )
        step = link_of(offset, part, GATHER_LINKS)
        return pltpu.make_async_remote_copy(
            src_ref=raw.at[offset - step, part],
            dst_ref=raw.at[offset, part],
            send_sem=send_sem.at[2 * offset + part],
            recv_sem=recv_sem.at[2 * offset + part],
            device_id=neighbour(step),
            device_id_type=MESH_IDS,
        )

    order = [tuple(what) for kind, *what in GATHER_PLAN if kind == "rows"]
    copies = {
        (offset, part): rows_copy(offset, part)
        for offset in range(reps)
        for part in (0, 1)
        if offset or part
    }

    def pass_on(offset, part):
        for later, part_of in order:
            if later and part_of == part and later - link_of(later, part, GATHER_LINKS) == offset:
                copies[later, part].start()
        copies[offset + 1, part].start()

    gain_copy = side(0, gains.at[here], gains.at[here])
    gain_copy.start()
    copies[0, 1].start()
    pass_on(0, 0)
    for one in local:
        one.wait()
    weight_copy = side(1, weight_ref.at[here], weight_ref.at[here])
    weight_copy.start()

    stripes = [
        (grp, high, low)
        for grp in range(2)
        for high in range(reps // 8)
        for low in range(2)
    ]
    place = 4 * ((there // 4) % 2) + there % 2
    stripe_loads = []

    def load(source, target_ref):
        stripe_loads.append(
            pltpu.make_async_copy(source, target_ref, stripe_sem.at[len(stripe_loads)])
        )

    def columns_of(weight, grp, high, low):
        first = (grp * reps + 8 * high + 2 * low + place) * LANES
        return weight.at[:, pl.ds(pl.multiple_of(first, LANES), LANES)]

    for weight, target_ref in ((w_gate, gate_own), (w_up, up_ref)):
        for at, stripe in enumerate(stripes):
            load(columns_of(weight, *stripe), target_ref.at[:, pl.ds(at * LANES, LANES)])
    for at, (grp, high, low) in enumerate(stripes[: len(stripes) // 2]):
        first = (8 * high + 2 * low + place) * LANES
        load(
            w_down.at[pl.ds(pl.multiple_of(first, LANES), LANES)],
            (down_first, down_second)[at // 2].at[pl.ds(at % 2 * LANES, LANES)],
        )
    piece_rows = up_piece.shape[0]
    low = (there // 2) % 2
    for at, stripe in enumerate(stripes):
        load(
            columns_of(w_up, *stripe).at[
                pl.ds(pl.multiple_of(low * piece_rows, piece_rows), piece_rows)
            ],
            up_piece.at[:, pl.ds(at * LANES, LANES)],
        )
    load(out_rows, out_away)
    for one in stripe_loads:
        one.start()
    quarter = output_ref.shape[0]
    output_copy = side(
        2,
        w_output.at[pl.ds(pl.multiple_of((there % 4) * quarter, quarter), quarter)],
        output_ref,
    )
    output_copy.start()
    gate_copy = side(
        3, gate_own.at[pl.ds(pl.multiple_of(low * piece_rows, piece_rows), piece_rows)], gate_met
    )
    for one in stripe_loads[: len(stripes)]:
        one.wait()
    gate_copy.start()

    written = {}
    used = [None] * slots
    tile = 32

    def project(count, offset):
        slot = count % slots
        if used[slot] is not None:
            written[used[slot]].wait()
        used[slot] = offset
        gain = jnp.concatenate([gains[0, 0:1], gains[1, 0:1]], axis=1).astype(jnp.float32)
        for part in range(2):

            def norm_rows(at, unused):
                cut = pl.ds(pl.multiple_of(at * tile, tile), tile)
                values = raw[offset, part, cut, :].astype(jnp.float32)
                scaled = values * rms_scale(values) * gain
                normed[slot, pl.ds(pl.multiple_of(part * row_count + at * tile, tile), tile), :] = (
                    scaled.astype(jnp.bfloat16)
                )
                return unused

            lax.fori_loop(0, row_count // tile, norm_rows, 0)
        written[offset] = pltpu.make_async_copy(
            normed.at[slot], normed_out.at[offset], out_sem.at[offset]
        )
        written[offset].start()
        half = width // 2
        product = jnp.dot(
            normed[slot, :, :half], weight_ref[0], preferred_element_type=jnp.float32
        ) + jnp.dot(normed[slot, :, half:], weight_ref[1], preferred_element_type=jnp.float32)
        qkv_ref[pl.ds(2 * offset, 2)] = product.astype(jnp.bfloat16).reshape(
            2, row_count, 3 * LANES
        )

    count = 0
    for kind, *what in GATHER_PLAN:
        if kind == "rows":
            copies[tuple(what)].wait_recv()
            pass_on(*what)
            continue
        if count == 0:
            gain_copy.wait_recv()
            weight_copy.wait_recv()
        if what[0] % 2:
            for part in (0, 1):
                copies[what[0], part].wait_recv()
        project(count, what[0])
        count += 1
    for offset in used:
        written[offset].wait()
    for one in copies.values():
        one.wait_send()
    gain_copy.wait_send()
    weight_copy.wait_send()
    for one in stripe_loads[len(stripes) :]:
        one.wait()
    gate_copy.wait()
    output_copy.wait()


def gather_heads(
    tokens, gains, w_query, w_key, w_value, w_gate, w_up, w_down, w_output, out_rows
):
    reps = lax.axis_size("rep")
    _, row_count, width = tokens.shape
    half = width // 2
    own_width = reps // 2 * LANES
    gain_rows = jnp.concatenate(
        [gains[0][None], gains[1][None], jnp.zeros((14, half), jnp.bfloat16)], axis=0
    )
    vmem = pl.BlockSpec(memory_space=pltpu.VMEM)
    anywhere = pl.BlockSpec(memory_space=pl.ANY)
    return pl.pallas_call(
        gather_kernel,
        out_shape=(
            jax.ShapeDtypeStruct((reps, 2 * row_count, width), jnp.bfloat16),
            jax.ShapeDtypeStruct((2 * reps, row_count, 3 * LANES), jnp.bfloat16),
            jax.ShapeDtypeStruct((2, half, 3 * LANES), jnp.bfloat16),
            jax.ShapeDtypeStruct((half, own_width), jnp.bfloat16),
            jax.ShapeDtypeStruct((half // 2, own_width), jnp.bfloat16),
            jax.ShapeDtypeStruct((half, own_width), jnp.bfloat16),
            jax.ShapeDtypeStruct((half // 2, own_width), jnp.bfloat16),
            jax.ShapeDtypeStruct((own_width // 4, width), jnp.bfloat16),
            jax.ShapeDtypeStruct((own_width // 4, width), jnp.bfloat16),
            jax.ShapeDtypeStruct((half // 4, width), jnp.bfloat16),
            jax.ShapeDtypeStruct(out_rows.shape, jnp.bfloat16),
            jax.ShapeDtypeStruct((2, 16, half), jnp.bfloat16),
        ),
        in_specs=[vmem, vmem] + [anywhere] * 8,
        out_specs=(anywhere,) + (vmem,) * 11,
        scratch_shapes=[
            pltpu.VMEM((reps, 2, row_count, width), jnp.bfloat16),
            pltpu.VMEM((4, 2 * row_count, width), jnp.bfloat16),
            pltpu.SemaphoreType.DMA((3,)),
            pltpu.SemaphoreType.DMA((reps,)),
            pltpu.SemaphoreType.DMA((2 * reps,)),
            pltpu.SemaphoreType.DMA((2 * reps,)),
            pltpu.SemaphoreType.DMA((4,)),
            pltpu.SemaphoreType.DMA((4,)),
            pltpu.SemaphoreType.DMA((reps // 2 * 7 // 2 + 1,)),
        ],
        compiler_params=pltpu.CompilerParams(
            vmem_limit_bytes=KERNEL_VMEM, collective_id=0, has_side_effects=True
        ),
        cost_estimate=pl.CostEstimate(
            flops=8 * 10**9, bytes_accessed=250 << 20, transcendentals=0
        ),
        name="gather_heads",
    )(tokens, gain_rows, w_query, w_key, w_value, w_gate, w_up, w_down, w_output, out_rows)


SCATTER_PLAN = (
    ("first", "down"), ("first", "up"), ("rows", 5, 0), ("rows", 4, 0), ("rows", 15, 0),
    ("rows", 15, 1), ("weights", 1), ("first", "gate"), ("rows", 14, 1), ("weights", 1),
    ("rows", 7, 0), ("first", "out"), ("sum", "down"), ("rows", 3, 1), ("rows", 13, 1),
    ("rows", 11, 0), ("rows", 6, 0), ("rows", 11, 1), ("rows", 5, 1), ("rows", 10, 1),
    ("sum", "up"), ("weights", 2), ("rows", 9, 1), ("rows", 1, 1), ("weights", 1),
    ("rows", 14, 0), ("weights", 1), ("rows", 12, 1), ("weights", 1), ("sum", "gate"),
    ("weights", 2), ("rows", 10, 0), ("weights", 1), ("rows", 7, 1), ("sum", "out"),
    ("rows", 13, 0), ("rows", 6, 1), ("weights", 1), ("rows", 3, 0), ("rows", 12, 0),
    ("rows", 1, 0), ("rows", 9, 0), ("weights", 3), ("rows", 8, 1), ("sum", "quad"),
    ("rows", 2, 1), ("rows", 2, 0), ("weights", 2), ("sum", "out next"), ("rows", 8, 0),
    ("weights over",), ("rows", 4, 1), ("sum", "quad next"), ("weights out",), ("rows", 0, 1),
    ("rows", 0, 0),
)
SCATTER_LINKS = {(6, 0): 4}


def scatter_kernel(
    back_ref,
    weight_ref,
    tokens_ref,
    mixed_grad,
    gain_ref,
    normed_ref,
    gate_kept,
    gate_met,
    up_kept,
    up_met,
    down_kept,
    down_met,
    output_kept,
    output_met,
    token_ref,
    pieces_ref,
    quad_ref,
    down_ref,
    output_ref,
    away,
    landed,
    grad_in,
    normed,
    back_t,
    weight_t,
    weights_total,
    half_out,
    half_in,
    piece_out,
    gate_away,
    gate_landed,
    up_away,
    up_landed,
    up_last,
    down_away,
    down_landed,
    down_last,
    output_away,
    output_landed,
    output_next,
    output_last,
    gate_stage,
    up_stage,
    wide_stage,
    gate_crossed,
    up_crossed,
    normed_sem,
    send_sem,
    recv_sem,
    side_send,
    side_recv,
    piece_send,
    piece_recv,
    stage_sem,
    sum_send,
    sum_recv,
):
    here, there = lax.axis_index("grp"), lax.axis_index("rep")
    reps, rows, columns = back_ref.shape
    row_count = rows // 2
    width = token_ref.shape[1]
    half = width // 2
    own_rows = half // reps
    steps = [1 << place for place in range(reps.bit_length() - 1)]
    bit = {step: (there // step) % 2 for step in steps}
    across = (1 - here, there)

    def other(offset):
        index = there
        for step in steps:
            if offset & step:
                index = flipped(index, step)
        return (here, index)

    barrier = pltpu.get_barrier_semaphore()
    for target in [across] + [other(offset) for offset in range(1, reps)]:
        pl.semaphore_signal(barrier, inc=1, device_id=target, device_id_type=MESH_IDS)

    slots = normed.shape[0]
    fetch = [
        pltpu.make_async_copy(normed_ref.at[offset], normed.at[offset % slots], normed_sem.at[offset])
        for offset in range(reps)
    ]
    for offset in range(slots):
        fetch[offset].start()

    def part_of(ref, axis, index):
        return ref.at[(slice(None),) * axis + (index,)]

    def load(at, source, target_ref):
        copy = pltpu.make_async_copy(source, target_ref, stage_sem.at[at])
        copy.start()
        return copy

    def open_half(at, kept, met, axis, flag, stage, target_ref):
        loads = [load(2 * at + 1, part_of(met, axis, flag), target_ref)]
        if stage is not None:
            loads.append(load(2 * at, part_of(kept, axis, flag), stage))
        return loads

    firsts = [
        open_half(0, down_kept, down_met, 1, 1 - bit[2], wide_stage, down_away),
        open_half(1, output_kept, output_met, 0, 1 - here, None, output_away),
        open_half(2, gate_kept, gate_met, 1, 1 - bit[2], gate_stage.at[0], gate_away),
        open_half(3, up_kept, up_met, 0, 1 - here, up_stage, up_away),
    ]

    for at in range(2):
        turned = jnp.transpose(weight_ref[at].astype(jnp.float32)).astype(jnp.bfloat16)
        weight_t[:, pl.ds(at * half, half)] = turned
    pl.semaphore_wait(barrier, reps)

    def add_to(target_ref, *sources):
        lead = target_ref.shape[:-2]
        count = 1
        for size in lead:
            count *= size
        for at in range(count):
            index, rest = [], at
            for size in lead[::-1]:
                index.insert(0, rest % size)
                rest //= size

            def some_rows(step, unused):
                place = tuple(index) + (pl.ds(pl.multiple_of(step * 16, 16), 16),)
                total = target_ref[place].astype(jnp.float32)
                for source in sources:
                    total = total + source[place].astype(jnp.float32)
                target_ref[place] = total.astype(target_ref.dtype)
                return unused

            lax.fori_loop(0, target_ref.shape[-2] // 16, some_rows, 0)

    def sum_copy(at, source, target_ref, target):
        return pltpu.make_async_remote_copy(
            src_ref=source,
            dst_ref=target_ref,
            send_sem=sum_send.at[at],
            recv_sem=sum_recv.at[at],
            device_id=target,
            device_id_type=MESH_IDS,
        )

    down_cross = sum_copy(0, down_away, down_landed, other(2))
    output_cross = sum_copy(1, output_away, output_landed, across)
    gate_low = sum_copy(2, gate_away, gate_landed, other(2))
    up_low = sum_copy(3, up_away, up_landed, across)
    down_high = sum_copy(4, down_landed.at[1 - bit[8]], down_last, other(8))
    up_high = sum_copy(5, up_landed.at[1 - bit[8]], up_last, other(8))
    output_low = sum_copy(6, output_landed.at[:, 1 - bit[2]], output_next, other(2))
    output_high = sum_copy(7, output_next.at[1 - bit[8]], output_last, other(8))
    quad_far = [
        sum_copy(8, gate_landed.at[1 - bit[4]], gate_crossed, other(4)),
        sum_copy(9, up_last.at[1 - bit[4]], up_crossed, other(4)),
    ]
    early_width = gate_crossed.shape[2]
    early = pl.ds(0, early_width)
    late = pl.ds(early_width, quad_ref.shape[3] - early_width)
    beside = 1 - bit[1]
    quad_near = [
        sum_copy(at, source, quad_ref.at[far, bit[1], :, cols], other(1))
        for at, source, far, cols in (
            (10, gate_landed.at[bit[4], beside], bit[4], early),
            (11, up_last.at[bit[4], beside], bit[4], late),
            (12, gate_crossed.at[beside], 1 - bit[4], early),
            (13, up_crossed.at[beside], 1 - bit[4], late),
        )
    ]
    def first_send(at, target_ref, stage, copy):
        for one in firsts[at]:
            one.wait()
        add_to(target_ref, stage)
        copy.start()

    def down_first():
        first_send(0, down_away, wide_stage, down_cross)
        firsts[1].append(load(2, part_of(output_kept, 0, 1 - here), wide_stage))

    def own_half(at, kept, met, axis, flag, stage_a, stage_b, copy, target_ref):
        loads = (
            load(2 * at, part_of(kept, axis, flag), stage_a),
            load(2 * at + 1, part_of(met, axis, flag), stage_b),
        )
        for one in loads:
            one.wait()
        copy.wait_recv()
        add_to(target_ref, stage_a, stage_b)

    def down_sum():
        down_cross.wait_send()
        own_half(
            0, down_kept, down_met, 1, bit[2], wide_stage, down_away, down_cross, down_landed
        )
        down_high.start()

    def output_sum():
        output_cross.wait_send()
        own_half(
            1, output_kept, output_met, 0, here, wide_stage, output_away, output_cross,
            output_landed,
        )
        output_low.start()

    def gate_sum():
        own_half(
            2, gate_kept, gate_met, 1, bit[2], gate_stage.at[0], gate_stage.at[1],
            gate_low, gate_landed,
        )

    def up_sum():
        up_low.wait_send()
        own_half(
            3, up_kept, up_met, 0, here, up_stage, up_away, up_low,
            up_landed,
        )
        up_high.start()

    def output_next_sum():
        output_low.wait_recv()
        add_to(output_next, output_landed.at[:, bit[2]])
        output_high.start()

    def quad_send():
        up_high.wait_recv()
        add_to(up_last, up_landed.at[bit[8]])
        for one in quad_far + quad_near[:2]:
            one.start()
        quad_ref[bit[4], bit[1], :, early] = gate_landed[bit[4], bit[1]]
        quad_ref[bit[4], bit[1], :, late] = up_last[bit[4], bit[1]]

    def quad_pass():
        for one in quad_far:
            one.wait_recv()
        for one in quad_near[2:]:
            one.start()
        quad_ref[1 - bit[4], bit[1], :, early] = gate_crossed[bit[1]]
        quad_ref[1 - bit[4], bit[1], :, late] = up_crossed[bit[1]]

    def last_sums():
        down_high.wait_recv()
        output_high.wait_recv()

        def down_rows(step, unused):
            cut = pl.ds(pl.multiple_of(step * 16, 16), 16)
            for at in range(down_last.shape[0]):
                down_ref[at, cut] = down_last[at, cut].astype(jnp.float32) + down_landed[
                    bit[8], at, cut
                ].astype(jnp.float32)
            output_ref[cut] = output_last[cut].astype(jnp.float32) + output_next[
                bit[8], cut
            ].astype(jnp.float32)
            return unused

        lax.fori_loop(0, own_rows // 16, down_rows, 0)

    def rows_copy(offset, part):
        if offset == 0:
            return pltpu.make_async_remote_copy(
                src_ref=away.at[0, 1],
                dst_ref=landed.at[0, 1],
                send_sem=send_sem.at[1],
                recv_sem=recv_sem.at[1],
                device_id=across,
                device_id_type=MESH_IDS,
            )
        return pltpu.make_async_remote_copy(
            src_ref=away.at[offset // 2, part],
            dst_ref=landed.at[offset, part],
            send_sem=send_sem.at[2 * offset + part],
            recv_sem=recv_sem.at[2 * offset + part],
            device_id=other(link_of(offset, part, SCATTER_LINKS)),
            device_id_type=MESH_IDS,
        )

    copies = {
        (offset, part): rows_copy(offset, part)
        for offset in range(reps)
        for part in (0, 1)
        if offset or part
    }

    def send(offset, part):
        sources = [
            later
            for later in range(1, reps)
            if later - link_of(later, part, SCATTER_LINKS) == offset
        ]
        for later in sources:
            copies[later, part].wait_recv()
        total = jnp.dot(
            back_ref[offset, pl.ds(part * row_count, row_count), :],
            weight_t[...],
            preferred_element_type=jnp.float32,
        )
        for later in sources:
            total = total + landed[later, part].astype(jnp.float32)
        if offset == 0 and part == 0:
            grad_in[...] = total
        else:
            if offset % 2 == 0:
                copies[offset + 1, part].wait_send()
            away[offset // 2, part] = total.astype(jnp.bfloat16)
            copies[offset, part].start()

    def weight_step(offset):
        fetch[offset].wait()
        back_t[...] = jnp.transpose(back_ref[offset].astype(jnp.float32)).astype(jnp.bfloat16)

        def columns_at(at, unused):
            cut = pl.ds(pl.multiple_of(at * 512, 512), 512)
            term = jnp.dot(
                back_t[...], normed[offset % slots, :, cut], preferred_element_type=jnp.float32
            )
            if offset == 0:
                weights_total[:, cut] = term
            else:
                weights_total[:, cut] += term
            return unused

        lax.fori_loop(0, width // 512, columns_at, 0)
        if offset + slots < reps:
            fetch[offset + slots].start()

    half_copy = pltpu.make_async_remote_copy(
        src_ref=half_out,
        dst_ref=half_in,
        send_sem=side_send,
        recv_sem=side_recv,
        device_id=across,
        device_id_type=MESH_IDS,
    )
    piece_copies = [
        pltpu.make_async_remote_copy(
            src_ref=piece_out.at[other(offset)[1]],
            dst_ref=pieces_ref.at[there],
            send_sem=piece_send.at[offset],
            recv_sem=piece_recv.at[offset],
            device_id=other(offset),
            device_id_type=MESH_IDS,
        )
        for offset in range(1, reps)
    ]

    def cross_weights():
        cut = pl.ds(pl.multiple_of((1 - here) * half, half), half)
        half_out[...] = weights_total[:, cut].astype(jnp.bfloat16)
        half_copy.start()

    def share_weights():
        half_copy.wait_recv()
        cut = pl.ds(pl.multiple_of(here * half, half), half)
        total = jnp.transpose(weights_total[:, cut] + half_in[...].astype(jnp.float32))
        piece_out[...] = total.astype(jnp.bfloat16).reshape(reps, own_rows, columns)
        pieces_ref[there] = piece_out[there]
        for one in piece_copies:
            one.start()

    weights = list(range(reps))

    def weight_steps(count):
        for _ in range(min(count, len(weights))):
            weight_step(weights.pop(0))

    firsts_by = {
        "down": down_first,
        "out": lambda: first_send(1, output_away, wide_stage, output_cross),
        "gate": lambda: first_send(2, gate_away, gate_stage.at[0], gate_low),
        "up": lambda: first_send(3, up_away, up_stage, up_low),
    }
    sums_by = {
        "down": down_sum,
        "out": output_sum,
        "gate": gate_sum,
        "up": up_sum,
        "out next": output_next_sum,
        "quad": quad_send,
        "quad next": quad_pass,
    }
    for kind, *what in SCATTER_PLAN:
        if kind == "rows":
            send(*what)
        elif kind == "weights":
            weight_steps(*what)
        elif kind == "first":
            firsts_by[what[0]]()
        elif kind == "sum":
            sums_by[what[0]]()
        elif kind == "weights over":
            cross_weights()
        else:
            share_weights()
    last_sums()
    copies[0, 1].wait_recv()

    tile = 32

    def norm_rows(grp, step, grad_rows):
        place = pl.ds(pl.multiple_of(grp * row_count + step * tile, tile), tile)
        values = tokens_ref[place, :].astype(jnp.float32)
        inverse = rms_scale(values)
        normed_rows = values * inverse
        weighted = grad_rows * gain_ref[0:1, :]
        token_ref[place, :] = (
            mixed_grad[place, :]
            + inverse
            * (weighted - normed_rows * jnp.mean(weighted * normed_rows, axis=-1, keepdims=True))
        ).astype(jnp.bfloat16)

    def norm_back(step, unused):
        cut = pl.ds(pl.multiple_of(step * tile, tile), tile)
        norm_rows(here, step, grad_in[cut, :])
        norm_rows(1 - here, step, landed[0, 1, cut, :].astype(jnp.float32))
        return unused

    lax.fori_loop(0, row_count // tile, norm_back, 0)
    for one in piece_copies:
        one.wait()
    for one in quad_near:
        one.wait_recv()
    half_copy.wait_send()
    for one in [gate_low, down_high, up_high, output_low, output_high] + quad_far + quad_near:
        one.wait_send()
    for (offset, part), one in copies.items():
        if offset % 2 == 0 or (offset == 1 and part == 0):
            one.wait_send()


def scatter_heads(back, weights, tokens, mixed_grad, gain, normed, sums):
    reps, rows, columns = back.shape
    width = normed.shape[2]
    row_count = rows // 2
    half = width // 2
    own_rows = half // reps
    vmem = pl.BlockSpec(memory_space=pltpu.VMEM)
    anywhere = pl.BlockSpec(memory_space=pl.ANY)
    low, full = jnp.bfloat16, jnp.float32
    wide = (2, 2, own_rows, width)
    thin = (2, 2, own_rows, sums[0].shape[-1])
    slim = (2, 2, 2, own_rows, sums[2].shape[-1])
    return pl.pallas_call(
        scatter_kernel,
        out_shape=(
            jax.ShapeDtypeStruct((rows, width), low),
            jax.ShapeDtypeStruct((reps, own_rows, columns), low),
            jax.ShapeDtypeStruct((2, 2, own_rows, width), low),
            jax.ShapeDtypeStruct(wide[1:], full),
            jax.ShapeDtypeStruct(wide[2:], full),
        ),
        in_specs=[vmem] * 5 + [anywhere] * 9,
        out_specs=(vmem,) * 5,
        scratch_shapes=[
            pltpu.VMEM((reps // 2, 2, row_count, width), low),
            pltpu.VMEM((reps, 2, row_count, width), low),
            pltpu.VMEM((row_count, width), full),
            pltpu.VMEM((2, rows, width), low),
            pltpu.VMEM((columns, rows), low),
            pltpu.VMEM((columns, width), low),
            pltpu.VMEM((columns, width), full),
            pltpu.VMEM((columns, half), low),
            pltpu.VMEM((columns, half), low),
            pltpu.VMEM((reps, own_rows, columns), low),
            pltpu.VMEM(thin, low),
            pltpu.VMEM(thin, low),
            pltpu.VMEM(slim, low),
            pltpu.VMEM(slim, low),
            pltpu.VMEM(slim[1:], low),
            pltpu.VMEM(wide, low),
            pltpu.VMEM(wide, low),
            pltpu.VMEM(wide[1:], low),
            pltpu.VMEM(wide, low),
            pltpu.VMEM(wide, low),
            pltpu.VMEM(wide[1:], low),
            pltpu.VMEM(wide[2:], low),
            pltpu.VMEM((2,) + thin, low),
            pltpu.VMEM(slim, low),
            pltpu.VMEM(wide, low),
            pltpu.VMEM(thin[1:], low),
            pltpu.VMEM(slim[2:], low),
            pltpu.SemaphoreType.DMA((reps,)),
            pltpu.SemaphoreType.DMA((2 * reps,)),
            pltpu.SemaphoreType.DMA((2 * reps,)),
            pltpu.SemaphoreType.DMA,
            pltpu.SemaphoreType.DMA,
            pltpu.SemaphoreType.DMA((reps,)),
            pltpu.SemaphoreType.DMA((reps,)),
            pltpu.SemaphoreType.DMA((8,)),
            pltpu.SemaphoreType.DMA((14,)),
            pltpu.SemaphoreType.DMA((14,)),
        ],
        compiler_params=pltpu.CompilerParams(
            vmem_limit_bytes=62 * 1024 * 1024, collective_id=1, has_side_effects=True
        ),
        cost_estimate=pl.CostEstimate(
            flops=14 * 10**9, bytes_accessed=250 << 20, transcendentals=0
        ),
        name="scatter_heads",
    )(back, weights, tokens, mixed_grad, gain, normed, *sums)


def mlp_kernel(
    heads_ref,
    tokens_ref,
    gain_ref,
    out_rows,
    out_across,
    output_own,
    output_part,
    output_beside,
    gate_own,
    gate_met,
    gate_beside,
    up_own,
    up_other,
    down_first,
    down_second,
    down_other,
    block_ref,
    grad_ref,
    back_ref,
    gate_ref,
    late_kept,
    late_sent,
    down_kept,
    down_sent,
    output_kept,
    output_sent,
    mixed_ref,
    down_own_ref,
    down_far_landed,
    attended,
    branch_ref,
    returned,
    out_ref,
    mid_ref,
    hidden_ref,
    slope_ref,
    w_output,
    w_in,
    w_out,
    near_away,
    near_landed,
    far_away,
    far_landed,
    down_landed,
    load_sem,
    part_sem,
    send_sem,
    recv_sem,
    heads_send,
    heads_recv,
    back_send,
    back_recv,
    piece_sem,
    late_sem,
    place_sem,
    core_send,
    core_recv,
    free_sem,
):
    here, there = lax.axis_index("grp"), lax.axis_index("rep")
    across = (here, flipped(there, 4))
    sibling = (here, flipped(there, 1))
    groups, heads, row_count, _ = returned.shape
    rows, width = tokens_ref.shape
    half = width // 2
    quarter = half // 4
    own_width = w_out.shape[0]

    low = (there // 2) % 2
    up_rows = up_other.shape[0]

    def in_cut(part, first):
        cut = pl.ds(pl.multiple_of(part * up_rows, up_rows), up_rows)
        return w_in.at[1 - here, cut, pl.ds(first, own_width)]

    loads = [
        pltpu.make_async_copy(output_own, w_output.at[here], load_sem.at[0]),
        pltpu.make_async_copy(gate_own, w_in.at[here, :, pl.ds(0, own_width)], load_sem.at[1]),
        pltpu.make_async_copy(gate_met, in_cut(low, 0), load_sem.at[11]),
        pltpu.make_async_copy(gate_beside, in_cut(1 - low, 0), load_sem.at[12]),
        pltpu.make_async_copy(
            up_own, w_in.at[here, :, pl.ds(own_width, own_width)], load_sem.at[2]
        ),
        pltpu.make_async_copy(up_other, in_cut(low, own_width), load_sem.at[3]),
    ]
    own_part = own_width // 2

    early_rows = down_first.shape[0]
    late_rows = own_part - early_rows

    def down_cut(grp, first, count):
        return w_out.at[pl.ds(pl.multiple_of(grp * own_part + first, LANES), count)]

    loads += [
        pltpu.make_async_copy(down_first, down_cut(here, 0, early_rows), load_sem.at[4]),
        pltpu.make_async_copy(down_second, down_cut(here, early_rows, late_rows), load_sem.at[9]),
        pltpu.make_async_copy(down_other, down_cut(1 - here, 0, early_rows), load_sem.at[10]),
        pltpu.make_async_copy(out_rows.at[pl.ds(0, row_count)], out_ref.at[0, 0], load_sem.at[5]),
        pltpu.make_async_copy(
            out_rows.at[pl.ds(row_count, row_count)], out_ref.at[1, 0], load_sem.at[6]
        ),
        pltpu.make_async_copy(out_across.at[pl.ds(0, row_count)], out_ref.at[0, 2], load_sem.at[7]),
        pltpu.make_async_copy(
            out_across.at[pl.ds(row_count, row_count)], out_ref.at[1, 2], load_sem.at[8]
        ),
    ]
    place = there % 4
    core = there % 2

    def output_cut(part):
        return w_output.at[1 - here, pl.ds(pl.multiple_of(part * quarter, quarter), quarter)]

    output_pieces = ((output_part, place), (output_beside, flipped(place, 2)))
    rest = [
        pltpu.make_async_copy(piece, output_cut(part), part_sem.at[at])
        for at, (piece, part) in enumerate(output_pieces)
    ]
    loads = loads[:1] + rest + loads[1:]
    for one in loads:
        one.start()
    steps = [1 << place for place in range(heads.bit_length() - 1)]

    def other(crossing, offset):
        index = there
        for step in steps:
            if offset & step:
                index = flipped(index, step)
        return (1 - here if crossing else here, index)

    others = [
        (crossing, offset) for offset in range(heads) for crossing in (0, 1) if offset or crossing
    ]
    barrier = pltpu.get_barrier_semaphore()
    for key in others:
        pl.semaphore_signal(barrier, inc=1, device_id=other(*key), device_id_type=MESH_IDS)
    pl.semaphore_wait(barrier, len(others))

    facing = (1 - here, there)

    def copy(at, source, target_ref, target):
        return pltpu.make_async_remote_copy(
            src_ref=source,
            dst_ref=target_ref,
            send_sem=send_sem.at[at],
            recv_sem=recv_sem.at[at],
            device_id=target,
            device_id_type=MESH_IDS,
        )

    heads_copies, back_copies = [], []
    for at, key in enumerate(others):
        target = other(*key)
        heads_copies.append(
            pltpu.make_async_remote_copy(
                src_ref=heads_ref.at[target[0] * heads + target[1]],
                dst_ref=returned.at[here, there],
                send_sem=heads_send.at[at],
                recv_sem=heads_recv.at[at],
                device_id=target,
                device_id_type=MESH_IDS,
            )
        )
        back_copies.append(
            pltpu.make_async_remote_copy(
                src_ref=returned.at[target[0], target[1]],
                dst_ref=back_ref.at[here * heads + there],
                send_sem=back_send.at[at],
                recv_sem=back_recv.at[at],
                device_id=target,
                device_id_type=MESH_IDS,
            )
        )
    for one in heads_copies[::-1]:
        one.start()
    parts = range(groups)

    def rows_of(part):
        return pl.ds(part * row_count, row_count)

    output_near = [
        copy(at, piece, output_cut(part), sibling) for at, (piece, part) in enumerate(output_pieces)
    ]
    down_far = copy(2, down_second, down_cut(here, early_rows, late_rows), facing)
    up_beside = copy(26, up_other, in_cut(low, own_width), (here, flipped(there, 2)))
    out_near = [
        copy(3 + part, out_rows.at[rows_of(part)], out_ref.at[part, 1], sibling) for part in parts
    ]
    out_on = [
        copy(5 + part, out_across.at[rows_of(part)], out_ref.at[part, 3], sibling) for part in parts
    ]
    for one in output_near + out_near + out_on + [down_far, up_beside]:
        one.start()
    returned[here, there] = heads_ref[here * heads + there]

    early_width = gate_ref.shape[1]
    mid_near = [copy(7 + at, mid_ref.at[at, 0], mid_ref.at[at, 1], sibling) for at in parts]
    mid_far = [copy(9 + at, mid_ref.at[at, 0], mid_ref.at[at, 2], across) for at in parts]
    mid_on = [copy(11 + at, mid_ref.at[at, 2], mid_ref.at[at, 3], sibling) for at in parts]
    grad_near = {
        (side, at): copy(
            13 + 2 * side + at, near_away.at[side, at], near_landed.at[side, at], sibling
        )
        for side in range(2)
        for at in parts
    }
    grad_far = [copy(17 + at, far_away.at[at], far_landed.at[at], across) for at in parts]
    down_near = {
        (side, at): copy(
            19 + 2 * side + at, near_away.at[side, at], down_landed.at[side, at], sibling
        )
        for side in range(2)
        for at in parts
    }
    down_over = [
        copy(23 + at, down_own_ref.at[1, at], down_far_landed.at[at], across) for at in parts
    ]
    gate_cross = copy(25, w_in.at[1 - here, :, pl.ds(0, early_width)], gate_ref, facing)
    late_cut = pl.ds(early_width, 2 * own_width - early_width)
    late_block = late_kept.shape[1]

    def late_rows_of(at, bit):
        return pl.ds(pl.multiple_of((2 * at + bit) * late_block, late_block), late_block)

    up_outs = [
        pltpu.make_async_copy(
            w_in.at[at // 4, late_rows_of(at % 4, bit), late_cut], target_ref.at[at], late_sem.at[2 * at + kind]
        )
        for at in range(8)
        for kind, (target_ref, bit) in enumerate(((late_kept, low), (late_sent, 1 - low)))
    ]
    down_outs = [
        pltpu.make_async_copy(
            w_out.at[pl.ds(pl.multiple_of(grp * own_part, own_part), own_part)],
            target_ref,
            piece_sem.at[kind],
        )
        for kind, (target_ref, grp) in enumerate(((down_kept, here), (down_sent, 1 - here)))
    ]

    for one in heads_copies:
        one.wait()
    for group in range(groups):
        for head in range(heads):
            attended[
                group * row_count : (group + 1) * row_count, head * LANES : (head + 1) * LANES
            ] = returned[group, head]
    for one in loads[:3]:
        one.wait()
    for one in output_near:
        one.wait_recv()
    wide = 512

    def mix(at, unused):
        cut = pl.ds(pl.multiple_of(at * wide, wide), wide)
        mixed_ref[:, cut] = (
            tokens_ref[:, cut].astype(jnp.float32)
            + jnp.dot(attended[:, :half], w_output[0, :, cut], preferred_element_type=jnp.float32)
            + jnp.dot(attended[:, half:], w_output[1, :, cut], preferred_element_type=jnp.float32)
        )
        return unused

    lax.fori_loop(0, width // wide, mix, 0)
    tile = 32
    for part in parts:

        def norm_rows(at, unused):
            cut = pl.ds(pl.multiple_of(at * tile, tile), tile)
            values = mixed_ref[pl.ds(pl.multiple_of(part * row_count + at * tile, tile), tile), :]
            mid_ref[part, 0, cut, :] = (
                values * rms_scale(values) * gain_ref[0:1, :]
            ).astype(jnp.bfloat16)
            return unused

        lax.fori_loop(0, row_count // tile, norm_rows, 0)
        mid_far[part].start()
        mid_near[part].start()
    for one in loads[3:]:
        one.wait()
    up_beside.wait_recv()
    narrow_tile = 256
    per_half = own_part // narrow_tile
    every = (0, 1)

    def pair_rows(ref, side, part, cols):
        values = ref[part, pl.ds(2 * side, 2), :, cols]
        return values.reshape(rows, values.shape[2])

    def forward(side, part, halves):
        def columns(step, unused):
            at = jnp.where(step < per_half, halves[0] * per_half, halves[-1] * per_half - per_half)
            at = at + step
            cut = pl.ds(pl.multiple_of(at * narrow_tile, narrow_tile), narrow_tile)
            up_cut = pl.ds(pl.multiple_of(own_width + at * narrow_tile, narrow_tile), narrow_tile)
            low_rows = pair_rows(mid_ref, side, part, slice(0, half))
            high_rows = pair_rows(mid_ref, side, part, slice(half, width))

            def project(cols):
                return jnp.dot(
                    low_rows, w_in[0, :, cols], preferred_element_type=jnp.float32
                ) + jnp.dot(high_rows, w_in[1, :, cols], preferred_element_type=jnp.float32)

            gate_pre, up_pre = project(cut), project(up_cut)
            grad_hidden = contract(
                pair_rows(out_ref, side, part, slice(0, width)), w_out[cut, :], 1, 1
            )
            gate_sig = jax.nn.sigmoid(gate_pre)
            gate_silu = gate_pre * gate_sig

            def put(ref, cols, values):
                ref[part, pl.ds(2 * side, 2), :, cols] = values.astype(jnp.bfloat16).reshape(
                    2, row_count, narrow_tile
                )

            put(hidden_ref, cut, gate_silu * up_pre)
            put(
                slope_ref,
                cut,
                grad_hidden * up_pre * gate_sig * (1.0 + gate_pre * (1.0 - gate_sig)),
            )
            put(slope_ref, up_cut, grad_hidden * gate_silu)
            return unused

        lax.fori_loop(0, len(halves) * per_half, columns, 0)

    def backward(side, part):
        for at in range(2):

            def columns(step, unused):
                cut = pl.ds(pl.multiple_of(step * wide, wide), wide)
                whole = pl.ds(pl.multiple_of(at * half + step * wide, wide), wide)
                values = contract(
                    pair_rows(slope_ref, side, part, slice(0, 2 * own_width)),
                    w_in[at, cut, :],
                    1,
                    1,
                )
                near_away[side, part, :, whole] = values[row_count:].astype(jnp.bfloat16)
                if side == 0:
                    grad_ref[rows_of(part), whole] = values[:row_count]
                else:
                    far_away[part, :, whole] = values[:row_count].astype(jnp.bfloat16)
                return unused

            lax.fori_loop(0, half // wide, columns, 0)
        grad_near[side, part].start()

    def add_rows(target_ref, source_ref):
        def some_rows(at, unused):
            cut = pl.ds(pl.multiple_of(at * tile, tile), tile)
            target_ref[cut, :] = (
                target_ref[cut, :].astype(jnp.float32) + source_ref[cut, :].astype(jnp.float32)
            ).astype(target_ref.dtype)
            return unused

        lax.fori_loop(0, row_count // tile, some_rows, 0)

    def far_send(part):
        grad_near[1, part].wait_recv()
        add_rows(far_away.at[part], near_landed.at[1, part])
        grad_far[part].start()

    def down(side, part):
        grad_near[side, part].wait_send()

        def columns(step, unused):
            cut = pl.ds(pl.multiple_of(step * wide, wide), wide)
            values = jnp.dot(
                pair_rows(hidden_ref, side, part, slice(0, own_width)),
                w_out[:, cut],
                preferred_element_type=jnp.float32,
            ).astype(jnp.bfloat16)
            near_away[side, part, :, cut] = values[row_count:]
            down_own_ref[side, part, :, cut] = values[:row_count]
            return unused

        lax.fori_loop(0, width // wide, columns, 0)
        down_near[side, part].start()

    def down_meet(side, part):
        down_near[side, part].wait_recv()
        add_rows(down_own_ref.at[side, part], down_landed.at[side, part])

    for part in parts:
        mid_near[part].wait_recv()
        out_near[part].wait_recv()
        forward(0, part, (here,))
    for part in parts:
        mid_far[part].wait_recv()
        mid_on[part].start()
        if part == 0:
            down_far.wait_recv()
        else:
            forward(0, 0, (1 - here,))
            far_send(0)
        mid_on[part].wait_recv()
        out_on[part].wait_recv()
        forward(1, part, every)
        backward(1, part)
    forward(0, 1, (1 - here,))
    far_send(1)
    for part in parts:
        backward(0, part)

    def turned(values):
        flat = values.reshape(4 * rows, values.shape[3]).astype(jnp.float32)
        return jnp.transpose(flat).astype(jnp.bfloat16)

    def in_grads(at):
        def some_rows(step, unused):
            cut = pl.ds(pl.multiple_of(step * narrow_tile, narrow_tile), narrow_tile)
            source = pl.ds(pl.multiple_of(at * half + step * narrow_tile, narrow_tile), narrow_tile)
            left = turned(mid_ref[:, :, :, source])

            def columns(place_at, unused):
                cols = pl.ds(pl.multiple_of(place_at * wide, wide), wide)
                right = slope_ref[:, :, :, cols].reshape(4 * rows, wide)
                w_in[at, cut, cols] = jnp.dot(
                    left, right, preferred_element_type=jnp.float32
                ).astype(jnp.bfloat16)
                return unused

            return lax.fori_loop(0, 2 * own_width // wide, columns, unused)

        lax.fori_loop(0, half // narrow_tile, some_rows, 0)

    def down_rows(step, unused):
        cut = pl.ds(pl.multiple_of(step * narrow_tile, narrow_tile), narrow_tile)
        left = turned(hidden_ref[:, :, :, cut])

        def columns(place_at, unused):
            cols = pl.ds(pl.multiple_of(place_at * wide, wide), wide)
            right = out_ref[:, :, :, cols].reshape(4 * rows, wide)
            w_out[cut, cols] = jnp.dot(left, right, preferred_element_type=jnp.float32).astype(
                jnp.bfloat16
            )
            return unused

        return lax.fori_loop(0, width // wide, columns, unused)

    def finish(part):
        grad_near[0, part].wait_recv()
        grad_far[part].wait_recv()

        def norm_back(at, unused):
            cut = pl.ds(pl.multiple_of(at * tile, tile), tile)
            place = pl.ds(pl.multiple_of(part * row_count + at * tile, tile), tile)
            grad_mid = (
                grad_ref[place, :]
                + near_landed[0, part, cut, :].astype(jnp.float32)
                + far_landed[part, cut, :].astype(jnp.float32)
            )
            values = mixed_ref[place, :]
            inverse = rms_scale(values)
            normed = values * inverse
            weighted = grad_mid * gain_ref[0:1, :]
            grad = out_ref[part, 0, cut, :].astype(jnp.float32) + inverse * (
                weighted - normed * jnp.mean(weighted * normed, axis=-1, keepdims=True)
            )
            grad_ref[place, :] = grad
            branch_ref[place, :] = grad.astype(jnp.bfloat16)
            return unused

        lax.fori_loop(0, row_count // tile, norm_back, 0)
        for head in range(0, heads, 4):
            at = head * LANES // half
            start = head * LANES - at * half
            values = contract(
                branch_ref[rows_of(part), :],
                w_output[at, pl.ds(start, 4 * LANES), :],
                1,
                1,
                jnp.bfloat16,
            )
            for step in range(4):
                returned[part, head + step] = values[:, step * LANES : (step + 1) * LANES]
        for at, (crossing, _) in enumerate(others):

            @pl.when(jnp.where(crossing, 1 - here, here) == part)
            def _():
                back_copies[at].start()

    in_grads(1 - here)
    gate_cross.start()
    down(1, 0)
    finish(0)
    in_grads(here)
    for one in up_outs:
        one.start()
    for one in mid_near + mid_far + mid_on:
        one.wait_send()
    pl.semaphore_signal(free_sem, inc=1, device_id=sibling, device_id_type=MESH_IDS)
    finish(1)
    back_ref[here * heads + there] = returned[here, there]

    for at in range(2):

        def output_rows(step, unused):
            cut = pl.ds(pl.multiple_of(step * narrow_tile, narrow_tile), narrow_tile)
            source = pl.ds(pl.multiple_of(at * half + step * narrow_tile, narrow_tile), narrow_tile)
            left = jnp.transpose(attended[:, source].astype(jnp.float32)).astype(jnp.bfloat16)

            def columns(place_at, unused):
                cols = pl.ds(pl.multiple_of(place_at * wide, wide), wide)
                w_output[at, cut, cols] = jnp.dot(
                    left, branch_ref[:, cols], preferred_element_type=jnp.float32
                ).astype(jnp.bfloat16)
                return unused

            return lax.fori_loop(0, width // wide, columns, unused)

        lax.fori_loop(0, half // narrow_tile, output_rows, 0)

    own_rows = half // heads
    stripes = heads // 2
    pl.semaphore_wait(free_sem, 1)

    def stripe_of(at, bit):
        first = (at % stripes * 2 + bit) * own_rows
        return pl.ds(pl.multiple_of(first, own_rows), own_rows)

    def landed_at(at):
        per_slot = row_count // own_rows
        slot = at // per_slot
        return (slot // 4, slot % 4, pl.ds(at % per_slot * own_rows, own_rows))

    core_copies = []
    for at in range(2 * stripes):
        core_copies.append(
            pltpu.make_async_remote_copy(
                src_ref=w_output.at[at // stripes, stripe_of(at, 1 - core)],
                dst_ref=mid_ref.at[landed_at(at)],
                send_sem=core_send.at[at],
                recv_sem=core_recv.at[at],
                device_id=sibling,
                device_id_type=MESH_IDS,
            )
        )
        core_copies[-1].start()
    down(1, 1)
    for part in parts:
        down_meet(1, part)
        down_over[part].start()
    for part in parts:
        down(0, part)
    lax.fori_loop(0, own_width // narrow_tile, down_rows, 0)
    for one in down_outs:
        one.start()
    gate_cross.wait()

    def add_gate(at, unused):
        cut = pl.ds(pl.multiple_of(at * tile, tile), tile)
        gate_ref[cut, :] = (
            gate_ref[cut, :].astype(jnp.float32)
            + w_in[here, cut, pl.ds(0, early_width)].astype(jnp.float32)
        ).astype(jnp.bfloat16)
        return unused

    lax.fori_loop(0, half // tile, add_gate, 0)
    far_bit = (there // 4) % 2
    output_outs = []
    for at in range(2 * stripes):
        core_copies[at].wait_recv()
        own = stripe_of(at, core)
        w_output[at // stripes, own, :] = (
            w_output[at // stripes, own, :].astype(jnp.float32)
            + mid_ref[landed_at(at)].astype(jnp.float32)
        ).astype(jnp.bfloat16)
    for at in range(stripes):
        grp, high, low_bit = at // (stripes // 2), at // 2 % (stripes // 4), at % 2
        for kind, (target_ref, bit) in enumerate(
            ((output_kept, far_bit), (output_sent, 1 - far_bit))
        ):
            first = ((high * 4 + bit * 2 + low_bit) * 2 + core) * own_rows
            cut = pl.ds(pl.multiple_of(first, own_rows), own_rows)
            output_outs.append(
                pltpu.make_async_copy(
                    w_output.at[grp, cut], target_ref.at[at], place_sem.at[2 * at + kind]
                )
            )
            output_outs[-1].start()
    for part in parts:
        down_meet(0, part)
        down_over[part].wait_recv()

        def block_rows(at, unused):
            cut = pl.ds(pl.multiple_of(at * tile, tile), tile)
            place = pl.ds(pl.multiple_of(part * row_count + at * tile, tile), tile)
            block_ref[place, :] = (
                mixed_ref[place, :]
                + down_own_ref[0, part, cut, :].astype(jnp.float32)
                + down_far_landed[part, cut, :].astype(jnp.float32)
            ).astype(jnp.bfloat16)
            return unused

        lax.fori_loop(0, row_count // tile, block_rows, 0)
    for one in up_outs + down_outs + output_outs:
        one.wait()
    for one in back_copies:
        one.wait()
    for one in grad_far + out_near + out_on + down_over + [down_far, up_beside]:
        one.wait_send()
    for one in list(down_near.values()) + output_near + core_copies:
        one.wait_send()


def mlp(heads, tokens, gain, out_rows, out_across, output_parts, in_parts, down_parts):
    count, row_count, _ = heads.shape
    groups, reps = lax.axis_size("grp"), lax.axis_size("rep")
    rows, width = tokens.shape
    half = width // 2
    own_width = in_parts[0].shape[1]
    early_width = own_width // 2
    vmem = pl.BlockSpec(memory_space=pltpu.VMEM)
    anywhere = pl.BlockSpec(memory_space=pl.ANY)
    low, full = jnp.bfloat16, jnp.float32
    others = pltpu.SemaphoreType.DMA((count - 1,))
    return pl.pallas_call(
        mlp_kernel,
        out_shape=(
            jax.ShapeDtypeStruct((rows, width), low),
            jax.ShapeDtypeStruct((rows, width), full),
            jax.ShapeDtypeStruct((count, row_count, LANES), low),
            jax.ShapeDtypeStruct((half, early_width), low),
            jax.ShapeDtypeStruct((8, half // 8, 2 * own_width - early_width), low),
            jax.ShapeDtypeStruct((8, half // 8, 2 * own_width - early_width), low),
            jax.ShapeDtypeStruct((own_width // 2, width), low),
            jax.ShapeDtypeStruct((own_width // 2, width), low),
            jax.ShapeDtypeStruct((reps // 2, half // reps, width), low),
            jax.ShapeDtypeStruct((reps // 2, half // reps, width), low),
        ),
        in_specs=[vmem] * 3 + [anywhere] * 13,
        out_specs=(vmem,) * 4 + (anywhere,) * 6,
        scratch_shapes=[
            pltpu.VMEM((rows, width), full),
            pltpu.VMEM((2, 2, row_count, width), low),
            pltpu.VMEM((2, row_count, width), low),
            pltpu.VMEM((rows, width), low),
            pltpu.VMEM((rows, width), low),
            pltpu.VMEM((groups, reps, row_count, LANES), low),
            pltpu.VMEM((groups, 4, row_count, width), low),
            pltpu.VMEM((groups, 4, row_count, width), low),
            pltpu.VMEM((groups, 4, row_count, own_width), low),
            pltpu.VMEM((groups, 4, row_count, 2 * own_width), low),
            pltpu.VMEM((2, half, width), low),
            pltpu.VMEM((2, half, 2 * own_width), low),
            pltpu.VMEM((own_width, width), low),
            pltpu.VMEM((2, 2, row_count, width), low),
            pltpu.VMEM((2, 2, row_count, width), low),
            pltpu.VMEM((2, row_count, width), low),
            pltpu.VMEM((2, row_count, width), low),
            pltpu.VMEM((2, 2, row_count, width), low),
            pltpu.SemaphoreType.DMA((13,)),
            pltpu.SemaphoreType.DMA((2,)),
            pltpu.SemaphoreType.DMA((27,)),
            pltpu.SemaphoreType.DMA((27,)),
            others,
            others,
            others,
            others,
            pltpu.SemaphoreType.DMA((2,)),
            pltpu.SemaphoreType.DMA((16,)),
            pltpu.SemaphoreType.DMA((reps,)),
            pltpu.SemaphoreType.DMA((reps,)),
            pltpu.SemaphoreType.DMA((reps,)),
            pltpu.SemaphoreType.REGULAR,
        ],
        compiler_params=pltpu.CompilerParams(
            vmem_limit_bytes=62 * 1024 * 1024, collective_id=2, has_side_effects=True
        ),
        cost_estimate=pl.CostEstimate(
            flops=150 * 10**9, bytes_accessed=150 << 20, transcendentals=0
        ),
        name="mlp",
    )(heads, tokens, gain, out_rows, out_across, *output_parts, *in_parts, *down_parts)


def after_kernel(*refs):
    pass


def after(values, ahead):
    anywhere = pl.BlockSpec(memory_space=pl.ANY)
    return pl.pallas_call(
        after_kernel,
        out_shape=tuple(jax.ShapeDtypeStruct(one.shape, one.dtype) for one in values),
        in_specs=[anywhere] * (len(values) + 1),
        out_specs=(anywhere,) * len(values),
        input_output_aliases={at: at for at in range(len(values))},
        name="after",
    )(*values, ahead)


def heads_body(
    tokens,
    attn_gain,
    w_query,
    w_key,
    w_value,
    w_output,
    mlp_gain,
    w_gate,
    w_up,
    w_down,
    out_grad,
    lengths,
):
    groups, reps = lax.axis_size("grp"), lax.axis_size("rep")
    here, there = lax.axis_index("grp"), lax.axis_index("rep")
    micro_count, row_count, width = tokens.shape
    rows = micro_count * row_count
    hidden_width = w_gate.shape[1]
    own_width = hidden_width // (2 * groups)

    out_rows = out_grad.reshape(rows, width)
    (
        gathered_rows,
        qkv,
        w_heads,
        gate_own,
        gate_met,
        up_own,
        up_piece,
        down_first,
        down_second,
        output_part,
        out_own,
        gains,
    ) = gather_heads(
        tokens,
        (attn_gain, mlp_gain),
        w_query,
        w_key,
        w_value,
        w_gate,
        w_up,
        w_down,
        w_output,
        out_rows,
    )
    gain_one = gains[:, 0].reshape(width).astype(jnp.float32)
    gain_two = gains[:, 1].reshape(width).astype(jnp.float32)

    output_parts = (w_output, output_part, swap(output_part, 0, 2))
    in_parts = (gate_own, gate_met, swap(gate_met, 0, 2), up_own, swap(up_piece, 1, 0))
    down_parts = (down_first, down_second, swap(down_first, 1, 0))

    attended, out_heads, log_sum, query, key, value = attend(lengths, qkv)
    (
        block_out,
        grad_mixed,
        grad_heads,
        gate_part,
        late_kept,
        late_sent,
        down_kept,
        down_sent,
        output_kept,
        output_sent,
    ) = mlp(
        attended,
        tokens.reshape(rows, width),
        jnp.broadcast_to(gain_two[None], (8, width)),
        out_rows,
        swap(out_own, 0, 4),
        output_parts,
        in_parts,
        down_parts,
    )

    own_rows = width // (groups * reps)
    by_owner = (2, 2, 2, 2, own_rows, -1)
    gate_part = gate_part.reshape(by_owner)
    high_bit = there // 8 % 2
    gate_kept = pick(gate_part, high_bit, 0)
    sums = (
        swap(pick(gate_part, 1 - high_bit, 0), 0, 8),
        swap(late_sent, 0, 2),
        swap(down_sent, 1, 0),
        swap(output_sent, 0, 4),
    )
    back = attend_back(lengths, query, key, value, out_heads, log_sum, grad_heads)
    gate_met, late_met, down_met, output_met = after(sums, back)
    token_grad, heads_grad, quad_grad, down_grad, output_grad = scatter_heads(
        back.reshape(reps, groups * row_count, 3 * LANES),
        w_heads,
        tokens.reshape(rows, width),
        grad_mixed,
        jnp.broadcast_to(gain_one[None], (8, width)),
        gathered_rows,
        (
            gate_kept,
            gate_met,
            late_kept.reshape(by_owner),
            late_met.reshape(by_owner),
            down_kept.reshape(2, 2, 2, own_rows, width),
            down_met.reshape(2, 2, 2, own_rows, width),
            output_kept.reshape(2, 2, 2, own_rows, width),
            output_met.reshape(2, 2, 2, own_rows, width),
        ),
    )
    pieces = quad_grad.reshape(2, 2, own_rows, 2, groups, 2, 2, LANES)
    pieces = pieces.transpose(3, 2, 4, 5, 0, 6, 1, 7).reshape(2, own_rows, hidden_width)
    gate_grad, up_grad = pieces[0].astype(jnp.float32), pieces[1].astype(jnp.float32)
    heads_grad = (
        heads_grad.reshape(reps, own_rows, 3, LANES)
        .transpose(2, 1, 0, 3)
        .reshape(3, own_rows, width)
        .astype(jnp.float32)
    )

    def own_part(value):
        return lax.dynamic_slice_in_dim(value, there * own_rows, own_rows, axis=0).astype(
            jnp.float32
        )

    attn_gain_grad = (
        jnp.sum(own_part(w_query) * heads_grad[0], axis=1)
        + jnp.sum(own_part(w_key) * heads_grad[1], axis=1)
        + jnp.sum(own_part(w_value) * heads_grad[2], axis=1)
    ) / own_part(attn_gain)
    mlp_gain_grad = (
        jnp.sum(own_part(w_gate) * gate_grad, axis=1) + jnp.sum(own_part(w_up) * up_grad, axis=1)
    ) / own_part(mlp_gain)
    block_shape = tokens.shape
    return (
        block_out.reshape(block_shape),
        token_grad.reshape(block_shape),
        attn_gain_grad,
        heads_grad[0],
        heads_grad[1],
        heads_grad[2],
        output_grad,
        mlp_gain_grad,
        gate_grad,
        up_grad,
        down_grad.reshape(2 * own_rows, width),
    )


def pick_body(*arrays):
    tokens = arrays[0]
    groups, reps = lax.axis_size("grp"), lax.axis_size("rep")
    fits = (
        groups == 2
        and tokens.shape[0] == groups
        and tokens.shape[2] == reps * LANES
        and reps == 16
        and reps & (reps - 1) == 0
        and tokens.shape[1] % UNIT_PAIR == 0
        and arrays[7].shape[1] == groups * reps * LANES
    )
    return heads_body(*arrays) if fits else ring_body(*arrays)


def solution(mesh):
    in_specs = (
        P(None, ("grp", "rep"), None),
        P("grp"),
        P("grp", None),
        P("grp", None),
        P("grp", None),
        P("grp", None),
        P("grp"),
        P("grp", None),
        P("grp", None),
        P("grp", None),
        P(None, ("grp", "rep"), None),
        P(),
    )
    out_specs = (
        P(None, ("grp", "rep"), None),
        P(None, ("grp", "rep"), None),
        P(("grp", "rep")),
        P(("grp", "rep"), None),
        P(("grp", "rep"), None),
        P(("grp", "rep"), None),
        P(("grp", "rep"), None),
        P(("grp", "rep")),
        P(("grp", "rep"), None),
        P(("grp", "rep"), None),
        P(("grp", "rep"), None),
    )
    return jax.shard_map(pick_body, mesh=mesh, in_specs=in_specs, out_specs=out_specs, check_vma=False)
```

```python
import functools
import math

import jax
import jax.numpy as jnp
from jax import lax
from jax.experimental import pallas as pl
from jax.experimental.pallas import tpu as pltpu
from jax.sharding import PartitionSpec as P

HD = 64
WINDOW = 2048


epsilon = 1e-05
rope_base = 10000.0
masked_score = -1e30
BOTH = ("grp", "rep")
LANES = 128
UNIT_BLOCK = 8
UNIT_PAIR = 16
KERNEL_VMEM = 56 * 1024 * 1024
SCATTER_REFS = 18


def from_behind(value, axis, steps):
    count = lax.axis_size(axis)
    first, last = (max(0, -steps), min(count, count - steps))
    return lax.ppermute(value, axis, [(source, source + steps) for source in range(first, last)])


def rms_scale(values):
    return lax.rsqrt(jnp.mean(values * values, axis=-1, keepdims=True) + epsilon)


def norm_backward(values, gain_full, grad_normed):
    inverse = rms_scale(values)
    normed = values * inverse
    gain_grad = jnp.sum(grad_normed * normed, axis=0)
    weighted = grad_normed * gain_full
    return (
        inverse * (weighted - normed * jnp.mean(weighted * normed, axis=-1, keepdims=True)),
        gain_grad,
    )


def rotary(values, cosine, sine_table):
    half_width = values.shape[-1] // 2
    first_half = values[..., :half_width]
    second_half = values[..., half_width:]
    return jnp.concatenate(
        [
            first_half * cosine - second_half * sine_table,
            second_half * cosine + first_half * sine_table,
        ],
        axis=-1,
    )


def pick_rows(rows_block, row_ids):
    return jnp.take(rows_block, row_ids, axis=0)


def take_rows(values, row_ids):
    return jax.vmap(pick_rows)(values, row_ids)


def gather_attn(attn_gain, w_query, w_key, w_value, w_output):
    return (
        lax.all_gather(attn_gain, "grp", axis=0, tiled=True),
        lax.all_gather(w_query, "grp", axis=0, tiled=True),
        lax.all_gather(w_key, "grp", axis=0, tiled=True),
        lax.all_gather(w_value, "grp", axis=0, tiled=True),
        lax.all_gather(w_output, "grp", axis=0, tiled=True),
    )


def gather_mlp(mlp_gain, w_gate, w_up, w_down):
    return (
        lax.all_gather(mlp_gain, "grp", axis=0, tiled=True),
        lax.all_gather(w_gate, "grp", axis=0, tiled=True),
        lax.all_gather(w_up, "grp", axis=0, tiled=True),
        lax.all_gather(w_down, "grp", axis=0, tiled=True),
    )


def reduce_attn(gain_grad, query_grad, key_grad, value_grad, output_grad):
    return (
        lax.psum_scatter(gain_grad, ("grp", "rep"), scatter_dimension=0, tiled=True),
        lax.psum_scatter(query_grad, ("grp", "rep"), scatter_dimension=0, tiled=True),
        lax.psum_scatter(key_grad, ("grp", "rep"), scatter_dimension=0, tiled=True),
        lax.psum_scatter(value_grad, ("grp", "rep"), scatter_dimension=0, tiled=True),
        lax.psum_scatter(output_grad, ("grp", "rep"), scatter_dimension=0, tiled=True),
    )


def reduce_mlp(gain_grad, gate_grad, up_grad, down_grad):
    return (
        lax.psum_scatter(gain_grad, ("grp", "rep"), scatter_dimension=0, tiled=True),
        lax.psum_scatter(gate_grad, ("grp", "rep"), scatter_dimension=0, tiled=True),
        lax.psum_scatter(up_grad, ("grp", "rep"), scatter_dimension=0, tiled=True),
        lax.psum_scatter(down_grad, ("grp", "rep"), scatter_dimension=0, tiled=True),
    )


def pass_on(carried, unused):
    arrived = from_behind(carried, ("grp", "rep"), 1)
    return (arrived, arrived)


def pass_back(running, portion):
    arrived = from_behind(running.astype(jnp.bfloat16), ("grp", "rep"), -1).astype(running.dtype)
    return (arrived + portion, None)


def ring_body(
    tokens,
    attn_gain,
    w_query,
    w_key,
    w_value,
    w_output,
    mlp_gain,
    w_gate,
    w_up,
    w_down,
    out_grad,
    lengths,
):
    devices = lax.axis_size(("grp", "rep"))
    rank_here = lax.axis_index(("grp", "rep"))
    micro_count, row_count, model_width = tokens.shape
    per_dev = row_count // devices
    head_count = model_width // HD
    reach_count = (WINDOW + row_count - 2) // row_count
    head_group = math.gcd(head_count, 4)
    group_count = head_count // head_group
    score_scale = 1.0 / math.sqrt(HD)
    unit_ids = jnp.arange(row_count, dtype=jnp.int32)
    seq_ends = jnp.cumsum(lengths, axis=1)
    starts = seq_ends - lengths
    seq_order = jnp.arange(lengths.shape[1], dtype=jnp.int32)
    earlier = seq_order[None, :] < seq_order[:, None]
    dealt_start = jnp.sum(jnp.where(earlier[None], lengths[:, None, :], 0), axis=2)
    seq_of = jnp.sum((seq_ends[:, None, :] <= unit_ids[None, :, None]).astype(jnp.int32), axis=2)
    seq_dealt = jnp.take_along_axis(dealt_start, seq_of, axis=1)
    unit_of = seq_dealt + unit_ids[None, :] - jnp.take_along_axis(starts, seq_of, axis=1)
    micro_ids = jnp.arange(micro_count, dtype=jnp.int32)[:, None]
    source_unit = (
        jnp.zeros((micro_count, row_count), jnp.int32)
        .at[micro_ids, unit_of]
        .set(jnp.broadcast_to(unit_ids[None, :], unit_of.shape))
    )
    unit_begin = (
        jnp.zeros((micro_count, row_count), jnp.int32).at[micro_ids, unit_of].set(seq_dealt)
    )
    local_ids = jnp.arange(row_count, dtype=jnp.int32)
    local_step = local_ids % per_dev
    local_source = local_ids // per_dev
    distance = jnp.arange(reach_count + 1, dtype=jnp.int32)
    owner_dev = rank_here - distance
    owner_ok = owner_dev >= 0
    owner_unit = jnp.maximum(owner_dev, 0)[:, None] * per_dev + local_step[None, :]
    key_begin = unit_begin[:, owner_unit]
    key_pos = (owner_unit[None] - key_begin) * devices + local_source[None, None, :]
    query_begin = key_begin[:, 0]
    query_pos = key_pos[:, 0]
    allowed = (
        owner_ok[None, None, :, None]
        & (query_begin[:, :, None, None] == key_begin[:, None, :, :])
        & (key_pos[:, None, :, :] <= query_pos[:, :, None, None])
        & (query_pos[:, :, None, None] - key_pos[:, None, :, :] < WINDOW)
    )
    mask_full = allowed[:, None]
    half_width = HD // 2
    frequency = jnp.power(rope_base, -2.0 * jnp.arange(half_width, dtype=jnp.float32) / HD)
    angles = query_pos.astype(jnp.float32)[:, :, None] * frequency[None, None, :]
    cosine = jnp.cos(angles)[:, :, None, :]
    sine_table = jnp.sin(angles)[:, :, None, :]
    head_shape = (micro_count, row_count, head_count, HD)
    block_shape = (micro_count, row_count, model_width)
    gathered = gather_attn(attn_gain, w_query, w_key, w_value, w_output)
    gain_one = gathered[0].astype(jnp.float32)
    inputs = tokens.astype(jnp.float32).reshape(micro_count * row_count, model_width)
    normed_in = (inputs * rms_scale(inputs) * gain_one).astype(jnp.bfloat16)
    queries = jnp.dot(normed_in, gathered[1], preferred_element_type=jnp.float32).astype(
        jnp.bfloat16
    )
    keys_in = jnp.dot(normed_in, gathered[2], preferred_element_type=jnp.float32).astype(
        jnp.bfloat16
    )
    values_in = jnp.dot(normed_in, gathered[3], preferred_element_type=jnp.float32).astype(
        jnp.bfloat16
    )
    dealt = (
        lax.all_to_all(
            take_rows(queries.reshape(block_shape), source_unit),
            ("grp", "rep"),
            split_axis=1,
            concat_axis=1,
            tiled=True,
        ),
        lax.all_to_all(
            take_rows(keys_in.reshape(block_shape), source_unit),
            ("grp", "rep"),
            split_axis=1,
            concat_axis=1,
            tiled=True,
        ),
        lax.all_to_all(
            take_rows(values_in.reshape(block_shape), source_unit),
            ("grp", "rep"),
            split_axis=1,
            concat_axis=1,
            tiled=True,
        ),
    )
    rot_q = rotary(dealt[0].reshape(head_shape).astype(jnp.float32), cosine, sine_table).astype(
        jnp.bfloat16
    )
    rot_k = rotary(dealt[1].reshape(head_shape).astype(jnp.float32), cosine, sine_table).astype(
        jnp.bfloat16
    )
    own_pair = jnp.stack([rot_k.reshape(block_shape), dealt[2]], axis=0)
    last_pair, farther = lax.scan(pass_on, own_pair, None, length=reach_count)
    context = jnp.concatenate([own_pair[None], farther], axis=0).reshape(
        reach_count + 1, 2, micro_count, row_count, head_count, HD
    )

    def group_scores(query_part, pair_part):
        scores = (
            jnp.einsum(
                "mqge,dmkge->mgqdk", query_part, pair_part[:, 0], preferred_element_type=jnp.float32
            )
            * score_scale
        )
        return jnp.where(mask_full, scores, masked_score)

    def forward_group(group_index, carried):
        attended_all, log_all = carried
        head_start = group_index * head_group
        query_part = lax.dynamic_slice_in_dim(rot_q, head_start, head_group, axis=2)
        pair_part = lax.dynamic_slice_in_dim(context, head_start, head_group, axis=4)
        scores = group_scores(query_part, pair_part)
        row_max = jnp.max(scores, axis=(3, 4), keepdims=True)
        weights_exp = jnp.exp(scores - row_max)
        row_sum = jnp.sum(weights_exp, axis=(3, 4), keepdims=True)
        soft_probs = (weights_exp / row_sum).astype(jnp.bfloat16)
        attended = jnp.einsum(
            "mgqdk,dmkge->mqge", soft_probs, pair_part[:, 1], preferred_element_type=jnp.float32
        ).astype(jnp.bfloat16)
        attended_all = lax.dynamic_update_slice_in_dim(attended_all, attended, head_start, axis=2)
        log_all = lax.dynamic_update_slice_in_dim(
            log_all, row_max + jnp.log(row_sum), head_start, axis=1
        )
        return (attended_all, log_all)

    attended_heads, log_sum = lax.fori_loop(
        0,
        group_count,
        forward_group,
        (
            jnp.zeros(head_shape, jnp.bfloat16),
            jnp.zeros((micro_count, head_count, row_count, 1, 1), jnp.float32),
        ),
    )
    returned = lax.all_to_all(
        attended_heads.reshape(block_shape), ("grp", "rep"), split_axis=1, concat_axis=1, tiled=True
    )
    attn_rows = take_rows(returned, unit_of).reshape(micro_count * row_count, model_width)
    mixed = inputs + jnp.dot(attn_rows, gathered[4], preferred_element_type=jnp.float32)
    mlp_set = gather_mlp(mlp_gain, w_gate, w_up, w_down)
    gain_two = mlp_set[0].astype(jnp.float32)
    normed_mid = (mixed * rms_scale(mixed) * gain_two).astype(jnp.bfloat16)
    gate_pre = jnp.dot(normed_mid, mlp_set[1], preferred_element_type=jnp.float32)
    up_pre = jnp.dot(normed_mid, mlp_set[2], preferred_element_type=jnp.float32)
    gate_sig = jax.nn.sigmoid(gate_pre)
    gate_silu = gate_pre * gate_sig
    hidden = (gate_silu * up_pre).astype(jnp.bfloat16)
    block_out = (mixed + jnp.dot(hidden, mlp_set[3], preferred_element_type=jnp.float32)).astype(
        jnp.bfloat16
    )
    mlp_set = gather_mlp(mlp_gain, w_gate, w_up, w_down)
    out_rows = out_grad.reshape(micro_count * row_count, model_width)
    down_grad = jnp.einsum("tf,td->fd", hidden, out_rows, preferred_element_type=jnp.float32)
    grad_hidden = jnp.einsum("td,fd->tf", out_rows, mlp_set[3], preferred_element_type=jnp.float32)
    grad_gate = (grad_hidden * up_pre * gate_sig * (1.0 + gate_pre * (1.0 - gate_sig))).astype(
        jnp.bfloat16
    )
    grad_up = (grad_hidden * gate_silu).astype(jnp.bfloat16)
    gate_grad = jnp.einsum("td,tf->df", normed_mid, grad_gate, preferred_element_type=jnp.float32)
    up_grad = jnp.einsum("td,tf->df", normed_mid, grad_up, preferred_element_type=jnp.float32)
    grad_mid = jnp.einsum(
        "tf,df->td", grad_gate, mlp_set[1], preferred_element_type=jnp.float32
    ) + jnp.einsum("tf,df->td", grad_up, mlp_set[2], preferred_element_type=jnp.float32)
    grad_norm_mid, mlp_gain_grad = norm_backward(mixed, gain_two, grad_mid)
    grad_mixed = out_rows.astype(jnp.float32) + grad_norm_mid
    mlp_sums = reduce_mlp(mlp_gain_grad, gate_grad, up_grad, down_grad)
    gathered = gather_attn(attn_gain, w_query, w_key, w_value, w_output)
    grad_branch = grad_mixed.astype(jnp.bfloat16)
    output_grad = jnp.einsum(
        "td,te->de", attn_rows, grad_branch, preferred_element_type=jnp.float32
    )
    grad_att = jnp.einsum(
        "te,de->td", grad_branch, gathered[4], preferred_element_type=jnp.float32
    ).astype(jnp.bfloat16)
    grad_dealt = lax.all_to_all(
        take_rows(grad_att.reshape(block_shape), source_unit),
        ("grp", "rep"),
        split_axis=1,
        concat_axis=1,
        tiled=True,
    )
    grad_heads = grad_dealt.reshape(head_shape)

    def backward_group(group_index, carried):
        query_total, pair_total = carried
        head_start = group_index * head_group
        query_part = lax.dynamic_slice_in_dim(rot_q, head_start, head_group, axis=2)
        grad_part = lax.dynamic_slice_in_dim(grad_heads, head_start, head_group, axis=2)
        pair_part = lax.dynamic_slice_in_dim(context, head_start, head_group, axis=4)
        log_part = lax.dynamic_slice_in_dim(log_sum, head_start, head_group, axis=1)
        scores = group_scores(query_part, pair_part)
        soft_probs = jnp.exp(scores - log_part)
        grad_probs = jnp.einsum(
            "mqge,dmkge->mgqdk", grad_part, pair_part[:, 1], preferred_element_type=jnp.float32
        )
        inner_sum = jnp.sum(soft_probs * grad_probs, axis=(3, 4), keepdims=True)
        grad_scores = (soft_probs * (grad_probs - inner_sum)).astype(jnp.bfloat16)
        query_piece = (
            jnp.einsum(
                "mgqdk,dmkge->mqge",
                grad_scores,
                pair_part[:, 0],
                preferred_element_type=jnp.float32,
            )
            * score_scale
        )
        key_part = (
            jnp.einsum(
                "mgqdk,mqge->dmkge", grad_scores, query_part, preferred_element_type=jnp.float32
            )
            * score_scale
        )
        value_part = jnp.einsum(
            "mgqdk,mqge->dmkge",
            soft_probs.astype(jnp.bfloat16),
            grad_part,
            preferred_element_type=jnp.float32,
        )
        query_total = lax.dynamic_update_slice_in_dim(query_total, query_piece, head_start, axis=2)
        pair_total = lax.dynamic_update_slice_in_dim(
            pair_total, jnp.stack([key_part, value_part], axis=1), head_start, axis=4
        )
        return (query_total, pair_total)

    query_total, pair_total = lax.fori_loop(
        0,
        group_count,
        backward_group,
        (
            jnp.zeros(head_shape, jnp.float32),
            jnp.zeros((reach_count + 1, 2) + head_shape, jnp.float32),
        ),
    )
    partials = pair_total.reshape(reach_count + 1, 2, micro_count, row_count, model_width)
    own_total, unused_out = lax.scan(
        pass_back, partials[reach_count], partials[:reach_count], reverse=True
    )
    query_back = rotary(query_total, cosine, -sine_table).astype(jnp.bfloat16)
    key_back = rotary(own_total[0].reshape(head_shape), cosine, -sine_table).astype(jnp.bfloat16)
    value_back = own_total[1].astype(jnp.bfloat16)
    grad_back = (
        lax.all_to_all(
            query_back.reshape(block_shape), ("grp", "rep"), split_axis=1, concat_axis=1, tiled=True
        ),
        lax.all_to_all(
            key_back.reshape(block_shape), ("grp", "rep"), split_axis=1, concat_axis=1, tiled=True
        ),
        lax.all_to_all(value_back, ("grp", "rep"), split_axis=1, concat_axis=1, tiled=True),
    )
    query_rows = take_rows(grad_back[0], unit_of).reshape(micro_count * row_count, model_width)
    key_rows = take_rows(grad_back[1], unit_of).reshape(micro_count * row_count, model_width)
    value_rows = take_rows(grad_back[2], unit_of).reshape(micro_count * row_count, model_width)
    query_grad = jnp.einsum("td,te->de", normed_in, query_rows, preferred_element_type=jnp.float32)
    key_grad = jnp.einsum("td,te->de", normed_in, key_rows, preferred_element_type=jnp.float32)
    value_grad = jnp.einsum("td,te->de", normed_in, value_rows, preferred_element_type=jnp.float32)
    grad_in = jnp.einsum("te,de->td", query_rows, gathered[1], preferred_element_type=jnp.float32)
    grad_in = grad_in + jnp.einsum(
        "te,de->td", key_rows, gathered[2], preferred_element_type=jnp.float32
    )
    grad_in = grad_in + jnp.einsum(
        "te,de->td", value_rows, gathered[3], preferred_element_type=jnp.float32
    )
    grad_norm_in, attn_gain_grad = norm_backward(inputs, gain_one, grad_in)
    token_grad = (grad_mixed + grad_norm_in).astype(jnp.bfloat16)
    attn_sums = reduce_attn(attn_gain_grad, query_grad, key_grad, value_grad, output_grad)
    return (
        block_out.reshape(block_shape),
        token_grad.reshape(block_shape),
        attn_sums[0],
        attn_sums[1],
        attn_sums[2],
        attn_sums[3],
        attn_sums[4],
        mlp_sums[0],
        mlp_sums[1],
        mlp_sums[2],
        mlp_sums[3],
    )


def contract(left_side, right_side, left_dim, right_dim, kind=jnp.float32):
    return lax.dot_general(
        left_side,
        right_side,
        (((left_dim,), (right_dim,)), ((), ())),
        preferred_element_type=jnp.float32,
    ).astype(kind)


def swap_halves(values):
    lane = lax.broadcasted_iota(jnp.int32, values.shape, 1)
    ahead = pltpu.roll(values, LANES - HD // 2, 1)
    behind = pltpu.roll(values, HD // 2, 1)
    return jnp.where(lane % HD < HD // 2, -ahead, behind)


def fill_tables(lengths_ref, begin_at, cos_unit, sin_unit, cos_part, sin_part):
    parts, units = cos_part.shape[0], cos_unit.shape[0]
    here = lax.axis_index("grp")

    def frequency(shape):
        lane = lax.broadcasted_iota(jnp.int32, shape, 1) % (HD // 2)
        return jnp.exp(lane.astype(jnp.float32) * (-2.0 * math.log(rope_base) / HD))

    unit = lax.broadcasted_iota(jnp.int32, (units, LANES), 0)
    begin = jnp.zeros((units, LANES), jnp.int32)
    end = 0
    for seq in range(lengths_ref.shape[1]):
        end = end + lengths_ref[here, seq]
        begin = jnp.where(unit >= end, end, begin)
    begin_at[...] = begin
    angle = ((unit - begin) * parts).astype(jnp.float32) * frequency((units, LANES))
    cos_unit[...] = jnp.cos(angle)
    sin_unit[...] = jnp.sin(angle)
    part = lax.broadcasted_iota(jnp.int32, (parts, LANES), 0).astype(jnp.float32)
    angle = part * frequency((parts, LANES))
    cos_part[...] = jnp.cos(angle)
    sin_part[...] = jnp.sin(angle)


def begin_of(lengths_ref, unit):
    here = lax.axis_index("grp")
    begin, end = 0, 0
    for seq in range(lengths_ref.shape[1]):
        end = end + lengths_ref[here, seq]
        begin = jnp.where(unit >= end, end, begin)
    return begin


def key_range(lengths_ref, at, parts, block):
    first_unit = at * UNIT_BLOCK
    last_unit = first_unit + UNIT_BLOCK - 1
    least = jnp.maximum(begin_of(lengths_ref, first_unit) * parts, at * block - (WINDOW - 1))
    most = jnp.maximum(
        begin_of(lengths_ref, last_unit) * parts, (at + 1) * block - 1 - (WINDOW - 1)
    )
    first = jnp.maximum(least, 0) // block
    return first, jnp.minimum(jnp.maximum((most + block - 1) // block, first), at)


def low_of(begin_at, at, parts):
    begin = begin_at[pl.ds(pl.multiple_of(at * UNIT_BLOCK, UNIT_BLOCK), UNIT_BLOCK), :] * parts
    shape = (parts, UNIT_BLOCK, LANES)
    part = lax.broadcasted_iota(jnp.int32, shape, 0)
    unit = lax.broadcasted_iota(jnp.int32, shape, 1) + at * UNIT_BLOCK
    low = jnp.maximum(begin[None], unit * parts + part - (WINDOW - 1))
    return low.reshape(parts * UNIT_BLOCK, LANES).astype(jnp.float32)


def slot_of(part):
    groups, reps = lax.axis_size("grp"), lax.axis_size("rep")
    offset = (part % reps) ^ lax.axis_index("rep")
    return offset * groups + ((part // reps) ^ lax.axis_index("grp"))


def pair_angles(unit_at, cos_unit, sin_unit, cos_part, sin_part):
    unit_cos = cos_unit[pl.ds(unit_at, UNIT_PAIR), :][None]
    unit_sin = sin_unit[pl.ds(unit_at, UNIT_PAIR), :][None]
    part_cos = cos_part[...][:, None, :]
    part_sin = sin_part[...][:, None, :]
    cosine = unit_cos * part_cos - unit_sin * part_sin
    sine = unit_sin * part_cos + unit_cos * part_sin
    return cosine, sine


def key_offsets(block):
    row = lax.broadcasted_iota(jnp.int32, (block, block), 0)
    return (row % UNIT_BLOCK) * (block // UNIT_BLOCK) + row // UNIT_BLOCK


def query_offsets(block):
    column = lax.broadcasted_iota(jnp.int32, (block, block), 1)
    return (column % UNIT_BLOCK) * (block // UNIT_BLOCK) + column // UNIT_BLOCK


def attend_kernel(
    lengths_ref,
    qkv_ref,
    att_ref,
    out_ref,
    log_ref,
    query_ref,
    key_ref,
    value_ref,
    query_heads,
    key_t,
    tops,
    sums,
    totals,
    lows,
    causal_at,
    key_at,
    begin_at,
    cos_unit,
    sin_unit,
    cos_part,
    sin_part,
):
    parts, units, _ = qkv_ref.shape
    block = parts * UNIT_BLOCK
    pairs = units // UNIT_PAIR
    halves = UNIT_PAIR // UNIT_BLOCK
    wide = block // LANES
    fill_tables(lengths_ref, begin_at, cos_unit, sin_unit, cos_part, sin_part)
    key_at[...] = query_offsets(block).astype(jnp.float32)
    causal_at[...] = jnp.where(query_offsets(block) <= key_offsets(block), 0.0, masked_score)

    def lay_out(pair, unused):
        unit_at = pl.multiple_of(pair * UNIT_PAIR, UNIT_PAIR)
        rows = jnp.stack(
            [qkv_ref[slot_of(part), pl.ds(unit_at, UNIT_PAIR), :] for part in range(parts)]
        )
        cosine, sine = pair_angles(unit_at, cos_unit, sin_unit, cos_part, sin_part)
        flat = (parts * UNIT_PAIR, LANES)
        cosine = cosine.reshape(flat)
        sine = sine.reshape(flat)

        def rotated(values):
            values = values.astype(jnp.float32).reshape(flat)
            turned = values * cosine + swap_halves(values) * sine
            return turned.reshape(parts, UNIT_PAIR, LANES)

        query = rotated(rows[:, :, :LANES]) * (1.0 / math.sqrt(HD))
        key = rotated(rows[:, :, LANES : 2 * LANES])
        value = rows[:, :, 2 * LANES :].astype(jnp.float32)
        for half in range(halves):
            at = pair * halves + half
            cut = slice(half * UNIT_BLOCK, (half + 1) * UNIT_BLOCK)
            query_rows = query[:, cut].reshape(block, LANES)
            key_rows = key[:, cut].reshape(block, LANES)
            query_ref[at] = query_rows.astype(jnp.bfloat16)
            key_ref[at] = key_rows.astype(jnp.bfloat16)
            value_ref[at] = value[:, cut].reshape(block, LANES).astype(jnp.bfloat16)
            lane = lax.broadcasted_iota(jnp.int32, query_rows.shape, 1)
            query_heads[at, 0] = jnp.where(lane < HD, query_rows, 0.0).astype(jnp.bfloat16)
            query_heads[at, 1] = jnp.where(lane < HD, 0.0, query_rows).astype(jnp.bfloat16)
            key_t[at] = jnp.transpose(key_rows).astype(jnp.bfloat16)
        return unused

    lax.fori_loop(0, pairs, lay_out, 0)

    def query_pair(pair, unused):
        ids = [pair * halves + half for half in range(halves)]
        for half, at in enumerate(ids):
            lows[half] = low_of(begin_at, at, parts)
        first, _ = key_range(lengths_ref, ids[0], parts, block)
        _, plain = key_range(lengths_ref, ids[-1], parts, block)
        plain = jnp.minimum(plain, ids[0])

        def wider(value):
            return jnp.concatenate([value] * wide, axis=1)

        def scores_of(half, head, key_block, causal, bounded):
            scores = jnp.dot(
                query_heads[ids[half], head], key_t[key_block], preferred_element_type=jnp.float32
            )
            if causal:
                scores = scores + causal_at[...]
            if bounded:
                bound = wider(lows[half] - (key_block * block).astype(jnp.float32))
                scores = jnp.where(key_at[...] >= bound, scores, masked_score)
            return scores

        def folded(combine, values):
            result = values[:, :LANES]
            for at in range(1, wide):
                result = combine(result, values[:, at * LANES : (at + 1) * LANES])
            return result

        def top_step(half, head, key_block, causal, bounded, fresh):
            high = folded(jnp.maximum, scores_of(half, head, key_block, causal, bounded))
            tops[half, head] = high if fresh else jnp.maximum(tops[half, head], high)

        def sum_step(half, head, key_block, causal, bounded, fresh):
            scores = scores_of(half, head, key_block, causal, bounded)
            weights = jnp.exp(scores - wider(tops[half, head]))
            part = folded(jnp.add, weights)
            product = jnp.dot(
                weights.astype(jnp.bfloat16),
                value_ref[key_block],
                preferred_element_type=jnp.float32,
            )
            sums[half, head] = part if fresh else sums[half, head] + part
            totals[half, head] = product if fresh else totals[half, head] + product

        def over_keys(step):
            for half, at in enumerate(ids):
                for head in range(2):
                    step(half, head, at, True, True, True)
                    for earlier in ids[:half]:
                        step(half, head, earlier, False, True, False)

            def all_steps(bounded):
                def go(key_block, unused):
                    for half in range(halves):
                        for head in range(2):
                            step(half, head, key_block, False, bounded, False)
                    return unused

                return go

            lax.fori_loop(first, plain, all_steps(True), 0)
            lax.fori_loop(plain, ids[0], all_steps(False), 0)

        over_keys(top_step)
        for half in range(halves):
            for head in range(2):
                high = jnp.max(tops[half, head], axis=1, keepdims=True)
                tops[half, head] = jnp.broadcast_to(high, (block, LANES))
        over_keys(sum_step)
        done = []
        for half, at in enumerate(ids):
            rows = []
            for head in range(2):
                total = jnp.broadcast_to(
                    jnp.sum(sums[half, head], axis=1, keepdims=True), (block, LANES)
                )
                rows.append(totals[half, head] / total)
                log = jnp.transpose(tops[half, head] + jnp.log(total))
                log_ref[at, head : head + 1, :] = log[0:1]
            lane = lax.broadcasted_iota(jnp.int32, (block, LANES), 1)
            both = jnp.where(lane < HD, rows[0], rows[1])
            out_ref[at] = jnp.transpose(both)
            done.append(both.reshape(parts, UNIT_BLOCK, LANES))
        unit_at = pl.multiple_of(pair * UNIT_PAIR, UNIT_PAIR)
        att_ref[:, pl.ds(unit_at, UNIT_PAIR), :] = jnp.concatenate(done, axis=1).astype(
            jnp.bfloat16
        )
        return unused

    lax.fori_loop(0, pairs, query_pair, 0)


def attend_back_kernel(
    lengths_ref,
    query_ref,
    key_ref,
    value_ref,
    out_ref,
    log_ref,
    grad_ref,
    back_ref,
    key_t,
    key_total,
    value_total,
    key_at,
    causal_at,
    begin_at,
    cos_unit,
    sin_unit,
    cos_part,
    sin_part,
):
    parts, units, _ = grad_ref.shape
    block = parts * UNIT_BLOCK
    pairs = units // UNIT_PAIR
    halves = UNIT_PAIR // UNIT_BLOCK
    fill_tables(lengths_ref, begin_at, cos_unit, sin_unit, cos_part, sin_part)
    key_at[...] = key_offsets(block).astype(jnp.float32)
    causal_at[...] = jnp.where(key_offsets(block) <= query_offsets(block), 0.0, masked_score)

    def lay_out(at, unused):
        key_t[at] = jnp.transpose(key_ref[at].astype(jnp.float32)).astype(jnp.bfloat16)
        key_total[at] = jnp.zeros((block, LANES), jnp.float32)
        value_total[at] = jnp.zeros((block, LANES), jnp.float32)
        return unused

    lax.fori_loop(0, pairs * halves, lay_out, 0)

    def split_heads(values, axis):
        place = lax.broadcasted_iota(jnp.int32, values.shape, axis)
        zero = jnp.zeros_like(values)
        return [
            jnp.where(place < HD, values, zero).astype(jnp.bfloat16),
            jnp.where(place < HD, zero, values).astype(jnp.bfloat16),
        ]

    def prepare(at, grad_rows):
        query_rows = query_ref[at].astype(jnp.float32)
        grad_turned = jnp.transpose(grad_rows)
        product = grad_turned * out_ref[at]
        return dict(
            low=jnp.transpose(low_of(begin_at, at, parts))[0:1],
            query=jnp.concatenate(split_heads(query_rows, 1), axis=0),
            grad=jnp.concatenate(split_heads(grad_rows, 1), axis=0),
            query_t=split_heads(jnp.transpose(query_rows), 0),
            grad_t=split_heads(grad_turned, 0),
            inner=[
                jnp.sum(product[head * HD : (head + 1) * HD], axis=0, keepdims=True)
                for head in range(2)
            ],
            logs=[log_ref[at, head : head + 1, :] for head in range(2)],
        )

    def step(held, key_block, carried, causal, bounded):
        probs, slopes, new = [], [], []
        for head in range(2):
            scores = jnp.dot(
                key_ref[key_block], held["query_t"][head], preferred_element_type=jnp.float32
            )
            if causal:
                scores = scores + causal_at[...]
            if bounded:
                scores = jnp.where(
                    key_at[...] >= held["low"] - (key_block * block).astype(jnp.float32), scores, masked_score
                )
            soft = jnp.exp(scores - held["logs"][head])
            grad_probs = jnp.dot(
                value_ref[key_block], held["grad_t"][head], preferred_element_type=jnp.float32
            )
            slope = (soft * (grad_probs - held["inner"][head])).astype(jnp.bfloat16)
            probs.append(soft.astype(jnp.bfloat16))
            slopes.append(slope)
            new.append(
                carried[head]
                + jnp.dot(
                    key_t[key_block, pl.ds(head * HD, HD), :],
                    slope,
                    preferred_element_type=jnp.float32,
                )
            )
        return tuple(new), probs, slopes

    def add_key(key_block, held, probs, slopes):
        value_total[key_block] += jnp.dot(
            jnp.concatenate(probs, axis=1),
            jnp.concatenate([one["grad"] for one in held], axis=0),
            preferred_element_type=jnp.float32,
        )
        key_total[key_block] += jnp.dot(
            jnp.concatenate(slopes, axis=1),
            jnp.concatenate([one["query"] for one in held], axis=0),
            preferred_element_type=jnp.float32,
        )

    def query_blocks(pair, grads):
        ids = [pair * halves + half for half in range(halves)]
        held = [prepare(at, rows) for at, rows in zip(ids, grads)]
        states = []
        for half, at in enumerate(ids):
            state, probs, slopes = step(
                held[half], at, (jnp.zeros((HD, block), jnp.float32),) * 2, True, True
            )
            add_key(at, held[half : half + 1], probs, slopes)
            for earlier in ids[:half]:
                state, probs, slopes = step(held[half], earlier, state, False, True)
                add_key(earlier, held[half : half + 1], probs, slopes)
            states.append(state)

        def all_steps(bounded):
            def run(key_block, carried):
                new, probs, slopes = [], [], []
                for half in range(halves):
                    state, prob, slope = step(held[half], key_block, carried[half], False, bounded)
                    new.append(state)
                    probs += prob
                    slopes += slope
                add_key(key_block, held, probs, slopes)
                return tuple(new)

            return run

        first, _ = key_range(lengths_ref, ids[0], parts, block)
        _, plain = key_range(lengths_ref, ids[-1], parts, block)
        plain = jnp.minimum(plain, ids[0])
        states = lax.fori_loop(first, plain, all_steps(True), tuple(states))
        states = lax.fori_loop(plain, ids[0], all_steps(False), states)
        return [
            jnp.transpose(jnp.concatenate(state, axis=0)) * (1.0 / math.sqrt(HD))
            for state in states
        ]

    def turn_back(rows, cosine, sine):
        flat = (parts * UNIT_PAIR, LANES)
        rows = jnp.concatenate(
            [one.reshape(parts, UNIT_BLOCK, LANES) for one in rows], axis=1
        ).reshape(flat)
        turned = rows * cosine.reshape(flat) - swap_halves(rows) * sine.reshape(flat)
        return turned.reshape(parts, UNIT_PAIR, LANES).astype(jnp.bfloat16)

    def put(values, unit_at, lane_at):
        for part in range(parts):
            back_ref[slot_of(part), pl.ds(unit_at, UNIT_PAIR), pl.ds(lane_at, LANES)] = values[part]

    def query_pair(pair, unused):
        unit_at = pl.multiple_of(pair * UNIT_PAIR, UNIT_PAIR)
        grads = grad_ref[:, pl.ds(unit_at, UNIT_PAIR), :].astype(jnp.float32)
        done = query_blocks(
            pair,
            [
                grads[:, half * UNIT_BLOCK : (half + 1) * UNIT_BLOCK].reshape(block, LANES)
                for half in range(halves)
            ],
        )
        cosine, sine = pair_angles(unit_at, cos_unit, sin_unit, cos_part, sin_part)
        put(turn_back(done, cosine, sine), unit_at, 0)
        return unused

    lax.fori_loop(0, pairs, query_pair, 0)

    def key_pair(pair, unused):
        unit_at = pl.multiple_of(pair * UNIT_PAIR, UNIT_PAIR)
        cosine, sine = pair_angles(unit_at, cos_unit, sin_unit, cos_part, sin_part)
        ids = [pair * halves + half for half in range(halves)]
        put(turn_back([key_total[at] for at in ids], cosine, sine), unit_at, LANES)
        values = jnp.concatenate(
            [value_total[at].reshape(parts, UNIT_BLOCK, LANES) for at in ids], axis=1
        ).astype(jnp.bfloat16)
        put(values, unit_at, 2 * LANES)
        return unused

    lax.fori_loop(0, pairs, key_pair, 0)


def table_shapes(parts, units):
    table = pltpu.VMEM((units, LANES), jnp.float32)
    row = pltpu.VMEM((parts, LANES), jnp.float32)
    return [pltpu.VMEM((units, LANES), jnp.int32), table, table, row, row]


def attend(lengths, qkv):
    parts, units, _ = qkv.shape
    block = parts * UNIT_BLOCK
    blocks = units // UNIT_BLOCK
    smem = pl.BlockSpec(memory_space=pltpu.SMEM)
    vmem = pl.BlockSpec(memory_space=pltpu.VMEM)
    rows = jax.ShapeDtypeStruct((blocks, block, LANES), jnp.bfloat16)
    halves = UNIT_PAIR // UNIT_BLOCK
    held = pltpu.VMEM((halves, 2, block, LANES), jnp.float32)
    return pl.pallas_call(
        attend_kernel,
        out_shape=(
            jax.ShapeDtypeStruct((parts, units, LANES), jnp.bfloat16),
            jax.ShapeDtypeStruct((blocks, LANES, block), jnp.float32),
            jax.ShapeDtypeStruct((blocks, 8, block), jnp.float32),
            rows,
            rows,
            rows,
        ),
        in_specs=[smem, vmem],
        out_specs=(vmem,) * 6,
        scratch_shapes=[
            pltpu.VMEM((blocks, 2, block, LANES), jnp.bfloat16),
            pltpu.VMEM((blocks, LANES, block), jnp.bfloat16),
            held,
            held,
            held,
            pltpu.VMEM((halves, block, LANES), jnp.float32),
            pltpu.VMEM((block, block), jnp.float32),
            pltpu.VMEM((block, block), jnp.float32),
        ]
        + table_shapes(parts, units),
        compiler_params=pltpu.CompilerParams(vmem_limit_bytes=KERNEL_VMEM),
        cost_estimate=pl.CostEstimate(
            flops=20 * 10**9, bytes_accessed=16 << 20, transcendentals=20 * 10**6
        ),
        name="attend",
    )(lengths, qkv)


def attend_back(lengths, query, key, value, out, log, grad):
    parts, units, _ = grad.shape
    block = parts * UNIT_BLOCK
    blocks = units // UNIT_BLOCK
    smem = pl.BlockSpec(memory_space=pltpu.SMEM)
    vmem = pl.BlockSpec(memory_space=pltpu.VMEM)
    return pl.pallas_call(
        attend_back_kernel,
        out_shape=jax.ShapeDtypeStruct((parts, units, 3 * LANES), jnp.bfloat16),
        in_specs=[smem] + [vmem] * 6,
        out_specs=vmem,
        scratch_shapes=[
            pltpu.VMEM((blocks, LANES, block), jnp.bfloat16),
            pltpu.VMEM((blocks, block, LANES), jnp.float32),
            pltpu.VMEM((blocks, block, LANES), jnp.float32),
            pltpu.VMEM((block, block), jnp.float32),
            pltpu.VMEM((block, block), jnp.float32),
        ]
        + table_shapes(parts, units),
        compiler_params=pltpu.CompilerParams(vmem_limit_bytes=KERNEL_VMEM),
        cost_estimate=pl.CostEstimate(
            flops=50 * 10**9, bytes_accessed=16 << 20, transcendentals=20 * 10**6
        ),
        name="attend_back",
    )(lengths, query, key, value, out, log, grad)


def swap(value, grp_step, rep_step):
    groups, reps = lax.axis_size("grp"), lax.axis_size("rep")
    pairs = [
        (grp * reps + rep, (grp ^ grp_step) * reps + (rep ^ rep_step))
        for grp in range(groups)
        for rep in range(reps)
    ]
    return lax.ppermute(value, BOTH, pairs)


def ordered(flag, own, other, axis=0):
    return jnp.where(
        flag == 0,
        jnp.concatenate([own, other], axis=axis),
        jnp.concatenate([other, own], axis=axis),
    )


def pick(value, index, axis):
    return lax.dynamic_index_in_dim(value, index, axis, keepdims=False)


def halve(value, axis, bit, grp_step, rep_step):
    kept = pick(value, bit, axis)
    sent = pick(value, 1 - bit, axis).astype(jnp.bfloat16)
    arrived = swap(sent, grp_step, rep_step)
    return kept.astype(jnp.float32) + arrived.astype(jnp.float32)


def narrow(value):
    return value.astype(jnp.bfloat16)


MESH_IDS = pl.DeviceIdType.MESH


def flipped(index, step):
    return index + step - 2 * step * ((index // step) % 2)


def lowest(offset):
    return offset & -offset


def link_of(offset, part, turned):
    return turned.get((offset, part), lowest(offset))


GATHER_LINKS = {(14, 0): 4}
GATHER_PLAN = (
    ("rows", 4, 0), ("rows", 0, 1), ("rows", 4, 1), ("rows", 8, 0), ("rows", 8, 1),
    ("rows", 6, 0), ("rows", 2, 0), ("rows", 6, 1), ("project", 5), ("project", 0),
    ("project", 9), ("project", 4), ("rows", 10, 0), ("project", 6), ("project", 8),
    ("project", 1), ("rows", 12, 1), ("rows", 2, 1), ("project", 2), ("project", 7),
    ("rows", 12, 0), ("rows", 10, 1), ("project", 10), ("project", 3), ("project", 12),
    ("rows", 14, 0), ("project", 13), ("rows", 14, 1), ("project", 14), ("project", 11),
    ("project", 15),
)


def gather_kernel(
    tokens_ref,
    gain_ref,
    w_query,
    w_key,
    w_value,
    w_gate,
    w_up,
    w_down,
    w_output,
    out_rows,
    normed_out,
    qkv_ref,
    weight_ref,
    gate_own,
    gate_met,
    up_ref,
    up_piece,
    down_first,
    down_second,
    output_ref,
    out_away,
    gains,
    qkv_at,
    gate_own_at,
    gate_met_at,
    up_at,
    up_piece_at,
    down_first_at,
    down_second_at,
    output_at,
    out_at,
    raw,
    normed,
    weight_sem,
    out_sem,
    send_sem,
    recv_sem,
    side_send,
    side_recv,
    stripe_sem,
    leave_sem,
):
    here, there = lax.axis_index("grp"), lax.axis_index("rep")
    core = there % 2
    reps = raw.shape[0]
    slots = normed.shape[0]
    row_count, width = raw.shape[2:]
    steps = [1 << place for place in range(reps.bit_length() - 1)]
    across = (1 - here, there)

    def neighbour(step):
        return (here, flipped(there, step))

    barrier = pltpu.get_barrier_semaphore()
    for target in [across] + [neighbour(step) for step in steps]:
        pl.semaphore_signal(barrier, inc=1, device_id=target, device_id_type=MESH_IDS)
    local = []
    for at, weight in enumerate((w_query, w_key, w_value)):
        local.append(
            pltpu.make_async_copy(
                weight.at[:, pl.ds(pl.multiple_of(there * LANES, LANES), LANES)],
                weight_ref.at[here, :, pl.ds(at * LANES, LANES)],
                weight_sem.at[at],
            )
        )
        local[-1].start()
    raw[0, 0] = tokens_ref[here]
    gains[here] = gain_ref[...]
    pl.semaphore_wait(barrier, len(steps) + 1)

    def side(at, source, target_ref):
        return pltpu.make_async_remote_copy(
            src_ref=source,
            dst_ref=target_ref,
            send_sem=side_send.at[at],
            recv_sem=side_recv.at[at],
            device_id=across,
            device_id_type=MESH_IDS,
        )

    def rows_copy(offset, part):
        if offset == 0:
            return pltpu.make_async_remote_copy(
                src_ref=tokens_ref.at[1 - here],
                dst_ref=raw.at[0, 1],
                send_sem=send_sem.at[1],
                recv_sem=recv_sem.at[1],
                device_id=across,
                device_id_type=MESH_IDS,
            )
        step = link_of(offset, part, GATHER_LINKS)
        return pltpu.make_async_remote_copy(
            src_ref=raw.at[offset - step, part],
            dst_ref=raw.at[offset, part],
            send_sem=send_sem.at[2 * offset + part],
            recv_sem=recv_sem.at[2 * offset + part],
            device_id=neighbour(step),
            device_id_type=MESH_IDS,
        )

    order = [tuple(what) for kind, *what in GATHER_PLAN if kind == "rows"]
    copies = {
        (offset, part): rows_copy(offset, part)
        for offset in range(reps)
        for part in (0, 1)
        if offset or part
    }

    def pass_on(offset, part):
        for later, part_of in order:
            if later and part_of == part and later - link_of(later, part, GATHER_LINKS) == offset:
                copies[later, part].start()
        copies[offset + 1, part].start()

    gain_copy = side(0, gains.at[here], gains.at[here])
    gain_copy.start()
    copies[0, 1].start()
    pass_on(0, 0)
    for one in local:
        one.wait()
    weight_copy = side(1, weight_ref.at[here], weight_ref.at[here])
    weight_copy.start()

    stripes = [
        (grp, high, low)
        for grp in range(2)
        for high in range(reps // 8)
        for low in range(2)
    ]
    place = 4 * ((there // 4) % 2) + there % 2
    stripe_loads = []

    def load(source, target_ref):
        stripe_loads.append(
            pltpu.make_async_copy(source, target_ref, stripe_sem.at[len(stripe_loads)])
        )

    def columns_of(weight, grp, high, low):
        first = (grp * reps + 8 * high + 2 * low + place) * LANES
        return weight.at[:, pl.ds(pl.multiple_of(first, LANES), LANES)]

    for weight, target_ref in ((w_gate, gate_own_at), (w_up, up_at)):
        for at, stripe in enumerate(stripes):
            load(columns_of(weight, *stripe), target_ref.at[:, pl.ds(at * LANES, LANES)])
    for at, (grp, high, low) in enumerate(stripes[: len(stripes) // 2]):
        first = (8 * high + 2 * low + place) * LANES
        load(
            w_down.at[pl.ds(pl.multiple_of(first, LANES), LANES)],
            (down_first_at, down_second_at)[at // 2].at[pl.ds(at % 2 * LANES, LANES)],
        )
    piece_rows = up_piece.shape[0]
    low = (there // 2) % 2
    for at, stripe in enumerate(stripes):
        load(
            columns_of(w_up, *stripe).at[
                pl.ds(pl.multiple_of(low * piece_rows, piece_rows), piece_rows)
            ],
            up_piece_at.at[:, pl.ds(at * LANES, LANES)],
        )
    load(out_rows, out_at)
    for one in stripe_loads:
        one.start()
    quarter = output_ref.shape[0]
    output_copy = side(
        2,
        w_output.at[pl.ds(pl.multiple_of((there % 4) * quarter, quarter), quarter)],
        output_at,
    )
    output_copy.start()
    gate_copy = side(
        3, gate_own_at.at[pl.ds(pl.multiple_of(low * piece_rows, piece_rows), piece_rows)], gate_met_at
    )
    for one in stripe_loads[: len(stripes)]:
        one.wait()
    gate_copy.start()

    leaving = []

    def leave(at, source, target_ref):
        leaving.append(pltpu.make_async_copy(source, target_ref, leave_sem.at[at]))
        leaving[-1].start()

    written = {}
    used = [None] * slots
    tile = 32

    def project(count, offset):
        slot = count % slots
        if used[slot] is not None:
            written[used[slot]].wait()
        used[slot] = offset
        gain = jnp.concatenate([gains[0, 0:1], gains[1, 0:1]], axis=1).astype(jnp.float32)
        for part in range(2):

            def norm_rows(at, unused):
                cut = pl.ds(pl.multiple_of(at * tile, tile), tile)
                values = raw[offset, part, cut, :].astype(jnp.float32)
                scaled = values * rms_scale(values) * gain
                normed[slot, pl.ds(pl.multiple_of(part * row_count + at * tile, tile), tile), :] = (
                    scaled.astype(jnp.bfloat16)
                )
                return unused

            lax.fori_loop(0, row_count // tile, norm_rows, 0)
        written[offset] = pltpu.make_async_copy(
            normed.at[slot], normed_out.at[offset], out_sem.at[offset]
        )
        written[offset].start()
        half = width // 2
        product = jnp.dot(
            normed[slot, :, :half], weight_ref[0], preferred_element_type=jnp.float32
        ) + jnp.dot(normed[slot, :, half:], weight_ref[1], preferred_element_type=jnp.float32)
        qkv_at[pl.ds(2 * offset, 2)] = product.astype(jnp.bfloat16).reshape(
            2, row_count, 3 * LANES
        )
        leave(
            offset, qkv_at.at[pl.ds(2 * offset, 2)], qkv_ref.at[pl.ds(2 * offset, 2)]
        )

    count = 0
    for kind, *what in GATHER_PLAN:
        if kind == "rows":
            copies[tuple(what)].wait_recv()
            pass_on(*what)
            continue
        if count == 0:
            gain_copy.wait_recv()
            weight_copy.wait_recv()
        if what[0] % 2:
            for part in (0, 1):
                copies[what[0], part].wait_recv()
        project(count, what[0])
        count += 1
        if count == reps // 2:
            for one in stripe_loads[len(stripes) :]:
                one.wait()
            for at, pair in enumerate(
                (
                    (gate_own_at, gate_own),
                    (up_at, up_ref),
                    (up_piece_at, up_piece),
                    (down_first_at, down_first),
                    (down_second_at, down_second),
                    (out_at, out_away),
                )
            ):
                leave(reps + at, *pair)
    for offset in used:
        written[offset].wait()
    for one in copies.values():
        one.wait_send()
    gain_copy.wait_send()
    weight_copy.wait_send()
    output_copy.wait()
    leave(reps + 6, output_at, output_ref)
    gate_copy.wait()
    leave(reps + 7, gate_met_at, gate_met)
    for one in leaving:
        one.wait()


def gather_heads(
    tokens, gains, w_query, w_key, w_value, w_gate, w_up, w_down, w_output, out_rows
):
    reps = lax.axis_size("rep")
    _, row_count, width = tokens.shape
    half = width // 2
    own_width = reps // 2 * LANES
    gain_rows = jnp.concatenate(
        [gains[0][None], gains[1][None], jnp.zeros((14, half), jnp.bfloat16)], axis=0
    )
    vmem = pl.BlockSpec(memory_space=pltpu.VMEM)
    anywhere = pl.BlockSpec(memory_space=pl.ANY)
    return pl.pallas_call(
        gather_kernel,
        out_shape=(
            jax.ShapeDtypeStruct((reps, 2 * row_count, width), jnp.bfloat16),
            jax.ShapeDtypeStruct((2 * reps, row_count, 3 * LANES), jnp.bfloat16),
            jax.ShapeDtypeStruct((2, half, 3 * LANES), jnp.bfloat16),
            jax.ShapeDtypeStruct((half, own_width), jnp.bfloat16),
            jax.ShapeDtypeStruct((half // 2, own_width), jnp.bfloat16),
            jax.ShapeDtypeStruct((half, own_width), jnp.bfloat16),
            jax.ShapeDtypeStruct((half // 2, own_width), jnp.bfloat16),
            jax.ShapeDtypeStruct((own_width // 4, width), jnp.bfloat16),
            jax.ShapeDtypeStruct((own_width // 4, width), jnp.bfloat16),
            jax.ShapeDtypeStruct((half // 4, width), jnp.bfloat16),
            jax.ShapeDtypeStruct(out_rows.shape, jnp.bfloat16),
            jax.ShapeDtypeStruct((2, 16, half), jnp.bfloat16),
        ),
        in_specs=[vmem, vmem] + [anywhere] * 8,
        out_specs=(anywhere, anywhere, vmem) + (anywhere,) * 8 + (vmem,),
        scratch_shapes=[
            pltpu.VMEM((2 * reps, row_count, 3 * LANES), jnp.bfloat16),
            pltpu.VMEM((half, own_width), jnp.bfloat16),
            pltpu.VMEM((half // 2, own_width), jnp.bfloat16),
            pltpu.VMEM((half, own_width), jnp.bfloat16),
            pltpu.VMEM((half // 2, own_width), jnp.bfloat16),
            pltpu.VMEM((own_width // 4, width), jnp.bfloat16),
            pltpu.VMEM((own_width // 4, width), jnp.bfloat16),
            pltpu.VMEM((half // 4, width), jnp.bfloat16),
            pltpu.VMEM(out_rows.shape, jnp.bfloat16),
            pltpu.VMEM((reps, 2, row_count, width), jnp.bfloat16),
            pltpu.VMEM((4, 2 * row_count, width), jnp.bfloat16),
            pltpu.SemaphoreType.DMA((3,)),
            pltpu.SemaphoreType.DMA((reps,)),
            pltpu.SemaphoreType.DMA((2 * reps,)),
            pltpu.SemaphoreType.DMA((2 * reps,)),
            pltpu.SemaphoreType.DMA((4,)),
            pltpu.SemaphoreType.DMA((4,)),
            pltpu.SemaphoreType.DMA((reps // 2 * 7 // 2 + 1,)),
            pltpu.SemaphoreType.DMA((reps + 8,)),
        ],
        compiler_params=pltpu.CompilerParams(
            vmem_limit_bytes=KERNEL_VMEM, collective_id=0, has_side_effects=True
        ),
        cost_estimate=pl.CostEstimate(
            flops=8 * 10**9, bytes_accessed=250 << 20, transcendentals=0
        ),
        name="gather_heads",
    )(tokens, gain_rows, w_query, w_key, w_value, w_gate, w_up, w_down, w_output, out_rows)


SCATTER_PLAN = (
    ("first", "down"), ("rows", 13, 0), ("rows", 15, 0), ("rows", 7, 0), ("first", "up"),
    ("first", "gate"), ("rows", 7, 1), ("first", "out"), ("rows", 14, 0), ("rows", 5, 1),
    ("rows", 12, 0), ("sum", "down"), ("rows", 11, 0), ("rows", 1, 0), ("weights", 2),
    ("rows", 11, 1), ("rows", 15, 1), ("weights", 1), ("sum", "up"), ("rows", 14, 1),
    ("weights", 1), ("rows", 6, 1), ("rows", 13, 1), ("rows", 10, 1), ("rows", 12, 1),
    ("rows", 9, 0), ("rows", 10, 0), ("weights", 1), ("rows", 5, 0), ("weights", 1),
    ("rows", 4, 1), ("rows", 3, 1), ("weights", 2), ("rows", 6, 0), ("rows", 9, 1),
    ("sum", "gate"), ("weights", 1), ("sum", "out"), ("rows", 2, 1), ("rows", 8, 1),
    ("rows", 3, 0), ("weights", 2), ("rows", 8, 0), ("weights", 1), ("rows", 2, 0),
    ("weights", 2), ("rows", 1, 1), ("sum", "quad"), ("rows", 4, 0), ("weights", 2),
    ("weights over",), ("sum", "out next"), ("rows", 0, 1), ("sum", "quad next"),
    ("weights out",), ("rows", 0, 0),
)
SCATTER_LINKS = {(14, 0): 4}


def scatter_kernel(
    back_ref,
    weight_ref,
    tokens_ref,
    mixed_grad,
    gain_ref,
    normed_ref,
    gate_kept,
    gate_met,
    up_kept,
    up_met,
    down_kept,
    down_met,
    output_kept,
    output_met,
    token_ref,
    pieces_ref,
    quad_ref,
    down_ref,
    output_ref,
    away,
    landed,
    grad_in,
    normed,
    back_t,
    weight_t,
    weights_total,
    half_out,
    half_in,
    piece_out,
    gate_away,
    gate_landed,
    up_away,
    up_landed,
    up_last,
    down_away,
    down_landed,
    down_last,
    output_away,
    output_landed,
    output_next,
    output_last,
    gate_stage,
    up_stage,
    wide_stage,
    gate_crossed,
    up_crossed,
    normed_sem,
    send_sem,
    recv_sem,
    side_send,
    side_recv,
    piece_send,
    piece_recv,
    stage_sem,
    sum_send,
    sum_recv,
):
    here, there = lax.axis_index("grp"), lax.axis_index("rep")
    reps, rows, columns = back_ref.shape
    row_count = rows // 2
    width = token_ref.shape[1]
    half = width // 2
    own_rows = half // reps
    steps = [1 << place for place in range(reps.bit_length() - 1)]
    bit = {step: (there // step) % 2 for step in steps}
    across = (1 - here, there)

    def other(offset):
        index = there
        for step in steps:
            if offset & step:
                index = flipped(index, step)
        return (here, index)

    barrier = pltpu.get_barrier_semaphore()
    for target in [across] + [other(offset) for offset in range(1, reps)]:
        pl.semaphore_signal(barrier, inc=1, device_id=target, device_id_type=MESH_IDS)

    slots = normed.shape[0]
    fetch = [
        pltpu.make_async_copy(normed_ref.at[offset], normed.at[offset % slots], normed_sem.at[offset])
        for offset in range(reps)
    ]
    for offset in range(slots):
        fetch[offset].start()

    def part_of(ref, axis, index):
        return ref.at[(slice(None),) * axis + (index,)]

    def load(at, source, target_ref):
        copy = pltpu.make_async_copy(source, target_ref, stage_sem.at[at])
        copy.start()
        return copy

    def open_half(at, kept, met, axis, flag, stage, target_ref):
        loads = [load(2 * at + 1, part_of(met, axis, flag), target_ref)]
        if stage is not None:
            loads.append(load(2 * at, part_of(kept, axis, flag), stage))
        return loads

    firsts = [
        open_half(0, down_kept, down_met, 1, 1 - bit[2], wide_stage, down_away),
        open_half(1, output_kept, output_met, 0, 1 - here, None, output_away),
        open_half(2, gate_kept, gate_met, 1, 1 - bit[2], gate_stage.at[0], gate_away),
        open_half(3, up_kept, up_met, 0, 1 - here, up_stage, up_away),
    ]

    for at in range(2):
        turned = jnp.transpose(weight_ref[at].astype(jnp.float32)).astype(jnp.bfloat16)
        weight_t[:, pl.ds(at * half, half)] = turned
    pl.semaphore_wait(barrier, reps)

    def add_to(target_ref, *sources):
        lead = target_ref.shape[:-2]
        count = 1
        for size in lead:
            count *= size
        for at in range(count):
            index, rest = [], at
            for size in lead[::-1]:
                index.insert(0, rest % size)
                rest //= size

            def some_rows(step, unused):
                place = tuple(index) + (pl.ds(pl.multiple_of(step * 16, 16), 16),)
                total = target_ref[place].astype(jnp.float32)
                for source in sources:
                    total = total + source[place].astype(jnp.float32)
                target_ref[place] = total.astype(target_ref.dtype)
                return unused

            lax.fori_loop(0, target_ref.shape[-2] // 16, some_rows, 0)

    def sum_copy(at, source, target_ref, target):
        return pltpu.make_async_remote_copy(
            src_ref=source,
            dst_ref=target_ref,
            send_sem=sum_send.at[at],
            recv_sem=sum_recv.at[at],
            device_id=target,
            device_id_type=MESH_IDS,
        )

    down_cross = sum_copy(0, down_away, down_landed, other(2))
    output_cross = sum_copy(1, output_away, output_landed, across)
    gate_low = sum_copy(2, gate_away, gate_landed, other(2))
    up_low = sum_copy(3, up_away, up_landed, across)
    down_high = sum_copy(4, down_landed.at[1 - bit[8]], down_last, other(8))
    up_high = sum_copy(5, up_landed.at[1 - bit[8]], up_last, other(8))
    output_low = sum_copy(6, output_landed.at[:, 1 - bit[2]], output_next, other(2))
    output_high = sum_copy(7, output_next.at[1 - bit[8]], output_last, other(8))
    quad_far = [
        sum_copy(8, gate_landed.at[1 - bit[4]], gate_crossed, other(4)),
        sum_copy(9, up_last.at[1 - bit[4]], up_crossed, other(4)),
    ]
    early_width = gate_crossed.shape[2]
    early = pl.ds(0, early_width)
    late = pl.ds(early_width, quad_ref.shape[3] - early_width)
    beside = 1 - bit[1]
    quad_near = [
        sum_copy(at, source, quad_ref.at[far, bit[1], :, cols], other(1))
        for at, source, far, cols in (
            (10, gate_landed.at[bit[4], beside], bit[4], early),
            (11, up_last.at[bit[4], beside], bit[4], late),
            (12, gate_crossed.at[beside], 1 - bit[4], early),
            (13, up_crossed.at[beside], 1 - bit[4], late),
        )
    ]
    def first_send(at, target_ref, stage, copy):
        for one in firsts[at]:
            one.wait()
        add_to(target_ref, stage)
        copy.start()

    def down_first():
        first_send(0, down_away, wide_stage, down_cross)
        firsts[1].append(load(2, part_of(output_kept, 0, 1 - here), wide_stage))

    def own_half(at, kept, met, axis, flag, stage_a, stage_b, copy, target_ref):
        loads = (
            load(2 * at, part_of(kept, axis, flag), stage_a),
            load(2 * at + 1, part_of(met, axis, flag), stage_b),
        )
        for one in loads:
            one.wait()
        copy.wait_recv()
        add_to(target_ref, stage_a, stage_b)

    def down_sum():
        down_cross.wait_send()
        own_half(
            0, down_kept, down_met, 1, bit[2], wide_stage, down_away, down_cross, down_landed
        )
        down_high.start()

    def output_sum():
        output_cross.wait_send()
        own_half(
            1, output_kept, output_met, 0, here, wide_stage, output_away, output_cross,
            output_landed,
        )
        output_low.start()

    def gate_sum():
        own_half(
            2, gate_kept, gate_met, 1, bit[2], gate_stage.at[0], gate_stage.at[1],
            gate_low, gate_landed,
        )

    def up_sum():
        up_low.wait_send()
        own_half(
            3, up_kept, up_met, 0, here, up_stage, up_away, up_low,
            up_landed,
        )
        up_high.start()

    def output_next_sum():
        output_low.wait_recv()
        add_to(output_next, output_landed.at[:, bit[2]])
        output_high.start()

    def quad_send():
        up_high.wait_recv()
        add_to(up_last, up_landed.at[bit[8]])
        for one in quad_far + quad_near[:2]:
            one.start()
        quad_ref[bit[4], bit[1], :, early] = gate_landed[bit[4], bit[1]]
        quad_ref[bit[4], bit[1], :, late] = up_last[bit[4], bit[1]]

    def quad_pass():
        for one in quad_far:
            one.wait_recv()
        for one in quad_near[2:]:
            one.start()
        quad_ref[1 - bit[4], bit[1], :, early] = gate_crossed[bit[1]]
        quad_ref[1 - bit[4], bit[1], :, late] = up_crossed[bit[1]]

    def last_sums():
        down_high.wait_recv()
        output_high.wait_recv()

        def down_rows(step, unused):
            cut = pl.ds(pl.multiple_of(step * 16, 16), 16)
            for at in range(down_last.shape[0]):
                down_ref[at, cut] = down_last[at, cut].astype(jnp.float32) + down_landed[
                    bit[8], at, cut
                ].astype(jnp.float32)
            output_ref[cut] = output_last[cut].astype(jnp.float32) + output_next[
                bit[8], cut
            ].astype(jnp.float32)
            return unused

        lax.fori_loop(0, own_rows // 16, down_rows, 0)

    def rows_copy(offset, part):
        if offset == 0:
            return pltpu.make_async_remote_copy(
                src_ref=away.at[0, 1],
                dst_ref=landed.at[0, 1],
                send_sem=send_sem.at[1],
                recv_sem=recv_sem.at[1],
                device_id=across,
                device_id_type=MESH_IDS,
            )
        return pltpu.make_async_remote_copy(
            src_ref=away.at[offset // 2, part],
            dst_ref=landed.at[offset, part],
            send_sem=send_sem.at[2 * offset + part],
            recv_sem=recv_sem.at[2 * offset + part],
            device_id=other(link_of(offset, part, SCATTER_LINKS)),
            device_id_type=MESH_IDS,
        )

    copies = {
        (offset, part): rows_copy(offset, part)
        for offset in range(reps)
        for part in (0, 1)
        if offset or part
    }

    def send(offset, part):
        sources = [
            later
            for later in range(1, reps)
            if later - link_of(later, part, SCATTER_LINKS) == offset
        ]
        for later in sources:
            copies[later, part].wait_recv()
        total = jnp.dot(
            back_ref[offset, pl.ds(part * row_count, row_count), :],
            weight_t[...],
            preferred_element_type=jnp.float32,
        )
        for later in sources:
            total = total + landed[later, part].astype(jnp.float32)
        if offset == 0 and part == 0:
            grad_in[...] = total
        else:
            if offset % 2 == 0:
                copies[offset + 1, part].wait_send()
            away[offset // 2, part] = total.astype(jnp.bfloat16)
            copies[offset, part].start()

    def weight_step(offset):
        fetch[offset].wait()
        back_t[...] = jnp.transpose(back_ref[offset].astype(jnp.float32)).astype(jnp.bfloat16)

        def columns_at(at, unused):
            cut = pl.ds(pl.multiple_of(at * 512, 512), 512)
            term = jnp.dot(
                back_t[...], normed[offset % slots, :, cut], preferred_element_type=jnp.float32
            )
            if offset == 0:
                weights_total[:, cut] = term
            else:
                weights_total[:, cut] += term
            return unused

        lax.fori_loop(0, width // 512, columns_at, 0)
        if offset + slots < reps:
            fetch[offset + slots].start()

    half_copy = pltpu.make_async_remote_copy(
        src_ref=half_out,
        dst_ref=half_in,
        send_sem=side_send,
        recv_sem=side_recv,
        device_id=across,
        device_id_type=MESH_IDS,
    )
    piece_copies = [
        pltpu.make_async_remote_copy(
            src_ref=piece_out.at[other(offset)[1]],
            dst_ref=pieces_ref.at[there],
            send_sem=piece_send.at[offset],
            recv_sem=piece_recv.at[offset],
            device_id=other(offset),
            device_id_type=MESH_IDS,
        )
        for offset in range(1, reps)
    ]

    def cross_weights():
        cut = pl.ds(pl.multiple_of((1 - here) * half, half), half)
        half_out[...] = weights_total[:, cut].astype(jnp.bfloat16)
        half_copy.start()

    def share_weights():
        half_copy.wait_recv()
        cut = pl.ds(pl.multiple_of(here * half, half), half)
        total = jnp.transpose(weights_total[:, cut] + half_in[...].astype(jnp.float32))
        piece_out[...] = total.astype(jnp.bfloat16).reshape(reps, own_rows, columns)
        pieces_ref[there] = piece_out[there]
        for one in piece_copies:
            one.start()

    weights = list(range(reps))

    def weight_steps(count):
        for _ in range(min(count, len(weights))):
            weight_step(weights.pop(0))

    firsts_by = {
        "down": down_first,
        "out": lambda: first_send(1, output_away, wide_stage, output_cross),
        "gate": lambda: first_send(2, gate_away, gate_stage.at[0], gate_low),
        "up": lambda: first_send(3, up_away, up_stage, up_low),
    }
    sums_by = {
        "down": down_sum,
        "out": output_sum,
        "gate": gate_sum,
        "up": up_sum,
        "out next": output_next_sum,
        "quad": quad_send,
        "quad next": quad_pass,
    }
    for kind, *what in SCATTER_PLAN:
        if kind == "rows":
            send(*what)
        elif kind == "weights":
            weight_steps(*what)
        elif kind == "first":
            firsts_by[what[0]]()
        elif kind == "sum":
            sums_by[what[0]]()
        elif kind == "weights over":
            cross_weights()
        else:
            share_weights()
    last_sums()
    copies[0, 1].wait_recv()

    tile = 32

    def norm_rows(grp, step, grad_rows):
        place = pl.ds(pl.multiple_of(grp * row_count + step * tile, tile), tile)
        values = tokens_ref[place, :].astype(jnp.float32)
        inverse = rms_scale(values)
        normed_rows = values * inverse
        weighted = grad_rows * gain_ref[0:1, :]
        token_ref[place, :] = (
            mixed_grad[place, :]
            + inverse
            * (weighted - normed_rows * jnp.mean(weighted * normed_rows, axis=-1, keepdims=True))
        ).astype(jnp.bfloat16)

    def norm_back(step, unused):
        cut = pl.ds(pl.multiple_of(step * tile, tile), tile)
        norm_rows(here, step, grad_in[cut, :])
        norm_rows(1 - here, step, landed[0, 1, cut, :].astype(jnp.float32))
        return unused

    lax.fori_loop(0, row_count // tile, norm_back, 0)
    for one in piece_copies:
        one.wait()
    for one in quad_near:
        one.wait_recv()
    half_copy.wait_send()
    for one in [gate_low, down_high, up_high, output_low, output_high] + quad_far + quad_near:
        one.wait_send()
    for (offset, part), one in copies.items():
        if offset % 2 == 0 or (offset == 1 and part == 0):
            one.wait_send()


def scatter_heads(back, weights, tokens, mixed_grad, gain, normed, sums):
    reps, rows, columns = back.shape
    width = normed.shape[2]
    row_count = rows // 2
    half = width // 2
    own_rows = half // reps
    vmem = pl.BlockSpec(memory_space=pltpu.VMEM)
    anywhere = pl.BlockSpec(memory_space=pl.ANY)
    low, full = jnp.bfloat16, jnp.float32
    wide = (2, 2, own_rows, width)
    thin = (2, 2, own_rows, sums[0].shape[-1])
    slim = (2, 2, 2, own_rows, sums[2].shape[-1])
    return pl.pallas_call(
        scatter_kernel,
        out_shape=(
            jax.ShapeDtypeStruct((rows, width), low),
            jax.ShapeDtypeStruct((reps, own_rows, columns), low),
            jax.ShapeDtypeStruct((2, 2, own_rows, width), low),
            jax.ShapeDtypeStruct(wide[1:], full),
            jax.ShapeDtypeStruct(wide[2:], full),
        ),
        in_specs=[vmem] * 5 + [anywhere] * 9,
        out_specs=(vmem,) * 5,
        scratch_shapes=[
            pltpu.VMEM((reps // 2, 2, row_count, width), low),
            pltpu.VMEM((reps, 2, row_count, width), low),
            pltpu.VMEM((row_count, width), full),
            pltpu.VMEM((2, rows, width), low),
            pltpu.VMEM((columns, rows), low),
            pltpu.VMEM((columns, width), low),
            pltpu.VMEM((columns, width), full),
            pltpu.VMEM((columns, half), low),
            pltpu.VMEM((columns, half), low),
            pltpu.VMEM((reps, own_rows, columns), low),
            pltpu.VMEM(thin, low),
            pltpu.VMEM(thin, low),
            pltpu.VMEM(slim, low),
            pltpu.VMEM(slim, low),
            pltpu.VMEM(slim[1:], low),
            pltpu.VMEM(wide, low),
            pltpu.VMEM(wide, low),
            pltpu.VMEM(wide[1:], low),
            pltpu.VMEM(wide, low),
            pltpu.VMEM(wide, low),
            pltpu.VMEM(wide[1:], low),
            pltpu.VMEM(wide[2:], low),
            pltpu.VMEM((2,) + thin, low),
            pltpu.VMEM(slim, low),
            pltpu.VMEM(wide, low),
            pltpu.VMEM(thin[1:], low),
            pltpu.VMEM(slim[2:], low),
            pltpu.SemaphoreType.DMA((reps,)),
            pltpu.SemaphoreType.DMA((2 * reps,)),
            pltpu.SemaphoreType.DMA((2 * reps,)),
            pltpu.SemaphoreType.DMA,
            pltpu.SemaphoreType.DMA,
            pltpu.SemaphoreType.DMA((reps,)),
            pltpu.SemaphoreType.DMA((reps,)),
            pltpu.SemaphoreType.DMA((8,)),
            pltpu.SemaphoreType.DMA((14,)),
            pltpu.SemaphoreType.DMA((14,)),
        ],
        compiler_params=pltpu.CompilerParams(
            vmem_limit_bytes=62 * 1024 * 1024, collective_id=1, has_side_effects=True
        ),
        cost_estimate=pl.CostEstimate(
            flops=14 * 10**9, bytes_accessed=250 << 20, transcendentals=0
        ),
        name="scatter_heads",
    )(back, weights, tokens, mixed_grad, gain, normed, *sums)


def finish_kernel(
    pieces_ref,
    quad_ref,
    down_ref,
    output_ref,
    token_ref,
    block_ref,
    gains_ref,
    w_query,
    w_key,
    w_value,
    w_gate,
    w_up,
    query_out,
    key_out,
    value_out,
    gate_out,
    up_out,
    sums_out,
    down_out,
    output_out,
    token_out,
    block_out,
    own_in,
    own_up,
    own_sem,
):
    reps, own_rows, _ = pieces_ref.shape
    width = query_out.shape[1]
    there = lax.axis_index("rep")
    own_cut = pl.ds(pl.multiple_of(there * own_rows, own_rows), own_rows)
    loads = [
        pltpu.make_async_copy(weight.at[own_cut], target_ref, own_sem.at[at])
        for at, (weight, target_ref) in enumerate(
            (
                (w_query, own_in.at[0]),
                (w_key, own_in.at[1]),
                (w_value, own_in.at[2]),
                (w_gate, own_up.at[0]),
                (w_up, own_up.at[1]),
            )
        )
    ]
    for one in loads:
        one.start()
    token_out[...] = token_ref[...]
    block_out[...] = block_ref[...]
    output_out[...] = output_ref[...]
    for half in range(2):
        down_out[pl.ds(half * own_rows, own_rows), :] = down_ref[half]
    for kind, target_ref in enumerate((query_out, key_out, value_out)):
        for place in range(reps):
            target_ref[:, place * LANES : (place + 1) * LANES] = pieces_ref[
                place, :, kind * LANES : (kind + 1) * LANES
            ].astype(jnp.float32)
    for kind, target_ref in enumerate((gate_out, up_out)):
        for at in range(reps // 2):
            source = (kind * (reps // 2) + at) * LANES
            for far in range(2):
                for near in range(2):
                    target = ((at // 2) * 8 + far * 4 + (at % 2) * 2 + near) * LANES
                    target_ref[:, target : target + LANES] = quad_ref[
                        far, near, :, source : source + LANES
                    ].astype(jnp.float32)
    for one in loads:
        one.wait()

    def rows_sum(pairs):
        total = jnp.zeros((own_rows, 1), jnp.float32)
        for grad, weight in pairs:
            total = total + jnp.sum(grad[...] * weight.astype(jnp.float32), axis=1, keepdims=True)
        return jnp.broadcast_to(total, (own_rows, LANES))

    sums_out[0] = (
        rows_sum(((query_out, own_in[0]), (key_out, own_in[1]), (value_out, own_in[2])))
        / gains_ref[0]
    )
    sums_out[1] = rows_sum(((gate_out, own_up[0]), (up_out, own_up[1]))) / gains_ref[1]


def finish(pieces, quad, down, output, token_grad, block_out, gains, owned):
    reps, own_rows, _ = pieces.shape
    rows, width = token_grad.shape
    hidden_width = owned[3].shape[1]
    vmem = pl.BlockSpec(memory_space=pltpu.VMEM)
    anywhere = pl.BlockSpec(memory_space=pl.ANY)
    low, full = jnp.bfloat16, jnp.float32
    narrow_rows = jax.ShapeDtypeStruct((own_rows, width), full)
    wide_rows = jax.ShapeDtypeStruct((own_rows, hidden_width), full)
    return pl.pallas_call(
        finish_kernel,
        out_shape=(
            narrow_rows,
            narrow_rows,
            narrow_rows,
            wide_rows,
            wide_rows,
            jax.ShapeDtypeStruct((2, own_rows, LANES), full),
            jax.ShapeDtypeStruct((2 * own_rows, width), full),
            narrow_rows,
            jax.ShapeDtypeStruct((rows, width), low),
            jax.ShapeDtypeStruct((rows, width), low),
        ),
        in_specs=[vmem] * 7 + [anywhere] * 5,
        out_specs=(vmem,) * 10,
        scratch_shapes=[
            pltpu.VMEM((3, own_rows, width), low),
            pltpu.VMEM((2, own_rows, hidden_width), low),
            pltpu.SemaphoreType.DMA((5,)),
        ],
        compiler_params=pltpu.CompilerParams(vmem_limit_bytes=KERNEL_VMEM),
        name="finish",
    )(pieces, quad, down, output, token_grad, block_out, gains, *owned)


def mlp_kernel(
    heads_ref,
    tokens_ref,
    gain_ref,
    out_rows,
    out_across,
    output_own,
    output_part,
    output_beside,
    gate_own,
    gate_met,
    gate_beside,
    up_own,
    up_other,
    down_first,
    down_second,
    down_other,
    block_ref,
    grad_ref,
    back_ref,
    gate_kept,
    gate_sent,
    late_kept,
    late_sent,
    down_kept,
    down_sent,
    output_kept,
    output_sent,
    gate_ref,
    mixed_ref,
    down_own_ref,
    down_far_landed,
    attended,
    branch_ref,
    returned,
    out_ref,
    mid_ref,
    hidden_ref,
    slope_ref,
    w_output,
    w_in,
    w_out,
    near_away,
    near_landed,
    far_away,
    far_landed,
    down_landed,
    load_sem,
    part_sem,
    send_sem,
    recv_sem,
    heads_send,
    heads_recv,
    back_send,
    back_recv,
    piece_sem,
    late_sem,
    gate_sem,
    place_sem,
    core_send,
    core_recv,
    free_sem,
):
    here, there = lax.axis_index("grp"), lax.axis_index("rep")
    across = (here, flipped(there, 4))
    sibling = (here, flipped(there, 1))
    groups, heads, row_count, _ = returned.shape
    rows, width = tokens_ref.shape
    half = width // 2
    quarter = half // 4
    own_width = w_out.shape[0]

    low = (there // 2) % 2
    up_rows = up_other.shape[0]

    def in_cut(part, first):
        cut = pl.ds(pl.multiple_of(part * up_rows, up_rows), up_rows)
        return w_in.at[1 - here, cut, pl.ds(first, own_width)]

    loads = [
        pltpu.make_async_copy(output_own, w_output.at[here], load_sem.at[0]),
        pltpu.make_async_copy(gate_own, w_in.at[here, :, pl.ds(0, own_width)], load_sem.at[1]),
        pltpu.make_async_copy(gate_met, in_cut(low, 0), load_sem.at[11]),
        pltpu.make_async_copy(gate_beside, in_cut(1 - low, 0), load_sem.at[12]),
        pltpu.make_async_copy(
            up_own, w_in.at[here, :, pl.ds(own_width, own_width)], load_sem.at[2]
        ),
        pltpu.make_async_copy(up_other, in_cut(low, own_width), load_sem.at[3]),
    ]
    own_part = own_width // 2

    early_rows = down_first.shape[0]
    late_rows = own_part - early_rows

    def down_cut(grp, first, count):
        return w_out.at[pl.ds(pl.multiple_of(grp * own_part + first, LANES), count)]

    loads += [
        pltpu.make_async_copy(down_first, down_cut(here, 0, early_rows), load_sem.at[4]),
        pltpu.make_async_copy(down_second, down_cut(here, early_rows, late_rows), load_sem.at[9]),
        pltpu.make_async_copy(down_other, down_cut(1 - here, 0, early_rows), load_sem.at[10]),
        pltpu.make_async_copy(out_rows.at[pl.ds(0, row_count)], out_ref.at[0, 0], load_sem.at[5]),
        pltpu.make_async_copy(
            out_rows.at[pl.ds(row_count, row_count)], out_ref.at[1, 0], load_sem.at[6]
        ),
        pltpu.make_async_copy(out_across.at[pl.ds(0, row_count)], out_ref.at[0, 2], load_sem.at[7]),
        pltpu.make_async_copy(
            out_across.at[pl.ds(row_count, row_count)], out_ref.at[1, 2], load_sem.at[8]
        ),
    ]
    place = there % 4
    core = there % 2

    def output_cut(part):
        return w_output.at[1 - here, pl.ds(pl.multiple_of(part * quarter, quarter), quarter)]

    output_pieces = ((output_part, place), (output_beside, flipped(place, 2)))
    rest = [
        pltpu.make_async_copy(piece, output_cut(part), part_sem.at[at])
        for at, (piece, part) in enumerate(output_pieces)
    ]
    loads = loads[:1] + rest + loads[1:]
    for one in loads:
        one.start()
    steps = [1 << place for place in range(heads.bit_length() - 1)]

    def other(crossing, offset):
        index = there
        for step in steps:
            if offset & step:
                index = flipped(index, step)
        return (1 - here if crossing else here, index)

    others = [
        (crossing, offset) for offset in range(heads) for crossing in (0, 1) if offset or crossing
    ]
    barrier = pltpu.get_barrier_semaphore()
    for key in others:
        pl.semaphore_signal(barrier, inc=1, device_id=other(*key), device_id_type=MESH_IDS)
    pl.semaphore_wait(barrier, len(others))

    facing = (1 - here, there)

    def copy(at, source, target_ref, target):
        return pltpu.make_async_remote_copy(
            src_ref=source,
            dst_ref=target_ref,
            send_sem=send_sem.at[at],
            recv_sem=recv_sem.at[at],
            device_id=target,
            device_id_type=MESH_IDS,
        )

    heads_copies, back_copies = [], []
    for at, key in enumerate(others):
        target = other(*key)
        heads_copies.append(
            pltpu.make_async_remote_copy(
                src_ref=heads_ref.at[target[0] * heads + target[1]],
                dst_ref=returned.at[here, there],
                send_sem=heads_send.at[at],
                recv_sem=heads_recv.at[at],
                device_id=target,
                device_id_type=MESH_IDS,
            )
        )
        back_copies.append(
            pltpu.make_async_remote_copy(
                src_ref=returned.at[target[0], target[1]],
                dst_ref=back_ref.at[here * heads + there],
                send_sem=back_send.at[at],
                recv_sem=back_recv.at[at],
                device_id=target,
                device_id_type=MESH_IDS,
            )
        )
    for one in heads_copies[::-1]:
        one.start()
    parts = range(groups)

    def rows_of(part):
        return pl.ds(part * row_count, row_count)

    output_near = [
        copy(at, piece, output_cut(part), sibling) for at, (piece, part) in enumerate(output_pieces)
    ]
    down_far = copy(2, down_second, down_cut(here, early_rows, late_rows), facing)
    up_beside = copy(26, up_other, in_cut(low, own_width), (here, flipped(there, 2)))
    out_near = [
        copy(3 + part, out_rows.at[rows_of(part)], out_ref.at[part, 1], sibling) for part in parts
    ]
    out_on = [
        copy(5 + part, out_across.at[rows_of(part)], out_ref.at[part, 3], sibling) for part in parts
    ]
    for one in output_near + out_near + out_on + [down_far, up_beside]:
        one.start()
    returned[here, there] = heads_ref[here * heads + there]

    early_width = gate_ref.shape[1]
    mid_near = [copy(7 + at, mid_ref.at[at, 0], mid_ref.at[at, 1], sibling) for at in parts]
    mid_far = [copy(9 + at, mid_ref.at[at, 0], mid_ref.at[at, 2], across) for at in parts]
    mid_on = [copy(11 + at, mid_ref.at[at, 2], mid_ref.at[at, 3], sibling) for at in parts]
    grad_near = {
        (side, at): copy(
            13 + 2 * side + at, near_away.at[side, at], near_landed.at[side, at], sibling
        )
        for side in range(2)
        for at in parts
    }
    grad_far = [copy(17 + at, far_away.at[at], far_landed.at[at], across) for at in parts]
    down_near = {
        (side, at): copy(
            19 + 2 * side + at, near_away.at[side, at], down_landed.at[side, at], sibling
        )
        for side in range(2)
        for at in parts
    }
    down_over = [
        copy(23 + at, down_own_ref.at[1, at], down_far_landed.at[at], across) for at in parts
    ]
    gate_cross = copy(25, w_in.at[1 - here, :, pl.ds(0, early_width)], gate_ref, facing)
    late_cut = pl.ds(early_width, 2 * own_width - early_width)
    late_block = late_kept.shape[1]

    def late_rows_of(at, bit):
        return pl.ds(pl.multiple_of((2 * at + bit) * late_block, late_block), late_block)

    up_outs = [
        pltpu.make_async_copy(
            w_in.at[at // 4, late_rows_of(at % 4, bit), late_cut], target_ref.at[at], late_sem.at[2 * at + kind]
        )
        for at in range(8)
        for kind, (target_ref, bit) in enumerate(((late_kept, low), (late_sent, 1 - low)))
    ]
    down_outs = [
        pltpu.make_async_copy(
            w_out.at[pl.ds(pl.multiple_of(grp * own_part, own_part), own_part)],
            target_ref,
            piece_sem.at[kind],
        )
        for kind, (target_ref, grp) in enumerate(((down_kept, here), (down_sent, 1 - here)))
    ]

    for one in heads_copies:
        one.wait()
    for group in range(groups):
        for head in range(heads):
            attended[
                group * row_count : (group + 1) * row_count, head * LANES : (head + 1) * LANES
            ] = returned[group, head]
    for one in loads[:3]:
        one.wait()
    for one in output_near:
        one.wait_recv()
    wide = 512

    def mix(at, unused):
        cut = pl.ds(pl.multiple_of(at * wide, wide), wide)
        mixed_ref[:, cut] = (
            tokens_ref[:, cut].astype(jnp.float32)
            + jnp.dot(attended[:, :half], w_output[0, :, cut], preferred_element_type=jnp.float32)
            + jnp.dot(attended[:, half:], w_output[1, :, cut], preferred_element_type=jnp.float32)
        )
        return unused

    lax.fori_loop(0, width // wide, mix, 0)
    tile = 32
    for part in parts:

        def norm_rows(at, unused):
            cut = pl.ds(pl.multiple_of(at * tile, tile), tile)
            values = mixed_ref[pl.ds(pl.multiple_of(part * row_count + at * tile, tile), tile), :]
            mid_ref[part, 0, cut, :] = (
                values * rms_scale(values) * gain_ref[0:1, :]
            ).astype(jnp.bfloat16)
            return unused

        lax.fori_loop(0, row_count // tile, norm_rows, 0)
        mid_far[part].start()
        mid_near[part].start()
    for one in loads[3:]:
        one.wait()
    up_beside.wait_recv()
    narrow_tile = 256
    per_half = own_part // narrow_tile
    every = (0, 1)

    def pair_rows(ref, side, part, cols):
        values = ref[part, pl.ds(2 * side, 2), :, cols]
        return values.reshape(rows, values.shape[2])

    def forward(side, part, halves):
        def columns(step, unused):
            at = jnp.where(step < per_half, halves[0] * per_half, halves[-1] * per_half - per_half)
            at = at + step
            cut = pl.ds(pl.multiple_of(at * narrow_tile, narrow_tile), narrow_tile)
            up_cut = pl.ds(pl.multiple_of(own_width + at * narrow_tile, narrow_tile), narrow_tile)
            low_rows = pair_rows(mid_ref, side, part, slice(0, half))
            high_rows = pair_rows(mid_ref, side, part, slice(half, width))

            def project(cols):
                return jnp.dot(
                    low_rows, w_in[0, :, cols], preferred_element_type=jnp.float32
                ) + jnp.dot(high_rows, w_in[1, :, cols], preferred_element_type=jnp.float32)

            gate_pre, up_pre = project(cut), project(up_cut)
            grad_hidden = contract(
                pair_rows(out_ref, side, part, slice(0, width)), w_out[cut, :], 1, 1
            )
            gate_sig = jax.nn.sigmoid(gate_pre)
            gate_silu = gate_pre * gate_sig

            def put(ref, cols, values):
                ref[part, pl.ds(2 * side, 2), :, cols] = values.astype(jnp.bfloat16).reshape(
                    2, row_count, narrow_tile
                )

            put(hidden_ref, cut, gate_silu * up_pre)
            put(
                slope_ref,
                cut,
                grad_hidden * up_pre * gate_sig * (1.0 + gate_pre * (1.0 - gate_sig)),
            )
            put(slope_ref, up_cut, grad_hidden * gate_silu)
            return unused

        lax.fori_loop(0, len(halves) * per_half, columns, 0)

    def backward(side, part):
        for at in range(2):

            def columns(step, unused):
                cut = pl.ds(pl.multiple_of(step * wide, wide), wide)
                whole = pl.ds(pl.multiple_of(at * half + step * wide, wide), wide)
                values = contract(
                    pair_rows(slope_ref, side, part, slice(0, 2 * own_width)),
                    w_in[at, cut, :],
                    1,
                    1,
                )
                near_away[side, part, :, whole] = values[row_count:].astype(jnp.bfloat16)
                if side == 0:
                    grad_ref[rows_of(part), whole] = values[:row_count]
                else:
                    far_away[part, :, whole] = values[:row_count].astype(jnp.bfloat16)
                return unused

            lax.fori_loop(0, half // wide, columns, 0)
        grad_near[side, part].start()

    def add_rows(target_ref, source_ref):
        def some_rows(at, unused):
            cut = pl.ds(pl.multiple_of(at * tile, tile), tile)
            target_ref[cut, :] = (
                target_ref[cut, :].astype(jnp.float32) + source_ref[cut, :].astype(jnp.float32)
            ).astype(target_ref.dtype)
            return unused

        lax.fori_loop(0, row_count // tile, some_rows, 0)

    def far_send(part):
        grad_near[1, part].wait_recv()
        add_rows(far_away.at[part], near_landed.at[1, part])
        grad_far[part].start()

    def down(side, part):
        grad_near[side, part].wait_send()

        def columns(step, unused):
            cut = pl.ds(pl.multiple_of(step * wide, wide), wide)
            values = jnp.dot(
                pair_rows(hidden_ref, side, part, slice(0, own_width)),
                w_out[:, cut],
                preferred_element_type=jnp.float32,
            ).astype(jnp.bfloat16)
            near_away[side, part, :, cut] = values[row_count:]
            down_own_ref[side, part, :, cut] = values[:row_count]
            return unused

        lax.fori_loop(0, width // wide, columns, 0)
        down_near[side, part].start()

    def down_meet(side, part):
        down_near[side, part].wait_recv()
        add_rows(down_own_ref.at[side, part], down_landed.at[side, part])

    for part in parts:
        mid_near[part].wait_recv()
        out_near[part].wait_recv()
        forward(0, part, (here,))
    for part in parts:
        mid_far[part].wait_recv()
        mid_on[part].start()
        if part == 0:
            down_far.wait_recv()
        else:
            forward(0, 0, (1 - here,))
            far_send(0)
        mid_on[part].wait_recv()
        out_on[part].wait_recv()
        forward(1, part, every)
        backward(1, part)
    forward(0, 1, (1 - here,))
    far_send(1)
    for part in parts:
        backward(0, part)

    def turned(values):
        flat = values.reshape(4 * rows, values.shape[3]).astype(jnp.float32)
        return jnp.transpose(flat).astype(jnp.bfloat16)

    def in_grads(at):
        def some_rows(step, unused):
            cut = pl.ds(pl.multiple_of(step * narrow_tile, narrow_tile), narrow_tile)
            source = pl.ds(pl.multiple_of(at * half + step * narrow_tile, narrow_tile), narrow_tile)
            left = turned(mid_ref[:, :, :, source])

            def columns(place_at, unused):
                cols = pl.ds(pl.multiple_of(place_at * wide, wide), wide)
                right = slope_ref[:, :, :, cols].reshape(4 * rows, wide)
                w_in[at, cut, cols] = jnp.dot(
                    left, right, preferred_element_type=jnp.float32
                ).astype(jnp.bfloat16)
                return unused

            return lax.fori_loop(0, 2 * own_width // wide, columns, unused)

        lax.fori_loop(0, half // narrow_tile, some_rows, 0)

    def down_rows(step, unused):
        cut = pl.ds(pl.multiple_of(step * narrow_tile, narrow_tile), narrow_tile)
        left = turned(hidden_ref[:, :, :, cut])

        def columns(place_at, unused):
            cols = pl.ds(pl.multiple_of(place_at * wide, wide), wide)
            right = out_ref[:, :, :, cols].reshape(4 * rows, wide)
            w_out[cut, cols] = jnp.dot(left, right, preferred_element_type=jnp.float32).astype(
                jnp.bfloat16
            )
            return unused

        return lax.fori_loop(0, width // wide, columns, unused)

    def finish(part):
        grad_near[0, part].wait_recv()
        grad_far[part].wait_recv()

        def norm_back(at, unused):
            cut = pl.ds(pl.multiple_of(at * tile, tile), tile)
            place = pl.ds(pl.multiple_of(part * row_count + at * tile, tile), tile)
            grad_mid = (
                grad_ref[place, :]
                + near_landed[0, part, cut, :].astype(jnp.float32)
                + far_landed[part, cut, :].astype(jnp.float32)
            )
            values = mixed_ref[place, :]
            inverse = rms_scale(values)
            normed = values * inverse
            weighted = grad_mid * gain_ref[0:1, :]
            grad = out_ref[part, 0, cut, :].astype(jnp.float32) + inverse * (
                weighted - normed * jnp.mean(weighted * normed, axis=-1, keepdims=True)
            )
            grad_ref[place, :] = grad
            branch_ref[place, :] = grad.astype(jnp.bfloat16)
            return unused

        lax.fori_loop(0, row_count // tile, norm_back, 0)
        for head in range(0, heads, 4):
            at = head * LANES // half
            start = head * LANES - at * half
            values = contract(
                branch_ref[rows_of(part), :],
                w_output[at, pl.ds(start, 4 * LANES), :],
                1,
                1,
                jnp.bfloat16,
            )
            for step in range(4):
                returned[part, head + step] = values[:, step * LANES : (step + 1) * LANES]
        for at, (crossing, _) in enumerate(others):

            @pl.when(jnp.where(crossing, 1 - here, here) == part)
            def _():
                back_copies[at].start()

    in_grads(1 - here)
    gate_cross.start()
    down(1, 0)
    finish(0)
    in_grads(here)
    for one in up_outs:
        one.start()
    for one in mid_near + mid_far + mid_on:
        one.wait_send()
    pl.semaphore_signal(free_sem, inc=1, device_id=sibling, device_id_type=MESH_IDS)
    finish(1)
    back_ref[here * heads + there] = returned[here, there]

    for at in range(2):

        def output_rows(step, unused):
            cut = pl.ds(pl.multiple_of(step * narrow_tile, narrow_tile), narrow_tile)
            source = pl.ds(pl.multiple_of(at * half + step * narrow_tile, narrow_tile), narrow_tile)
            left = jnp.transpose(attended[:, source].astype(jnp.float32)).astype(jnp.bfloat16)

            def columns(place_at, unused):
                cols = pl.ds(pl.multiple_of(place_at * wide, wide), wide)
                w_output[at, cut, cols] = jnp.dot(
                    left, branch_ref[:, cols], preferred_element_type=jnp.float32
                ).astype(jnp.bfloat16)
                return unused

            return lax.fori_loop(0, width // wide, columns, unused)

        lax.fori_loop(0, half // narrow_tile, output_rows, 0)

    own_rows = half // heads
    stripes = heads // 2
    pl.semaphore_wait(free_sem, 1)

    def stripe_of(at, bit):
        first = (at % stripes * 2 + bit) * own_rows
        return pl.ds(pl.multiple_of(first, own_rows), own_rows)

    def landed_at(at):
        per_slot = row_count // own_rows
        slot = at // per_slot
        return (slot // 4, slot % 4, pl.ds(at % per_slot * own_rows, own_rows))

    core_copies = []
    for at in range(2 * stripes):
        core_copies.append(
            pltpu.make_async_remote_copy(
                src_ref=w_output.at[at // stripes, stripe_of(at, 1 - core)],
                dst_ref=mid_ref.at[landed_at(at)],
                send_sem=core_send.at[at],
                recv_sem=core_recv.at[at],
                device_id=sibling,
                device_id_type=MESH_IDS,
            )
        )
        core_copies[-1].start()
    down(1, 1)
    for part in parts:
        down_meet(1, part)
        down_over[part].start()
    for part in parts:
        down(0, part)
    lax.fori_loop(0, own_width // narrow_tile, down_rows, 0)
    for one in down_outs:
        one.start()
    gate_cross.wait()

    def add_gate(at, unused):
        cut = pl.ds(pl.multiple_of(at * tile, tile), tile)
        gate_ref[cut, :] = (
            gate_ref[cut, :].astype(jnp.float32)
            + w_in[here, cut, pl.ds(0, early_width)].astype(jnp.float32)
        ).astype(jnp.bfloat16)
        return unused

    lax.fori_loop(0, half // tile, add_gate, 0)
    gate_outs = []
    for kind, (target_ref, flag) in enumerate(
        ((gate_kept, there // 8 % 2), (gate_sent, 1 - there // 8 % 2))
    ):
        cut = pl.ds(pl.multiple_of(flag * (half // 2), half // 2), half // 2)
        gate_outs.append(pltpu.make_async_copy(gate_ref.at[cut], target_ref, gate_sem.at[kind]))
        gate_outs[-1].start()
    far_bit = (there // 4) % 2
    output_outs = []
    for at in range(2 * stripes):
        core_copies[at].wait_recv()
        own = stripe_of(at, core)
        w_output[at // stripes, own, :] = (
            w_output[at // stripes, own, :].astype(jnp.float32)
            + mid_ref[landed_at(at)].astype(jnp.float32)
        ).astype(jnp.bfloat16)
    for at in range(stripes):
        grp, high, low_bit = at // (stripes // 2), at // 2 % (stripes // 4), at % 2
        for kind, (target_ref, bit) in enumerate(
            ((output_kept, far_bit), (output_sent, 1 - far_bit))
        ):
            first = ((high * 4 + bit * 2 + low_bit) * 2 + core) * own_rows
            cut = pl.ds(pl.multiple_of(first, own_rows), own_rows)
            output_outs.append(
                pltpu.make_async_copy(
                    w_output.at[grp, cut], target_ref.at[at], place_sem.at[2 * at + kind]
                )
            )
            output_outs[-1].start()
    for part in parts:
        down_meet(0, part)
        down_over[part].wait_recv()

        def block_rows(at, unused):
            cut = pl.ds(pl.multiple_of(at * tile, tile), tile)
            place = pl.ds(pl.multiple_of(part * row_count + at * tile, tile), tile)
            block_ref[place, :] = (
                mixed_ref[place, :]
                + down_own_ref[0, part, cut, :].astype(jnp.float32)
                + down_far_landed[part, cut, :].astype(jnp.float32)
            ).astype(jnp.bfloat16)
            return unused

        lax.fori_loop(0, row_count // tile, block_rows, 0)
    for one in up_outs + down_outs + output_outs + gate_outs:
        one.wait()
    for one in back_copies:
        one.wait()
    for one in grad_far + out_near + out_on + down_over + [down_far, up_beside]:
        one.wait_send()
    for one in list(down_near.values()) + output_near + core_copies:
        one.wait_send()


def mlp(heads, tokens, gain, out_rows, out_across, output_parts, in_parts, down_parts):
    count, row_count, _ = heads.shape
    groups, reps = lax.axis_size("grp"), lax.axis_size("rep")
    rows, width = tokens.shape
    half = width // 2
    own_width = in_parts[0].shape[1]
    early_width = own_width * 6 // 8
    vmem = pl.BlockSpec(memory_space=pltpu.VMEM)
    anywhere = pl.BlockSpec(memory_space=pl.ANY)
    low, full = jnp.bfloat16, jnp.float32
    others = pltpu.SemaphoreType.DMA((count - 1,))
    return pl.pallas_call(
        mlp_kernel,
        out_shape=(
            jax.ShapeDtypeStruct((rows, width), low),
            jax.ShapeDtypeStruct((rows, width), full),
            jax.ShapeDtypeStruct((count, row_count, LANES), low),
            jax.ShapeDtypeStruct((half // 2, early_width), low),
            jax.ShapeDtypeStruct((half // 2, early_width), low),
            jax.ShapeDtypeStruct((8, half // 8, 2 * own_width - early_width), low),
            jax.ShapeDtypeStruct((8, half // 8, 2 * own_width - early_width), low),
            jax.ShapeDtypeStruct((own_width // 2, width), low),
            jax.ShapeDtypeStruct((own_width // 2, width), low),
            jax.ShapeDtypeStruct((reps // 2, half // reps, width), low),
            jax.ShapeDtypeStruct((reps // 2, half // reps, width), low),
        ),
        in_specs=[vmem] * 3 + [anywhere] * 13,
        out_specs=(vmem,) * 3 + (anywhere,) * 8,
        scratch_shapes=[
            pltpu.VMEM((half, early_width), low),
            pltpu.VMEM((rows, width), full),
            pltpu.VMEM((2, 2, row_count, width), low),
            pltpu.VMEM((2, row_count, width), low),
            pltpu.VMEM((rows, width), low),
            pltpu.VMEM((rows, width), low),
            pltpu.VMEM((groups, reps, row_count, LANES), low),
            pltpu.VMEM((groups, 4, row_count, width), low),
            pltpu.VMEM((groups, 4, row_count, width), low),
            pltpu.VMEM((groups, 4, row_count, own_width), low),
            pltpu.VMEM((groups, 4, row_count, 2 * own_width), low),
            pltpu.VMEM((2, half, width), low),
            pltpu.VMEM((2, half, 2 * own_width), low),
            pltpu.VMEM((own_width, width), low),
            pltpu.VMEM((2, 2, row_count, width), low),
            pltpu.VMEM((2, 2, row_count, width), low),
            pltpu.VMEM((2, row_count, width), low),
            pltpu.VMEM((2, row_count, width), low),
            pltpu.VMEM((2, 2, row_count, width), low),
            pltpu.SemaphoreType.DMA((13,)),
            pltpu.SemaphoreType.DMA((2,)),
            pltpu.SemaphoreType.DMA((27,)),
            pltpu.SemaphoreType.DMA((27,)),
            others,
            others,
            others,
            others,
            pltpu.SemaphoreType.DMA((2,)),
            pltpu.SemaphoreType.DMA((16,)),
            pltpu.SemaphoreType.DMA((2,)),
            pltpu.SemaphoreType.DMA((reps,)),
            pltpu.SemaphoreType.DMA((reps,)),
            pltpu.SemaphoreType.DMA((reps,)),
            pltpu.SemaphoreType.REGULAR,
        ],
        compiler_params=pltpu.CompilerParams(
            vmem_limit_bytes=62 * 1024 * 1024, collective_id=2, has_side_effects=True
        ),
        cost_estimate=pl.CostEstimate(
            flops=150 * 10**9, bytes_accessed=150 << 20, transcendentals=0
        ),
        name="mlp",
    )(heads, tokens, gain, out_rows, out_across, *output_parts, *in_parts, *down_parts)


def after_kernel(*refs):
    pass


def after(values, ahead):
    anywhere = pl.BlockSpec(memory_space=pl.ANY)
    return pl.pallas_call(
        after_kernel,
        out_shape=tuple(jax.ShapeDtypeStruct(one.shape, one.dtype) for one in values),
        in_specs=[anywhere] * (len(values) + 1),
        out_specs=(anywhere,) * len(values),
        input_output_aliases={at: at for at in range(len(values))},
        name="after",
    )(*values, ahead)


def heads_body(
    tokens,
    attn_gain,
    w_query,
    w_key,
    w_value,
    w_output,
    mlp_gain,
    w_gate,
    w_up,
    w_down,
    out_grad,
    lengths,
):
    groups, reps = lax.axis_size("grp"), lax.axis_size("rep")
    here, there = lax.axis_index("grp"), lax.axis_index("rep")
    micro_count, row_count, width = tokens.shape
    rows = micro_count * row_count
    hidden_width = w_gate.shape[1]
    own_width = hidden_width // (2 * groups)

    out_rows = out_grad.reshape(rows, width)
    (
        gathered_rows,
        qkv,
        w_heads,
        gate_own,
        gate_met,
        up_own,
        up_piece,
        down_first,
        down_second,
        output_part,
        out_own,
        gains,
    ) = gather_heads(
        tokens,
        (attn_gain, mlp_gain),
        w_query,
        w_key,
        w_value,
        w_gate,
        w_up,
        w_down,
        w_output,
        out_rows,
    )
    gain_one = gains[:, 0].reshape(width).astype(jnp.float32)
    gain_two = gains[:, 1].reshape(width).astype(jnp.float32)

    output_parts = (w_output, output_part, swap(output_part, 0, 2))
    in_parts = (gate_own, gate_met, swap(gate_met, 0, 2), up_own, swap(up_piece, 1, 0))
    down_parts = (down_first, down_second, swap(down_first, 1, 0))

    attended, out_heads, log_sum, query, key, value = attend(lengths, qkv)
    (
        block_out,
        grad_mixed,
        grad_heads,
        gate_kept,
        gate_sent,
        late_kept,
        late_sent,
        down_kept,
        down_sent,
        output_kept,
        output_sent,
    ) = mlp(
        attended,
        tokens.reshape(rows, width),
        jnp.broadcast_to(gain_two[None], (8, width)),
        out_rows,
        swap(out_own, 0, 4),
        output_parts,
        in_parts,
        down_parts,
    )

    own_rows = width // (groups * reps)
    by_owner = (2, 2, 2, 2, own_rows, -1)
    sums = (
        swap(gate_sent, 0, 8),
        swap(late_sent, 0, 2),
        swap(down_sent, 1, 0),
        swap(output_sent, 0, 4),
    )
    back = attend_back(lengths, query, key, value, out_heads, log_sum, grad_heads)
    gate_met, late_met, down_met, output_met = after(sums, back)
    token_grad, heads_grad, quad_grad, down_grad, output_grad = scatter_heads(
        back.reshape(reps, groups * row_count, 3 * LANES),
        w_heads,
        tokens.reshape(rows, width),
        grad_mixed,
        jnp.broadcast_to(gain_one[None], (8, width)),
        gathered_rows,
        (
            gate_kept.reshape(by_owner[1:]),
            gate_met.reshape(by_owner[1:]),
            late_kept.reshape(by_owner),
            late_met.reshape(by_owner),
            down_kept.reshape(2, 2, 2, own_rows, width),
            down_met.reshape(2, 2, 2, own_rows, width),
            output_kept.reshape(2, 2, 2, own_rows, width),
            output_met.reshape(2, 2, 2, own_rows, width),
        ),
    )

    def own_gain(gain):
        own = lax.dynamic_slice_in_dim(gain, there * own_rows, own_rows, axis=0)
        return jnp.broadcast_to(own.astype(jnp.float32)[:, None], (own_rows, LANES))

    (
        query_grad,
        key_grad,
        value_grad,
        gate_grad,
        up_grad,
        gain_sums,
        down_grad,
        output_grad,
        token_grad,
        block_out,
    ) = finish(
        heads_grad,
        quad_grad,
        down_grad,
        output_grad,
        token_grad,
        block_out,
        jnp.stack([own_gain(attn_gain), own_gain(mlp_gain)], axis=0),
        (w_query, w_key, w_value, w_gate, w_up),
    )
    block_shape = tokens.shape
    return (
        block_out.reshape(block_shape),
        token_grad.reshape(block_shape),
        gain_sums[0, :, 0],
        query_grad,
        key_grad,
        value_grad,
        output_grad,
        gain_sums[1, :, 0],
        gate_grad,
        up_grad,
        down_grad,
    )


def pick_body(*arrays):
    tokens = arrays[0]
    groups, reps = lax.axis_size("grp"), lax.axis_size("rep")
    fits = (
        groups == 2
        and tokens.shape[0] == groups
        and tokens.shape[2] == reps * LANES
        and reps == 16
        and reps & (reps - 1) == 0
        and tokens.shape[1] % UNIT_PAIR == 0
        and arrays[7].shape[1] == groups * reps * LANES
    )
    return heads_body(*arrays) if fits else ring_body(*arrays)


def solution(mesh):
    in_specs = (
        P(None, ("grp", "rep"), None),
        P("grp"),
        P("grp", None),
        P("grp", None),
        P("grp", None),
        P("grp", None),
        P("grp"),
        P("grp", None),
        P("grp", None),
        P("grp", None),
        P(None, ("grp", "rep"), None),
        P(),
    )
    out_specs = (
        P(None, ("grp", "rep"), None),
        P(None, ("grp", "rep"), None),
        P(("grp", "rep")),
        P(("grp", "rep"), None),
        P(("grp", "rep"), None),
        P(("grp", "rep"), None),
        P(("grp", "rep"), None),
        P(("grp", "rep")),
        P(("grp", "rep"), None),
        P(("grp", "rep"), None),
        P(("grp", "rep"), None),
    )
    return jax.shard_map(pick_body, mesh=mesh, in_specs=in_specs, out_specs=out_specs, check_vma=False)
```

```python
import functools
import math

import jax
import jax.numpy as jnp
from jax import lax
from jax.experimental import pallas as pl
from jax.experimental.pallas import tpu as pltpu
from jax.sharding import PartitionSpec as P

HD = 64
WINDOW = 2048


epsilon = 1e-05
rope_base = 10000.0
masked_score = -1e30
BOTH = ("grp", "rep")
LANES = 128
UNIT_BLOCK = 8
UNIT_PAIR = 16
KERNEL_VMEM = 56 * 1024 * 1024
SCATTER_REFS = 18


def from_behind(value, axis, steps):
    count = lax.axis_size(axis)
    first, last = (max(0, -steps), min(count, count - steps))
    return lax.ppermute(value, axis, [(source, source + steps) for source in range(first, last)])


def rms_scale(values):
    return lax.rsqrt(jnp.mean(values * values, axis=-1, keepdims=True) + epsilon)


def norm_backward(values, gain_full, grad_normed):
    inverse = rms_scale(values)
    normed = values * inverse
    gain_grad = jnp.sum(grad_normed * normed, axis=0)
    weighted = grad_normed * gain_full
    return (
        inverse * (weighted - normed * jnp.mean(weighted * normed, axis=-1, keepdims=True)),
        gain_grad,
    )


def rotary(values, cosine, sine_table):
    half_width = values.shape[-1] // 2
    first_half = values[..., :half_width]
    second_half = values[..., half_width:]
    return jnp.concatenate(
        [
            first_half * cosine - second_half * sine_table,
            second_half * cosine + first_half * sine_table,
        ],
        axis=-1,
    )


def pick_rows(rows_block, row_ids):
    return jnp.take(rows_block, row_ids, axis=0)


def take_rows(values, row_ids):
    return jax.vmap(pick_rows)(values, row_ids)


def gather_attn(attn_gain, w_query, w_key, w_value, w_output):
    return (
        lax.all_gather(attn_gain, "grp", axis=0, tiled=True),
        lax.all_gather(w_query, "grp", axis=0, tiled=True),
        lax.all_gather(w_key, "grp", axis=0, tiled=True),
        lax.all_gather(w_value, "grp", axis=0, tiled=True),
        lax.all_gather(w_output, "grp", axis=0, tiled=True),
    )


def gather_mlp(mlp_gain, w_gate, w_up, w_down):
    return (
        lax.all_gather(mlp_gain, "grp", axis=0, tiled=True),
        lax.all_gather(w_gate, "grp", axis=0, tiled=True),
        lax.all_gather(w_up, "grp", axis=0, tiled=True),
        lax.all_gather(w_down, "grp", axis=0, tiled=True),
    )


def reduce_attn(gain_grad, query_grad, key_grad, value_grad, output_grad):
    return (
        lax.psum_scatter(gain_grad, ("grp", "rep"), scatter_dimension=0, tiled=True),
        lax.psum_scatter(query_grad, ("grp", "rep"), scatter_dimension=0, tiled=True),
        lax.psum_scatter(key_grad, ("grp", "rep"), scatter_dimension=0, tiled=True),
        lax.psum_scatter(value_grad, ("grp", "rep"), scatter_dimension=0, tiled=True),
        lax.psum_scatter(output_grad, ("grp", "rep"), scatter_dimension=0, tiled=True),
    )


def reduce_mlp(gain_grad, gate_grad, up_grad, down_grad):
    return (
        lax.psum_scatter(gain_grad, ("grp", "rep"), scatter_dimension=0, tiled=True),
        lax.psum_scatter(gate_grad, ("grp", "rep"), scatter_dimension=0, tiled=True),
        lax.psum_scatter(up_grad, ("grp", "rep"), scatter_dimension=0, tiled=True),
        lax.psum_scatter(down_grad, ("grp", "rep"), scatter_dimension=0, tiled=True),
    )


def pass_on(carried, unused):
    arrived = from_behind(carried, ("grp", "rep"), 1)
    return (arrived, arrived)


def pass_back(running, portion):
    arrived = from_behind(running.astype(jnp.bfloat16), ("grp", "rep"), -1).astype(running.dtype)
    return (arrived + portion, None)


def ring_body(
    tokens,
    attn_gain,
    w_query,
    w_key,
    w_value,
    w_output,
    mlp_gain,
    w_gate,
    w_up,
    w_down,
    out_grad,
    lengths,
):
    devices = lax.axis_size(("grp", "rep"))
    rank_here = lax.axis_index(("grp", "rep"))
    micro_count, row_count, model_width = tokens.shape
    per_dev = row_count // devices
    head_count = model_width // HD
    reach_count = (WINDOW + row_count - 2) // row_count
    head_group = math.gcd(head_count, 4)
    group_count = head_count // head_group
    score_scale = 1.0 / math.sqrt(HD)
    unit_ids = jnp.arange(row_count, dtype=jnp.int32)
    seq_ends = jnp.cumsum(lengths, axis=1)
    starts = seq_ends - lengths
    seq_order = jnp.arange(lengths.shape[1], dtype=jnp.int32)
    earlier = seq_order[None, :] < seq_order[:, None]
    dealt_start = jnp.sum(jnp.where(earlier[None], lengths[:, None, :], 0), axis=2)
    seq_of = jnp.sum((seq_ends[:, None, :] <= unit_ids[None, :, None]).astype(jnp.int32), axis=2)
    seq_dealt = jnp.take_along_axis(dealt_start, seq_of, axis=1)
    unit_of = seq_dealt + unit_ids[None, :] - jnp.take_along_axis(starts, seq_of, axis=1)
    micro_ids = jnp.arange(micro_count, dtype=jnp.int32)[:, None]
    source_unit = (
        jnp.zeros((micro_count, row_count), jnp.int32)
        .at[micro_ids, unit_of]
        .set(jnp.broadcast_to(unit_ids[None, :], unit_of.shape))
    )
    unit_begin = (
        jnp.zeros((micro_count, row_count), jnp.int32).at[micro_ids, unit_of].set(seq_dealt)
    )
    local_ids = jnp.arange(row_count, dtype=jnp.int32)
    local_step = local_ids % per_dev
    local_source = local_ids // per_dev
    distance = jnp.arange(reach_count + 1, dtype=jnp.int32)
    owner_dev = rank_here - distance
    owner_ok = owner_dev >= 0
    owner_unit = jnp.maximum(owner_dev, 0)[:, None] * per_dev + local_step[None, :]
    key_begin = unit_begin[:, owner_unit]
    key_pos = (owner_unit[None] - key_begin) * devices + local_source[None, None, :]
    query_begin = key_begin[:, 0]
    query_pos = key_pos[:, 0]
    allowed = (
        owner_ok[None, None, :, None]
        & (query_begin[:, :, None, None] == key_begin[:, None, :, :])
        & (key_pos[:, None, :, :] <= query_pos[:, :, None, None])
        & (query_pos[:, :, None, None] - key_pos[:, None, :, :] < WINDOW)
    )
    mask_full = allowed[:, None]
    half_width = HD // 2
    frequency = jnp.power(rope_base, -2.0 * jnp.arange(half_width, dtype=jnp.float32) / HD)
    angles = query_pos.astype(jnp.float32)[:, :, None] * frequency[None, None, :]
    cosine = jnp.cos(angles)[:, :, None, :]
    sine_table = jnp.sin(angles)[:, :, None, :]
    head_shape = (micro_count, row_count, head_count, HD)
    block_shape = (micro_count, row_count, model_width)
    gathered = gather_attn(attn_gain, w_query, w_key, w_value, w_output)
    gain_one = gathered[0].astype(jnp.float32)
    inputs = tokens.astype(jnp.float32).reshape(micro_count * row_count, model_width)
    normed_in = (inputs * rms_scale(inputs) * gain_one).astype(jnp.bfloat16)
    queries = jnp.dot(normed_in, gathered[1], preferred_element_type=jnp.float32).astype(
        jnp.bfloat16
    )
    keys_in = jnp.dot(normed_in, gathered[2], preferred_element_type=jnp.float32).astype(
        jnp.bfloat16
    )
    values_in = jnp.dot(normed_in, gathered[3], preferred_element_type=jnp.float32).astype(
        jnp.bfloat16
    )
    dealt = (
        lax.all_to_all(
            take_rows(queries.reshape(block_shape), source_unit),
            ("grp", "rep"),
            split_axis=1,
            concat_axis=1,
            tiled=True,
        ),
        lax.all_to_all(
            take_rows(keys_in.reshape(block_shape), source_unit),
            ("grp", "rep"),
            split_axis=1,
            concat_axis=1,
            tiled=True,
        ),
        lax.all_to_all(
            take_rows(values_in.reshape(block_shape), source_unit),
            ("grp", "rep"),
            split_axis=1,
            concat_axis=1,
            tiled=True,
        ),
    )
    rot_q = rotary(dealt[0].reshape(head_shape).astype(jnp.float32), cosine, sine_table).astype(
        jnp.bfloat16
    )
    rot_k = rotary(dealt[1].reshape(head_shape).astype(jnp.float32), cosine, sine_table).astype(
        jnp.bfloat16
    )
    own_pair = jnp.stack([rot_k.reshape(block_shape), dealt[2]], axis=0)
    last_pair, farther = lax.scan(pass_on, own_pair, None, length=reach_count)
    context = jnp.concatenate([own_pair[None], farther], axis=0).reshape(
        reach_count + 1, 2, micro_count, row_count, head_count, HD
    )

    def group_scores(query_part, pair_part):
        scores = (
            jnp.einsum(
                "mqge,dmkge->mgqdk", query_part, pair_part[:, 0], preferred_element_type=jnp.float32
            )
            * score_scale
        )
        return jnp.where(mask_full, scores, masked_score)

    def forward_group(group_index, carried):
        attended_all, log_all = carried
        head_start = group_index * head_group
        query_part = lax.dynamic_slice_in_dim(rot_q, head_start, head_group, axis=2)
        pair_part = lax.dynamic_slice_in_dim(context, head_start, head_group, axis=4)
        scores = group_scores(query_part, pair_part)
        row_max = jnp.max(scores, axis=(3, 4), keepdims=True)
        weights_exp = jnp.exp(scores - row_max)
        row_sum = jnp.sum(weights_exp, axis=(3, 4), keepdims=True)
        soft_probs = (weights_exp / row_sum).astype(jnp.bfloat16)
        attended = jnp.einsum(
            "mgqdk,dmkge->mqge", soft_probs, pair_part[:, 1], preferred_element_type=jnp.float32
        ).astype(jnp.bfloat16)
        attended_all = lax.dynamic_update_slice_in_dim(attended_all, attended, head_start, axis=2)
        log_all = lax.dynamic_update_slice_in_dim(
            log_all, row_max + jnp.log(row_sum), head_start, axis=1
        )
        return (attended_all, log_all)

    attended_heads, log_sum = lax.fori_loop(
        0,
        group_count,
        forward_group,
        (
            jnp.zeros(head_shape, jnp.bfloat16),
            jnp.zeros((micro_count, head_count, row_count, 1, 1), jnp.float32),
        ),
    )
    returned = lax.all_to_all(
        attended_heads.reshape(block_shape), ("grp", "rep"), split_axis=1, concat_axis=1, tiled=True
    )
    attn_rows = take_rows(returned, unit_of).reshape(micro_count * row_count, model_width)
    mixed = inputs + jnp.dot(attn_rows, gathered[4], preferred_element_type=jnp.float32)
    mlp_set = gather_mlp(mlp_gain, w_gate, w_up, w_down)
    gain_two = mlp_set[0].astype(jnp.float32)
    normed_mid = (mixed * rms_scale(mixed) * gain_two).astype(jnp.bfloat16)
    gate_pre = jnp.dot(normed_mid, mlp_set[1], preferred_element_type=jnp.float32)
    up_pre = jnp.dot(normed_mid, mlp_set[2], preferred_element_type=jnp.float32)
    gate_sig = jax.nn.sigmoid(gate_pre)
    gate_silu = gate_pre * gate_sig
    hidden = (gate_silu * up_pre).astype(jnp.bfloat16)
    block_out = (mixed + jnp.dot(hidden, mlp_set[3], preferred_element_type=jnp.float32)).astype(
        jnp.bfloat16
    )
    mlp_set = gather_mlp(mlp_gain, w_gate, w_up, w_down)
    out_rows = out_grad.reshape(micro_count * row_count, model_width)
    down_grad = jnp.einsum("tf,td->fd", hidden, out_rows, preferred_element_type=jnp.float32)
    grad_hidden = jnp.einsum("td,fd->tf", out_rows, mlp_set[3], preferred_element_type=jnp.float32)
    grad_gate = (grad_hidden * up_pre * gate_sig * (1.0 + gate_pre * (1.0 - gate_sig))).astype(
        jnp.bfloat16
    )
    grad_up = (grad_hidden * gate_silu).astype(jnp.bfloat16)
    gate_grad = jnp.einsum("td,tf->df", normed_mid, grad_gate, preferred_element_type=jnp.float32)
    up_grad = jnp.einsum("td,tf->df", normed_mid, grad_up, preferred_element_type=jnp.float32)
    grad_mid = jnp.einsum(
        "tf,df->td", grad_gate, mlp_set[1], preferred_element_type=jnp.float32
    ) + jnp.einsum("tf,df->td", grad_up, mlp_set[2], preferred_element_type=jnp.float32)
    grad_norm_mid, mlp_gain_grad = norm_backward(mixed, gain_two, grad_mid)
    grad_mixed = out_rows.astype(jnp.float32) + grad_norm_mid
    mlp_sums = reduce_mlp(mlp_gain_grad, gate_grad, up_grad, down_grad)
    gathered = gather_attn(attn_gain, w_query, w_key, w_value, w_output)
    grad_branch = grad_mixed.astype(jnp.bfloat16)
    output_grad = jnp.einsum(
        "td,te->de", attn_rows, grad_branch, preferred_element_type=jnp.float32
    )
    grad_att = jnp.einsum(
        "te,de->td", grad_branch, gathered[4], preferred_element_type=jnp.float32
    ).astype(jnp.bfloat16)
    grad_dealt = lax.all_to_all(
        take_rows(grad_att.reshape(block_shape), source_unit),
        ("grp", "rep"),
        split_axis=1,
        concat_axis=1,
        tiled=True,
    )
    grad_heads = grad_dealt.reshape(head_shape)

    def backward_group(group_index, carried):
        query_total, pair_total = carried
        head_start = group_index * head_group
        query_part = lax.dynamic_slice_in_dim(rot_q, head_start, head_group, axis=2)
        grad_part = lax.dynamic_slice_in_dim(grad_heads, head_start, head_group, axis=2)
        pair_part = lax.dynamic_slice_in_dim(context, head_start, head_group, axis=4)
        log_part = lax.dynamic_slice_in_dim(log_sum, head_start, head_group, axis=1)
        scores = group_scores(query_part, pair_part)
        soft_probs = jnp.exp(scores - log_part)
        grad_probs = jnp.einsum(
            "mqge,dmkge->mgqdk", grad_part, pair_part[:, 1], preferred_element_type=jnp.float32
        )
        inner_sum = jnp.sum(soft_probs * grad_probs, axis=(3, 4), keepdims=True)
        grad_scores = (soft_probs * (grad_probs - inner_sum)).astype(jnp.bfloat16)
        query_piece = (
            jnp.einsum(
                "mgqdk,dmkge->mqge",
                grad_scores,
                pair_part[:, 0],
                preferred_element_type=jnp.float32,
            )
            * score_scale
        )
        key_part = (
            jnp.einsum(
                "mgqdk,mqge->dmkge", grad_scores, query_part, preferred_element_type=jnp.float32
            )
            * score_scale
        )
        value_part = jnp.einsum(
            "mgqdk,mqge->dmkge",
            soft_probs.astype(jnp.bfloat16),
            grad_part,
            preferred_element_type=jnp.float32,
        )
        query_total = lax.dynamic_update_slice_in_dim(query_total, query_piece, head_start, axis=2)
        pair_total = lax.dynamic_update_slice_in_dim(
            pair_total, jnp.stack([key_part, value_part], axis=1), head_start, axis=4
        )
        return (query_total, pair_total)

    query_total, pair_total = lax.fori_loop(
        0,
        group_count,
        backward_group,
        (
            jnp.zeros(head_shape, jnp.float32),
            jnp.zeros((reach_count + 1, 2) + head_shape, jnp.float32),
        ),
    )
    partials = pair_total.reshape(reach_count + 1, 2, micro_count, row_count, model_width)
    own_total, unused_out = lax.scan(
        pass_back, partials[reach_count], partials[:reach_count], reverse=True
    )
    query_back = rotary(query_total, cosine, -sine_table).astype(jnp.bfloat16)
    key_back = rotary(own_total[0].reshape(head_shape), cosine, -sine_table).astype(jnp.bfloat16)
    value_back = own_total[1].astype(jnp.bfloat16)
    grad_back = (
        lax.all_to_all(
            query_back.reshape(block_shape), ("grp", "rep"), split_axis=1, concat_axis=1, tiled=True
        ),
        lax.all_to_all(
            key_back.reshape(block_shape), ("grp", "rep"), split_axis=1, concat_axis=1, tiled=True
        ),
        lax.all_to_all(value_back, ("grp", "rep"), split_axis=1, concat_axis=1, tiled=True),
    )
    query_rows = take_rows(grad_back[0], unit_of).reshape(micro_count * row_count, model_width)
    key_rows = take_rows(grad_back[1], unit_of).reshape(micro_count * row_count, model_width)
    value_rows = take_rows(grad_back[2], unit_of).reshape(micro_count * row_count, model_width)
    query_grad = jnp.einsum("td,te->de", normed_in, query_rows, preferred_element_type=jnp.float32)
    key_grad = jnp.einsum("td,te->de", normed_in, key_rows, preferred_element_type=jnp.float32)
    value_grad = jnp.einsum("td,te->de", normed_in, value_rows, preferred_element_type=jnp.float32)
    grad_in = jnp.einsum("te,de->td", query_rows, gathered[1], preferred_element_type=jnp.float32)
    grad_in = grad_in + jnp.einsum(
        "te,de->td", key_rows, gathered[2], preferred_element_type=jnp.float32
    )
    grad_in = grad_in + jnp.einsum(
        "te,de->td", value_rows, gathered[3], preferred_element_type=jnp.float32
    )
    grad_norm_in, attn_gain_grad = norm_backward(inputs, gain_one, grad_in)
    token_grad = (grad_mixed + grad_norm_in).astype(jnp.bfloat16)
    attn_sums = reduce_attn(attn_gain_grad, query_grad, key_grad, value_grad, output_grad)
    return (
        block_out.reshape(block_shape),
        token_grad.reshape(block_shape),
        attn_sums[0],
        attn_sums[1],
        attn_sums[2],
        attn_sums[3],
        attn_sums[4],
        mlp_sums[0],
        mlp_sums[1],
        mlp_sums[2],
        mlp_sums[3],
    )


def contract(left_side, right_side, left_dim, right_dim, kind=jnp.float32):
    return lax.dot_general(
        left_side,
        right_side,
        (((left_dim,), (right_dim,)), ((), ())),
        preferred_element_type=jnp.float32,
    ).astype(kind)


def swap_halves(values):
    lane = lax.broadcasted_iota(jnp.int32, values.shape, 1)
    ahead = pltpu.roll(values, LANES - HD // 2, 1)
    behind = pltpu.roll(values, HD // 2, 1)
    return jnp.where(lane % HD < HD // 2, -ahead, behind)


def fill_tables(lengths_ref, begin_at, cos_unit, sin_unit, cos_part, sin_part):
    parts, units = cos_part.shape[0], cos_unit.shape[0]
    here = lax.axis_index("grp")

    def frequency(shape):
        lane = lax.broadcasted_iota(jnp.int32, shape, 1) % (HD // 2)
        return jnp.exp(lane.astype(jnp.float32) * (-2.0 * math.log(rope_base) / HD))

    unit = lax.broadcasted_iota(jnp.int32, (units, LANES), 0)
    begin = jnp.zeros((units, LANES), jnp.int32)
    end = 0
    for seq in range(lengths_ref.shape[1]):
        end = end + lengths_ref[here, seq]
        begin = jnp.where(unit >= end, end, begin)
    begin_at[...] = begin
    angle = ((unit - begin) * parts).astype(jnp.float32) * frequency((units, LANES))
    cos_unit[...] = jnp.cos(angle)
    sin_unit[...] = jnp.sin(angle)
    part = lax.broadcasted_iota(jnp.int32, (parts, LANES), 0).astype(jnp.float32)
    angle = part * frequency((parts, LANES))
    cos_part[...] = jnp.cos(angle)
    sin_part[...] = jnp.sin(angle)


def begin_of(lengths_ref, unit):
    here = lax.axis_index("grp")
    begin, end = 0, 0
    for seq in range(lengths_ref.shape[1]):
        end = end + lengths_ref[here, seq]
        begin = jnp.where(unit >= end, end, begin)
    return begin


def key_range(lengths_ref, at, parts, block):
    first_unit = at * UNIT_BLOCK
    last_unit = first_unit + UNIT_BLOCK - 1
    least = jnp.maximum(begin_of(lengths_ref, first_unit) * parts, at * block - (WINDOW - 1))
    most = jnp.maximum(
        begin_of(lengths_ref, last_unit) * parts, (at + 1) * block - 1 - (WINDOW - 1)
    )
    first = jnp.maximum(least, 0) // block
    return first, jnp.minimum(jnp.maximum((most + block - 1) // block, first), at)


def low_of(begin_at, at, parts):
    begin = begin_at[pl.ds(pl.multiple_of(at * UNIT_BLOCK, UNIT_BLOCK), UNIT_BLOCK), :] * parts
    shape = (parts, UNIT_BLOCK, LANES)
    part = lax.broadcasted_iota(jnp.int32, shape, 0)
    unit = lax.broadcasted_iota(jnp.int32, shape, 1) + at * UNIT_BLOCK
    low = jnp.maximum(begin[None], unit * parts + part - (WINDOW - 1))
    return low.reshape(parts * UNIT_BLOCK, LANES).astype(jnp.float32)


def slot_of(part):
    groups, reps = lax.axis_size("grp"), lax.axis_size("rep")
    offset = (part % reps) ^ lax.axis_index("rep")
    return offset * groups + ((part // reps) ^ lax.axis_index("grp"))


def pair_angles(unit_at, cos_unit, sin_unit, cos_part, sin_part):
    unit_cos = cos_unit[pl.ds(unit_at, UNIT_PAIR), :][None]
    unit_sin = sin_unit[pl.ds(unit_at, UNIT_PAIR), :][None]
    part_cos = cos_part[...][:, None, :]
    part_sin = sin_part[...][:, None, :]
    cosine = unit_cos * part_cos - unit_sin * part_sin
    sine = unit_sin * part_cos + unit_cos * part_sin
    return cosine, sine


def key_offsets(block):
    row = lax.broadcasted_iota(jnp.int32, (block, block), 0)
    return (row % UNIT_BLOCK) * (block // UNIT_BLOCK) + row // UNIT_BLOCK


def query_offsets(block):
    column = lax.broadcasted_iota(jnp.int32, (block, block), 1)
    return (column % UNIT_BLOCK) * (block // UNIT_BLOCK) + column // UNIT_BLOCK


def attend_kernel(
    lengths_ref,
    qkv_ref,
    att_ref,
    out_ref,
    log_ref,
    query_ref,
    key_ref,
    value_ref,
    query_heads,
    key_t,
    tops,
    sums,
    totals,
    lows,
    causal_at,
    key_at,
    begin_at,
    cos_unit,
    sin_unit,
    cos_part,
    sin_part,
):
    parts, units, _ = qkv_ref.shape
    block = parts * UNIT_BLOCK
    pairs = units // UNIT_PAIR
    halves = UNIT_PAIR // UNIT_BLOCK
    wide = block // LANES
    fill_tables(lengths_ref, begin_at, cos_unit, sin_unit, cos_part, sin_part)
    key_at[...] = query_offsets(block).astype(jnp.float32)
    causal_at[...] = jnp.where(query_offsets(block) <= key_offsets(block), 0.0, masked_score)

    def lay_out(pair, unused):
        unit_at = pl.multiple_of(pair * UNIT_PAIR, UNIT_PAIR)
        rows = jnp.stack(
            [qkv_ref[slot_of(part), pl.ds(unit_at, UNIT_PAIR), :] for part in range(parts)]
        )
        cosine, sine = pair_angles(unit_at, cos_unit, sin_unit, cos_part, sin_part)
        flat = (parts * UNIT_PAIR, LANES)
        cosine = cosine.reshape(flat)
        sine = sine.reshape(flat)

        def rotated(values):
            values = values.astype(jnp.float32).reshape(flat)
            turned = values * cosine + swap_halves(values) * sine
            return turned.reshape(parts, UNIT_PAIR, LANES)

        query = rotated(rows[:, :, :LANES]) * (1.0 / math.sqrt(HD))
        key = rotated(rows[:, :, LANES : 2 * LANES])
        value = rows[:, :, 2 * LANES :].astype(jnp.float32)
        for half in range(halves):
            at = pair * halves + half
            cut = slice(half * UNIT_BLOCK, (half + 1) * UNIT_BLOCK)
            query_rows = query[:, cut].reshape(block, LANES)
            key_rows = key[:, cut].reshape(block, LANES)
            query_ref[at] = query_rows.astype(jnp.bfloat16)
            key_ref[at] = key_rows.astype(jnp.bfloat16)
            value_ref[at] = value[:, cut].reshape(block, LANES).astype(jnp.bfloat16)
            lane = lax.broadcasted_iota(jnp.int32, query_rows.shape, 1)
            query_heads[at, 0] = jnp.where(lane < HD, query_rows, 0.0).astype(jnp.bfloat16)
            query_heads[at, 1] = jnp.where(lane < HD, 0.0, query_rows).astype(jnp.bfloat16)
            key_t[at] = jnp.transpose(key_rows).astype(jnp.bfloat16)
        return unused

    lax.fori_loop(0, pairs, lay_out, 0)

    def query_pair(pair, unused):
        ids = [pair * halves + half for half in range(halves)]
        for half, at in enumerate(ids):
            lows[half] = low_of(begin_at, at, parts)
        first, _ = key_range(lengths_ref, ids[0], parts, block)
        _, plain = key_range(lengths_ref, ids[-1], parts, block)
        plain = jnp.minimum(plain, ids[0])

        def wider(value):
            return jnp.concatenate([value] * wide, axis=1)

        def scores_of(half, head, key_block, causal, bounded):
            scores = jnp.dot(
                query_heads[ids[half], head], key_t[key_block], preferred_element_type=jnp.float32
            )
            if causal:
                scores = scores + causal_at[...]
            if bounded:
                bound = wider(lows[half] - (key_block * block).astype(jnp.float32))
                scores = jnp.where(key_at[...] >= bound, scores, masked_score)
            return scores

        def folded(combine, values):
            result = values[:, :LANES]
            for at in range(1, wide):
                result = combine(result, values[:, at * LANES : (at + 1) * LANES])
            return result

        def top_step(half, head, key_block, causal, bounded, fresh):
            high = folded(jnp.maximum, scores_of(half, head, key_block, causal, bounded))
            tops[half, head] = high if fresh else jnp.maximum(tops[half, head], high)

        def sum_step(half, head, key_block, causal, bounded, fresh):
            scores = scores_of(half, head, key_block, causal, bounded)
            weights = jnp.exp(scores - wider(tops[half, head]))
            part = folded(jnp.add, weights)
            product = jnp.dot(
                weights.astype(jnp.bfloat16),
                value_ref[key_block],
                preferred_element_type=jnp.float32,
            )
            sums[half, head] = part if fresh else sums[half, head] + part
            totals[half, head] = product if fresh else totals[half, head] + product

        def over_keys(step):
            for half, at in enumerate(ids):
                for head in range(2):
                    step(half, head, at, True, True, True)
                    for earlier in ids[:half]:
                        step(half, head, earlier, False, True, False)

            def all_steps(bounded):
                def go(key_block, unused):
                    for half in range(halves):
                        for head in range(2):
                            step(half, head, key_block, False, bounded, False)
                    return unused

                return go

            lax.fori_loop(first, plain, all_steps(True), 0)
            lax.fori_loop(plain, ids[0], all_steps(False), 0)

        over_keys(top_step)
        for half in range(halves):
            for head in range(2):
                high = jnp.max(tops[half, head], axis=1, keepdims=True)
                tops[half, head] = jnp.broadcast_to(high, (block, LANES))
        over_keys(sum_step)
        done = []
        for half, at in enumerate(ids):
            rows = []
            for head in range(2):
                total = jnp.broadcast_to(
                    jnp.sum(sums[half, head], axis=1, keepdims=True), (block, LANES)
                )
                rows.append(totals[half, head] / total)
                log = jnp.transpose(tops[half, head] + jnp.log(total))
                log_ref[at, head : head + 1, :] = log[0:1]
            lane = lax.broadcasted_iota(jnp.int32, (block, LANES), 1)
            both = jnp.where(lane < HD, rows[0], rows[1])
            out_ref[at] = jnp.transpose(both)
            done.append(both.reshape(parts, UNIT_BLOCK, LANES))
        unit_at = pl.multiple_of(pair * UNIT_PAIR, UNIT_PAIR)
        att_ref[:, pl.ds(unit_at, UNIT_PAIR), :] = jnp.concatenate(done, axis=1).astype(
            jnp.bfloat16
        )
        return unused

    lax.fori_loop(0, pairs, query_pair, 0)


def attend_back_kernel(
    lengths_ref,
    query_ref,
    key_ref,
    value_ref,
    out_ref,
    log_ref,
    grad_ref,
    back_ref,
    key_t,
    key_total,
    value_total,
    key_at,
    causal_at,
    begin_at,
    cos_unit,
    sin_unit,
    cos_part,
    sin_part,
):
    parts, units, _ = grad_ref.shape
    block = parts * UNIT_BLOCK
    pairs = units // UNIT_PAIR
    halves = UNIT_PAIR // UNIT_BLOCK
    fill_tables(lengths_ref, begin_at, cos_unit, sin_unit, cos_part, sin_part)
    key_at[...] = key_offsets(block).astype(jnp.float32)
    causal_at[...] = jnp.where(key_offsets(block) <= query_offsets(block), 0.0, masked_score)

    def lay_out(at, unused):
        key_t[at] = jnp.concatenate(split_heads(key_ref[at].astype(jnp.float32), 1), axis=0)
        key_total[at] = jnp.zeros((block, LANES), jnp.float32)
        value_total[at] = jnp.zeros((block, LANES), jnp.float32)
        return unused

    def split_heads(values, axis):
        place = lax.broadcasted_iota(jnp.int32, values.shape, axis)
        zero = jnp.zeros_like(values)
        return [
            jnp.where(place < HD, values, zero).astype(jnp.bfloat16),
            jnp.where(place < HD, zero, values).astype(jnp.bfloat16),
        ]

    lax.fori_loop(0, pairs * halves, lay_out, 0)

    def prepare(at, grad_rows):
        query_rows = query_ref[at].astype(jnp.float32)
        grad_turned = jnp.transpose(grad_rows)
        product = grad_turned * out_ref[at]
        return dict(
            low=jnp.transpose(low_of(begin_at, at, parts))[0:1],
            query=jnp.concatenate(split_heads(query_rows, 1), axis=0),
            grad=jnp.concatenate(split_heads(grad_rows, 1), axis=0),
            query_t=split_heads(jnp.transpose(query_rows), 0),
            grad_t=split_heads(grad_turned, 0),
            inner=[
                jnp.sum(product[head * HD : (head + 1) * HD], axis=0, keepdims=True)
                for head in range(2)
            ],
            logs=[log_ref[at, head : head + 1, :] for head in range(2)],
        )

    def step(held, key_block, carried, causal, bounded):
        probs, slopes, new = [], [], []
        for head in range(2):
            scores = jnp.dot(
                key_ref[key_block], held["query_t"][head], preferred_element_type=jnp.float32
            )
            if causal:
                scores = scores + causal_at[...]
            if bounded:
                scores = jnp.where(
                    key_at[...] >= held["low"] - (key_block * block).astype(jnp.float32), scores, masked_score
                )
            soft = jnp.exp(scores - held["logs"][head])
            grad_probs = jnp.dot(
                value_ref[key_block], held["grad_t"][head], preferred_element_type=jnp.float32
            )
            slope = soft * (grad_probs - held["inner"][head])
            probs.append(soft.astype(jnp.bfloat16))
            slopes.append(slope.astype(jnp.bfloat16))
            new.append(jnp.transpose(slope).astype(jnp.bfloat16))
        total = carried + jnp.dot(
            jnp.concatenate(new, axis=1), key_t[key_block], preferred_element_type=jnp.float32
        )
        return total, probs, slopes

    def add_key(key_block, held, probs, slopes):
        value_total[key_block] += jnp.dot(
            jnp.concatenate(probs, axis=1),
            jnp.concatenate([one["grad"] for one in held], axis=0),
            preferred_element_type=jnp.float32,
        )
        key_total[key_block] += jnp.dot(
            jnp.concatenate(slopes, axis=1),
            jnp.concatenate([one["query"] for one in held], axis=0),
            preferred_element_type=jnp.float32,
        )

    def query_blocks(pair, grads):
        ids = [pair * halves + half for half in range(halves)]
        held = [prepare(at, rows) for at, rows in zip(ids, grads)]
        states = []
        for half, at in enumerate(ids):
            state, probs, slopes = step(
                held[half], at, jnp.zeros((block, LANES), jnp.float32), True, True
            )
            add_key(at, held[half : half + 1], probs, slopes)
            for earlier in ids[:half]:
                state, probs, slopes = step(held[half], earlier, state, False, True)
                add_key(earlier, held[half : half + 1], probs, slopes)
            states.append(state)

        def all_steps(bounded):
            def run(key_block, carried):
                new, probs, slopes = [], [], []
                for half in range(halves):
                    state, prob, slope = step(held[half], key_block, carried[half], False, bounded)
                    new.append(state)
                    probs += prob
                    slopes += slope
                add_key(key_block, held, probs, slopes)
                return tuple(new)

            return run

        first, _ = key_range(lengths_ref, ids[0], parts, block)
        _, plain = key_range(lengths_ref, ids[-1], parts, block)
        plain = jnp.minimum(plain, ids[0])
        states = lax.fori_loop(first, plain, all_steps(True), tuple(states))
        states = lax.fori_loop(plain, ids[0], all_steps(False), states)
        return [state * (1.0 / math.sqrt(HD)) for state in states]

    def turn_back(rows, cosine, sine):
        flat = (parts * UNIT_PAIR, LANES)
        rows = jnp.concatenate(
            [one.reshape(parts, UNIT_BLOCK, LANES) for one in rows], axis=1
        ).reshape(flat)
        turned = rows * cosine.reshape(flat) - swap_halves(rows) * sine.reshape(flat)
        return turned.reshape(parts, UNIT_PAIR, LANES).astype(jnp.bfloat16)

    def put(values, unit_at, lane_at):
        for part in range(parts):
            back_ref[slot_of(part), pl.ds(unit_at, UNIT_PAIR), pl.ds(lane_at, LANES)] = values[part]

    def query_pair(pair, unused):
        unit_at = pl.multiple_of(pair * UNIT_PAIR, UNIT_PAIR)
        grads = grad_ref[:, pl.ds(unit_at, UNIT_PAIR), :].astype(jnp.float32)
        done = query_blocks(
            pair,
            [
                grads[:, half * UNIT_BLOCK : (half + 1) * UNIT_BLOCK].reshape(block, LANES)
                for half in range(halves)
            ],
        )
        cosine, sine = pair_angles(unit_at, cos_unit, sin_unit, cos_part, sin_part)
        put(turn_back(done, cosine, sine), unit_at, 0)
        return unused

    lax.fori_loop(0, pairs, query_pair, 0)

    def key_pair(pair, unused):
        unit_at = pl.multiple_of(pair * UNIT_PAIR, UNIT_PAIR)
        cosine, sine = pair_angles(unit_at, cos_unit, sin_unit, cos_part, sin_part)
        ids = [pair * halves + half for half in range(halves)]
        put(turn_back([key_total[at] for at in ids], cosine, sine), unit_at, LANES)
        values = jnp.concatenate(
            [value_total[at].reshape(parts, UNIT_BLOCK, LANES) for at in ids], axis=1
        ).astype(jnp.bfloat16)
        put(values, unit_at, 2 * LANES)
        return unused

    lax.fori_loop(0, pairs, key_pair, 0)


def table_shapes(parts, units):
    table = pltpu.VMEM((units, LANES), jnp.float32)
    row = pltpu.VMEM((parts, LANES), jnp.float32)
    return [pltpu.VMEM((units, LANES), jnp.int32), table, table, row, row]


def attend(lengths, qkv):
    parts, units, _ = qkv.shape
    block = parts * UNIT_BLOCK
    blocks = units // UNIT_BLOCK
    smem = pl.BlockSpec(memory_space=pltpu.SMEM)
    vmem = pl.BlockSpec(memory_space=pltpu.VMEM)
    rows = jax.ShapeDtypeStruct((blocks, block, LANES), jnp.bfloat16)
    halves = UNIT_PAIR // UNIT_BLOCK
    held = pltpu.VMEM((halves, 2, block, LANES), jnp.float32)
    return pl.pallas_call(
        attend_kernel,
        out_shape=(
            jax.ShapeDtypeStruct((parts, units, LANES), jnp.bfloat16),
            jax.ShapeDtypeStruct((blocks, LANES, block), jnp.float32),
            jax.ShapeDtypeStruct((blocks, 8, block), jnp.float32),
            rows,
            rows,
            rows,
        ),
        in_specs=[smem, vmem],
        out_specs=(vmem,) * 6,
        scratch_shapes=[
            pltpu.VMEM((blocks, 2, block, LANES), jnp.bfloat16),
            pltpu.VMEM((blocks, LANES, block), jnp.bfloat16),
            held,
            held,
            held,
            pltpu.VMEM((halves, block, LANES), jnp.float32),
            pltpu.VMEM((block, block), jnp.float32),
            pltpu.VMEM((block, block), jnp.float32),
        ]
        + table_shapes(parts, units),
        compiler_params=pltpu.CompilerParams(vmem_limit_bytes=KERNEL_VMEM),
        cost_estimate=pl.CostEstimate(
            flops=20 * 10**9, bytes_accessed=16 << 20, transcendentals=20 * 10**6
        ),
        name="attend",
    )(lengths, qkv)


def attend_back(lengths, query, key, value, out, log, grad):
    parts, units, _ = grad.shape
    block = parts * UNIT_BLOCK
    blocks = units // UNIT_BLOCK
    smem = pl.BlockSpec(memory_space=pltpu.SMEM)
    vmem = pl.BlockSpec(memory_space=pltpu.VMEM)
    return pl.pallas_call(
        attend_back_kernel,
        out_shape=jax.ShapeDtypeStruct((parts, units, 3 * LANES), jnp.bfloat16),
        in_specs=[smem] + [vmem] * 6,
        out_specs=vmem,
        scratch_shapes=[
            pltpu.VMEM((blocks, 2 * block, LANES), jnp.bfloat16),
            pltpu.VMEM((blocks, block, LANES), jnp.float32),
            pltpu.VMEM((blocks, block, LANES), jnp.float32),
            pltpu.VMEM((block, block), jnp.float32),
            pltpu.VMEM((block, block), jnp.float32),
        ]
        + table_shapes(parts, units),
        compiler_params=pltpu.CompilerParams(vmem_limit_bytes=KERNEL_VMEM),
        cost_estimate=pl.CostEstimate(
            flops=50 * 10**9, bytes_accessed=16 << 20, transcendentals=20 * 10**6
        ),
        name="attend_back",
    )(lengths, query, key, value, out, log, grad)


def swap(value, grp_step, rep_step):
    groups, reps = lax.axis_size("grp"), lax.axis_size("rep")
    pairs = [
        (grp * reps + rep, (grp ^ grp_step) * reps + (rep ^ rep_step))
        for grp in range(groups)
        for rep in range(reps)
    ]
    return lax.ppermute(value, BOTH, pairs)


def ordered(flag, own, other, axis=0):
    return jnp.where(
        flag == 0,
        jnp.concatenate([own, other], axis=axis),
        jnp.concatenate([other, own], axis=axis),
    )


def pick(value, index, axis):
    return lax.dynamic_index_in_dim(value, index, axis, keepdims=False)


def halve(value, axis, bit, grp_step, rep_step):
    kept = pick(value, bit, axis)
    sent = pick(value, 1 - bit, axis).astype(jnp.bfloat16)
    arrived = swap(sent, grp_step, rep_step)
    return kept.astype(jnp.float32) + arrived.astype(jnp.float32)


def narrow(value):
    return value.astype(jnp.bfloat16)


MESH_IDS = pl.DeviceIdType.MESH


def flipped(index, step):
    return index + step - 2 * step * ((index // step) % 2)


def lowest(offset):
    return offset & -offset


def link_of(offset, part, turned):
    return turned.get((offset, part), lowest(offset))


GATHER_LINKS = {(14, 0): 4}
GATHER_PLAN = (
    ("rows", 4, 0), ("rows", 0, 1), ("rows", 4, 1), ("rows", 8, 0), ("rows", 8, 1),
    ("rows", 6, 0), ("rows", 2, 0), ("rows", 6, 1), ("project", 5), ("project", 0),
    ("project", 9), ("project", 4), ("rows", 10, 0), ("project", 6), ("project", 8),
    ("project", 1), ("rows", 12, 1), ("rows", 2, 1), ("project", 2), ("project", 7),
    ("rows", 12, 0), ("rows", 10, 1), ("project", 10), ("project", 3), ("project", 12),
    ("rows", 14, 0), ("project", 13), ("rows", 14, 1), ("project", 14), ("project", 11),
    ("project", 15),
)


def gather_kernel(
    tokens_ref,
    attn_gain,
    mlp_gain,
    w_query,
    w_key,
    w_value,
    w_gate,
    w_up,
    w_down,
    w_output,
    out_rows,
    normed_out,
    qkv_ref,
    weight_ref,
    gate_own,
    gate_met,
    up_ref,
    up_piece,
    down_first,
    down_second,
    output_ref,
    out_away,
    gains,
    qkv_at,
    gate_own_at,
    gate_met_at,
    up_at,
    up_piece_at,
    down_first_at,
    down_second_at,
    output_at,
    out_at,
    raw,
    normed,
    weight_sem,
    out_sem,
    send_sem,
    recv_sem,
    side_send,
    side_recv,
    stripe_sem,
    leave_sem,
):
    here, there = lax.axis_index("grp"), lax.axis_index("rep")
    core = there % 2
    reps = raw.shape[0]
    slots = normed.shape[0]
    row_count, width = raw.shape[2:]
    steps = [1 << place for place in range(reps.bit_length() - 1)]
    across = (1 - here, there)

    def neighbour(step):
        return (here, flipped(there, step))

    barrier = pltpu.get_barrier_semaphore()
    for target in [across] + [neighbour(step) for step in steps]:
        pl.semaphore_signal(barrier, inc=1, device_id=target, device_id_type=MESH_IDS)
    local = []
    for at, weight in enumerate((w_query, w_key, w_value)):
        local.append(
            pltpu.make_async_copy(
                weight.at[:, pl.ds(pl.multiple_of(there * LANES, LANES), LANES)],
                weight_ref.at[here, :, pl.ds(at * LANES, LANES)],
                weight_sem.at[at],
            )
        )
        local[-1].start()
    raw[0, 0] = tokens_ref[here]
    gains[here] = jnp.zeros(gains.shape[1:], jnp.float32)
    gains[here, 0:1, :] = attn_gain[...].astype(jnp.float32)
    gains[here, 1:2, :] = mlp_gain[...].astype(jnp.float32)
    pl.semaphore_wait(barrier, len(steps) + 1)

    def side(at, source, target_ref):
        return pltpu.make_async_remote_copy(
            src_ref=source,
            dst_ref=target_ref,
            send_sem=side_send.at[at],
            recv_sem=side_recv.at[at],
            device_id=across,
            device_id_type=MESH_IDS,
        )

    def rows_copy(offset, part):
        if offset == 0:
            return pltpu.make_async_remote_copy(
                src_ref=tokens_ref.at[1 - here],
                dst_ref=raw.at[0, 1],
                send_sem=send_sem.at[1],
                recv_sem=recv_sem.at[1],
                device_id=across,
                device_id_type=MESH_IDS,
            )
        step = link_of(offset, part, GATHER_LINKS)
        return pltpu.make_async_remote_copy(
            src_ref=raw.at[offset - step, part],
            dst_ref=raw.at[offset, part],
            send_sem=send_sem.at[2 * offset + part],
            recv_sem=recv_sem.at[2 * offset + part],
            device_id=neighbour(step),
            device_id_type=MESH_IDS,
        )

    order = [tuple(what) for kind, *what in GATHER_PLAN if kind == "rows"]
    copies = {
        (offset, part): rows_copy(offset, part)
        for offset in range(reps)
        for part in (0, 1)
        if offset or part
    }

    def pass_on(offset, part):
        for later, part_of in order:
            if later and part_of == part and later - link_of(later, part, GATHER_LINKS) == offset:
                copies[later, part].start()
        copies[offset + 1, part].start()

    gain_copy = side(0, gains.at[here], gains.at[here])
    gain_copy.start()
    copies[0, 1].start()
    pass_on(0, 0)
    for one in local:
        one.wait()
    weight_copy = side(1, weight_ref.at[here], weight_ref.at[here])
    weight_copy.start()

    stripes = [
        (grp, high, low)
        for grp in range(2)
        for high in range(reps // 8)
        for low in range(2)
    ]
    place = 4 * ((there // 4) % 2) + there % 2
    stripe_loads = []

    def load(source, target_ref):
        stripe_loads.append(
            pltpu.make_async_copy(source, target_ref, stripe_sem.at[len(stripe_loads)])
        )

    def columns_of(weight, grp, high, low):
        first = (grp * reps + 8 * high + 2 * low + place) * LANES
        return weight.at[:, pl.ds(pl.multiple_of(first, LANES), LANES)]

    for weight, target_ref in ((w_gate, gate_own_at), (w_up, up_at)):
        for at, stripe in enumerate(stripes):
            load(columns_of(weight, *stripe), target_ref.at[:, pl.ds(at * LANES, LANES)])
    for at, (grp, high, low) in enumerate(stripes[: len(stripes) // 2]):
        first = (8 * high + 2 * low + place) * LANES
        load(
            w_down.at[pl.ds(pl.multiple_of(first, LANES), LANES)],
            (down_first_at, down_second_at)[at // 2].at[pl.ds(at % 2 * LANES, LANES)],
        )
    piece_rows = up_piece.shape[0]
    low = (there // 2) % 2
    for at, stripe in enumerate(stripes):
        load(
            columns_of(w_up, *stripe).at[
                pl.ds(pl.multiple_of(low * piece_rows, piece_rows), piece_rows)
            ],
            up_piece_at.at[:, pl.ds(at * LANES, LANES)],
        )
    load(out_rows, out_at)
    for one in stripe_loads:
        one.start()
    quarter = output_ref.shape[0]
    output_copy = side(
        2,
        w_output.at[pl.ds(pl.multiple_of((there % 4) * quarter, quarter), quarter)],
        output_at,
    )
    output_copy.start()
    gate_copy = side(
        3, gate_own_at.at[pl.ds(pl.multiple_of(low * piece_rows, piece_rows), piece_rows)], gate_met_at
    )
    for one in stripe_loads[: len(stripes)]:
        one.wait()
    gate_copy.start()

    leaving = []

    def leave(at, source, target_ref):
        leaving.append(pltpu.make_async_copy(source, target_ref, leave_sem.at[at]))
        leaving[-1].start()

    written = {}
    used = [None] * slots
    tile = 32

    def project(count, offset):
        slot = count % slots
        if used[slot] is not None:
            written[used[slot]].wait()
        used[slot] = offset
        gain = jnp.concatenate([gains[0, 0:1], gains[1, 0:1]], axis=1)
        for part in range(2):

            def norm_rows(at, unused):
                cut = pl.ds(pl.multiple_of(at * tile, tile), tile)
                values = raw[offset, part, cut, :].astype(jnp.float32)
                scaled = values * rms_scale(values) * gain
                normed[slot, pl.ds(pl.multiple_of(part * row_count + at * tile, tile), tile), :] = (
                    scaled.astype(jnp.bfloat16)
                )
                return unused

            lax.fori_loop(0, row_count // tile, norm_rows, 0)
        written[offset] = pltpu.make_async_copy(
            normed.at[slot], normed_out.at[offset], out_sem.at[offset]
        )
        written[offset].start()
        half = width // 2
        product = jnp.dot(
            normed[slot, :, :half], weight_ref[0], preferred_element_type=jnp.float32
        ) + jnp.dot(normed[slot, :, half:], weight_ref[1], preferred_element_type=jnp.float32)
        qkv_at[pl.ds(2 * offset, 2)] = product.astype(jnp.bfloat16).reshape(
            2, row_count, 3 * LANES
        )
        leave(
            offset, qkv_at.at[pl.ds(2 * offset, 2)], qkv_ref.at[pl.ds(2 * offset, 2)]
        )

    count = 0
    for kind, *what in GATHER_PLAN:
        if kind == "rows":
            copies[tuple(what)].wait_recv()
            pass_on(*what)
            continue
        if count == 0:
            gain_copy.wait_recv()
            weight_copy.wait_recv()
        if what[0] % 2:
            for part in (0, 1):
                copies[what[0], part].wait_recv()
        project(count, what[0])
        count += 1
        if count == reps // 2:
            for one in stripe_loads[len(stripes) :]:
                one.wait()
            for at, pair in enumerate(
                (
                    (gate_own_at, gate_own),
                    (up_at, up_ref),
                    (up_piece_at, up_piece),
                    (down_first_at, down_first),
                    (down_second_at, down_second),
                    (out_at, out_away),
                )
            ):
                leave(reps + at, *pair)
    for offset in used:
        written[offset].wait()
    for one in copies.values():
        one.wait_send()
    gain_copy.wait_send()
    weight_copy.wait_send()
    output_copy.wait()
    leave(reps + 6, output_at, output_ref)
    gate_copy.wait()
    leave(reps + 7, gate_met_at, gate_met)
    for one in leaving:
        one.wait()


def gather_heads(
    tokens, gains, w_query, w_key, w_value, w_gate, w_up, w_down, w_output, out_rows
):
    reps = lax.axis_size("rep")
    _, row_count, width = tokens.shape
    half = width // 2
    own_width = reps // 2 * LANES
    vmem = pl.BlockSpec(memory_space=pltpu.VMEM)
    anywhere = pl.BlockSpec(memory_space=pl.ANY)
    return pl.pallas_call(
        gather_kernel,
        out_shape=(
            jax.ShapeDtypeStruct((reps, 2 * row_count, width), jnp.bfloat16),
            jax.ShapeDtypeStruct((2 * reps, row_count, 3 * LANES), jnp.bfloat16),
            jax.ShapeDtypeStruct((2, half, 3 * LANES), jnp.bfloat16),
            jax.ShapeDtypeStruct((half, own_width), jnp.bfloat16),
            jax.ShapeDtypeStruct((half // 2, own_width), jnp.bfloat16),
            jax.ShapeDtypeStruct((half, own_width), jnp.bfloat16),
            jax.ShapeDtypeStruct((half // 2, own_width), jnp.bfloat16),
            jax.ShapeDtypeStruct((own_width // 4, width), jnp.bfloat16),
            jax.ShapeDtypeStruct((own_width // 4, width), jnp.bfloat16),
            jax.ShapeDtypeStruct((half // 4, width), jnp.bfloat16),
            jax.ShapeDtypeStruct(out_rows.shape, jnp.bfloat16),
            jax.ShapeDtypeStruct((2, 8, half), jnp.float32),
        ),
        in_specs=[vmem, vmem, vmem] + [anywhere] * 8,
        out_specs=(anywhere, anywhere, vmem) + (anywhere,) * 8 + (vmem,),
        scratch_shapes=[
            pltpu.VMEM((2 * reps, row_count, 3 * LANES), jnp.bfloat16),
            pltpu.VMEM((half, own_width), jnp.bfloat16),
            pltpu.VMEM((half // 2, own_width), jnp.bfloat16),
            pltpu.VMEM((half, own_width), jnp.bfloat16),
            pltpu.VMEM((half // 2, own_width), jnp.bfloat16),
            pltpu.VMEM((own_width // 4, width), jnp.bfloat16),
            pltpu.VMEM((own_width // 4, width), jnp.bfloat16),
            pltpu.VMEM((half // 4, width), jnp.bfloat16),
            pltpu.VMEM(out_rows.shape, jnp.bfloat16),
            pltpu.VMEM((reps, 2, row_count, width), jnp.bfloat16),
            pltpu.VMEM((4, 2 * row_count, width), jnp.bfloat16),
            pltpu.SemaphoreType.DMA((3,)),
            pltpu.SemaphoreType.DMA((reps,)),
            pltpu.SemaphoreType.DMA((2 * reps,)),
            pltpu.SemaphoreType.DMA((2 * reps,)),
            pltpu.SemaphoreType.DMA((4,)),
            pltpu.SemaphoreType.DMA((4,)),
            pltpu.SemaphoreType.DMA((reps // 2 * 7 // 2 + 1,)),
            pltpu.SemaphoreType.DMA((reps + 8,)),
        ],
        compiler_params=pltpu.CompilerParams(
            vmem_limit_bytes=KERNEL_VMEM, collective_id=0, has_side_effects=True
        ),
        cost_estimate=pl.CostEstimate(
            flops=8 * 10**9, bytes_accessed=250 << 20, transcendentals=0
        ),
        name="gather_heads",
    )(tokens, gains[0][None], gains[1][None], w_query, w_key, w_value, w_gate, w_up, w_down, w_output, out_rows)


SCATTER_PLAN = (
    ("first", "down"), ("rows", 13, 0), ("rows", 15, 0), ("rows", 7, 0), ("first", "up"),
    ("first", "gate"), ("rows", 7, 1), ("first", "out"), ("rows", 14, 0), ("rows", 5, 1),
    ("rows", 12, 0), ("sum", "down"), ("rows", 11, 0), ("rows", 1, 0), ("weights", 2),
    ("rows", 11, 1), ("rows", 15, 1), ("weights", 1), ("sum", "up"), ("rows", 14, 1),
    ("weights", 1), ("rows", 6, 1), ("rows", 13, 1), ("rows", 10, 1), ("rows", 12, 1),
    ("rows", 9, 0), ("rows", 10, 0), ("weights", 1), ("rows", 5, 0), ("weights", 1),
    ("rows", 4, 1), ("rows", 3, 1), ("weights", 2), ("rows", 6, 0), ("rows", 9, 1),
    ("sum", "gate"), ("weights", 1), ("sum", "out"), ("rows", 2, 1), ("rows", 8, 1),
    ("rows", 3, 0), ("weights", 2), ("rows", 8, 0), ("weights", 1), ("rows", 2, 0),
    ("weights", 2), ("rows", 1, 1), ("sum", "quad"), ("rows", 4, 0), ("weights", 2),
    ("weights over",), ("sum", "out next"), ("rows", 0, 1), ("sum", "quad next"),
    ("weights out",), ("rows", 0, 0),
)
SCATTER_LINKS = {(14, 0): 4}


def scatter_kernel(
    back_ref,
    weight_ref,
    tokens_ref,
    mixed_grad,
    gain_ref,
    normed_ref,
    gate_kept,
    gate_met,
    up_kept,
    up_met,
    down_kept,
    down_met,
    output_kept,
    output_met,
    token_ref,
    pieces_ref,
    quad_ref,
    down_ref,
    output_ref,
    away,
    landed,
    grad_in,
    normed,
    back_t,
    weight_t,
    weights_total,
    half_out,
    half_in,
    piece_out,
    gate_away,
    gate_landed,
    up_away,
    up_landed,
    up_last,
    down_away,
    down_landed,
    down_last,
    output_away,
    output_landed,
    output_next,
    output_last,
    gate_stage,
    up_stage,
    wide_stage,
    gate_crossed,
    up_crossed,
    normed_sem,
    send_sem,
    recv_sem,
    side_send,
    side_recv,
    piece_send,
    piece_recv,
    stage_sem,
    sum_send,
    sum_recv,
):
    here, there = lax.axis_index("grp"), lax.axis_index("rep")
    reps, rows, columns = back_ref.shape
    row_count = rows // 2
    width = token_ref.shape[1]
    half = width // 2
    own_rows = half // reps
    steps = [1 << place for place in range(reps.bit_length() - 1)]
    bit = {step: (there // step) % 2 for step in steps}
    across = (1 - here, there)

    def other(offset):
        index = there
        for step in steps:
            if offset & step:
                index = flipped(index, step)
        return (here, index)

    barrier = pltpu.get_barrier_semaphore()
    for target in [across] + [other(offset) for offset in range(1, reps)]:
        pl.semaphore_signal(barrier, inc=1, device_id=target, device_id_type=MESH_IDS)

    slots = normed.shape[0]
    fetch = [
        pltpu.make_async_copy(normed_ref.at[offset], normed.at[offset % slots], normed_sem.at[offset])
        for offset in range(reps)
    ]
    for offset in range(slots):
        fetch[offset].start()

    def part_of(ref, axis, index):
        return ref.at[(slice(None),) * axis + (index,)]

    def load(at, source, target_ref):
        copy = pltpu.make_async_copy(source, target_ref, stage_sem.at[at])
        copy.start()
        return copy

    def open_half(at, kept, met, axis, flag, stage, target_ref):
        loads = [load(2 * at + 1, part_of(met, axis, flag), target_ref)]
        if stage is not None:
            loads.append(load(2 * at, part_of(kept, axis, flag), stage))
        return loads

    firsts = [
        open_half(0, down_kept, down_met, 1, 1 - bit[2], wide_stage, down_away),
        open_half(1, output_kept, output_met, 0, 1 - here, None, output_away),
        open_half(2, gate_kept, gate_met, 1, 1 - bit[2], gate_stage.at[0], gate_away),
        open_half(3, up_kept, up_met, 0, 1 - here, up_stage, up_away),
    ]

    for at in range(2):
        turned = jnp.transpose(weight_ref[at].astype(jnp.float32)).astype(jnp.bfloat16)
        weight_t[:, pl.ds(at * half, half)] = turned
    pl.semaphore_wait(barrier, reps)

    def add_to(target_ref, *sources):
        lead = target_ref.shape[:-2]
        count = 1
        for size in lead:
            count *= size
        for at in range(count):
            index, rest = [], at
            for size in lead[::-1]:
                index.insert(0, rest % size)
                rest //= size

            def some_rows(step, unused):
                place = tuple(index) + (pl.ds(pl.multiple_of(step * 16, 16), 16),)
                total = target_ref[place].astype(jnp.float32)
                for source in sources:
                    total = total + source[place].astype(jnp.float32)
                target_ref[place] = total.astype(target_ref.dtype)
                return unused

            lax.fori_loop(0, target_ref.shape[-2] // 16, some_rows, 0)

    def sum_copy(at, source, target_ref, target):
        return pltpu.make_async_remote_copy(
            src_ref=source,
            dst_ref=target_ref,
            send_sem=sum_send.at[at],
            recv_sem=sum_recv.at[at],
            device_id=target,
            device_id_type=MESH_IDS,
        )

    down_cross = sum_copy(0, down_away, down_landed, other(2))
    output_cross = sum_copy(1, output_away, output_landed, across)
    gate_low = sum_copy(2, gate_away, gate_landed, other(2))
    up_low = sum_copy(3, up_away, up_landed, across)
    down_high = sum_copy(4, down_landed.at[1 - bit[8]], down_last, other(8))
    up_high = sum_copy(5, up_landed.at[1 - bit[8]], up_last, other(8))
    output_low = sum_copy(6, output_landed.at[:, 1 - bit[2]], output_next, other(2))
    output_high = sum_copy(7, output_next.at[1 - bit[8]], output_last, other(8))
    quad_far = [
        sum_copy(8, gate_landed.at[1 - bit[4]], gate_crossed, other(4)),
        sum_copy(9, up_last.at[1 - bit[4]], up_crossed, other(4)),
    ]
    early_width = gate_crossed.shape[2]
    early = pl.ds(0, early_width)
    late = pl.ds(early_width, quad_ref.shape[3] - early_width)
    beside = 1 - bit[1]
    quad_near = [
        sum_copy(at, source, quad_ref.at[far, bit[1], :, cols], other(1))
        for at, source, far, cols in (
            (10, gate_landed.at[bit[4], beside], bit[4], early),
            (11, up_last.at[bit[4], beside], bit[4], late),
            (12, gate_crossed.at[beside], 1 - bit[4], early),
            (13, up_crossed.at[beside], 1 - bit[4], late),
        )
    ]
    def first_send(at, target_ref, stage, copy):
        for one in firsts[at]:
            one.wait()
        add_to(target_ref, stage)
        copy.start()

    def down_first():
        first_send(0, down_away, wide_stage, down_cross)
        firsts[1].append(load(2, part_of(output_kept, 0, 1 - here), wide_stage))

    def own_half(at, kept, met, axis, flag, stage_a, stage_b, copy, target_ref):
        loads = (
            load(2 * at, part_of(kept, axis, flag), stage_a),
            load(2 * at + 1, part_of(met, axis, flag), stage_b),
        )
        for one in loads:
            one.wait()
        copy.wait_recv()
        add_to(target_ref, stage_a, stage_b)

    def down_sum():
        down_cross.wait_send()
        own_half(
            0, down_kept, down_met, 1, bit[2], wide_stage, down_away, down_cross, down_landed
        )
        down_high.start()

    def output_sum():
        output_cross.wait_send()
        own_half(
            1, output_kept, output_met, 0, here, wide_stage, output_away, output_cross,
            output_landed,
        )
        output_low.start()

    def gate_sum():
        own_half(
            2, gate_kept, gate_met, 1, bit[2], gate_stage.at[0], gate_stage.at[1],
            gate_low, gate_landed,
        )

    def up_sum():
        up_low.wait_send()
        own_half(
            3, up_kept, up_met, 0, here, up_stage, up_away, up_low,
            up_landed,
        )
        up_high.start()

    def output_next_sum():
        output_low.wait_recv()
        add_to(output_next, output_landed.at[:, bit[2]])
        output_high.start()

    def quad_send():
        up_high.wait_recv()
        add_to(up_last, up_landed.at[bit[8]])
        for one in quad_far + quad_near[:2]:
            one.start()
        quad_ref[bit[4], bit[1], :, early] = gate_landed[bit[4], bit[1]]
        quad_ref[bit[4], bit[1], :, late] = up_last[bit[4], bit[1]]

    def quad_pass():
        for one in quad_far:
            one.wait_recv()
        for one in quad_near[2:]:
            one.start()
        quad_ref[1 - bit[4], bit[1], :, early] = gate_crossed[bit[1]]
        quad_ref[1 - bit[4], bit[1], :, late] = up_crossed[bit[1]]

    def last_sums():
        down_high.wait_recv()
        output_high.wait_recv()

        def down_rows(step, unused):
            cut = pl.ds(pl.multiple_of(step * 16, 16), 16)
            for at in range(down_last.shape[0]):
                down_ref[at, cut] = down_last[at, cut].astype(jnp.float32) + down_landed[
                    bit[8], at, cut
                ].astype(jnp.float32)
            output_ref[cut] = output_last[cut].astype(jnp.float32) + output_next[
                bit[8], cut
            ].astype(jnp.float32)
            return unused

        lax.fori_loop(0, own_rows // 16, down_rows, 0)

    def rows_copy(offset, part):
        if offset == 0:
            return pltpu.make_async_remote_copy(
                src_ref=away.at[0, 1],
                dst_ref=landed.at[0, 1],
                send_sem=send_sem.at[1],
                recv_sem=recv_sem.at[1],
                device_id=across,
                device_id_type=MESH_IDS,
            )
        return pltpu.make_async_remote_copy(
            src_ref=away.at[offset // 2, part],
            dst_ref=landed.at[offset, part],
            send_sem=send_sem.at[2 * offset + part],
            recv_sem=recv_sem.at[2 * offset + part],
            device_id=other(link_of(offset, part, SCATTER_LINKS)),
            device_id_type=MESH_IDS,
        )

    copies = {
        (offset, part): rows_copy(offset, part)
        for offset in range(reps)
        for part in (0, 1)
        if offset or part
    }

    def send(offset, part):
        sources = [
            later
            for later in range(1, reps)
            if later - link_of(later, part, SCATTER_LINKS) == offset
        ]
        for later in sources:
            copies[later, part].wait_recv()
        total = jnp.dot(
            back_ref[offset, pl.ds(part * row_count, row_count), :],
            weight_t[...],
            preferred_element_type=jnp.float32,
        )
        for later in sources:
            total = total + landed[later, part].astype(jnp.float32)
        if offset == 0 and part == 0:
            grad_in[...] = total
        else:
            if offset % 2 == 0:
                copies[offset + 1, part].wait_send()
            away[offset // 2, part] = total.astype(jnp.bfloat16)
            copies[offset, part].start()

    def weight_step(offset):
        fetch[offset].wait()
        back_t[...] = jnp.transpose(back_ref[offset].astype(jnp.float32)).astype(jnp.bfloat16)

        def columns_at(at, unused):
            cut = pl.ds(pl.multiple_of(at * 512, 512), 512)
            term = jnp.dot(
                back_t[...], normed[offset % slots, :, cut], preferred_element_type=jnp.float32
            )
            if offset == 0:
                weights_total[:, cut] = term
            else:
                weights_total[:, cut] += term
            return unused

        lax.fori_loop(0, width // 512, columns_at, 0)
        if offset + slots < reps:
            fetch[offset + slots].start()

    half_copy = pltpu.make_async_remote_copy(
        src_ref=half_out,
        dst_ref=half_in,
        send_sem=side_send,
        recv_sem=side_recv,
        device_id=across,
        device_id_type=MESH_IDS,
    )
    piece_copies = [
        pltpu.make_async_remote_copy(
            src_ref=piece_out.at[other(offset)[1]],
            dst_ref=pieces_ref.at[there],
            send_sem=piece_send.at[offset],
            recv_sem=piece_recv.at[offset],
            device_id=other(offset),
            device_id_type=MESH_IDS,
        )
        for offset in range(1, reps)
    ]

    def cross_weights():
        cut = pl.ds(pl.multiple_of((1 - here) * half, half), half)
        half_out[...] = weights_total[:, cut].astype(jnp.bfloat16)
        half_copy.start()

    def share_weights():
        half_copy.wait_recv()
        cut = pl.ds(pl.multiple_of(here * half, half), half)
        total = jnp.transpose(weights_total[:, cut] + half_in[...].astype(jnp.float32))
        piece_out[...] = total.astype(jnp.bfloat16).reshape(reps, own_rows, columns)
        pieces_ref[there] = piece_out[there]
        for one in piece_copies:
            one.start()

    weights = list(range(reps))

    def weight_steps(count):
        for _ in range(min(count, len(weights))):
            weight_step(weights.pop(0))

    firsts_by = {
        "down": down_first,
        "out": lambda: first_send(1, output_away, wide_stage, output_cross),
        "gate": lambda: first_send(2, gate_away, gate_stage.at[0], gate_low),
        "up": lambda: first_send(3, up_away, up_stage, up_low),
    }
    sums_by = {
        "down": down_sum,
        "out": output_sum,
        "gate": gate_sum,
        "up": up_sum,
        "out next": output_next_sum,
        "quad": quad_send,
        "quad next": quad_pass,
    }
    for kind, *what in SCATTER_PLAN:
        if kind == "rows":
            send(*what)
        elif kind == "weights":
            weight_steps(*what)
        elif kind == "first":
            firsts_by[what[0]]()
        elif kind == "sum":
            sums_by[what[0]]()
        elif kind == "weights over":
            cross_weights()
        else:
            share_weights()
    last_sums()
    copies[0, 1].wait_recv()

    tile = 32
    gain_row = jnp.concatenate([gain_ref[0, 0:1], gain_ref[1, 0:1]], axis=1)

    def norm_rows(grp, step, grad_rows):
        place = pl.ds(pl.multiple_of(grp * row_count + step * tile, tile), tile)
        values = tokens_ref[place, :].astype(jnp.float32)
        inverse = rms_scale(values)
        normed_rows = values * inverse
        weighted = grad_rows * gain_row
        token_ref[place, :] = (
            mixed_grad[place, :]
            + inverse
            * (weighted - normed_rows * jnp.mean(weighted * normed_rows, axis=-1, keepdims=True))
        ).astype(jnp.bfloat16)

    def norm_back(step, unused):
        cut = pl.ds(pl.multiple_of(step * tile, tile), tile)
        norm_rows(here, step, grad_in[cut, :])
        norm_rows(1 - here, step, landed[0, 1, cut, :].astype(jnp.float32))
        return unused

    lax.fori_loop(0, row_count // tile, norm_back, 0)
    for one in piece_copies:
        one.wait()
    for one in quad_near:
        one.wait_recv()
    half_copy.wait_send()
    for one in [gate_low, down_high, up_high, output_low, output_high] + quad_far + quad_near:
        one.wait_send()
    for (offset, part), one in copies.items():
        if offset % 2 == 0 or (offset == 1 and part == 0):
            one.wait_send()


def scatter_heads(back, weights, tokens, mixed_grad, gain, normed, sums):
    reps, rows, columns = back.shape
    width = normed.shape[2]
    row_count = rows // 2
    half = width // 2
    own_rows = half // reps
    vmem = pl.BlockSpec(memory_space=pltpu.VMEM)
    anywhere = pl.BlockSpec(memory_space=pl.ANY)
    low, full = jnp.bfloat16, jnp.float32
    wide = (2, 2, own_rows, width)
    thin = (2, 2, own_rows, sums[0].shape[-1])
    slim = (2, 2, 2, own_rows, sums[2].shape[-1])
    return pl.pallas_call(
        scatter_kernel,
        out_shape=(
            jax.ShapeDtypeStruct((rows, width), low),
            jax.ShapeDtypeStruct((reps, own_rows, columns), low),
            jax.ShapeDtypeStruct((2, 2, own_rows, width), low),
            jax.ShapeDtypeStruct(wide[1:], full),
            jax.ShapeDtypeStruct(wide[2:], full),
        ),
        in_specs=[vmem] * 5 + [anywhere] * 9,
        out_specs=(vmem,) * 5,
        scratch_shapes=[
            pltpu.VMEM((reps // 2, 2, row_count, width), low),
            pltpu.VMEM((reps, 2, row_count, width), low),
            pltpu.VMEM((row_count, width), full),
            pltpu.VMEM((2, rows, width), low),
            pltpu.VMEM((columns, rows), low),
            pltpu.VMEM((columns, width), low),
            pltpu.VMEM((columns, width), full),
            pltpu.VMEM((columns, half), low),
            pltpu.VMEM((columns, half), low),
            pltpu.VMEM((reps, own_rows, columns), low),
            pltpu.VMEM(thin, low),
            pltpu.VMEM(thin, low),
            pltpu.VMEM(slim, low),
            pltpu.VMEM(slim, low),
            pltpu.VMEM(slim[1:], low),
            pltpu.VMEM(wide, low),
            pltpu.VMEM(wide, low),
            pltpu.VMEM(wide[1:], low),
            pltpu.VMEM(wide, low),
            pltpu.VMEM(wide, low),
            pltpu.VMEM(wide[1:], low),
            pltpu.VMEM(wide[2:], low),
            pltpu.VMEM((2,) + thin, low),
            pltpu.VMEM(slim, low),
            pltpu.VMEM(wide, low),
            pltpu.VMEM(thin[1:], low),
            pltpu.VMEM(slim[2:], low),
            pltpu.SemaphoreType.DMA((reps,)),
            pltpu.SemaphoreType.DMA((2 * reps,)),
            pltpu.SemaphoreType.DMA((2 * reps,)),
            pltpu.SemaphoreType.DMA,
            pltpu.SemaphoreType.DMA,
            pltpu.SemaphoreType.DMA((reps,)),
            pltpu.SemaphoreType.DMA((reps,)),
            pltpu.SemaphoreType.DMA((8,)),
            pltpu.SemaphoreType.DMA((14,)),
            pltpu.SemaphoreType.DMA((14,)),
        ],
        compiler_params=pltpu.CompilerParams(
            vmem_limit_bytes=62 * 1024 * 1024, collective_id=1, has_side_effects=True
        ),
        cost_estimate=pl.CostEstimate(
            flops=14 * 10**9, bytes_accessed=250 << 20, transcendentals=0
        ),
        name="scatter_heads",
    )(back, weights, tokens, mixed_grad, gain, normed, *sums)


def finish_kernel(
    pieces_ref,
    quad_ref,
    down_ref,
    output_ref,
    token_ref,
    block_ref,
    gains_ref,
    w_query,
    w_key,
    w_value,
    w_gate,
    w_up,
    query_out,
    key_out,
    value_out,
    gate_out,
    up_out,
    sums_out,
    down_out,
    output_out,
    token_out,
    block_out,
    own_in,
    own_up,
    own_sem,
):
    reps, own_rows, _ = pieces_ref.shape
    width = query_out.shape[1]
    there = lax.axis_index("rep")
    own_cut = pl.ds(pl.multiple_of(there * own_rows, own_rows), own_rows)
    loads = [
        pltpu.make_async_copy(weight.at[own_cut], target_ref, own_sem.at[at])
        for at, (weight, target_ref) in enumerate(
            (
                (w_query, own_in.at[0]),
                (w_key, own_in.at[1]),
                (w_value, own_in.at[2]),
                (w_gate, own_up.at[0]),
                (w_up, own_up.at[1]),
            )
        )
    ]
    for one in loads:
        one.start()
    token_out[...] = token_ref[...]
    block_out[...] = block_ref[...]
    output_out[...] = output_ref[...]
    for half in range(2):
        down_out[pl.ds(half * own_rows, own_rows), :] = down_ref[half]
    for kind, target_ref in enumerate((query_out, key_out, value_out)):
        for place in range(reps):
            target_ref[:, place * LANES : (place + 1) * LANES] = pieces_ref[
                place, :, kind * LANES : (kind + 1) * LANES
            ].astype(jnp.float32)
    for kind, target_ref in enumerate((gate_out, up_out)):
        for at in range(reps // 2):
            source = (kind * (reps // 2) + at) * LANES
            for far in range(2):
                for near in range(2):
                    target = ((at // 2) * 8 + far * 4 + (at % 2) * 2 + near) * LANES
                    target_ref[:, target : target + LANES] = quad_ref[
                        far, near, :, source : source + LANES
                    ].astype(jnp.float32)
    for one in loads:
        one.wait()

    def rows_sum(pairs):
        total = jnp.zeros((own_rows, 1), jnp.float32)
        for grad, weight in pairs:
            total = total + jnp.sum(grad[...] * weight.astype(jnp.float32), axis=1, keepdims=True)
        return jnp.broadcast_to(total, (own_rows, LANES))

    sums_out[0] = (
        rows_sum(((query_out, own_in[0]), (key_out, own_in[1]), (value_out, own_in[2])))
        / gains_ref[0]
    )
    sums_out[1] = rows_sum(((gate_out, own_up[0]), (up_out, own_up[1]))) / gains_ref[1]


def finish(pieces, quad, down, output, token_grad, block_out, gains, owned):
    reps, own_rows, _ = pieces.shape
    rows, width = token_grad.shape
    hidden_width = owned[3].shape[1]
    vmem = pl.BlockSpec(memory_space=pltpu.VMEM)
    anywhere = pl.BlockSpec(memory_space=pl.ANY)
    low, full = jnp.bfloat16, jnp.float32
    narrow_rows = jax.ShapeDtypeStruct((own_rows, width), full)
    wide_rows = jax.ShapeDtypeStruct((own_rows, hidden_width), full)
    return pl.pallas_call(
        finish_kernel,
        out_shape=(
            narrow_rows,
            narrow_rows,
            narrow_rows,
            wide_rows,
            wide_rows,
            jax.ShapeDtypeStruct((2, own_rows, LANES), full),
            jax.ShapeDtypeStruct((2 * own_rows, width), full),
            narrow_rows,
            jax.ShapeDtypeStruct((rows, width), low),
            jax.ShapeDtypeStruct((rows, width), low),
        ),
        in_specs=[vmem] * 7 + [anywhere] * 5,
        out_specs=(vmem,) * 10,
        scratch_shapes=[
            pltpu.VMEM((3, own_rows, width), low),
            pltpu.VMEM((2, own_rows, hidden_width), low),
            pltpu.SemaphoreType.DMA((5,)),
        ],
        compiler_params=pltpu.CompilerParams(vmem_limit_bytes=KERNEL_VMEM),
        name="finish",
    )(pieces, quad, down, output, token_grad, block_out, gains, *owned)


def mlp_kernel(
    heads_ref,
    tokens_ref,
    gain_ref,
    out_rows,
    out_across,
    output_own,
    output_part,
    output_beside,
    gate_own,
    gate_met,
    gate_beside,
    up_own,
    up_other,
    down_first,
    down_second,
    down_other,
    block_ref,
    grad_ref,
    back_ref,
    gate_kept,
    gate_sent,
    late_kept,
    late_sent,
    down_kept,
    down_sent,
    output_kept,
    output_sent,
    gate_ref,
    mixed_ref,
    down_own_ref,
    down_far_landed,
    attended,
    branch_ref,
    returned,
    out_ref,
    mid_ref,
    hidden_ref,
    slope_ref,
    w_output,
    w_in,
    w_out,
    near_away,
    near_landed,
    far_away,
    far_landed,
    down_landed,
    load_sem,
    part_sem,
    send_sem,
    recv_sem,
    heads_send,
    heads_recv,
    back_send,
    back_recv,
    piece_sem,
    late_sem,
    gate_sem,
    place_sem,
    core_send,
    core_recv,
    free_sem,
):
    here, there = lax.axis_index("grp"), lax.axis_index("rep")
    across = (here, flipped(there, 4))
    sibling = (here, flipped(there, 1))
    groups, heads, row_count, _ = returned.shape
    rows, width = tokens_ref.shape
    half = width // 2
    quarter = half // 4
    own_width = w_out.shape[0]

    low = (there // 2) % 2
    up_rows = up_other.shape[0]

    def in_cut(part, first):
        cut = pl.ds(pl.multiple_of(part * up_rows, up_rows), up_rows)
        return w_in.at[1 - here, cut, pl.ds(first, own_width)]

    gain_row = jnp.concatenate([gain_ref[0, 1:2], gain_ref[1, 1:2]], axis=1)
    loads = [
        pltpu.make_async_copy(output_own, w_output.at[here], load_sem.at[0]),
        pltpu.make_async_copy(gate_own, w_in.at[here, :, pl.ds(0, own_width)], load_sem.at[1]),
        pltpu.make_async_copy(gate_met, in_cut(low, 0), load_sem.at[11]),
        pltpu.make_async_copy(gate_beside, in_cut(1 - low, 0), load_sem.at[12]),
        pltpu.make_async_copy(
            up_own, w_in.at[here, :, pl.ds(own_width, own_width)], load_sem.at[2]
        ),
        pltpu.make_async_copy(up_other, in_cut(low, own_width), load_sem.at[3]),
    ]
    own_part = own_width // 2

    early_rows = down_first.shape[0]
    late_rows = own_part - early_rows

    def down_cut(grp, first, count):
        return w_out.at[pl.ds(pl.multiple_of(grp * own_part + first, LANES), count)]

    loads += [
        pltpu.make_async_copy(down_first, down_cut(here, 0, early_rows), load_sem.at[4]),
        pltpu.make_async_copy(down_second, down_cut(here, early_rows, late_rows), load_sem.at[9]),
        pltpu.make_async_copy(down_other, down_cut(1 - here, 0, early_rows), load_sem.at[10]),
        pltpu.make_async_copy(out_rows.at[pl.ds(0, row_count)], out_ref.at[0, 0], load_sem.at[5]),
        pltpu.make_async_copy(
            out_rows.at[pl.ds(row_count, row_count)], out_ref.at[1, 0], load_sem.at[6]
        ),
        pltpu.make_async_copy(out_across.at[pl.ds(0, row_count)], out_ref.at[0, 2], load_sem.at[7]),
        pltpu.make_async_copy(
            out_across.at[pl.ds(row_count, row_count)], out_ref.at[1, 2], load_sem.at[8]
        ),
    ]
    place = there % 4
    core = there % 2

    def output_cut(part):
        return w_output.at[1 - here, pl.ds(pl.multiple_of(part * quarter, quarter), quarter)]

    output_pieces = ((output_part, place), (output_beside, flipped(place, 2)))
    rest = [
        pltpu.make_async_copy(piece, output_cut(part), part_sem.at[at])
        for at, (piece, part) in enumerate(output_pieces)
    ]
    loads = loads[:1] + rest + loads[1:]
    for one in loads:
        one.start()
    steps = [1 << place for place in range(heads.bit_length() - 1)]

    def other(crossing, offset):
        index = there
        for step in steps:
            if offset & step:
                index = flipped(index, step)
        return (1 - here if crossing else here, index)

    others = [
        (crossing, offset) for offset in range(heads) for crossing in (0, 1) if offset or crossing
    ]
    barrier = pltpu.get_barrier_semaphore()
    for key in others:
        pl.semaphore_signal(barrier, inc=1, device_id=other(*key), device_id_type=MESH_IDS)
    pl.semaphore_wait(barrier, len(others))

    facing = (1 - here, there)

    def copy(at, source, target_ref, target):
        return pltpu.make_async_remote_copy(
            src_ref=source,
            dst_ref=target_ref,
            send_sem=send_sem.at[at],
            recv_sem=recv_sem.at[at],
            device_id=target,
            device_id_type=MESH_IDS,
        )

    heads_copies, back_copies = [], []
    for at, key in enumerate(others):
        target = other(*key)
        heads_copies.append(
            pltpu.make_async_remote_copy(
                src_ref=heads_ref.at[target[0] * heads + target[1]],
                dst_ref=returned.at[here, there],
                send_sem=heads_send.at[at],
                recv_sem=heads_recv.at[at],
                device_id=target,
                device_id_type=MESH_IDS,
            )
        )
        back_copies.append(
            pltpu.make_async_remote_copy(
                src_ref=returned.at[target[0], target[1]],
                dst_ref=back_ref.at[here * heads + there],
                send_sem=back_send.at[at],
                recv_sem=back_recv.at[at],
                device_id=target,
                device_id_type=MESH_IDS,
            )
        )
    for one in heads_copies[::-1]:
        one.start()
    parts = range(groups)

    def rows_of(part):
        return pl.ds(part * row_count, row_count)

    output_near = [
        copy(at, piece, output_cut(part), sibling) for at, (piece, part) in enumerate(output_pieces)
    ]
    down_far = copy(2, down_second, down_cut(here, early_rows, late_rows), facing)
    up_beside = copy(26, up_other, in_cut(low, own_width), (here, flipped(there, 2)))
    out_near = [
        copy(3 + part, out_rows.at[rows_of(part)], out_ref.at[part, 1], sibling) for part in parts
    ]
    out_on = [
        copy(5 + part, out_across.at[rows_of(part)], out_ref.at[part, 3], sibling) for part in parts
    ]
    for one in output_near + out_near + out_on + [down_far, up_beside]:
        one.start()
    returned[here, there] = heads_ref[here * heads + there]

    early_width = gate_ref.shape[1]
    mid_near = [copy(7 + at, mid_ref.at[at, 0], mid_ref.at[at, 1], sibling) for at in parts]
    mid_far = [copy(9 + at, mid_ref.at[at, 0], mid_ref.at[at, 2], across) for at in parts]
    mid_on = [copy(11 + at, mid_ref.at[at, 2], mid_ref.at[at, 3], sibling) for at in parts]
    grad_near = {
        (side, at): copy(
            13 + 2 * side + at, near_away.at[side, at], near_landed.at[side, at], sibling
        )
        for side in range(2)
        for at in parts
    }
    grad_far = [copy(17 + at, far_away.at[at], far_landed.at[at], across) for at in parts]
    down_near = {
        (side, at): copy(
            19 + 2 * side + at, near_away.at[side, at], down_landed.at[side, at], sibling
        )
        for side in range(2)
        for at in parts
    }
    down_over = [
        copy(23 + at, down_own_ref.at[1, at], down_far_landed.at[at], across) for at in parts
    ]
    gate_cross = copy(25, w_in.at[1 - here, :, pl.ds(0, early_width)], gate_ref, facing)
    late_cut = pl.ds(early_width, 2 * own_width - early_width)
    late_block = late_kept.shape[1]

    def late_rows_of(at, bit):
        return pl.ds(pl.multiple_of((2 * at + bit) * late_block, late_block), late_block)

    up_outs = [
        pltpu.make_async_copy(
            w_in.at[at // 4, late_rows_of(at % 4, bit), late_cut], target_ref.at[at], late_sem.at[2 * at + kind]
        )
        for at in range(8)
        for kind, (target_ref, bit) in enumerate(((late_kept, low), (late_sent, 1 - low)))
    ]
    down_outs = [
        pltpu.make_async_copy(
            w_out.at[pl.ds(pl.multiple_of(grp * own_part, own_part), own_part)],
            target_ref,
            piece_sem.at[kind],
        )
        for kind, (target_ref, grp) in enumerate(((down_kept, here), (down_sent, 1 - here)))
    ]

    for one in heads_copies:
        one.wait()
    for group in range(groups):
        for head in range(heads):
            attended[
                group * row_count : (group + 1) * row_count, head * LANES : (head + 1) * LANES
            ] = returned[group, head]
    for one in loads[:3]:
        one.wait()
    for one in output_near:
        one.wait_recv()
    wide = 512

    def mix(at, unused):
        cut = pl.ds(pl.multiple_of(at * wide, wide), wide)
        mixed_ref[:, cut] = (
            tokens_ref[:, cut].astype(jnp.float32)
            + jnp.dot(attended[:, :half], w_output[0, :, cut], preferred_element_type=jnp.float32)
            + jnp.dot(attended[:, half:], w_output[1, :, cut], preferred_element_type=jnp.float32)
        )
        return unused

    lax.fori_loop(0, width // wide, mix, 0)
    tile = 32
    for part in parts:

        def norm_rows(at, unused):
            cut = pl.ds(pl.multiple_of(at * tile, tile), tile)
            values = mixed_ref[pl.ds(pl.multiple_of(part * row_count + at * tile, tile), tile), :]
            mid_ref[part, 0, cut, :] = (
                values * rms_scale(values) * gain_row
            ).astype(jnp.bfloat16)
            return unused

        lax.fori_loop(0, row_count // tile, norm_rows, 0)
        mid_far[part].start()
        mid_near[part].start()
    for one in loads[3:]:
        one.wait()
    up_beside.wait_recv()
    narrow_tile = 256
    per_half = own_part // narrow_tile
    every = (0, 1)

    def pair_rows(ref, side, part, cols):
        values = ref[part, pl.ds(2 * side, 2), :, cols]
        return values.reshape(rows, values.shape[2])

    def forward(side, part, halves):
        def columns(step, unused):
            at = jnp.where(step < per_half, halves[0] * per_half, halves[-1] * per_half - per_half)
            at = at + step
            cut = pl.ds(pl.multiple_of(at * narrow_tile, narrow_tile), narrow_tile)
            up_cut = pl.ds(pl.multiple_of(own_width + at * narrow_tile, narrow_tile), narrow_tile)
            low_rows = pair_rows(mid_ref, side, part, slice(0, half))
            high_rows = pair_rows(mid_ref, side, part, slice(half, width))

            def project(cols):
                return jnp.dot(
                    low_rows, w_in[0, :, cols], preferred_element_type=jnp.float32
                ) + jnp.dot(high_rows, w_in[1, :, cols], preferred_element_type=jnp.float32)

            gate_pre, up_pre = project(cut), project(up_cut)
            grad_hidden = contract(
                pair_rows(out_ref, side, part, slice(0, width)), w_out[cut, :], 1, 1
            )
            gate_sig = jax.nn.sigmoid(gate_pre)
            gate_silu = gate_pre * gate_sig

            def put(ref, cols, values):
                ref[part, pl.ds(2 * side, 2), :, cols] = values.astype(jnp.bfloat16).reshape(
                    2, row_count, narrow_tile
                )

            put(hidden_ref, cut, gate_silu * up_pre)
            put(
                slope_ref,
                cut,
                grad_hidden * up_pre * gate_sig * (1.0 + gate_pre * (1.0 - gate_sig)),
            )
            put(slope_ref, up_cut, grad_hidden * gate_silu)
            return unused

        lax.fori_loop(0, len(halves) * per_half, columns, 0)

    def backward(side, part):
        for at in range(2):

            def columns(step, unused):
                cut = pl.ds(pl.multiple_of(step * wide, wide), wide)
                whole = pl.ds(pl.multiple_of(at * half + step * wide, wide), wide)
                values = contract(
                    pair_rows(slope_ref, side, part, slice(0, 2 * own_width)),
                    w_in[at, cut, :],
                    1,
                    1,
                )
                near_away[side, part, :, whole] = values[row_count:].astype(jnp.bfloat16)
                if side == 0:
                    grad_ref[rows_of(part), whole] = values[:row_count]
                else:
                    far_away[part, :, whole] = values[:row_count].astype(jnp.bfloat16)
                return unused

            lax.fori_loop(0, half // wide, columns, 0)
        grad_near[side, part].start()

    def add_rows(target_ref, source_ref):
        def some_rows(at, unused):
            cut = pl.ds(pl.multiple_of(at * tile, tile), tile)
            target_ref[cut, :] = (
                target_ref[cut, :].astype(jnp.float32) + source_ref[cut, :].astype(jnp.float32)
            ).astype(target_ref.dtype)
            return unused

        lax.fori_loop(0, row_count // tile, some_rows, 0)

    def far_send(part):
        grad_near[1, part].wait_recv()
        add_rows(far_away.at[part], near_landed.at[1, part])
        grad_far[part].start()

    def down(side, part):
        grad_near[side, part].wait_send()

        def columns(step, unused):
            cut = pl.ds(pl.multiple_of(step * wide, wide), wide)
            values = jnp.dot(
                pair_rows(hidden_ref, side, part, slice(0, own_width)),
                w_out[:, cut],
                preferred_element_type=jnp.float32,
            ).astype(jnp.bfloat16)
            near_away[side, part, :, cut] = values[row_count:]
            down_own_ref[side, part, :, cut] = values[:row_count]
            return unused

        lax.fori_loop(0, width // wide, columns, 0)
        down_near[side, part].start()

    def down_meet(side, part):
        down_near[side, part].wait_recv()
        add_rows(down_own_ref.at[side, part], down_landed.at[side, part])

    for part in parts:
        mid_near[part].wait_recv()
        out_near[part].wait_recv()
        forward(0, part, (here,))
    for part in parts:
        mid_far[part].wait_recv()
        mid_on[part].start()
        if part == 0:
            down_far.wait_recv()
        else:
            forward(0, 0, (1 - here,))
            far_send(0)
        mid_on[part].wait_recv()
        out_on[part].wait_recv()
        forward(1, part, every)
        backward(1, part)
    forward(0, 1, (1 - here,))
    far_send(1)
    for part in parts:
        backward(0, part)

    def turned(values):
        flat = values.reshape(4 * rows, values.shape[3]).astype(jnp.float32)
        return jnp.transpose(flat).astype(jnp.bfloat16)

    def in_grads(at):
        def some_rows(step, unused):
            cut = pl.ds(pl.multiple_of(step * narrow_tile, narrow_tile), narrow_tile)
            source = pl.ds(pl.multiple_of(at * half + step * narrow_tile, narrow_tile), narrow_tile)
            left = turned(mid_ref[:, :, :, source])

            def columns(place_at, unused):
                cols = pl.ds(pl.multiple_of(place_at * wide, wide), wide)
                right = slope_ref[:, :, :, cols].reshape(4 * rows, wide)
                w_in[at, cut, cols] = jnp.dot(
                    left, right, preferred_element_type=jnp.float32
                ).astype(jnp.bfloat16)
                return unused

            return lax.fori_loop(0, 2 * own_width // wide, columns, unused)

        lax.fori_loop(0, half // narrow_tile, some_rows, 0)

    def down_rows(step, unused):
        cut = pl.ds(pl.multiple_of(step * narrow_tile, narrow_tile), narrow_tile)
        left = turned(hidden_ref[:, :, :, cut])

        def columns(place_at, unused):
            cols = pl.ds(pl.multiple_of(place_at * wide, wide), wide)
            right = out_ref[:, :, :, cols].reshape(4 * rows, wide)
            w_out[cut, cols] = jnp.dot(left, right, preferred_element_type=jnp.float32).astype(
                jnp.bfloat16
            )
            return unused

        return lax.fori_loop(0, width // wide, columns, unused)

    def finish(part):
        grad_near[0, part].wait_recv()
        grad_far[part].wait_recv()

        def norm_back(at, unused):
            cut = pl.ds(pl.multiple_of(at * tile, tile), tile)
            place = pl.ds(pl.multiple_of(part * row_count + at * tile, tile), tile)
            grad_mid = (
                grad_ref[place, :]
                + near_landed[0, part, cut, :].astype(jnp.float32)
                + far_landed[part, cut, :].astype(jnp.float32)
            )
            values = mixed_ref[place, :]
            inverse = rms_scale(values)
            normed = values * inverse
            weighted = grad_mid * gain_row
            grad = out_ref[part, 0, cut, :].astype(jnp.float32) + inverse * (
                weighted - normed * jnp.mean(weighted * normed, axis=-1, keepdims=True)
            )
            grad_ref[place, :] = grad
            branch_ref[place, :] = grad.astype(jnp.bfloat16)
            return unused

        lax.fori_loop(0, row_count // tile, norm_back, 0)
        for head in range(0, heads, 4):
            at = head * LANES // half
            start = head * LANES - at * half
            values = contract(
                branch_ref[rows_of(part), :],
                w_output[at, pl.ds(start, 4 * LANES), :],
                1,
                1,
                jnp.bfloat16,
            )
            for step in range(4):
                returned[part, head + step] = values[:, step * LANES : (step + 1) * LANES]
        for at, (crossing, _) in enumerate(others):

            @pl.when(jnp.where(crossing, 1 - here, here) == part)
            def _():
                back_copies[at].start()

    in_grads(1 - here)
    gate_cross.start()
    down(1, 0)
    finish(0)
    in_grads(here)
    for one in up_outs:
        one.start()
    for one in mid_near + mid_far + mid_on:
        one.wait_send()
    pl.semaphore_signal(free_sem, inc=1, device_id=sibling, device_id_type=MESH_IDS)
    finish(1)
    back_ref[here * heads + there] = returned[here, there]

    for at in range(2):

        def output_rows(step, unused):
            cut = pl.ds(pl.multiple_of(step * narrow_tile, narrow_tile), narrow_tile)
            source = pl.ds(pl.multiple_of(at * half + step * narrow_tile, narrow_tile), narrow_tile)
            left = jnp.transpose(attended[:, source].astype(jnp.float32)).astype(jnp.bfloat16)

            def columns(place_at, unused):
                cols = pl.ds(pl.multiple_of(place_at * wide, wide), wide)
                w_output[at, cut, cols] = jnp.dot(
                    left, branch_ref[:, cols], preferred_element_type=jnp.float32
                ).astype(jnp.bfloat16)
                return unused

            return lax.fori_loop(0, width // wide, columns, unused)

        lax.fori_loop(0, half // narrow_tile, output_rows, 0)

    own_rows = half // heads
    stripes = heads // 2
    pl.semaphore_wait(free_sem, 1)

    def stripe_of(at, bit):
        first = (at % stripes * 2 + bit) * own_rows
        return pl.ds(pl.multiple_of(first, own_rows), own_rows)

    def landed_at(at):
        per_slot = row_count // own_rows
        slot = at // per_slot
        return (slot // 4, slot % 4, pl.ds(at % per_slot * own_rows, own_rows))

    core_copies = []
    for at in range(2 * stripes):
        core_copies.append(
            pltpu.make_async_remote_copy(
                src_ref=w_output.at[at // stripes, stripe_of(at, 1 - core)],
                dst_ref=mid_ref.at[landed_at(at)],
                send_sem=core_send.at[at],
                recv_sem=core_recv.at[at],
                device_id=sibling,
                device_id_type=MESH_IDS,
            )
        )
        core_copies[-1].start()
    down(1, 1)
    for part in parts:
        down_meet(1, part)
        down_over[part].start()
    for part in parts:
        down(0, part)
    lax.fori_loop(0, own_width // narrow_tile, down_rows, 0)
    for one in down_outs:
        one.start()
    gate_cross.wait()

    def add_gate(at, unused):
        cut = pl.ds(pl.multiple_of(at * tile, tile), tile)
        gate_ref[cut, :] = (
            gate_ref[cut, :].astype(jnp.float32)
            + w_in[here, cut, pl.ds(0, early_width)].astype(jnp.float32)
        ).astype(jnp.bfloat16)
        return unused

    lax.fori_loop(0, half // tile, add_gate, 0)
    gate_outs = []
    for kind, (target_ref, flag) in enumerate(
        ((gate_kept, there // 8 % 2), (gate_sent, 1 - there // 8 % 2))
    ):
        cut = pl.ds(pl.multiple_of(flag * (half // 2), half // 2), half // 2)
        gate_outs.append(pltpu.make_async_copy(gate_ref.at[cut], target_ref, gate_sem.at[kind]))
        gate_outs[-1].start()
    far_bit = (there // 4) % 2
    output_outs = []
    for at in range(2 * stripes):
        core_copies[at].wait_recv()
        own = stripe_of(at, core)
        w_output[at // stripes, own, :] = (
            w_output[at // stripes, own, :].astype(jnp.float32)
            + mid_ref[landed_at(at)].astype(jnp.float32)
        ).astype(jnp.bfloat16)
    for at in range(stripes):
        grp, high, low_bit = at // (stripes // 2), at // 2 % (stripes // 4), at % 2
        for kind, (target_ref, bit) in enumerate(
            ((output_kept, far_bit), (output_sent, 1 - far_bit))
        ):
            first = ((high * 4 + bit * 2 + low_bit) * 2 + core) * own_rows
            cut = pl.ds(pl.multiple_of(first, own_rows), own_rows)
            output_outs.append(
                pltpu.make_async_copy(
                    w_output.at[grp, cut], target_ref.at[at], place_sem.at[2 * at + kind]
                )
            )
            output_outs[-1].start()
    for part in parts:
        down_meet(0, part)
        down_over[part].wait_recv()

        def block_rows(at, unused):
            cut = pl.ds(pl.multiple_of(at * tile, tile), tile)
            place = pl.ds(pl.multiple_of(part * row_count + at * tile, tile), tile)
            block_ref[place, :] = (
                mixed_ref[place, :]
                + down_own_ref[0, part, cut, :].astype(jnp.float32)
                + down_far_landed[part, cut, :].astype(jnp.float32)
            ).astype(jnp.bfloat16)
            return unused

        lax.fori_loop(0, row_count // tile, block_rows, 0)
    for one in up_outs + down_outs + output_outs + gate_outs:
        one.wait()
    for one in back_copies:
        one.wait()
    for one in grad_far + out_near + out_on + down_over + [down_far, up_beside]:
        one.wait_send()
    for one in list(down_near.values()) + output_near + core_copies:
        one.wait_send()


def mlp(heads, tokens, gain, out_rows, out_across, output_parts, in_parts, down_parts):
    count, row_count, _ = heads.shape
    groups, reps = lax.axis_size("grp"), lax.axis_size("rep")
    rows, width = tokens.shape
    half = width // 2
    own_width = in_parts[0].shape[1]
    early_width = own_width * 6 // 8
    vmem = pl.BlockSpec(memory_space=pltpu.VMEM)
    anywhere = pl.BlockSpec(memory_space=pl.ANY)
    low, full = jnp.bfloat16, jnp.float32
    others = pltpu.SemaphoreType.DMA((count - 1,))
    return pl.pallas_call(
        mlp_kernel,
        out_shape=(
            jax.ShapeDtypeStruct((rows, width), low),
            jax.ShapeDtypeStruct((rows, width), full),
            jax.ShapeDtypeStruct((count, row_count, LANES), low),
            jax.ShapeDtypeStruct((half // 2, early_width), low),
            jax.ShapeDtypeStruct((half // 2, early_width), low),
            jax.ShapeDtypeStruct((8, half // 8, 2 * own_width - early_width), low),
            jax.ShapeDtypeStruct((8, half // 8, 2 * own_width - early_width), low),
            jax.ShapeDtypeStruct((own_width // 2, width), low),
            jax.ShapeDtypeStruct((own_width // 2, width), low),
            jax.ShapeDtypeStruct((reps // 2, half // reps, width), low),
            jax.ShapeDtypeStruct((reps // 2, half // reps, width), low),
        ),
        in_specs=[vmem] * 3 + [anywhere] * 13,
        out_specs=(vmem,) * 3 + (anywhere,) * 8,
        scratch_shapes=[
            pltpu.VMEM((half, early_width), low),
            pltpu.VMEM((rows, width), full),
            pltpu.VMEM((2, 2, row_count, width), low),
            pltpu.VMEM((2, row_count, width), low),
            pltpu.VMEM((rows, width), low),
            pltpu.VMEM((rows, width), low),
            pltpu.VMEM((groups, reps, row_count, LANES), low),
            pltpu.VMEM((groups, 4, row_count, width), low),
            pltpu.VMEM((groups, 4, row_count, width), low),
            pltpu.VMEM((groups, 4, row_count, own_width), low),
            pltpu.VMEM((groups, 4, row_count, 2 * own_width), low),
            pltpu.VMEM((2, half, width), low),
            pltpu.VMEM((2, half, 2 * own_width), low),
            pltpu.VMEM((own_width, width), low),
            pltpu.VMEM((2, 2, row_count, width), low),
            pltpu.VMEM((2, 2, row_count, width), low),
            pltpu.VMEM((2, row_count, width), low),
            pltpu.VMEM((2, row_count, width), low),
            pltpu.VMEM((2, 2, row_count, width), low),
            pltpu.SemaphoreType.DMA((13,)),
            pltpu.SemaphoreType.DMA((2,)),
            pltpu.SemaphoreType.DMA((27,)),
            pltpu.SemaphoreType.DMA((27,)),
            others,
            others,
            others,
            others,
            pltpu.SemaphoreType.DMA((2,)),
            pltpu.SemaphoreType.DMA((16,)),
            pltpu.SemaphoreType.DMA((2,)),
            pltpu.SemaphoreType.DMA((reps,)),
            pltpu.SemaphoreType.DMA((reps,)),
            pltpu.SemaphoreType.DMA((reps,)),
            pltpu.SemaphoreType.REGULAR,
        ],
        compiler_params=pltpu.CompilerParams(
            vmem_limit_bytes=62 * 1024 * 1024, collective_id=2, has_side_effects=True
        ),
        cost_estimate=pl.CostEstimate(
            flops=150 * 10**9, bytes_accessed=150 << 20, transcendentals=0
        ),
        name="mlp",
    )(heads, tokens, gain, out_rows, out_across, *output_parts, *in_parts, *down_parts)


def after_kernel(*refs):
    pass


def after(values, ahead):
    anywhere = pl.BlockSpec(memory_space=pl.ANY)
    return pl.pallas_call(
        after_kernel,
        out_shape=tuple(jax.ShapeDtypeStruct(one.shape, one.dtype) for one in values),
        in_specs=[anywhere] * (len(values) + 1),
        out_specs=(anywhere,) * len(values),
        input_output_aliases={at: at for at in range(len(values))},
        name="after",
    )(*values, ahead)


def heads_body(
    tokens,
    attn_gain,
    w_query,
    w_key,
    w_value,
    w_output,
    mlp_gain,
    w_gate,
    w_up,
    w_down,
    out_grad,
    lengths,
):
    groups, reps = lax.axis_size("grp"), lax.axis_size("rep")
    here, there = lax.axis_index("grp"), lax.axis_index("rep")
    micro_count, row_count, width = tokens.shape
    rows = micro_count * row_count
    hidden_width = w_gate.shape[1]
    own_width = hidden_width // (2 * groups)

    out_rows = out_grad.reshape(rows, width)
    (
        gathered_rows,
        qkv,
        w_heads,
        gate_own,
        gate_met,
        up_own,
        up_piece,
        down_first,
        down_second,
        output_part,
        out_own,
        gains,
    ) = gather_heads(
        tokens,
        (attn_gain, mlp_gain),
        w_query,
        w_key,
        w_value,
        w_gate,
        w_up,
        w_down,
        w_output,
        out_rows,
    )

    output_parts = (w_output, output_part, swap(output_part, 0, 2))
    in_parts = (gate_own, gate_met, swap(gate_met, 0, 2), up_own, swap(up_piece, 1, 0))
    down_parts = (down_first, down_second, swap(down_first, 1, 0))

    attended, out_heads, log_sum, query, key, value = attend(lengths, qkv)
    (
        block_out,
        grad_mixed,
        grad_heads,
        gate_kept,
        gate_sent,
        late_kept,
        late_sent,
        down_kept,
        down_sent,
        output_kept,
        output_sent,
    ) = mlp(
        attended,
        tokens.reshape(rows, width),
        gains,
        out_rows,
        swap(out_own, 0, 4),
        output_parts,
        in_parts,
        down_parts,
    )

    own_rows = width // (groups * reps)
    by_owner = (2, 2, 2, 2, own_rows, -1)
    sums = (
        swap(gate_sent, 0, 8),
        swap(late_sent, 0, 2),
        swap(down_sent, 1, 0),
        swap(output_sent, 0, 4),
    )
    back = attend_back(lengths, query, key, value, out_heads, log_sum, grad_heads)
    gate_met, late_met, down_met, output_met = after(sums, back)
    token_grad, heads_grad, quad_grad, down_grad, output_grad = scatter_heads(
        back.reshape(reps, groups * row_count, 3 * LANES),
        w_heads,
        tokens.reshape(rows, width),
        grad_mixed,
        gains,
        gathered_rows,
        (
            gate_kept.reshape(by_owner[1:]),
            gate_met.reshape(by_owner[1:]),
            late_kept.reshape(by_owner),
            late_met.reshape(by_owner),
            down_kept.reshape(2, 2, 2, own_rows, width),
            down_met.reshape(2, 2, 2, own_rows, width),
            output_kept.reshape(2, 2, 2, own_rows, width),
            output_met.reshape(2, 2, 2, own_rows, width),
        ),
    )

    def own_gain(gain):
        own = lax.dynamic_slice_in_dim(gain, there * own_rows, own_rows, axis=0)
        return jnp.broadcast_to(own.astype(jnp.float32)[:, None], (own_rows, LANES))

    (
        query_grad,
        key_grad,
        value_grad,
        gate_grad,
        up_grad,
        gain_sums,
        down_grad,
        output_grad,
        token_grad,
        block_out,
    ) = finish(
        heads_grad,
        quad_grad,
        down_grad,
        output_grad,
        token_grad,
        block_out,
        jnp.stack([own_gain(attn_gain), own_gain(mlp_gain)], axis=0),
        (w_query, w_key, w_value, w_gate, w_up),
    )
    block_shape = tokens.shape
    return (
        block_out.reshape(block_shape),
        token_grad.reshape(block_shape),
        gain_sums[0, :, 0],
        query_grad,
        key_grad,
        value_grad,
        output_grad,
        gain_sums[1, :, 0],
        gate_grad,
        up_grad,
        down_grad,
    )


def pick_body(*arrays):
    tokens = arrays[0]
    groups, reps = lax.axis_size("grp"), lax.axis_size("rep")
    fits = (
        groups == 2
        and tokens.shape[0] == groups
        and tokens.shape[2] == reps * LANES
        and reps == 16
        and reps & (reps - 1) == 0
        and tokens.shape[1] % UNIT_PAIR == 0
        and arrays[7].shape[1] == groups * reps * LANES
    )
    return heads_body(*arrays) if fits else ring_body(*arrays)


def solution(mesh):
    in_specs = (
        P(None, ("grp", "rep"), None),
        P("grp"),
        P("grp", None),
        P("grp", None),
        P("grp", None),
        P("grp", None),
        P("grp"),
        P("grp", None),
        P("grp", None),
        P("grp", None),
        P(None, ("grp", "rep"), None),
        P(),
    )
    out_specs = (
        P(None, ("grp", "rep"), None),
        P(None, ("grp", "rep"), None),
        P(("grp", "rep")),
        P(("grp", "rep"), None),
        P(("grp", "rep"), None),
        P(("grp", "rep"), None),
        P(("grp", "rep"), None),
        P(("grp", "rep")),
        P(("grp", "rep"), None),
        P(("grp", "rep"), None),
        P(("grp", "rep"), None),
    )
    return jax.shard_map(pick_body, mesh=mesh, in_specs=in_specs, out_specs=out_specs, check_vma=False)
```
